32 devices in a mesh: group: 2 (over y), ep: 8 (over z, core), tp: 2 (over x).
Axes of the slice: x: 2, y: 2, z: 4, core: 2. Of those that a mesh axis runs over, the one named last changes fastest.
Arguments:
- layer_input: bfloat16 [2048, 4096], P(('group', 'ep'), 'tp'), parts along dimension 0, may hold values from -6 to 6
- stream: bfloat16 [2048, 4096], P(('group', 'ep'), 'tp'), parts along dimension 0, may hold values from -6 to 6
- expert_ids: int32 [2048, 8], P(('group', 'ep')), parts along dimension 0, may hold values from 0 to 15, all different within a row; in each aligned block of 128 rows (0 to 127, 128 to 255, ...) at most 96 rows name the same one
- kv_owner: int32 [2048, 1], P(('group', 'ep')), parts along dimension 0, may hold values from 0 to 1; in each aligned block of 128 rows (0 to 127, 128 to 255, ...) at most 128 rows name the same one
- attn_norm: bfloat16 [4096], P('tp'), may hold values from 0.099609375 to 1.8984375
- moe_norm: bfloat16 [4096], P('tp'), may hold values from 0.099609375 to 1.8984375
- k_norm: bfloat16 [128], replicated, may hold values from 0.099609375 to 1.8984375
- w_kv: bfloat16 [4096, 1024], P('tp'), may hold values from -0.09375 to 0.09375
- router: bfloat16 [4096, 16], P('tp')
- w_gate: bfloat16 [16, 4096, 1536], P('ep', None, 'tp'), may hold values from -0.09375 to 0.09375
- w_up: bfloat16 [16, 4096, 1536], P('ep', None, 'tp'), may hold values from -0.09375 to 0.09375
- w_down: bfloat16 [16, 1536, 4096], P('ep', 'tp'), may hold values from -0.21875 to 0.21875
Outputs:
- moe_out: bfloat16 [2048, 4096], P(('group', 'ep'), 'tp'), parts along dimension 0
- kv_cache: bfloat16 [16, 2, 128, 1024], P(('group', 'ep'), 'tp'), parts along dimension 0
The draws below stay inside these ranges and needn't reach their ends.
There are 2 independent parts, one for each index of `group`. The reference program is written for one: setup_inputs(seed, part) draws one part's arguments, and reference() takes and returns one part's arrays. A program takes and returns all parts, laid end to end along the dimension named above; an argument that names none is the same for every part. Nothing has to cross between parts.
Inputs may be any that keep to these rules, and one draw needn't show every extreme that they name: `expert_ids`: each row names 8 different experts. Among the 128 rows of one index of ep no expert is named more than 96 times, a bound that some block reaches. `kv_owner`: among the 128 rows of one index of ep no owner is named more than 128 times, a bound that some block reaches.
All inputs are finite; a program needn't handle non-finite values.
Results may differ from the reference program's by a relative error of at most 0.012.
Values may be sent and summed in bfloat16 or wider, within the bound.
No kernel may reach another device: no remote copies, remote signals or barrier semaphores. Data moves between devices by JAX's collectives and lax.ppermute only.
A program may use at most 192 MiB of HBM per device.

```python
import math
import jax
import jax.numpy as jnp
import numpy as np
from jax import lax

D = 4096
FF = 1536
KVH = 4
HD = 128
TOPK = 8
TOK_DEV = 128
EXPERTS = 16
TOKENS = 1024
CAP = 96
KV_CAP = 128
N_EP = 8
N_TP = 2


def draw_router(key, part):
    key = jax.random.fold_in(key, 7)
    base = jax.random.normal(key, (D, EXPERTS), jnp.float32) / math.sqrt(D)
    scale_key = jax.random.fold_in(key, 11)
    scale = jnp.exp(jax.random.uniform(scale_key, (1, EXPERTS), jnp.float32, math.log(0.3), math.log(0.8)))
    return (base * scale).astype(jnp.bfloat16)


def raised(result, own_key, source, target, blocks, factor):
    owner, partner = [(jnp.arange(result.shape[position]) // (result.shape[position] // blocks)).reshape([-1 if axis == position else 1 for axis in range(result.ndim)]) for position in (source, target)]
    chosen = jax.random.permutation(own_key, blocks)[partner]
    strong = (owner == chosen) | (owner == (partner + blocks // 2) % blocks)
    return jnp.where(strong, factor * result, result)


def block_scale(stream_key, dims, shards, least, top_value):
    factor_of = 1.0
    for dim, blocks in shards:
        steps = jax.random.uniform(jax.random.fold_in(jax.random.fold_in(stream_key, 6), dim), (blocks,), jnp.float32, least / len(shards), top_value / len(shards))
        factor_of = factor_of * jnp.repeat(jnp.exp(steps), dims[dim] // blocks).reshape((-1,) + (1,) * (len(dims) - 1 - dim))
    return factor_of


def routed_block(own_key, own, number, rows, number_of, top, reach, lean):
    ranking = jax.random.permutation(own_key, number_of)
    packed, usual = portions_of(number_of, rows * top, reach, lean, True), portions_of(number_of, rows * top, reach, lean, False)
    places = jnp.arange(number_of)

    def named(lengths, turn):
        used = int((lengths > 0).sum())
        fixed = max(1, used // 4)
        shifted = fixed + (places - fixed + turn * (used - fixed)) % max(1, number_of - fixed)
        return jnp.zeros((number_of,), jnp.int32).at[ranking[jnp.where(places < fixed, places, shifted)]].set(jnp.asarray(lengths, jnp.int32))

    lengths = jnp.where(number % 4 == 0, named(packed, number // 4), named(usual, number - number // 4 - 1))
    mixed = jax.random.permutation(jax.random.fold_in(own, 3), number_of)
    source_of, sink = mixed[0:number_of // 2 * 2:2], mixed[1:number_of // 2 * 2:2]
    margin = jnp.minimum(lengths[source_of] - 1, reach - lengths[sink]) // 2
    margin = jnp.where((source_of == ranking[0]) | (sink == ranking[0]) | (lengths[sink] == 0), 0, jnp.maximum(margin, 0))
    shifted = jax.random.randint(jax.random.fold_in(own, 4), (number_of // 2,), 0, 1 << 20) % (margin + 1)
    lengths = lengths.at[source_of].add(-shifted).at[sink].add(shifted)
    items = jnp.searchsorted(jnp.cumsum(lengths), jnp.arange(rows * top), side="right").astype(jnp.int32)
    grid = items.reshape(top, rows).T
    grid = grid[jax.random.permutation(jax.random.fold_in(own, 1), rows)]
    turn = jax.random.randint(jax.random.fold_in(own, 2), (rows, 1), 0, top)
    return jnp.take_along_axis(grid, (jnp.arange(top)[None, :] + turn) % top, axis=1)


def portions_of(count, total, bound, skew, full):
    portions = [(1 << 20) // math.isqrt(standing ** skew) + 1 for standing in range(1, count + 1)]
    largest = bound if full else min(bound, max(-(-total // count), total * portions[0] // sum(portions)))
    least = 1 if total - largest >= count - 1 else 0
    given, rest = [largest] + [least] * (count - 1), total - largest - least * (count - 1)
    while rest > 0:
        candidates = [i for i in range(1, count) if given[i] < largest] or [i for i in range(1, count) if given[i] < bound]
        whole, left = sum([portions[i] for i in candidates]), rest
        for i in candidates:
            extra = min(bound - given[i], max(1, left * portions[i] // whole), rest)
            given[i] = given[i] + extra
            rest = rest - extra
    return np.array(given)


def gaussian(stream_key, shape, deviation, bound, split=(), held_as=jnp.bfloat16):
    gain = block_scale(stream_key, shape, split, -0.22, 0.18) if split else 1.0
    values = jax.random.normal(stream_key, shape, jnp.float32) * deviation * gain
    return jnp.minimum(jnp.maximum(values, -bound), bound).astype(held_as)


def bell_draw_with(rng, extent, deviation, reach, split, heavy, held_as=jnp.bfloat16):
    entries = deviation * jax.random.normal(rng, extent, jnp.float32)
    if split:
        entries = entries * block_scale(rng, extent, split, -0.22, 0.18)
    return jnp.clip(raised(entries, jax.random.fold_in(rng, 3), *heavy), -reach, reach).astype(held_as)


def setup_inputs(seed: int = 0, part: int = 0) -> dict:
    splits = jax.random.split(jax.random.key(seed), 13)
    part_splits = jax.random.split(jax.random.fold_in(splits[12], part), 13)
    layer_input = gaussian(part_splits[0], (TOKENS, D), 1.0, 6.0, ((0, 8), (1, 2)))
    stream = gaussian(part_splits[1], (TOKENS, D), 1.0, 6.0, ((0, 8), (1, 2)))
    expert_ids_keys = jax.random.split(jax.random.fold_in(part_splits[2], 1), TOKENS // TOK_DEV)
    expert_ids_turns = jax.random.permutation(jax.random.fold_in(part_splits[2], 3), TOKENS // TOK_DEV)
    expert_ids = jax.vmap(lambda own, number: routed_block(jax.random.fold_in(part_splits[2], 2), own, number, TOK_DEV, EXPERTS, TOPK, CAP, 2))(expert_ids_keys, expert_ids_turns).reshape((TOKENS, TOPK))
    kv_owner_keys = jax.random.split(jax.random.fold_in(part_splits[3], 1), TOKENS // TOK_DEV)
    kv_owner_turns = jax.random.permutation(jax.random.fold_in(part_splits[3], 3), TOKENS // TOK_DEV)
    kv_owner = jax.vmap(lambda own, number: routed_block(jax.random.fold_in(part_splits[3], 2), own, number, TOK_DEV, N_TP, 1, KV_CAP, 1))(kv_owner_keys, kv_owner_turns).reshape((TOKENS, 1))
    attn_norm = jnp.clip(1.0 + 0.18 * jax.random.normal(splits[4], (D,), jnp.float32), 0.099609375, 1.8984375).astype(jnp.bfloat16)
    moe_norm = jnp.clip(1.0 + 0.18 * jax.random.normal(splits[5], (D,), jnp.float32), 0.099609375, 1.8984375).astype(jnp.bfloat16)
    k_norm = jnp.clip(1.0 + 0.18 * jax.random.normal(splits[6], (HD,), jnp.float32), 0.099609375, 1.8984375).astype(jnp.bfloat16)
    w_kv = gaussian(splits[7], (D, 2 * KVH * HD), D ** -0.5, 0.09375, ((0, 2),))
    router = draw_router(jax.random.fold_in(splits[12], 71), part)
    w_gate = gaussian(splits[9], (EXPERTS, D, FF), D ** -0.5, 0.09375, ((0, 8), (2, 2)))
    w_up = gaussian(splits[10], (EXPERTS, D, FF), D ** -0.5, 0.09375, ((0, 8), (2, 2)))
    w_down = bell_draw_with(splits[11], (EXPERTS, FF, D), FF ** -0.5, 0.21875, ((0, 8), (1, 2)), (1, 2, 2, 2.0))
    return {"layer_input": layer_input, "stream": stream, "expert_ids": expert_ids, "kv_owner": kv_owner, "attn_norm": attn_norm, "moe_norm": moe_norm, "k_norm": k_norm, "w_kv": w_kv, "router": router, "w_gate": w_gate, "w_up": w_up, "w_down": w_down}


EPS = 1e-06

def run_expert(args):
    rows, gate_w, up_w, down_w = args
    flat = rows.reshape(N_EP * CAP, D)
    gate = jnp.dot(flat, gate_w, preferred_element_type=jnp.float32)
    up = jnp.dot(flat, up_w, preferred_element_type=jnp.float32)
    hidden = (jax.nn.silu(gate) * up).astype(jnp.bfloat16)
    blocks = hidden.reshape(N_EP * CAP, N_TP, FF // N_TP).astype(jnp.float32)
    weights = down_w.reshape(N_TP, FF // N_TP, D).astype(jnp.float32)
    parts = jnp.einsum('rnf,nfd->rnd', blocks, weights).astype(jnp.bfloat16)
    total = lax.optimization_barrier(jnp.sum(parts.astype(jnp.float32), 1)).astype(jnp.bfloat16)
    return total.reshape(N_EP, CAP, D)

def reference(layer_input, stream, expert_ids, kv_owner, attn_norm, moe_norm, k_norm, w_kv, router, w_gate, w_up, w_down):
    first = layer_input.astype(jnp.float32)
    first_scale = lax.rsqrt(lax.optimization_barrier(jnp.sum(first * first, 1, keepdims=True)) / D + EPS)
    attn_in = (first * first_scale * attn_norm.astype(jnp.float32)).astype(jnp.bfloat16)
    kv = jnp.dot(attn_in, w_kv, preferred_element_type=jnp.float32).reshape(TOKENS, 2 * KVH, HD)
    keys = kv[:, :KVH]
    keys = keys * lax.rsqrt(lax.optimization_barrier(jnp.mean(keys * keys, 2, keepdims=True)) + EPS) * k_norm.astype(jnp.float32)
    kv_rows = jnp.concatenate([keys, kv[:, KVH:]], 1).reshape(TOKENS, 2 * KVH * HD).astype(jnp.bfloat16)
    block = (jnp.arange(TOKENS) // TOK_DEV).astype(jnp.int32)
    owner = kv_owner[:, 0].astype(jnp.int32)
    owner_hot = (owner[:, None] == jnp.arange(N_TP, dtype=jnp.int32)[None, :]).astype(jnp.int32)
    blocked = owner_hot.reshape(N_EP, TOK_DEV, N_TP)
    before = (jnp.cumsum(blocked, 1, dtype=jnp.int32) - blocked).reshape(TOKENS, N_TP)
    owner_slot = lax.optimization_barrier(jnp.sum(before * owner_hot, 1, dtype=jnp.int32))
    kv_cache = jnp.zeros((N_EP, N_TP, KV_CAP, 2 * KVH * HD), jnp.bfloat16).at[block, owner, owner_slot].set(kv_rows)
    second = stream.astype(jnp.float32)
    second_scale = lax.rsqrt(lax.optimization_barrier(jnp.sum(second * second, 1, keepdims=True)) / D + EPS)
    moe_in = (second * second_scale * moe_norm.astype(jnp.float32)).astype(jnp.bfloat16)
    logits = jnp.dot(moe_in, router, preferred_element_type=jnp.float32)
    chosen = jnp.take_along_axis(logits, expert_ids, 1)
    gates = jax.nn.softmax(chosen, -1)
    expert_hot = (expert_ids[:, :, None] == jnp.arange(EXPERTS, dtype=jnp.int32)[None, None, :]).astype(jnp.int32)
    counts = lax.optimization_barrier(jnp.sum(expert_hot, 1, dtype=jnp.int32)).reshape(N_EP, TOK_DEV, EXPERTS)
    earlier = (jnp.cumsum(counts, 1, dtype=jnp.int32) - counts).reshape(TOKENS, EXPERTS)
    slots = lax.optimization_barrier(jnp.sum(earlier[:, None, :] * expert_hot, 2, dtype=jnp.int32))
    spread = jnp.broadcast_to(moe_in[:, None, :], (TOKENS, TOPK, D))
    inputs = jnp.zeros((EXPERTS, N_EP, CAP, D), jnp.bfloat16).at[expert_ids, block[:, None], slots].set(spread)
    outputs = lax.map(run_expert, (inputs, w_gate, w_up, w_down))
    picked = outputs[expert_ids, block[:, None], slots].astype(jnp.float32)
    moe_out = lax.optimization_barrier(jnp.sum(gates[:, :, None] * picked, 1)).astype(jnp.bfloat16)
    return (moe_out, kv_cache)
```

```python
import functools

import jax
import jax.numpy as jnp
from jax import lax
from jax.experimental import pallas as pl
from jax.experimental.pallas import tpu as pltpu
from jax.sharding import PartitionSpec as P

D = 4096
KVH = 4
HD = 128
TOPK = 8


EPS = 1e-06
VMEM_LIMIT = 56 * 1024 * 1024


def tile_of(size, most):
    tile = size
    while tile > most and tile % 2 == 0 and (tile // 2) % 128 == 0:
        tile //= 2
    for candidate in range(most, 127, -128):
        if size % candidate == 0:
            return candidate
    return tile


def hidden_kernel(x_ref, wg_ref, wu_ref, scale_ref, weight_ref, out_ref):
    blocks, parts, rows, width = x_ref.shape
    gate = up = None
    for part in range(parts):
        x = x_ref[:, part].reshape(blocks * rows, width)
        depth = pl.ds(part * width, width)
        g = jnp.dot(x, wg_ref[0, depth], preferred_element_type=jnp.float32)
        u = jnp.dot(x, wu_ref[0, depth], preferred_element_type=jnp.float32)
        gate = g if gate is None else gate + g
        up = u if up is None else up + u
    scale = scale_ref[...]
    gate = gate * scale
    up = up * scale
    value = gate / (1.0 + jnp.exp(-gate)) * up * weight_ref[0]
    out_ref[0] = value.astype(jnp.bfloat16)


def hidden_of(x, w_gate, w_up, scale, weight):
    blocks, parts, rows, width = x.shape
    experts, depth, units = w_gate.shape
    tokens = blocks * rows
    tile = tile_of(units, 256)
    tiles = units // tile
    wspec = pl.BlockSpec((1, depth, tile), lambda e, f: (e, 0, f))
    return pl.pallas_call(
        hidden_kernel,
        grid=(experts, tiles),
        in_specs=[
            pl.BlockSpec(x.shape, lambda e, f: (0, 0, 0, 0)),
            wspec,
            wspec,
            pl.BlockSpec((tokens, 1), lambda e, f: (0, 0)),
            pl.BlockSpec((1, tokens, 1), lambda e, f: (e, 0, 0)),
        ],
        out_specs=pl.BlockSpec((1, tokens, tile), lambda e, f: (e, 0, f)),
        out_shape=jax.ShapeDtypeStruct((experts, tokens, units), jnp.bfloat16),
        compiler_params=pltpu.CompilerParams(vmem_limit_bytes=VMEM_LIMIT),
        cost_estimate=pl.CostEstimate(
            flops=4 * tokens * depth * units * experts,
            bytes_accessed=4 * experts * depth * units + 2 * tokens * depth,
            transcendentals=tokens * units * experts,
        ),
    )(x, w_gate, w_up, scale, weight)


def down_kernel(h_ref, w_ref, out_ref):
    blocks, _, rows, tile = out_ref.shape
    y = None
    for e in range(h_ref.shape[0]):
        term = jnp.dot(h_ref[e], w_ref[e], preferred_element_type=jnp.float32)
        y = term if y is None else y + term
    out_ref[:, 0] = y.astype(jnp.bfloat16).reshape(blocks, rows, tile)


def down_of(hidden, w_down, blocks, parts):
    experts, tokens, units = hidden.shape
    width = w_down.shape[2] // parts
    rows = tokens // blocks
    tile = tile_of(width, 512)
    tiles = width // tile
    return pl.pallas_call(
        down_kernel,
        grid=(parts * tiles,),
        in_specs=[
            pl.BlockSpec((experts, tokens, units), lambda n: (0, 0, 0)),
            pl.BlockSpec((experts, units, tile), lambda n: (0, 0, n)),
        ],
        out_specs=pl.BlockSpec(
            (blocks, 1, rows, tile), lambda n: (0, n // tiles, 0, n % tiles)
        ),
        out_shape=jax.ShapeDtypeStruct((blocks, parts, rows, width), jnp.bfloat16),
        compiler_params=pltpu.CompilerParams(vmem_limit_bytes=VMEM_LIMIT),
        cost_estimate=pl.CostEstimate(
            flops=2 * experts * tokens * units * width * parts,
            bytes_accessed=2 * (experts * units + tokens) * width * parts,
            transcendentals=0,
        ),
    )(hidden, w_down)


def per_device(
    layer_input,
    stream,
    expert_ids,
    kv_owner,
    attn_norm,
    moe_norm,
    k_norm,
    w_kv,
    router,
    w_gate,
    w_up,
    w_down,
):
    rows = layer_input.shape[0]
    tp_count = lax.axis_size("tp")
    ep_count = lax.axis_size("ep")
    columns = 2 * KVH * HD
    expert_count = router.shape[1]
    exp_local = w_gate.shape[0]
    first = layer_input.astype(jnp.float32)
    second = stream.astype(jnp.float32)

    rows_out = (second * moe_norm.astype(jnp.float32)).astype(jnp.bfloat16)
    gathered = lax.all_gather(rows_out, ("ep", "tp"), axis=0, tiled=False)
    gathered = gathered.reshape(ep_count, tp_count, rows, rows_out.shape[1])

    partial_logits = jnp.dot(rows_out, router, preferred_element_type=jnp.float32)
    squares = jnp.stack([jnp.sum(first * first, 1), jnp.sum(second * second, 1)], 1)
    small = lax.psum(jnp.concatenate([squares, partial_logits], 1), "tp")
    first_scale = lax.rsqrt(small[:, 0:1] / D + EPS)
    second_scale = lax.rsqrt(small[:, 1:2] / D + EPS)
    logits = small[:, 2:] * second_scale
    expert_range = jnp.arange(expert_count, dtype=jnp.int32)
    chosen = jnp.any(expert_ids[:, :, None] == expert_range[None, None, :], 1)
    top = jnp.max(jnp.where(chosen, logits, -jnp.inf), 1, keepdims=True)
    weights = jnp.where(chosen, jnp.exp(jnp.where(chosen, logits - top, 0.0)), 0.0)
    weights = weights / jnp.sum(weights, 1, keepdims=True)
    side = lax.all_gather(
        jnp.concatenate([second_scale, weights], 1), "ep", axis=0, tiled=True
    )
    scale = side[:, 0:1]
    mine = lax.dynamic_slice_in_dim(side, 1 + lax.axis_index("ep") * exp_local, exp_local, 1)
    weight = mine.T[:, :, None]

    attn_in = (first * attn_norm.astype(jnp.float32)).astype(jnp.bfloat16)
    kv = jnp.dot(attn_in, w_kv, preferred_element_type=jnp.float32) * first_scale
    owner_cap = 2 * rows // tp_count
    owner = kv_owner[:, 0]
    owner_hot = (owner[:, None] == jnp.arange(tp_count, dtype=jnp.int32)[None, :]).astype(jnp.int32)
    owner_slot = jnp.sum(
        (jnp.cumsum(owner_hot, 0, dtype=jnp.int32) - owner_hot) * owner_hot, 1, dtype=jnp.int32
    )
    target = owner * owner_cap + owner_slot
    placing = target[None, :] == jnp.arange(tp_count * owner_cap, dtype=jnp.int32)[:, None]
    placed = jnp.dot(
        placing.astype(jnp.bfloat16), kv.astype(jnp.bfloat16), preferred_element_type=jnp.float32
    )
    placed = placed.astype(jnp.bfloat16).reshape(tp_count, owner_cap, columns)
    arrived = lax.all_to_all(placed, "tp", split_axis=0, concat_axis=0, tiled=True)
    heads = jnp.sum(arrived.astype(jnp.float32), 0).reshape(owner_cap, 2 * KVH, HD)
    keys = heads[:, :KVH]
    keys = keys * lax.rsqrt(jnp.mean(keys * keys, 2, keepdims=True) + EPS)
    keys = keys * k_norm.astype(jnp.float32)
    kv_cache = jnp.concatenate([keys, heads[:, KVH:]], 1).astype(jnp.bfloat16)
    kv_cache = kv_cache.reshape(1, 1, owner_cap, columns)

    hidden = hidden_of(gathered, w_gate, w_up, scale, weight)
    partial = down_of(hidden, w_down, ep_count, tp_count)
    partial = partial.reshape(ep_count * tp_count, rows, -1)
    moe_out = lax.psum_scatter(partial, ("ep", "tp"), scatter_dimension=0, tiled=False)
    return (moe_out, kv_cache)


def solution(mesh):
    placed = (
        P(("group", "ep"), "tp"),
        P(("group", "ep"), "tp"),
        P(("group", "ep"), None),
        P(("group", "ep"), None),
        P("tp"),
        P("tp"),
        P(),
        P("tp", None),
        P("tp", None),
        P("ep", None, "tp"),
        P("ep", None, "tp"),
        P("ep", "tp", None),
    )
    return jax.shard_map(
        per_device,
        mesh=mesh,
        in_specs=placed,
        out_specs=(P(("group", "ep"), "tp"), P(("group", "ep"), "tp", None, None)),
        check_vma=False,
    )
```

```python
import functools

import jax
import jax.numpy as jnp
from jax import lax
from jax.experimental import pallas as pl
from jax.experimental.pallas import tpu as pltpu
from jax.sharding import PartitionSpec as P

D = 4096
KVH = 4
HD = 128
TOPK = 8


EPS = 1e-06
VMEM_LIMIT = 56 * 1024 * 1024


def tile_of(size, most):
    for candidate in range(most, 127, -128):
        if size % candidate == 0:
            return candidate
    return size


def silu_up(gate, up, scale, weight):
    gate = gate * scale
    up = up * scale
    return (gate / (1.0 + jnp.exp(-gate)) * up * weight).astype(jnp.bfloat16)


def column_of(side, index):
    lane = lax.broadcasted_iota(jnp.int32, side.shape, 1)
    return jnp.sum(jnp.where(lane == index, side, 0.0), 1, keepdims=True)


def gained_kernel(x_ref, gain_ref, out_ref):
    gained = x_ref[...].astype(jnp.float32) * gain_ref[...].astype(jnp.float32)
    out_ref[...] = gained.astype(jnp.bfloat16)


def gained(x, gain):
    return pl.pallas_call(
        gained_kernel, out_shape=jax.ShapeDtypeStruct(x.shape, jnp.bfloat16)
    )(x, gain[None])


def block_hidden_kernel(
    where_ref, own_ref, other_ref, sib_own_ref, sib_other_ref, side_ref, wg_ref, wu_ref,
    out_ref, x_ref, gates_ref,
):
    rows, width = own_ref.shape
    expert = pl.program_id(0)

    @pl.when((expert == 0) & (pl.program_id(1) == 0))
    def _():
        mine = pl.ds(pl.multiple_of(where_ref[0] * width, width), width)
        theirs = pl.ds(pl.multiple_of((1 - where_ref[0]) * width, width), width)
        x_ref[0:rows, mine] = own_ref[...]
        x_ref[0:rows, theirs] = other_ref[...]
        x_ref[rows : 2 * rows, mine] = sib_own_ref[...]
        x_ref[rows : 2 * rows, theirs] = sib_other_ref[...]
        gates_ref[...] = jnp.transpose(side_ref[...])

    x = x_ref[...]
    gate = jnp.dot(x, wg_ref[0], preferred_element_type=jnp.float32)
    up = jnp.dot(x, wu_ref[0], preferred_element_type=jnp.float32)
    side = gates_ref[...]
    weight = column_of(side, 1 + where_ref[1] + expert)
    out_ref[0] = silu_up(gate, up, column_of(side, 0), weight)


def block_hidden(where, chunks, side, w_gate, w_up):
    rows, width = chunks[0].shape
    experts, depth, units = w_gate.shape
    tile = tile_of(units, 256)
    chunk_spec = pl.BlockSpec((rows, width), lambda e, f, s: (0, 0))
    weight_spec = pl.BlockSpec((1, depth, tile), lambda e, f, s: (e, 0, f))
    return pl.pallas_call(
        block_hidden_kernel,
        grid_spec=pltpu.PrefetchScalarGridSpec(
            num_scalar_prefetch=1,
            grid=(experts, units // tile),
            in_specs=[chunk_spec] * 4
            + [pl.BlockSpec(side.shape, lambda e, f, s: (0, 0)), weight_spec, weight_spec],
            out_specs=pl.BlockSpec((1, 2 * rows, tile), lambda e, f, s: (e, 0, f)),
            scratch_shapes=[
                pltpu.VMEM((2 * rows, depth), jnp.bfloat16),
                pltpu.VMEM((2 * rows, side.shape[0]), jnp.float32),
            ],
        ),
        out_shape=jax.ShapeDtypeStruct((experts, 2 * rows, units), jnp.bfloat16),
        compiler_params=pltpu.CompilerParams(vmem_limit_bytes=VMEM_LIMIT),
        cost_estimate=pl.CostEstimate(
            flops=8 * rows * depth * units * experts,
            bytes_accessed=4 * experts * depth * units + 4 * rows * depth,
            transcendentals=2 * rows * units * experts,
        ),
    )(where, *chunks, side, w_gate, w_up)


def block_down_kernel(where_ref, h_ref, w_ref, own_ref, sib_ref):
    rows = own_ref.shape[1]
    y = None
    for e in range(h_ref.shape[0]):
        term = jnp.dot(h_ref[e], w_ref[e], preferred_element_type=jnp.float32)
        y = term if y is None else y + term
    own_ref[0] = y[:rows].astype(jnp.bfloat16)
    sib_ref[0] = y[rows:].astype(jnp.bfloat16)


def block_down(where, hidden, w_down):
    experts, tokens, units = hidden.shape
    rows, width = tokens // 2, w_down.shape[2] // 2
    tile = tile_of(width, 512)
    tiles = width // tile
    out_spec = pl.BlockSpec((1, rows, tile), lambda h, n, s: (h, 0, n))
    out = jax.ShapeDtypeStruct((2, rows, width), jnp.bfloat16)
    return pl.pallas_call(
        block_down_kernel,
        grid_spec=pltpu.PrefetchScalarGridSpec(
            num_scalar_prefetch=1,
            grid=(2, tiles),
            in_specs=[
                pl.BlockSpec((experts, tokens, units), lambda h, n, s: (0, 0, 0)),
                pl.BlockSpec(
                    (experts, units, tile),
                    lambda h, n, s: (0, 0, (h + s[0] - 2 * h * s[0]) * tiles + n),
                ),
            ],
            out_specs=[out_spec, out_spec],
        ),
        out_shape=[out, out],
        compiler_params=pltpu.CompilerParams(vmem_limit_bytes=VMEM_LIMIT),
        cost_estimate=pl.CostEstimate(
            flops=4 * experts * tokens * units * width,
            bytes_accessed=4 * (experts * units + tokens) * width,
            transcendentals=0,
        ),
    )(where, hidden, w_down)


def total(*terms):
    return sum(term.astype(jnp.float32) for term in terms).astype(jnp.bfloat16)


def ring_experts(rows_out, side, w_gate, w_up, w_down):
    ep_count = lax.axis_size("ep")
    chips = ep_count // 2
    forward = [(d, (d + 2) % ep_count) for d in range(ep_count)]
    siblings = [(d, d ^ 1) for d in range(ep_count)]
    along = functools.partial(lax.ppermute, axis_name="ep", perm=forward)
    beside = functools.partial(lax.ppermute, axis_name="ep", perm=siblings)
    across = functools.partial(lax.ppermute, axis_name="tp", perm=[(0, 1), (1, 0)])
    where = jnp.stack([lax.axis_index("tp"), lax.axis_index("ep") * w_gate.shape[0]])
    where = where.astype(jnp.int32)

    lane, sides = [rows_out], [jnp.concatenate([side, beside(side)], 1)]
    for _ in range(chips - 1):
        lane.append(along(lane[-1]))
        sides.append(along(sides[-1]))
    crossed = [across(chunk) for chunk in lane]
    hidden = []
    for s in range(chips):
        chunks = (lane[s], crossed[s], beside(lane[s]), beside(crossed[s]))
        hidden.append(block_hidden(where, chunks, sides[s], w_gate, w_up))

    travelling = None
    for s in list(range(1, chips)) + [0]:
        own, sib = block_down(where, hidden[s], w_down)
        back = beside(sib)
        swapped = across(total(own[1], back[1]))
        terms = (own[0], back[0], swapped)
        travelling = total(*terms) if travelling is None else total(along(travelling), *terms)
    return travelling


def hidden_kernel(x_ref, wg_ref, wu_ref, scale_ref, weight_ref, out_ref):
    blocks, parts, rows, width = x_ref.shape
    gate = up = None
    for part in range(parts):
        x = x_ref[:, part].reshape(blocks * rows, width)
        depth = pl.ds(part * width, width)
        g = jnp.dot(x, wg_ref[0, depth], preferred_element_type=jnp.float32)
        u = jnp.dot(x, wu_ref[0, depth], preferred_element_type=jnp.float32)
        gate = g if gate is None else gate + g
        up = u if up is None else up + u
    out_ref[0] = silu_up(gate, up, scale_ref[...], weight_ref[0])


def hidden_of(x, w_gate, w_up, scale, weight):
    blocks, parts, rows, width = x.shape
    experts, depth, units = w_gate.shape
    tokens = blocks * rows
    tile = tile_of(units, 256)
    tiles = units // tile
    wspec = pl.BlockSpec((1, depth, tile), lambda e, f: (e, 0, f))
    return pl.pallas_call(
        hidden_kernel,
        grid=(experts, tiles),
        in_specs=[
            pl.BlockSpec(x.shape, lambda e, f: (0, 0, 0, 0)),
            wspec,
            wspec,
            pl.BlockSpec((tokens, 1), lambda e, f: (0, 0)),
            pl.BlockSpec((1, tokens, 1), lambda e, f: (e, 0, 0)),
        ],
        out_specs=pl.BlockSpec((1, tokens, tile), lambda e, f: (e, 0, f)),
        out_shape=jax.ShapeDtypeStruct((experts, tokens, units), jnp.bfloat16),
        compiler_params=pltpu.CompilerParams(vmem_limit_bytes=VMEM_LIMIT),
    )(x, w_gate, w_up, scale, weight)


def down_kernel(h_ref, w_ref, out_ref):
    blocks, _, rows, tile = out_ref.shape
    y = None
    for e in range(h_ref.shape[0]):
        term = jnp.dot(h_ref[e], w_ref[e], preferred_element_type=jnp.float32)
        y = term if y is None else y + term
    out_ref[:, 0] = y.astype(jnp.bfloat16).reshape(blocks, rows, tile)


def down_of(hidden, w_down, blocks, parts):
    experts, tokens, units = hidden.shape
    width = w_down.shape[2] // parts
    rows = tokens // blocks
    tile = tile_of(width, 512)
    tiles = width // tile
    return pl.pallas_call(
        down_kernel,
        grid=(parts * tiles,),
        in_specs=[
            pl.BlockSpec((experts, tokens, units), lambda n: (0, 0, 0)),
            pl.BlockSpec((experts, units, tile), lambda n: (0, 0, n)),
        ],
        out_specs=pl.BlockSpec(
            (blocks, 1, rows, tile), lambda n: (0, n // tiles, 0, n % tiles)
        ),
        out_shape=jax.ShapeDtypeStruct((blocks, parts, rows, width), jnp.bfloat16),
        compiler_params=pltpu.CompilerParams(vmem_limit_bytes=VMEM_LIMIT),
    )(hidden, w_down)


def plain_experts(rows_out, side, w_gate, w_up, w_down):
    tp_count, ep_count = lax.axis_size("tp"), lax.axis_size("ep")
    rows, width = rows_out.shape
    exp_local = w_gate.shape[0]
    gathered = lax.all_gather(rows_out, ("ep", "tp"), axis=0, tiled=False)
    gathered = gathered.reshape(ep_count, tp_count, rows, width)
    side = lax.all_gather(side, "ep", axis=1, tiled=True)
    first_expert = 1 + lax.axis_index("ep") * exp_local
    weight = lax.dynamic_slice_in_dim(side, first_expert, exp_local, 0)[:, :, None]
    hidden = hidden_of(gathered, w_gate, w_up, side[0][:, None], weight)
    partial = down_of(hidden, w_down, ep_count, tp_count)
    partial = partial.reshape(ep_count * tp_count, rows, width)
    return lax.psum_scatter(partial, ("ep", "tp"), scatter_dimension=0, tiled=False)


def per_device(
    layer_input,
    stream,
    expert_ids,
    kv_owner,
    attn_norm,
    moe_norm,
    k_norm,
    w_kv,
    router,
    w_gate,
    w_up,
    w_down,
):
    rows = layer_input.shape[0]
    tp_count = lax.axis_size("tp")
    pair = tp_count == 2
    columns = 2 * KVH * HD
    expert_count = router.shape[1]
    first = layer_input.astype(jnp.float32)
    second = stream.astype(jnp.float32)

    rows_out = gained(stream, moe_norm)

    logits = lax.dot_general(
        router, rows_out, (((0,), (1,)), ((), ())), preferred_element_type=jnp.float32
    )
    squares = jnp.stack([jnp.sum(first * first, 1), jnp.sum(second * second, 1)], 0)
    small = jnp.concatenate([squares, logits], 0)
    if pair:
        small = small + lax.ppermute(small, "tp", [(0, 1), (1, 0)])
    else:
        small = lax.psum(small, "tp")
    first_scale = lax.rsqrt(small[0] / D + EPS)
    second_scale = lax.rsqrt(small[1:2] / D + EPS)
    logits = small[2:] * second_scale
    expert_range = jnp.arange(expert_count, dtype=jnp.int32)
    chosen = jnp.any(expert_ids.T[None, :, :] == expert_range[:, None, None], 1)
    top = jnp.max(jnp.where(chosen, logits, -jnp.inf), 0, keepdims=True)
    weights = jnp.where(chosen, jnp.exp(jnp.where(chosen, logits - top, 0.0)), 0.0)
    weights = weights / jnp.sum(weights, 0, keepdims=True)
    fill = jnp.zeros((-(1 + expert_count) % 8, rows), jnp.float32)
    side = jnp.concatenate([second_scale, weights, fill], 0)

    attn_in = (first * attn_norm.astype(jnp.float32)).astype(jnp.bfloat16)
    kv = jnp.dot(attn_in, w_kv, preferred_element_type=jnp.float32) * first_scale[:, None]
    owner_cap = 2 * rows // tp_count
    owner = kv_owner[:, 0]
    owner_hot = (owner[:, None] == jnp.arange(tp_count, dtype=jnp.int32)[None, :]).astype(jnp.int32)
    owner_slot = jnp.sum(
        (jnp.cumsum(owner_hot, 0, dtype=jnp.int32) - owner_hot) * owner_hot, 1, dtype=jnp.int32
    )
    if pair:
        owner = jnp.where(owner == lax.axis_index("tp"), 0, 1)
    target = owner * owner_cap + owner_slot
    placing = target[None, :] == jnp.arange(tp_count * owner_cap, dtype=jnp.int32)[:, None]
    placed = jnp.dot(
        placing.astype(jnp.bfloat16), kv.astype(jnp.bfloat16), preferred_element_type=jnp.float32
    )
    placed = placed.astype(jnp.bfloat16).reshape(tp_count, owner_cap, columns)
    if pair:
        arrived = lax.ppermute(placed[1], "tp", [(0, 1), (1, 0)])
        heads = placed[0].astype(jnp.float32) + arrived.astype(jnp.float32)
    else:
        arrived = lax.all_to_all(placed, "tp", split_axis=0, concat_axis=0, tiled=True)
        heads = jnp.sum(arrived.astype(jnp.float32), 0)
    heads = heads.reshape(owner_cap, 2 * KVH, HD)
    keys = heads[:, :KVH]
    keys = keys * lax.rsqrt(jnp.mean(keys * keys, 2, keepdims=True) + EPS)
    keys = keys * k_norm.astype(jnp.float32)
    kv_cache = jnp.concatenate([keys, heads[:, KVH:]], 1).astype(jnp.bfloat16)
    kv_cache = kv_cache.reshape(1, 1, owner_cap, columns)

    experts = ring_experts if pair and lax.axis_size("ep") % 2 == 0 else plain_experts
    moe_out = experts(rows_out, side, w_gate, w_up, w_down)
    return (moe_out, kv_cache)


def solution(mesh):
    placed = (
        P(("group", "ep"), "tp"),
        P(("group", "ep"), "tp"),
        P(("group", "ep"), None),
        P(("group", "ep"), None),
        P("tp"),
        P("tp"),
        P(),
        P("tp", None),
        P("tp", None),
        P("ep", None, "tp"),
        P("ep", None, "tp"),
        P("ep", "tp", None),
    )
    return jax.shard_map(
        per_device,
        mesh=mesh,
        in_specs=placed,
        out_specs=(P(("group", "ep"), "tp"), P(("group", "ep"), "tp", None, None)),
        check_vma=False,
    )
```

```python
import functools

import jax
import jax.numpy as jnp
from jax import lax
from jax.experimental import pallas as pl
from jax.experimental.pallas import tpu as pltpu
from jax.sharding import PartitionSpec as P

D = 4096
KVH = 4
HD = 128
TOPK = 8


EPS = 1e-06
VMEM_LIMIT = 56 * 1024 * 1024
BLOCK_VMEM_LIMIT = 24 * 1024 * 1024
MXU = 256


def tile_of(size, most):
    for candidate in range(most, 127, -128):
        if size % candidate == 0:
            return candidate
    return size


def silu_up(gate, up, scale, weight):
    gate = gate * scale
    up = up * scale
    return (gate / (1.0 + jnp.exp(-gate)) * up * weight).astype(jnp.bfloat16)


def column_of(side, index):
    lane = lax.broadcasted_iota(jnp.int32, side.shape, 1)
    return jnp.sum(jnp.where(lane == index, side, 0.0), 1, keepdims=True)


def gained_kernel(x_ref, gain_ref, out_ref):
    gained = x_ref[...].astype(jnp.float32) * gain_ref[...].astype(jnp.float32)
    out_ref[...] = gained.astype(jnp.bfloat16)


def gained(x, gain):
    return pl.pallas_call(
        gained_kernel, out_shape=jax.ShapeDtypeStruct(x.shape, jnp.bfloat16)
    )(x, gain[None])


def paired_products(rows, steps):
    def stage(index):
        _, first_tile, second_tile = steps[index]
        pltpu.matmul_push_rhs(first_tile(), index % 2, 0)
        pltpu.matmul_push_rhs(second_tile(), index % 2, 1)

    def run(first_acc, second_acc):
        stage(0)
        for index, (lhs, _, _) in enumerate(steps):
            if index + 1 < len(steps):
                stage(index + 1)
            left = lhs()
            pltpu.matmul_acc_lhs(first_acc, left, index % 2)
            pltpu.matmul_acc_lhs(second_acc, left, index % 2)
        return pltpu.matmul_pop(first_acc), pltpu.matmul_pop(second_acc)

    return pl.run_scoped(
        run, pltpu.ACC(0)((rows, MXU), jnp.float32), pltpu.ACC(1)((rows, MXU), jnp.float32)
    )


def block_hidden_kernel(
    where_ref, own_ref, other_ref, sib_own_ref, sib_other_ref, side_ref, wg_ref, wu_ref,
    _, out_ref, x_ref, gates_ref,
):
    rows, width = own_ref.shape
    expert = pl.program_id(0)

    @pl.when((expert == 0) & (pl.program_id(1) == 0))
    def _():
        mine = pl.ds(pl.multiple_of(where_ref[0] * width, width), width)
        theirs = pl.ds(pl.multiple_of((1 - where_ref[0]) * width, width), width)
        x_ref[0:rows, mine] = own_ref[...]
        x_ref[0:rows, theirs] = other_ref[...]
        x_ref[rows : 2 * rows, mine] = sib_own_ref[...]
        x_ref[rows : 2 * rows, theirs] = sib_other_ref[...]
        gates_ref[...] = jnp.transpose(side_ref[...])

    def step(k):
        depth = pl.ds(k * MXU, MXU)
        return (lambda: x_ref[:, depth], lambda: wg_ref[0, depth], lambda: wu_ref[0, depth])

    steps = [step(k) for k in range(2 * width // MXU)]
    gate, up = paired_products(2 * rows, steps)
    side = gates_ref[...]
    weight = column_of(side, 1 + where_ref[1] + expert)
    out_ref[0] = silu_up(gate, up, column_of(side, 0), weight)


def block_hidden(where, chunks, side, w_gate, w_up, after):
    rows, width = chunks[0].shape
    experts, depth, units = w_gate.shape
    tile = MXU
    chunk_spec = pl.BlockSpec((rows, width), lambda e, f, s: (0, 0))
    weight_spec = pl.BlockSpec((1, depth, tile), lambda e, f, s: (e, 0, f))
    return pl.pallas_call(
        block_hidden_kernel,
        grid_spec=pltpu.PrefetchScalarGridSpec(
            num_scalar_prefetch=1,
            grid=(experts, units // tile),
            in_specs=[chunk_spec] * 4
            + [pl.BlockSpec(side.shape, lambda e, f, s: (0, 0)), weight_spec, weight_spec]
            + [pl.BlockSpec(memory_space=pl.ANY)],
            out_specs=pl.BlockSpec((1, 2 * rows, tile), lambda e, f, s: (e, 0, f)),
            scratch_shapes=[
                pltpu.VMEM((2 * rows, depth), jnp.bfloat16),
                pltpu.VMEM((2 * rows, side.shape[0]), jnp.float32),
            ],
        ),
        out_shape=jax.ShapeDtypeStruct((experts, 2 * rows, units), jnp.bfloat16),
        compiler_params=pltpu.CompilerParams(vmem_limit_bytes=BLOCK_VMEM_LIMIT),
        cost_estimate=pl.CostEstimate(
            flops=8 * rows * depth * units * experts,
            bytes_accessed=4 * experts * depth * units + 4 * rows * depth,
            transcendentals=2 * rows * units * experts,
        ),
    )(where, *chunks, side, w_gate, w_up, after)


def block_down_kernel(where_ref, h_ref, w_ref, _, own_ref, sib_ref):
    rows = own_ref.shape[1]
    experts, _, units = h_ref.shape

    def step(e, k):
        depth = pl.ds(k * MXU, MXU)
        return (
            lambda: h_ref[e, :, depth],
            lambda: w_ref[e, depth, 0:MXU],
            lambda: w_ref[e, depth, MXU : 2 * MXU],
        )

    steps = [step(e, k) for e in range(experts) for k in range(units // MXU)]
    for half, y in enumerate(paired_products(2 * rows, steps)):
        columns = slice(half * MXU, (half + 1) * MXU)
        own_ref[0, :, columns] = y[:rows].astype(jnp.bfloat16)
        sib_ref[0, :, columns] = y[rows:].astype(jnp.bfloat16)


def block_down(where, hidden, w_down, after):
    experts, tokens, units = hidden.shape
    rows, width = tokens // 2, w_down.shape[2] // 2
    tile = 2 * MXU
    tiles = width // tile
    out_spec = pl.BlockSpec((1, rows, tile), lambda h, n, s: (h, 0, n))
    out = jax.ShapeDtypeStruct((2, rows, width), jnp.bfloat16)
    return pl.pallas_call(
        block_down_kernel,
        grid_spec=pltpu.PrefetchScalarGridSpec(
            num_scalar_prefetch=1,
            grid=(2, tiles),
            in_specs=[
                pl.BlockSpec((experts, tokens, units), lambda h, n, s: (0, 0, 0)),
                pl.BlockSpec(
                    (experts, units, tile),
                    lambda h, n, s: (0, 0, (h + s[0] - 2 * h * s[0]) * tiles + n),
                ),
                pl.BlockSpec(memory_space=pl.ANY),
            ],
            out_specs=[out_spec, out_spec],
        ),
        out_shape=[out, out],
        compiler_params=pltpu.CompilerParams(vmem_limit_bytes=BLOCK_VMEM_LIMIT),
        cost_estimate=pl.CostEstimate(
            flops=4 * experts * tokens * units * width,
            bytes_accessed=4 * (experts * units + tokens) * width,
            transcendentals=0,
        ),
    )(where, hidden, w_down, after)


def total(*terms):
    return sum(term.astype(jnp.float32) for term in terms).astype(jnp.bfloat16)


def ring_experts(rows_out, side, w_gate, w_up, w_down):
    ep_count = lax.axis_size("ep")
    chips = ep_count // 2
    forward = [(d, (d + 2) % ep_count) for d in range(ep_count)]
    siblings = [(d, d ^ 1) for d in range(ep_count)]
    along = functools.partial(lax.ppermute, axis_name="ep", perm=forward)
    beside = functools.partial(lax.ppermute, axis_name="ep", perm=siblings)
    across = functools.partial(lax.ppermute, axis_name="tp", perm=[(0, 1), (1, 0)])
    where = jnp.stack([lax.axis_index("tp"), lax.axis_index("ep") * w_gate.shape[0]])
    where = where.astype(jnp.int32)

    lane, sides = [rows_out], [jnp.concatenate([side, beside(side)], 1)]
    for _ in range(chips - 1):
        lane.append(along(lane[-1]))
        sides.append(along(sides[-1]))
    crossed = [across(chunk) for chunk in lane]
    hidden, after = [None] * chips, where

    def up_of(s, after):
        chunks = (lane[s], crossed[s], beside(lane[s]), beside(crossed[s]))
        hidden[s] = block_hidden(where, chunks, sides[s], w_gate, w_up, after)
        return hidden[s]

    after, travelling = up_of(0, where), None
    for s in list(range(1, chips)) + [0]:
        if s:
            after = up_of(s, after)
        own, sib = block_down(where, hidden[s], w_down, after)
        after = own
        back = beside(sib)
        swapped = across(total(own[1], back[1]))
        terms = (own[0], back[0], swapped)
        travelling = total(*terms) if travelling is None else total(along(travelling), *terms)
    return travelling


def hidden_kernel(x_ref, wg_ref, wu_ref, scale_ref, weight_ref, out_ref):
    blocks, parts, rows, width = x_ref.shape
    gate = up = None
    for part in range(parts):
        x = x_ref[:, part].reshape(blocks * rows, width)
        depth = pl.ds(part * width, width)
        g = jnp.dot(x, wg_ref[0, depth], preferred_element_type=jnp.float32)
        u = jnp.dot(x, wu_ref[0, depth], preferred_element_type=jnp.float32)
        gate = g if gate is None else gate + g
        up = u if up is None else up + u
    out_ref[0] = silu_up(gate, up, scale_ref[...], weight_ref[0])


def hidden_of(x, w_gate, w_up, scale, weight):
    blocks, parts, rows, width = x.shape
    experts, depth, units = w_gate.shape
    tokens = blocks * rows
    tile = tile_of(units, 256)
    tiles = units // tile
    wspec = pl.BlockSpec((1, depth, tile), lambda e, f: (e, 0, f))
    return pl.pallas_call(
        hidden_kernel,
        grid=(experts, tiles),
        in_specs=[
            pl.BlockSpec(x.shape, lambda e, f: (0, 0, 0, 0)),
            wspec,
            wspec,
            pl.BlockSpec((tokens, 1), lambda e, f: (0, 0)),
            pl.BlockSpec((1, tokens, 1), lambda e, f: (e, 0, 0)),
        ],
        out_specs=pl.BlockSpec((1, tokens, tile), lambda e, f: (e, 0, f)),
        out_shape=jax.ShapeDtypeStruct((experts, tokens, units), jnp.bfloat16),
        compiler_params=pltpu.CompilerParams(vmem_limit_bytes=VMEM_LIMIT),
    )(x, w_gate, w_up, scale, weight)


def down_kernel(h_ref, w_ref, out_ref):
    blocks, _, rows, tile = out_ref.shape
    y = None
    for e in range(h_ref.shape[0]):
        term = jnp.dot(h_ref[e], w_ref[e], preferred_element_type=jnp.float32)
        y = term if y is None else y + term
    out_ref[:, 0] = y.astype(jnp.bfloat16).reshape(blocks, rows, tile)


def down_of(hidden, w_down, blocks, parts):
    experts, tokens, units = hidden.shape
    width = w_down.shape[2] // parts
    rows = tokens // blocks
    tile = tile_of(width, 512)
    tiles = width // tile
    return pl.pallas_call(
        down_kernel,
        grid=(parts * tiles,),
        in_specs=[
            pl.BlockSpec((experts, tokens, units), lambda n: (0, 0, 0)),
            pl.BlockSpec((experts, units, tile), lambda n: (0, 0, n)),
        ],
        out_specs=pl.BlockSpec(
            (blocks, 1, rows, tile), lambda n: (0, n // tiles, 0, n % tiles)
        ),
        out_shape=jax.ShapeDtypeStruct((blocks, parts, rows, width), jnp.bfloat16),
        compiler_params=pltpu.CompilerParams(vmem_limit_bytes=VMEM_LIMIT),
    )(hidden, w_down)


def plain_experts(rows_out, side, w_gate, w_up, w_down):
    tp_count, ep_count = lax.axis_size("tp"), lax.axis_size("ep")
    rows, width = rows_out.shape
    exp_local = w_gate.shape[0]
    gathered = lax.all_gather(rows_out, ("ep", "tp"), axis=0, tiled=False)
    gathered = gathered.reshape(ep_count, tp_count, rows, width)
    side = lax.all_gather(side, "ep", axis=1, tiled=True)
    first_expert = 1 + lax.axis_index("ep") * exp_local
    weight = lax.dynamic_slice_in_dim(side, first_expert, exp_local, 0)[:, :, None]
    hidden = hidden_of(gathered, w_gate, w_up, side[0][:, None], weight)
    partial = down_of(hidden, w_down, ep_count, tp_count)
    partial = partial.reshape(ep_count * tp_count, rows, width)
    return lax.psum_scatter(partial, ("ep", "tp"), scatter_dimension=0, tiled=False)


def per_device(
    layer_input,
    stream,
    expert_ids,
    kv_owner,
    attn_norm,
    moe_norm,
    k_norm,
    w_kv,
    router,
    w_gate,
    w_up,
    w_down,
):
    rows = layer_input.shape[0]
    tp_count = lax.axis_size("tp")
    pair = tp_count == 2
    columns = 2 * KVH * HD
    expert_count = router.shape[1]
    first = layer_input.astype(jnp.float32)
    second = stream.astype(jnp.float32)

    rows_out = gained(stream, moe_norm)

    logits = lax.dot_general(
        router, rows_out, (((0,), (1,)), ((), ())), preferred_element_type=jnp.float32
    )
    squares = jnp.stack([jnp.sum(first * first, 1), jnp.sum(second * second, 1)], 0)
    small = jnp.concatenate([squares, logits], 0)
    if pair:
        small = small + lax.ppermute(small, "tp", [(0, 1), (1, 0)])
    else:
        small = lax.psum(small, "tp")
    first_scale = lax.rsqrt(small[0] / D + EPS)
    second_scale = lax.rsqrt(small[1:2] / D + EPS)
    logits = small[2:] * second_scale
    expert_range = jnp.arange(expert_count, dtype=jnp.int32)
    chosen = jnp.any(expert_ids.T[None, :, :] == expert_range[:, None, None], 1)
    top = jnp.max(jnp.where(chosen, logits, -jnp.inf), 0, keepdims=True)
    weights = jnp.where(chosen, jnp.exp(jnp.where(chosen, logits - top, 0.0)), 0.0)
    weights = weights / jnp.sum(weights, 0, keepdims=True)
    fill = jnp.zeros((-(1 + expert_count) % 8, rows), jnp.float32)
    side = jnp.concatenate([second_scale, weights, fill], 0)

    attn_in = (first * attn_norm.astype(jnp.float32)).astype(jnp.bfloat16)
    kv = jnp.dot(attn_in, w_kv, preferred_element_type=jnp.float32) * first_scale[:, None]
    owner_cap = 2 * rows // tp_count
    owner = kv_owner[:, 0]
    owner_hot = (owner[:, None] == jnp.arange(tp_count, dtype=jnp.int32)[None, :]).astype(jnp.int32)
    owner_slot = jnp.sum(
        (jnp.cumsum(owner_hot, 0, dtype=jnp.int32) - owner_hot) * owner_hot, 1, dtype=jnp.int32
    )
    if pair:
        owner = jnp.where(owner == lax.axis_index("tp"), 0, 1)
    target = owner * owner_cap + owner_slot
    placing = target[None, :] == jnp.arange(tp_count * owner_cap, dtype=jnp.int32)[:, None]
    placed = jnp.dot(
        placing.astype(jnp.bfloat16), kv.astype(jnp.bfloat16), preferred_element_type=jnp.float32
    )
    placed = placed.astype(jnp.bfloat16).reshape(tp_count, owner_cap, columns)
    if pair:
        arrived = lax.ppermute(placed[1], "tp", [(0, 1), (1, 0)])
        heads = placed[0].astype(jnp.float32) + arrived.astype(jnp.float32)
    else:
        arrived = lax.all_to_all(placed, "tp", split_axis=0, concat_axis=0, tiled=True)
        heads = jnp.sum(arrived.astype(jnp.float32), 0)
    heads = heads.reshape(owner_cap, 2 * KVH, HD)
    keys = heads[:, :KVH]
    keys = keys * lax.rsqrt(jnp.mean(keys * keys, 2, keepdims=True) + EPS)
    keys = keys * k_norm.astype(jnp.float32)
    kv_cache = jnp.concatenate([keys, heads[:, KVH:]], 1).astype(jnp.bfloat16)
    kv_cache = kv_cache.reshape(1, 1, owner_cap, columns)

    tiled = w_gate.shape[2] % MXU == 0 and stream.shape[1] % (2 * MXU) == 0
    ringed = pair and tiled and lax.axis_size("ep") % 2 == 0
    experts = ring_experts if ringed else plain_experts
    moe_out = experts(rows_out, side, w_gate, w_up, w_down)
    return (moe_out, kv_cache)


def solution(mesh):
    placed = (
        P(("group", "ep"), "tp"),
        P(("group", "ep"), "tp"),
        P(("group", "ep"), None),
        P(("group", "ep"), None),
        P("tp"),
        P("tp"),
        P(),
        P("tp", None),
        P("tp", None),
        P("ep", None, "tp"),
        P("ep", None, "tp"),
        P("ep", "tp", None),
    )
    return jax.shard_map(
        per_device,
        mesh=mesh,
        in_specs=placed,
        out_specs=(P(("group", "ep"), "tp"), P(("group", "ep"), "tp", None, None)),
        check_vma=False,
    )
```

```python
import functools

import jax
import jax.numpy as jnp
from jax import lax
from jax.experimental import pallas as pl
from jax.experimental.pallas import tpu as pltpu
from jax.sharding import PartitionSpec as P

D = 4096
KVH = 4
HD = 128
TOPK = 8


EPS = 1e-06
VMEM_LIMIT = 56 * 1024 * 1024
BLOCK_VMEM_LIMIT = 8 * 1024 * 1024
MXU = 256


def tile_of(size, most):
    for candidate in range(most, 127, -128):
        if size % candidate == 0:
            return candidate
    return size


def silu_up(gate, up, scale, weight):
    gate = gate * scale
    up = up * scale
    return (gate / (1.0 + jnp.exp(-gate)) * up * weight).astype(jnp.bfloat16)


def column_of(side, index):
    lane = lax.broadcasted_iota(jnp.int32, side.shape, 1)
    return jnp.sum(jnp.where(lane == index, side, 0.0), 1, keepdims=True)


def gained_kernel(x_ref, gain_ref, out_ref):
    gained = x_ref[...].astype(jnp.float32) * gain_ref[...].astype(jnp.float32)
    out_ref[...] = gained.astype(jnp.bfloat16)


def gained(x, gain):
    return pl.pallas_call(
        gained_kernel, out_shape=jax.ShapeDtypeStruct(x.shape, jnp.bfloat16)
    )(x, gain[None])


def paired_products(rows, steps):
    def stage(index):
        _, first_tile, second_tile = steps[index]
        pltpu.matmul_push_rhs(first_tile(), index % 2, 0)
        pltpu.matmul_push_rhs(second_tile(), index % 2, 1)

    def run(first_acc, second_acc):
        stage(0)
        for index, (lhs, _, _) in enumerate(steps):
            if index + 1 < len(steps):
                stage(index + 1)
            left = lhs()
            pltpu.matmul_acc_lhs(first_acc, left, index % 2)
            pltpu.matmul_acc_lhs(second_acc, left, index % 2)
        return pltpu.matmul_pop(first_acc), pltpu.matmul_pop(second_acc)

    return pl.run_scoped(
        run, pltpu.ACC(0)((rows, MXU), jnp.float32), pltpu.ACC(1)((rows, MXU), jnp.float32)
    )


def load_kernel(source_ref, held_ref, sem):
    copies = [
        pltpu.make_async_copy(source_ref.at[e], held_ref.at[e], sem.at[e])
        for e in range(source_ref.shape[0])
    ]
    for copy in copies:
        copy.start()
    for copy in copies:
        copy.wait()


def loaded(w, after):
    return pl.pallas_call(
        lambda source_ref, _, held_ref, sem: load_kernel(source_ref, held_ref, sem),
        in_specs=[pl.BlockSpec(memory_space=pl.ANY)] * 2,
        out_specs=pl.BlockSpec(memory_space=pltpu.VMEM),
        out_shape=pltpu.VMEM(w.shape, w.dtype),
        scratch_shapes=[pltpu.SemaphoreType.DMA((w.shape[0],))],
        compiler_params=pltpu.CompilerParams(vmem_limit_bytes=1024 * 1024),
        cost_estimate=pl.CostEstimate(flops=0, bytes_accessed=2 * w.size, transcendentals=0),
    )(pltpu.with_memory_space_constraint(w, pltpu.HBM), after)


def block_hidden_kernel(
    where_ref, own_ref, other_ref, sib_own_ref, sib_other_ref, side_ref, wg_ref, wu_ref,
    _, out_ref, x_ref,
):
    rows, width = own_ref.shape
    experts, depth, units = wg_ref.shape
    mine = pl.ds(pl.multiple_of(where_ref[0] * width, width), width)
    theirs = pl.ds(pl.multiple_of((1 - where_ref[0]) * width, width), width)
    x_ref[0:rows, mine] = own_ref[...]
    x_ref[0:rows, theirs] = other_ref[...]
    x_ref[rows : 2 * rows, mine] = sib_own_ref[...]
    x_ref[rows : 2 * rows, theirs] = sib_other_ref[...]
    side = jnp.transpose(side_ref[...])
    scale = column_of(side, 0)
    for e in range(experts):
        weight = column_of(side, 1 + where_ref[1] + e)

        @pl.loop(0, units // MXU)
        def _(tile):
            columns = pl.ds(pl.multiple_of(tile * MXU, MXU), MXU)

            def step(k):
                part = pl.ds(k * MXU, MXU)
                return (
                    lambda: x_ref[:, part],
                    lambda: wg_ref[e, part, columns],
                    lambda: wu_ref[e, part, columns],
                )

            steps = [step(k) for k in range(depth // MXU)]
            gate, up = paired_products(2 * rows, steps)
            out_ref[e, :, columns] = silu_up(gate, up, scale, weight)


def in_vmem(count):
    return [pl.BlockSpec(memory_space=pltpu.VMEM)] * count


def block_hidden(where, chunks, side, w_gate, w_up, after):
    rows, _ = chunks[0].shape
    experts, depth, units = w_gate.shape
    return pl.pallas_call(
        block_hidden_kernel,
        in_specs=[pl.BlockSpec(memory_space=pltpu.SMEM)]
        + in_vmem(7)
        + [pl.BlockSpec(memory_space=pl.ANY)],
        out_specs=pl.BlockSpec(memory_space=pltpu.VMEM),
        scratch_shapes=[pltpu.VMEM((2 * rows, depth), jnp.bfloat16)],
        out_shape=jax.ShapeDtypeStruct((experts, 2 * rows, units), jnp.bfloat16),
        compiler_params=pltpu.CompilerParams(vmem_limit_bytes=BLOCK_VMEM_LIMIT),
        cost_estimate=pl.CostEstimate(
            flops=8 * rows * depth * units * experts,
            bytes_accessed=4 * rows * depth,
            transcendentals=2 * rows * units * experts,
        ),
    )(where, *chunks, side, w_gate, w_up, after)


def block_down_kernel(where_ref, h_ref, w_ref, _, own_ref, sib_ref):
    rows = own_ref.shape[1]
    experts, _, units = h_ref.shape

    def step(e, k):
        depth = pl.ds(k * MXU, MXU)
        return (
            lambda: h_ref[e, :, depth],
            lambda: w_ref[e, depth, 0:MXU],
            lambda: w_ref[e, depth, MXU : 2 * MXU],
        )

    steps = [step(e, k) for e in range(experts) for k in range(units // MXU)]
    for half, y in enumerate(paired_products(2 * rows, steps)):
        columns = slice(half * MXU, (half + 1) * MXU)
        own_ref[0, :, columns] = y[:rows].astype(jnp.bfloat16)
        sib_ref[0, :, columns] = y[rows:].astype(jnp.bfloat16)


def block_down(where, hidden, w_down, after):
    experts, tokens, units = hidden.shape
    rows, width = tokens // 2, w_down.shape[2] // 2
    tile = 2 * MXU
    tiles = width // tile
    out_spec = pl.BlockSpec((1, rows, tile), lambda h, n, s: (h, 0, n))
    out = jax.ShapeDtypeStruct((2, rows, width), jnp.bfloat16)
    return pl.pallas_call(
        block_down_kernel,
        grid_spec=pltpu.PrefetchScalarGridSpec(
            num_scalar_prefetch=1,
            grid=(2, tiles),
            in_specs=[
                pl.BlockSpec((experts, tokens, units), lambda h, n, s: (0, 0, 0)),
                pl.BlockSpec(
                    (experts, units, tile),
                    lambda h, n, s: (0, 0, (h + s[0] - 2 * h * s[0]) * tiles + n),
                ),
                pl.BlockSpec(memory_space=pl.ANY),
            ],
            out_specs=[out_spec, out_spec],
        ),
        out_shape=[out, out],
        compiler_params=pltpu.CompilerParams(vmem_limit_bytes=BLOCK_VMEM_LIMIT),
        cost_estimate=pl.CostEstimate(
            flops=4 * experts * tokens * units * width,
            bytes_accessed=4 * (experts * units + tokens) * width,
            transcendentals=0,
        ),
    )(where, hidden, pltpu.with_memory_space_constraint(w_down, pltpu.HBM), after)


def total(*terms):
    return sum(term.astype(jnp.float32) for term in terms).astype(jnp.bfloat16)


def ring_experts(rows_out, side, w_gate, w_up, w_down):
    ep_count = lax.axis_size("ep")
    chips = ep_count // 2
    forward = [(d, (d + 2) % ep_count) for d in range(ep_count)]
    siblings = [(d, d ^ 1) for d in range(ep_count)]
    along = functools.partial(lax.ppermute, axis_name="ep", perm=forward)
    beside = functools.partial(lax.ppermute, axis_name="ep", perm=siblings)
    across = functools.partial(lax.ppermute, axis_name="tp", perm=[(0, 1), (1, 0)])
    where = jnp.stack([lax.axis_index("tp"), lax.axis_index("ep") * w_gate.shape[0]])
    where = where.astype(jnp.int32)
    w_gate, w_up = [loaded(w, where) for w in (w_gate, w_up)]

    lane, sides = [rows_out], [jnp.concatenate([side, beside(side)], 1)]
    for _ in range(chips - 1):
        lane.append(along(lane[-1]))
        sides.append(along(sides[-1]))
    crossed = [across(chunk) for chunk in lane]
    hidden, after = [None] * chips, where

    def up_of(s, after):
        chunks = (lane[s], crossed[s], beside(lane[s]), beside(crossed[s]))
        hidden[s] = block_hidden(where, chunks, sides[s], w_gate, w_up, after)
        return hidden[s]

    after, travelling = up_of(0, where), None
    for s in list(range(1, chips)) + [0]:
        if s:
            after = up_of(s, after)
        own, sib = block_down(where, hidden[s], w_down, after)
        after = own
        back = beside(sib)
        swapped = across(total(own[1], back[1]))
        terms = (own[0], back[0], swapped)
        travelling = total(*terms) if travelling is None else total(along(travelling), *terms)
    return travelling


def hidden_kernel(x_ref, wg_ref, wu_ref, scale_ref, weight_ref, out_ref):
    blocks, parts, rows, width = x_ref.shape
    gate = up = None
    for part in range(parts):
        x = x_ref[:, part].reshape(blocks * rows, width)
        depth = pl.ds(part * width, width)
        g = jnp.dot(x, wg_ref[0, depth], preferred_element_type=jnp.float32)
        u = jnp.dot(x, wu_ref[0, depth], preferred_element_type=jnp.float32)
        gate = g if gate is None else gate + g
        up = u if up is None else up + u
    out_ref[0] = silu_up(gate, up, scale_ref[...], weight_ref[0])


def hidden_of(x, w_gate, w_up, scale, weight):
    blocks, parts, rows, width = x.shape
    experts, depth, units = w_gate.shape
    tokens = blocks * rows
    tile = tile_of(units, 256)
    tiles = units // tile
    wspec = pl.BlockSpec((1, depth, tile), lambda e, f: (e, 0, f))
    return pl.pallas_call(
        hidden_kernel,
        grid=(experts, tiles),
        in_specs=[
            pl.BlockSpec(x.shape, lambda e, f: (0, 0, 0, 0)),
            wspec,
            wspec,
            pl.BlockSpec((tokens, 1), lambda e, f: (0, 0)),
            pl.BlockSpec((1, tokens, 1), lambda e, f: (e, 0, 0)),
        ],
        out_specs=pl.BlockSpec((1, tokens, tile), lambda e, f: (e, 0, f)),
        out_shape=jax.ShapeDtypeStruct((experts, tokens, units), jnp.bfloat16),
        compiler_params=pltpu.CompilerParams(vmem_limit_bytes=VMEM_LIMIT),
    )(x, w_gate, w_up, scale, weight)


def down_kernel(h_ref, w_ref, out_ref):
    blocks, _, rows, tile = out_ref.shape
    y = None
    for e in range(h_ref.shape[0]):
        term = jnp.dot(h_ref[e], w_ref[e], preferred_element_type=jnp.float32)
        y = term if y is None else y + term
    out_ref[:, 0] = y.astype(jnp.bfloat16).reshape(blocks, rows, tile)


def down_of(hidden, w_down, blocks, parts):
    experts, tokens, units = hidden.shape
    width = w_down.shape[2] // parts
    rows = tokens // blocks
    tile = tile_of(width, 512)
    tiles = width // tile
    return pl.pallas_call(
        down_kernel,
        grid=(parts * tiles,),
        in_specs=[
            pl.BlockSpec((experts, tokens, units), lambda n: (0, 0, 0)),
            pl.BlockSpec((experts, units, tile), lambda n: (0, 0, n)),
        ],
        out_specs=pl.BlockSpec(
            (blocks, 1, rows, tile), lambda n: (0, n // tiles, 0, n % tiles)
        ),
        out_shape=jax.ShapeDtypeStruct((blocks, parts, rows, width), jnp.bfloat16),
        compiler_params=pltpu.CompilerParams(vmem_limit_bytes=VMEM_LIMIT),
    )(hidden, w_down)


def plain_experts(rows_out, side, w_gate, w_up, w_down):
    tp_count, ep_count = lax.axis_size("tp"), lax.axis_size("ep")
    rows, width = rows_out.shape
    exp_local = w_gate.shape[0]
    gathered = lax.all_gather(rows_out, ("ep", "tp"), axis=0, tiled=False)
    gathered = gathered.reshape(ep_count, tp_count, rows, width)
    side = lax.all_gather(side, "ep", axis=1, tiled=True)
    first_expert = 1 + lax.axis_index("ep") * exp_local
    weight = lax.dynamic_slice_in_dim(side, first_expert, exp_local, 0)[:, :, None]
    hidden = hidden_of(gathered, w_gate, w_up, side[0][:, None], weight)
    partial = down_of(hidden, w_down, ep_count, tp_count)
    partial = partial.reshape(ep_count * tp_count, rows, width)
    return lax.psum_scatter(partial, ("ep", "tp"), scatter_dimension=0, tiled=False)


def per_device(
    layer_input,
    stream,
    expert_ids,
    kv_owner,
    attn_norm,
    moe_norm,
    k_norm,
    w_kv,
    router,
    w_gate,
    w_up,
    w_down,
):
    rows = layer_input.shape[0]
    tp_count = lax.axis_size("tp")
    pair = tp_count == 2
    columns = 2 * KVH * HD
    expert_count = router.shape[1]
    first = layer_input.astype(jnp.float32)
    second = stream.astype(jnp.float32)

    rows_out = gained(stream, moe_norm)

    logits = lax.dot_general(
        router, rows_out, (((0,), (1,)), ((), ())), preferred_element_type=jnp.float32
    )
    squares = jnp.stack([jnp.sum(first * first, 1), jnp.sum(second * second, 1)], 0)
    small = jnp.concatenate([squares, logits], 0)
    if pair:
        small = small + lax.ppermute(small, "tp", [(0, 1), (1, 0)])
    else:
        small = lax.psum(small, "tp")
    first_scale = lax.rsqrt(small[0] / D + EPS)
    second_scale = lax.rsqrt(small[1:2] / D + EPS)
    logits = small[2:] * second_scale
    expert_range = jnp.arange(expert_count, dtype=jnp.int32)
    chosen = jnp.any(expert_ids.T[None, :, :] == expert_range[:, None, None], 1)
    top = jnp.max(jnp.where(chosen, logits, -jnp.inf), 0, keepdims=True)
    weights = jnp.where(chosen, jnp.exp(jnp.where(chosen, logits - top, 0.0)), 0.0)
    weights = weights / jnp.sum(weights, 0, keepdims=True)
    fill = jnp.zeros((-(1 + expert_count) % 8, rows), jnp.float32)
    side = jnp.concatenate([second_scale, weights, fill], 0)

    attn_in = (first * attn_norm.astype(jnp.float32)).astype(jnp.bfloat16)
    kv = jnp.dot(attn_in, w_kv, preferred_element_type=jnp.float32) * first_scale[:, None]
    owner_cap = 2 * rows // tp_count
    owner = kv_owner[:, 0]
    owner_hot = (owner[:, None] == jnp.arange(tp_count, dtype=jnp.int32)[None, :]).astype(jnp.int32)
    owner_slot = jnp.sum(
        (jnp.cumsum(owner_hot, 0, dtype=jnp.int32) - owner_hot) * owner_hot, 1, dtype=jnp.int32
    )
    if pair:
        owner = jnp.where(owner == lax.axis_index("tp"), 0, 1)
    target = owner * owner_cap + owner_slot
    placing = target[None, :] == jnp.arange(tp_count * owner_cap, dtype=jnp.int32)[:, None]
    placed = jnp.dot(
        placing.astype(jnp.bfloat16), kv.astype(jnp.bfloat16), preferred_element_type=jnp.float32
    )
    placed = placed.astype(jnp.bfloat16).reshape(tp_count, owner_cap, columns)
    if pair:
        arrived = lax.ppermute(placed[1], "tp", [(0, 1), (1, 0)])
        heads = placed[0].astype(jnp.float32) + arrived.astype(jnp.float32)
    else:
        arrived = lax.all_to_all(placed, "tp", split_axis=0, concat_axis=0, tiled=True)
        heads = jnp.sum(arrived.astype(jnp.float32), 0)
    heads = heads.reshape(owner_cap, 2 * KVH, HD)
    keys = heads[:, :KVH]
    keys = keys * lax.rsqrt(jnp.mean(keys * keys, 2, keepdims=True) + EPS)
    keys = keys * k_norm.astype(jnp.float32)
    kv_cache = jnp.concatenate([keys, heads[:, KVH:]], 1).astype(jnp.bfloat16)
    kv_cache = kv_cache.reshape(1, 1, owner_cap, columns)

    tiled = w_gate.shape[2] % MXU == 0 and stream.shape[1] % (2 * MXU) == 0
    ringed = pair and tiled and lax.axis_size("ep") % 2 == 0
    experts = ring_experts if ringed else plain_experts
    moe_out = experts(rows_out, side, w_gate, w_up, w_down)
    return (moe_out, kv_cache)


def solution(mesh):
    placed = (
        P(("group", "ep"), "tp"),
        P(("group", "ep"), "tp"),
        P(("group", "ep"), None),
        P(("group", "ep"), None),
        P("tp"),
        P("tp"),
        P(),
        P("tp", None),
        P("tp", None),
        P("ep", None, "tp"),
        P("ep", None, "tp"),
        P("ep", "tp", None),
    )
    return jax.shard_map(
        per_device,
        mesh=mesh,
        in_specs=placed,
        out_specs=(P(("group", "ep"), "tp"), P(("group", "ep"), "tp", None, None)),
        check_vma=False,
    )
```

```python
import functools

import jax
import jax.numpy as jnp
from jax import lax
from jax.experimental import pallas as pl
from jax.experimental.pallas import tpu as pltpu
from jax.sharding import PartitionSpec as P

D = 4096
KVH = 4
HD = 128
TOPK = 8


EPS = 1e-06
VMEM_LIMIT = 56 * 1024 * 1024
MXU = 256


def tile_of(size, most):
    for candidate in range(most, 127, -128):
        if size % candidate == 0:
            return candidate
    return size


def silu_up(gate, up, scale, weight):
    gate = gate * scale
    up = up * scale
    return (gate / (1.0 + jnp.exp(-gate)) * up * weight).astype(jnp.bfloat16)


def column_of(side, index):
    lane = lax.broadcasted_iota(jnp.int32, side.shape, 1)
    return jnp.sum(jnp.where(lane == index, side, 0.0), 1, keepdims=True)


def in_vmem(count):
    return [pl.BlockSpec(memory_space=pltpu.VMEM)] * count


def whole_call(body, outs, operands, after=None, kinds=None, scratch=(), limit=6, cost=None):
    kinds = kinds or [pltpu.VMEM] * len(operands)
    count = len(operands)

    token = jax.ShapeDtypeStruct((8, 128), jnp.float32)

    def with_token(*refs):
        inputs, rest = refs[:count], refs[count + 1 :]
        results, spare = rest[: len(outs)], rest[len(outs) + 1 :]
        rest[len(outs)][...] = jnp.zeros((8, 128), jnp.float32)
        body(*inputs, *results, *spare)

    if after is None:
        after = jnp.zeros((8, 128), jnp.float32)
    return pl.pallas_call(
        with_token,
        in_specs=[pl.BlockSpec(memory_space=kind) for kind in kinds]
        + [pl.BlockSpec(memory_space=pl.ANY)],
        out_specs=in_vmem(len(outs) + 1),
        out_shape=[*outs, token],
        scratch_shapes=scratch,
        compiler_params=pltpu.CompilerParams(vmem_limit_bytes=limit * 1024 * 1024),
        cost_estimate=cost,
    )(*operands, after)


def opening_kernel(x_ref, gain_ref, out_ref):
    gained = x_ref[...].astype(jnp.float32) * gain_ref[...].astype(jnp.float32)
    out_ref[...] = gained.astype(jnp.bfloat16)


def stats_kernel(first_ref, second_ref, rows_ref, router_ref, gain_ref, w_ref, small_ref, kv_ref):
    first = first_ref[...].astype(jnp.float32)
    second = second_ref[...].astype(jnp.float32)
    tokens = first.shape[0]
    squares = [jnp.sum(x * x, 1, keepdims=True) for x in (first, second)]
    logits = jnp.dot(rows_ref[...], router_ref[...], preferred_element_type=jnp.float32)
    fill = jnp.zeros((tokens, 128 - 2 - logits.shape[1]), jnp.float32)
    small = jnp.concatenate([squares[0], squares[1], logits, fill], 1)
    small_ref[...] = jnp.transpose(small)[: small_ref.shape[0]]
    attn_in = (first * gain_ref[...].astype(jnp.float32)).astype(jnp.bfloat16)
    kv_ref[...] = jnp.dot(attn_in, w_ref[...], preferred_element_type=jnp.float32)


def sides_kernel(where_ref, mine_ref, other_ref, ids_ref, owner_ref, kv_ref, side_ref, kept_ref, sent_ref):
    small = mine_ref[...] + other_ref[...]
    tokens = small.shape[1]
    fill = jnp.zeros((128 - small.shape[0], tokens), jnp.float32)
    sums = jnp.transpose(jnp.concatenate([small, fill], 0))
    lane = lax.broadcasted_iota(jnp.int32, (tokens, 128), 1)
    first_scale = lax.rsqrt(sums[:, 0:1] / D + EPS)
    second_scale = lax.rsqrt(sums[:, 1:2] / D + EPS)
    logits = sums * second_scale
    ids = ids_ref[...]
    chosen = lane == ids[:, 0:1] + 2
    for k in range(1, ids.shape[1]):
        chosen = chosen | (lane == ids[:, k : k + 1] + 2)
    top = jnp.max(jnp.where(chosen, logits, -jnp.inf), 1, keepdims=True)
    weights = jnp.where(chosen, jnp.exp(jnp.where(chosen, logits - top, 0.0)), 0.0)
    weights = weights / jnp.sum(weights, 1, keepdims=True)
    side = jnp.where(lane == 1, second_scale, weights)
    side_ref[...] = jnp.transpose(side)[: side_ref.shape[0]]

    theirs = jnp.where(owner_ref[...] == where_ref[0], 0, 1)
    hot = (lane == theirs).astype(jnp.float32)
    row = lax.broadcasted_iota(jnp.int32, (tokens, tokens), 0)
    column = lax.broadcasted_iota(jnp.int32, (tokens, tokens), 1)
    before = (column < row).astype(jnp.bfloat16)
    earlier = jnp.dot(before, hot.astype(jnp.bfloat16), preferred_element_type=jnp.float32)
    slot = jnp.sum(earlier * hot, 1, keepdims=True).astype(jnp.int32)
    kv = (kv_ref[...] * first_scale).astype(jnp.bfloat16)
    for side_of, out_ref in enumerate((kept_ref, sent_ref)):
        placing = jnp.where((slot == column) & (theirs == side_of), 1.0, 0.0)
        placing = jnp.transpose(placing).astype(jnp.bfloat16)
        out = jnp.dot(placing, kv, preferred_element_type=jnp.float32)
        out_ref[...] = out.astype(jnp.bfloat16)


def cache_kernel(kept_ref, arrived_ref, gain_ref, out_ref):
    gain = gain_ref[...].astype(jnp.float32)
    for head in range(2 * KVH):
        columns = slice(head * HD, (head + 1) * HD)
        x = kept_ref[:, columns].astype(jnp.float32) + arrived_ref[:, columns].astype(jnp.float32)
        if head < KVH:
            x = x * lax.rsqrt(jnp.mean(x * x, 1, keepdims=True) + EPS) * gain
        out_ref[:, columns] = x.astype(jnp.bfloat16)


def joined_kernel(first_ref, second_ref, out_ref):
    tokens = first_ref.shape[1]
    out_ref[:, :tokens] = first_ref[...]
    out_ref[:, tokens:] = second_ref[...]


def tied(arrays, after):
    count = len(arrays)
    anywhere = pl.BlockSpec(memory_space=pl.ANY)

    def kernel(*refs):
        refs[-1][...] = jnp.zeros((8, 128), jnp.float32)

    shapes = [jax.ShapeDtypeStruct(x.shape, x.dtype) for x in arrays]
    return pl.pallas_call(
        kernel,
        in_specs=[anywhere] * (count + 1),
        out_specs=[anywhere] * count + in_vmem(1),
        out_shape=[*shapes, jax.ShapeDtypeStruct((8, 128), jnp.float32)],
        input_output_aliases={n: n for n in range(count)},
    )(*arrays, after)


def sum_kernel(part, count, *refs):
    terms = [ref[part] if len(ref.shape) == 3 else ref[...] for ref in refs[:count]]
    refs[count][...] = total(*terms)


def summed(part, terms, after):
    out = jax.ShapeDtypeStruct(terms[-1].shape[-2:], jnp.bfloat16)
    body = functools.partial(sum_kernel, part, len(terms))
    return whole_call(body, [out], terms, after)


def paired_products(rows, steps):
    def stage(index):
        _, first_tile, second_tile = steps[index]
        pltpu.matmul_push_rhs(first_tile(), index % 2, 0)
        pltpu.matmul_push_rhs(second_tile(), index % 2, 1)

    def run(first_acc, second_acc):
        stage(0)
        for index, (lhs, _, _) in enumerate(steps):
            if index + 1 < len(steps):
                stage(index + 1)
            left = lhs()
            pltpu.matmul_acc_lhs(first_acc, left, index % 2)
            pltpu.matmul_acc_lhs(second_acc, left, index % 2)
        return pltpu.matmul_pop(first_acc), pltpu.matmul_pop(second_acc)

    return pl.run_scoped(
        run, pltpu.ACC(0)((rows, MXU), jnp.float32), pltpu.ACC(1)((rows, MXU), jnp.float32)
    )


def load_kernel(source_ref, held_ref, sem):
    copies = [
        pltpu.make_async_copy(source_ref.at[e], held_ref.at[e], sem.at[e])
        for e in range(source_ref.shape[0])
    ]
    for copy in copies:
        copy.start()
    for copy in copies:
        copy.wait()


def loaded(w, after):
    return whole_call(
        load_kernel,
        [pltpu.VMEM(w.shape, w.dtype)],
        [pltpu.with_memory_space_constraint(w, pltpu.HBM)],
        after,
        kinds=[pl.ANY],
        scratch=[pltpu.SemaphoreType.DMA((w.shape[0],))],
        limit=1,
        cost=pl.CostEstimate(flops=0, bytes_accessed=2 * w.size, transcendentals=0),
    )


def block_hidden_kernel(
    where_ref, own_ref, other_ref, sib_own_ref, sib_other_ref, side_ref, wg_ref, wu_ref,
    out_ref, x_ref,
):
    rows, width = own_ref.shape
    experts, depth, units = wg_ref.shape
    mine = pl.ds(pl.multiple_of(where_ref[0] * width, width), width)
    theirs = pl.ds(pl.multiple_of((1 - where_ref[0]) * width, width), width)
    x_ref[0:rows, mine] = own_ref[...]
    x_ref[0:rows, theirs] = other_ref[...]
    x_ref[rows : 2 * rows, mine] = sib_own_ref[...]
    x_ref[rows : 2 * rows, theirs] = sib_other_ref[...]
    side = jnp.transpose(side_ref[...])
    scale = column_of(side, 1)

    @pl.loop(0, experts)
    def _(e):
        weight = column_of(side, 2 + where_ref[1] + e)
        for tile in range(units // MXU):
            columns = pl.ds(tile * MXU, MXU)

            def step(k):
                part = pl.ds(k * MXU, MXU)
                return (
                    lambda: x_ref[:, part],
                    lambda: wg_ref[e, part, columns],
                    lambda: wu_ref[e, part, columns],
                )

            steps = [step(k) for k in range(depth // MXU)]
            gate, up = paired_products(2 * rows, steps)
            out_ref[e, :, columns] = silu_up(gate, up, scale, weight)


def block_hidden(where, chunks, side, w_gate, w_up, after):
    rows, _ = chunks[0].shape
    experts, depth, units = w_gate.shape
    return whole_call(
        block_hidden_kernel,
        [jax.ShapeDtypeStruct((experts, 2 * rows, units), jnp.bfloat16)],
        [where, *chunks, side, w_gate, w_up],
        after,
        kinds=[pltpu.SMEM] + [pltpu.VMEM] * 7,
        scratch=[pltpu.VMEM((2 * rows, depth), jnp.bfloat16)],
        cost=pl.CostEstimate(
            flops=8 * rows * depth * units * experts,
            bytes_accessed=4 * rows * depth,
            transcendentals=2 * rows * units * experts,
        ),
    )


def block_down_kernel(where_ref, h_ref, w_ref, own_ref, sib_ref, held_ref, sem):
    _, rows, width = own_ref.shape
    experts, _, units = h_ref.shape
    slots, tile = held_ref.shape[0], held_ref.shape[3]
    tiles = width // tile

    def fetch(n):
        half, part = n // tiles, n % tiles
        first = (half + where_ref[0] - 2 * half * where_ref[0]) * width
        columns = pl.ds(pl.multiple_of(first + part * tile, tile), tile)
        return pltpu.make_async_copy(
            w_ref.at[:, :, columns], held_ref.at[n % slots], sem.at[n % slots]
        )

    for n in range(slots - 1):
        fetch(n).start()
    for n in range(2 * tiles):
        if n + slots - 1 < 2 * tiles:
            fetch(n + slots - 1).start()
        fetch(n).wait()

        def step(e, k):
            part = pl.ds(k * MXU, MXU)
            return (
                lambda: h_ref[e, :, part],
                lambda: held_ref[n % slots, e, part, 0:MXU],
                lambda: held_ref[n % slots, e, part, MXU : 2 * MXU],
            )

        steps = [step(e, k) for e in range(experts) for k in range(units // MXU)]
        for m, y in enumerate(paired_products(2 * rows, steps)):
            columns = pl.ds((n % tiles) * tile + m * MXU, MXU)
            own_ref[n // tiles, :, columns] = y[:rows].astype(jnp.bfloat16)
            sib_ref[n // tiles, :, columns] = y[rows:].astype(jnp.bfloat16)


def block_down(where, hidden, w_down, after):
    experts, tokens, units = hidden.shape
    rows, width = tokens // 2, w_down.shape[2] // 2
    out = jax.ShapeDtypeStruct((2, rows, width), jnp.bfloat16)
    slots = 4
    return whole_call(
        block_down_kernel,
        [out, out],
        [where, hidden, pltpu.with_memory_space_constraint(w_down, pltpu.HBM)],
        after,
        kinds=[pltpu.SMEM, pltpu.VMEM, pl.ANY],
        scratch=[
            pltpu.VMEM((slots, experts, units, 2 * MXU), jnp.bfloat16),
            pltpu.SemaphoreType.DMA((slots,)),
        ],
        limit=10,
        cost=pl.CostEstimate(
            flops=4 * experts * tokens * units * width,
            bytes_accessed=4 * (experts * units + tokens) * width,
            transcendentals=0,
        ),
    )


def total(*terms):
    return sum(term.astype(jnp.float32) for term in terms).astype(jnp.bfloat16)


def ring_device(
    layer_input,
    stream,
    expert_ids,
    kv_owner,
    attn_norm,
    moe_norm,
    k_norm,
    w_kv,
    router,
    w_gate,
    w_up,
    w_down,
):
    ep_count = lax.axis_size("ep")
    chips = ep_count // 2
    forward = [(d, (d + 2) % ep_count) for d in range(ep_count)]
    siblings = [(d, d ^ 1) for d in range(ep_count)]
    along = functools.partial(lax.ppermute, axis_name="ep", perm=forward)
    beside = functools.partial(lax.ppermute, axis_name="ep", perm=siblings)
    across = functools.partial(lax.ppermute, axis_name="tp", perm=[(0, 1), (1, 0)])
    where = jnp.stack([lax.axis_index("tp"), lax.axis_index("ep") * w_gate.shape[0]])
    where = where.astype(jnp.int32)
    rows = stream.shape[0]
    side_rows = -(-(2 + router.shape[1]) // 8) * 8
    columns = w_kv.shape[1]
    row_shape = jax.ShapeDtypeStruct(stream.shape, jnp.bfloat16)
    small_shape = jax.ShapeDtypeStruct((side_rows, rows), jnp.float32)
    kv_shape = jax.ShapeDtypeStruct((rows, columns), jnp.float32)
    pair_shape = jax.ShapeDtypeStruct((side_rows, 2 * rows), jnp.float32)
    placed_shape = jax.ShapeDtypeStruct((rows, columns), jnp.bfloat16)

    rows_out, token = whole_call(opening_kernel, [row_shape], [stream, moe_norm[None]])
    lane, crossed = [rows_out, along(rows_out)], [across(rows_out)]

    operands = [layer_input, stream, rows_out, router, attn_norm[None], w_kv]
    small, kv, token = whole_call(
        stats_kernel, [small_shape, kv_shape], operands, token, limit=16
    )
    small_other = across(small)
    gate_held, token = loaded(w_gate, token)
    up_held, token = loaded(w_up, token)
    lane[1], crossed[0], token = tied([lane[1], crossed[0]], token)
    for _ in range(chips - 2):
        lane.append(along(lane[-1]))
    for s in range(1, chips):
        crossed.append(across(lane[s]))

    operands = [where, small, small_other, expert_ids, kv_owner, kv]
    side, kept, sent, token = whole_call(
        sides_kernel,
        [small_shape, placed_shape, placed_shape],
        operands,
        token,
        kinds=[pltpu.SMEM] + [pltpu.VMEM] * 5,
    )
    arrived = across(sent)
    side, token = whole_call(joined_kernel, [pair_shape], [side, beside(side)], token)
    sides = [side]
    for _ in range(chips - 1):
        sides.append(along(sides[-1]))

    hidden, own, back, swapped = [[None] * chips for _ in range(4)]

    def up(s, after):
        chunks = (lane[s], crossed[s], beside(lane[s]), beside(crossed[s]))
        hidden[s], after = block_hidden(where, chunks, sides[s], gate_held, up_held, after)
        return after

    def down(s, after):
        own[s], sib, after = block_down(where, hidden[s], w_down, after)
        back[s] = beside(sib)
        return after

    def swap(s, after):
        sent, after = summed(1, [own[s], back[s]], after)
        swapped[s] = across(sent)
        return after

    def gather(s, travelling, after):
        terms = [own[s], back[s], swapped[s]] + travelling
        return summed(0, terms, after)

    token = up(0, token)
    token = up(1, token)
    token = down(1, token)
    kv_cache, token = whole_call(
        cache_kernel, [placed_shape], [kept, arrived, k_norm[None]], token
    )
    token = swap(1, token)
    travelling = []
    for s in range(1, chips - 1):
        token = up(s + 1, token) if s == 1 else token
        token = down(s + 1, token) if s == 1 else token
        passed, token = gather(s, travelling, token)
        travelling = [along(passed)]
        token = swap(s + 1, token)
        if s == 1:
            token = up(3, token)
            token = down(3, token)
    token = down(0, token)
    token = swap(0, token)
    passed, token = gather(chips - 1, travelling, token)
    moe_out, token = gather(0, [along(passed)], token)
    return moe_out, kv_cache.reshape(1, 1, rows, columns)


def hidden_kernel(x_ref, wg_ref, wu_ref, scale_ref, weight_ref, out_ref):
    blocks, parts, rows, width = x_ref.shape
    gate = up = None
    for part in range(parts):
        x = x_ref[:, part].reshape(blocks * rows, width)
        depth = pl.ds(part * width, width)
        g = jnp.dot(x, wg_ref[0, depth], preferred_element_type=jnp.float32)
        u = jnp.dot(x, wu_ref[0, depth], preferred_element_type=jnp.float32)
        gate = g if gate is None else gate + g
        up = u if up is None else up + u
    out_ref[0] = silu_up(gate, up, scale_ref[...], weight_ref[0])


def hidden_of(x, w_gate, w_up, scale, weight):
    blocks, parts, rows, width = x.shape
    experts, depth, units = w_gate.shape
    tokens = blocks * rows
    tile = tile_of(units, 256)
    tiles = units // tile
    wspec = pl.BlockSpec((1, depth, tile), lambda e, f: (e, 0, f))
    return pl.pallas_call(
        hidden_kernel,
        grid=(experts, tiles),
        in_specs=[
            pl.BlockSpec(x.shape, lambda e, f: (0, 0, 0, 0)),
            wspec,
            wspec,
            pl.BlockSpec((tokens, 1), lambda e, f: (0, 0)),
            pl.BlockSpec((1, tokens, 1), lambda e, f: (e, 0, 0)),
        ],
        out_specs=pl.BlockSpec((1, tokens, tile), lambda e, f: (e, 0, f)),
        out_shape=jax.ShapeDtypeStruct((experts, tokens, units), jnp.bfloat16),
        compiler_params=pltpu.CompilerParams(vmem_limit_bytes=VMEM_LIMIT),
    )(x, w_gate, w_up, scale, weight)


def down_kernel(h_ref, w_ref, out_ref):
    blocks, _, rows, tile = out_ref.shape
    y = None
    for e in range(h_ref.shape[0]):
        term = jnp.dot(h_ref[e], w_ref[e], preferred_element_type=jnp.float32)
        y = term if y is None else y + term
    out_ref[:, 0] = y.astype(jnp.bfloat16).reshape(blocks, rows, tile)


def down_of(hidden, w_down, blocks, parts):
    experts, tokens, units = hidden.shape
    width = w_down.shape[2] // parts
    rows = tokens // blocks
    tile = tile_of(width, 512)
    tiles = width // tile
    return pl.pallas_call(
        down_kernel,
        grid=(parts * tiles,),
        in_specs=[
            pl.BlockSpec((experts, tokens, units), lambda n: (0, 0, 0)),
            pl.BlockSpec((experts, units, tile), lambda n: (0, 0, n)),
        ],
        out_specs=pl.BlockSpec(
            (blocks, 1, rows, tile), lambda n: (0, n // tiles, 0, n % tiles)
        ),
        out_shape=jax.ShapeDtypeStruct((blocks, parts, rows, width), jnp.bfloat16),
        compiler_params=pltpu.CompilerParams(vmem_limit_bytes=VMEM_LIMIT),
    )(hidden, w_down)


def plain_experts(rows_out, side, w_gate, w_up, w_down):
    tp_count, ep_count = lax.axis_size("tp"), lax.axis_size("ep")
    rows, width = rows_out.shape
    exp_local = w_gate.shape[0]
    gathered = lax.all_gather(rows_out, ("ep", "tp"), axis=0, tiled=False)
    gathered = gathered.reshape(ep_count, tp_count, rows, width)
    side = lax.all_gather(side, "ep", axis=1, tiled=True)
    first_expert = 1 + lax.axis_index("ep") * exp_local
    weight = lax.dynamic_slice_in_dim(side, first_expert, exp_local, 0)[:, :, None]
    hidden = hidden_of(gathered, w_gate, w_up, side[0][:, None], weight)
    partial = down_of(hidden, w_down, ep_count, tp_count)
    partial = partial.reshape(ep_count * tp_count, rows, width)
    return lax.psum_scatter(partial, ("ep", "tp"), scatter_dimension=0, tiled=False)


def per_device(
    layer_input,
    stream,
    expert_ids,
    kv_owner,
    attn_norm,
    moe_norm,
    k_norm,
    w_kv,
    router,
    w_gate,
    w_up,
    w_down,
):
    rows = layer_input.shape[0]
    tp_count = lax.axis_size("tp")
    tiled = w_gate.shape[2] % MXU == 0 and stream.shape[1] % (2 * MXU) == 0
    if tp_count == 2 and tiled and rows == 128 and lax.axis_size("ep") == 8:
        return ring_device(
            layer_input, stream, expert_ids, kv_owner, attn_norm, moe_norm, k_norm, w_kv, router,
            w_gate, w_up, w_down,
        )
    columns = 2 * KVH * HD
    expert_count = router.shape[1]
    first = layer_input.astype(jnp.float32)
    second = stream.astype(jnp.float32)

    rows_out = (second * moe_norm.astype(jnp.float32)).astype(jnp.bfloat16)

    logits = lax.dot_general(
        router, rows_out, (((0,), (1,)), ((), ())), preferred_element_type=jnp.float32
    )
    squares = jnp.stack([jnp.sum(first * first, 1), jnp.sum(second * second, 1)], 0)
    small = jnp.concatenate([squares, logits], 0)
    small = lax.psum(small, "tp")
    first_scale = lax.rsqrt(small[0] / D + EPS)
    second_scale = lax.rsqrt(small[1:2] / D + EPS)
    logits = small[2:] * second_scale
    expert_range = jnp.arange(expert_count, dtype=jnp.int32)
    chosen = jnp.any(expert_ids.T[None, :, :] == expert_range[:, None, None], 1)
    top = jnp.max(jnp.where(chosen, logits, -jnp.inf), 0, keepdims=True)
    weights = jnp.where(chosen, jnp.exp(jnp.where(chosen, logits - top, 0.0)), 0.0)
    weights = weights / jnp.sum(weights, 0, keepdims=True)
    fill = jnp.zeros((-(1 + expert_count) % 8, rows), jnp.float32)
    side = jnp.concatenate([second_scale, weights, fill], 0)

    attn_in = (first * attn_norm.astype(jnp.float32)).astype(jnp.bfloat16)
    kv = jnp.dot(attn_in, w_kv, preferred_element_type=jnp.float32) * first_scale[:, None]
    owner_cap = 2 * rows // tp_count
    owner = kv_owner[:, 0]
    owner_hot = (owner[:, None] == jnp.arange(tp_count, dtype=jnp.int32)[None, :]).astype(jnp.int32)
    owner_slot = jnp.sum(
        (jnp.cumsum(owner_hot, 0, dtype=jnp.int32) - owner_hot) * owner_hot, 1, dtype=jnp.int32
    )
    target = owner * owner_cap + owner_slot
    placing = target[None, :] == jnp.arange(tp_count * owner_cap, dtype=jnp.int32)[:, None]
    placed = jnp.dot(
        placing.astype(jnp.bfloat16), kv.astype(jnp.bfloat16), preferred_element_type=jnp.float32
    )
    placed = placed.astype(jnp.bfloat16).reshape(tp_count, owner_cap, columns)
    arrived = lax.all_to_all(placed, "tp", split_axis=0, concat_axis=0, tiled=True)
    heads = jnp.sum(arrived.astype(jnp.float32), 0)
    heads = heads.reshape(owner_cap, 2 * KVH, HD)
    keys = heads[:, :KVH]
    keys = keys * lax.rsqrt(jnp.mean(keys * keys, 2, keepdims=True) + EPS)
    keys = keys * k_norm.astype(jnp.float32)
    kv_cache = jnp.concatenate([keys, heads[:, KVH:]], 1).astype(jnp.bfloat16)
    kv_cache = kv_cache.reshape(1, 1, owner_cap, columns)

    moe_out = plain_experts(rows_out, side, w_gate, w_up, w_down)
    return (moe_out, kv_cache)


def solution(mesh):
    placed = (
        P(("group", "ep"), "tp"),
        P(("group", "ep"), "tp"),
        P(("group", "ep"), None),
        P(("group", "ep"), None),
        P("tp"),
        P("tp"),
        P(),
        P("tp", None),
        P("tp", None),
        P("ep", None, "tp"),
        P("ep", None, "tp"),
        P("ep", "tp", None),
    )
    return jax.shard_map(
        per_device,
        mesh=mesh,
        in_specs=placed,
        out_specs=(P(("group", "ep"), "tp"), P(("group", "ep"), "tp", None, None)),
        check_vma=False,
    )
```

```python
import functools

import jax
import jax.numpy as jnp
from jax import lax
from jax.experimental import pallas as pl
from jax.experimental.pallas import tpu as pltpu
from jax.sharding import PartitionSpec as P

D = 4096
KVH = 4
HD = 128
TOPK = 8


EPS = 1e-06
VMEM_LIMIT = 56 * 1024 * 1024
MXU = 256


def weight_work(rows, *weights):
    size = sum(w.size for w in weights)
    return pl.CostEstimate(flops=2 * rows * size, bytes_accessed=2 * size, transcendentals=0)


BRIEF = pl.CostEstimate(flops=1, bytes_accessed=1, transcendentals=0)


def tile_of(size, most):
    for candidate in range(most, 127, -128):
        if size % candidate == 0:
            return candidate
    return size


def silu_up(gate, up, scale, weight):
    gate = gate * scale
    up = up * scale
    return (gate / (1.0 + jnp.exp(-gate)) * up * weight).astype(jnp.bfloat16)


def column_of(side, index):
    lane = lax.broadcasted_iota(jnp.int32, side.shape, 1)
    return jnp.sum(jnp.where(lane == index, side, 0.0), 1, keepdims=True)


def in_vmem(count):
    return [pl.BlockSpec(memory_space=pltpu.VMEM)] * count


def whole_call(body, outs, operands, after=None, kinds=None, scratch=(), limit=6, work=BRIEF):
    kinds = kinds or [pltpu.VMEM] * len(operands)
    count = len(operands)

    token = jax.ShapeDtypeStruct((8, 128), jnp.float32)

    def with_token(*refs):
        inputs, rest = refs[:count], refs[count + 1 :]
        results, spare = rest[: len(outs)], rest[len(outs) + 1 :]
        rest[len(outs)][...] = jnp.zeros((8, 128), jnp.float32)
        body(*inputs, *results, *spare)

    if after is None:
        after = jnp.zeros((8, 128), jnp.float32)
    return pl.pallas_call(
        with_token,
        in_specs=[pl.BlockSpec(memory_space=kind) for kind in kinds]
        + [pl.BlockSpec(memory_space=pl.ANY)],
        out_specs=in_vmem(len(outs) + 1),
        out_shape=[*outs, token],
        scratch_shapes=scratch,
        compiler_params=pltpu.CompilerParams(vmem_limit_bytes=limit * 1024 * 1024),
        cost_estimate=work,
    )(*operands, after)


def opening_kernel(x_ref, gain_ref, out_ref):
    gained = x_ref[...].astype(jnp.float32) * gain_ref[...].astype(jnp.float32)
    out_ref[...] = gained.astype(jnp.bfloat16)


def stats_kernel(first_ref, second_ref, rows_ref, router_ref, small_ref):
    first = first_ref[...].astype(jnp.float32)
    second = second_ref[...].astype(jnp.float32)
    squares = [jnp.sum(x * x, 1, keepdims=True) for x in (first, second)]
    logits = jnp.dot(rows_ref[...], router_ref[...], preferred_element_type=jnp.float32)
    fill = jnp.zeros((first.shape[0], 128 - 2 - logits.shape[1]), jnp.float32)
    small = jnp.concatenate([squares[0], squares[1], logits, fill], 1)
    small_ref[...] = jnp.transpose(small)[: small_ref.shape[0]]


def sides_kernel(mine_ref, other_ref, ids_ref, side_ref, scale_ref):
    small = mine_ref[...] + other_ref[...]
    tokens = small.shape[1]
    fill = jnp.zeros((128 - small.shape[0], tokens), jnp.float32)
    sums = jnp.transpose(jnp.concatenate([small, fill], 0))
    lane = lax.broadcasted_iota(jnp.int32, (tokens, 128), 1)
    scale_ref[...] = jnp.broadcast_to(lax.rsqrt(sums[:, 0:1] / D + EPS), scale_ref.shape)
    second_scale = lax.rsqrt(sums[:, 1:2] / D + EPS)
    logits = sums * second_scale
    ids = ids_ref[...]
    chosen = lane == ids[:, 0:1] + 2
    for k in range(1, ids.shape[1]):
        chosen = chosen | (lane == ids[:, k : k + 1] + 2)
    top = jnp.max(jnp.where(chosen, logits, -jnp.inf), 1, keepdims=True)
    weights = jnp.where(chosen, jnp.exp(jnp.where(chosen, logits - top, 0.0)), 0.0)
    weights = weights / jnp.sum(weights, 1, keepdims=True)
    side = jnp.where(lane == 1, second_scale, weights)
    side_ref[...] = jnp.transpose(side)[: side_ref.shape[0]]


def rows_kernel(where_ref, first_ref, gain_ref, w_ref, scale_ref, owner_ref, kept_ref, sent_ref):
    tokens = first_ref.shape[0]
    attn_in = first_ref[...].astype(jnp.float32) * gain_ref[...].astype(jnp.float32)
    kv = jnp.dot(attn_in.astype(jnp.bfloat16), w_ref[...], preferred_element_type=jnp.float32)
    kv = (kv * scale_ref[:, 0:1]).astype(jnp.bfloat16)
    lane = lax.broadcasted_iota(jnp.int32, (tokens, 128), 1)
    theirs = jnp.where(owner_ref[...] == where_ref[0], 0, 1)
    hot = (lane == theirs).astype(jnp.float32)
    row = lax.broadcasted_iota(jnp.int32, (tokens, tokens), 0)
    column = lax.broadcasted_iota(jnp.int32, (tokens, tokens), 1)
    before = (column < row).astype(jnp.bfloat16)
    earlier = jnp.dot(before, hot.astype(jnp.bfloat16), preferred_element_type=jnp.float32)
    slot = jnp.sum(earlier * hot, 1, keepdims=True).astype(jnp.int32)
    for side, out_ref in enumerate((kept_ref, sent_ref)):
        placing = jnp.where((slot == column) & (theirs == side), 1.0, 0.0)
        placing = jnp.transpose(placing).astype(jnp.bfloat16)
        out = jnp.dot(placing, kv, preferred_element_type=jnp.float32)
        out_ref[...] = out.astype(jnp.bfloat16)


def cache_kernel(kept_ref, arrived_ref, gain_ref, out_ref):
    gain = gain_ref[...].astype(jnp.float32)
    for head in range(2 * KVH):
        columns = slice(head * HD, (head + 1) * HD)
        x = kept_ref[:, columns].astype(jnp.float32) + arrived_ref[:, columns].astype(jnp.float32)
        if head < KVH:
            x = x * lax.rsqrt(jnp.mean(x * x, 1, keepdims=True) + EPS) * gain
        out_ref[:, columns] = x.astype(jnp.bfloat16)


def joined_kernel(first_ref, second_ref, out_ref):
    tokens = first_ref.shape[1]
    out_ref[:, :tokens] = first_ref[...]
    out_ref[:, tokens:] = second_ref[...]


def tied(arrays, after):
    count = len(arrays)
    anywhere = pl.BlockSpec(memory_space=pl.ANY)

    def kernel(*refs):
        refs[-1][...] = jnp.zeros((8, 128), jnp.float32)

    shapes = [jax.ShapeDtypeStruct(x.shape, x.dtype) for x in arrays]
    return pl.pallas_call(
        kernel,
        in_specs=[anywhere] * (count + 1),
        out_specs=[anywhere] * count + in_vmem(1),
        out_shape=[*shapes, jax.ShapeDtypeStruct((8, 128), jnp.float32)],
        input_output_aliases={n: n for n in range(count)},
        cost_estimate=BRIEF,
    )(*arrays, after)


def sum_kernel(part, count, *refs):
    terms = [ref[part] if len(ref.shape) == 3 else ref[...] for ref in refs[:count]]
    refs[count][...] = total(*terms)


def summed(part, terms, after):
    out = jax.ShapeDtypeStruct(terms[-1].shape[-2:], jnp.bfloat16)
    body = functools.partial(sum_kernel, part, len(terms))
    return whole_call(body, [out], terms, after)


def paired_products(rows, steps):
    def stage(index):
        _, first_tile, second_tile = steps[index]
        pltpu.matmul_push_rhs(first_tile(), index % 2, 0)
        pltpu.matmul_push_rhs(second_tile(), index % 2, 1)

    def run(first_acc, second_acc):
        stage(0)
        for index, (lhs, _, _) in enumerate(steps):
            if index + 1 < len(steps):
                stage(index + 1)
            left = lhs()
            pltpu.matmul_acc_lhs(first_acc, left, index % 2)
            pltpu.matmul_acc_lhs(second_acc, left, index % 2)
        return pltpu.matmul_pop(first_acc), pltpu.matmul_pop(second_acc)

    return pl.run_scoped(
        run, pltpu.ACC(0)((rows, MXU), jnp.float32), pltpu.ACC(1)((rows, MXU), jnp.float32)
    )


def load_kernel(source_ref, held_ref, sem):
    copies = [
        pltpu.make_async_copy(source_ref.at[e], held_ref.at[e], sem.at[e])
        for e in range(source_ref.shape[0])
    ]
    for copy in copies:
        copy.start()
    for copy in copies:
        copy.wait()


def loaded(w, after):
    return whole_call(
        load_kernel,
        [pltpu.VMEM(w.shape, w.dtype)],
        [pltpu.with_memory_space_constraint(w, pltpu.HBM)],
        after,
        kinds=[pl.ANY],
        scratch=[pltpu.SemaphoreType.DMA((w.shape[0],))],
        limit=1,
        work=weight_work(1, w),
    )


def block_hidden_kernel(
    where_ref, own_ref, other_ref, sib_own_ref, sib_other_ref, side_ref, wg_ref, wu_ref,
    out_ref, x_ref,
):
    rows, width = own_ref.shape
    experts, depth, units = wg_ref.shape
    mine = pl.ds(pl.multiple_of(where_ref[0] * width, width), width)
    theirs = pl.ds(pl.multiple_of((1 - where_ref[0]) * width, width), width)
    x_ref[0:rows, mine] = own_ref[...]
    x_ref[0:rows, theirs] = other_ref[...]
    x_ref[rows : 2 * rows, mine] = sib_own_ref[...]
    x_ref[rows : 2 * rows, theirs] = sib_other_ref[...]
    side = jnp.transpose(side_ref[...])
    scale = column_of(side, 1)

    @pl.loop(0, experts)
    def _(e):
        weight = column_of(side, 2 + where_ref[1] + e)
        for tile in range(units // MXU):
            columns = pl.ds(tile * MXU, MXU)

            def step(k):
                part = pl.ds(k * MXU, MXU)
                return (
                    lambda: x_ref[:, part],
                    lambda: wg_ref[e, part, columns],
                    lambda: wu_ref[e, part, columns],
                )

            steps = [step(k) for k in range(depth // MXU)]
            gate, up = paired_products(2 * rows, steps)
            out_ref[e, :, columns] = silu_up(gate, up, scale, weight)


def block_hidden(where, chunks, side, w_gate, w_up, after):
    rows, _ = chunks[0].shape
    experts, depth, units = w_gate.shape
    return whole_call(
        block_hidden_kernel,
        [jax.ShapeDtypeStruct((experts, 2 * rows, units), jnp.bfloat16)],
        [where, *chunks, side, w_gate, w_up],
        after,
        kinds=[pltpu.SMEM] + [pltpu.VMEM] * 7,
        scratch=[pltpu.VMEM((2 * rows, depth), jnp.bfloat16)],
        work=weight_work(2 * rows, w_gate, w_up),
    )


def block_down_kernel(where_ref, h_ref, w_ref, own_ref, sib_ref, held_ref, sem):
    _, rows, width = own_ref.shape
    experts, _, units = h_ref.shape
    slots, tile = held_ref.shape[0], held_ref.shape[3]
    tiles = width // tile

    def fetch(n):
        half, part = n // tiles, n % tiles
        first = (half + where_ref[0] - 2 * half * where_ref[0]) * width
        columns = pl.ds(pl.multiple_of(first + part * tile, tile), tile)
        return pltpu.make_async_copy(
            w_ref.at[:, :, columns], held_ref.at[n % slots], sem.at[n % slots]
        )

    for n in range(slots - 1):
        fetch(n).start()
    for n in range(2 * tiles):
        if n + slots - 1 < 2 * tiles:
            fetch(n + slots - 1).start()
        fetch(n).wait()

        def step(e, k):
            part = pl.ds(k * MXU, MXU)
            return (
                lambda: h_ref[e, :, part],
                lambda: held_ref[n % slots, e, part, 0:MXU],
                lambda: held_ref[n % slots, e, part, MXU : 2 * MXU],
            )

        steps = [step(e, k) for e in range(experts) for k in range(units // MXU)]
        for m, y in enumerate(paired_products(2 * rows, steps)):
            columns = pl.ds((n % tiles) * tile + m * MXU, MXU)
            own_ref[n // tiles, :, columns] = y[:rows].astype(jnp.bfloat16)
            sib_ref[n // tiles, :, columns] = y[rows:].astype(jnp.bfloat16)


def block_down(where, hidden, w_down, after):
    experts, tokens, units = hidden.shape
    rows, width = tokens // 2, w_down.shape[2] // 2
    out = jax.ShapeDtypeStruct((2, rows, width), jnp.bfloat16)
    slots = 4
    return whole_call(
        block_down_kernel,
        [out, out],
        [where, hidden, pltpu.with_memory_space_constraint(w_down, pltpu.HBM)],
        after,
        kinds=[pltpu.SMEM, pltpu.VMEM, pl.ANY],
        scratch=[
            pltpu.VMEM((slots, experts, units, 2 * MXU), jnp.bfloat16),
            pltpu.SemaphoreType.DMA((slots,)),
        ],
        limit=10,
        work=weight_work(tokens, w_down),
    )


def total(*terms):
    return sum(term.astype(jnp.float32) for term in terms).astype(jnp.bfloat16)


def ring_device(
    layer_input,
    stream,
    expert_ids,
    kv_owner,
    attn_norm,
    moe_norm,
    k_norm,
    w_kv,
    router,
    w_gate,
    w_up,
    w_down,
):
    ep_count = lax.axis_size("ep")
    chips = ep_count // 2
    forward = [(d, (d + 2) % ep_count) for d in range(ep_count)]
    siblings = [(d, d ^ 1) for d in range(ep_count)]
    along = functools.partial(lax.ppermute, axis_name="ep", perm=forward)
    beside = functools.partial(lax.ppermute, axis_name="ep", perm=siblings)
    across = functools.partial(lax.ppermute, axis_name="tp", perm=[(0, 1), (1, 0)])
    where = jnp.stack([lax.axis_index("tp"), lax.axis_index("ep") * w_gate.shape[0]])
    where = where.astype(jnp.int32)
    rows = stream.shape[0]
    side_rows = -(-(2 + router.shape[1]) // 8) * 8
    columns = w_kv.shape[1]
    row_shape = jax.ShapeDtypeStruct(stream.shape, jnp.bfloat16)
    small_shape = jax.ShapeDtypeStruct((side_rows, rows), jnp.float32)
    scale_shape = jax.ShapeDtypeStruct((rows, 128), jnp.float32)
    pair_shape = jax.ShapeDtypeStruct((side_rows, 2 * rows), jnp.float32)
    placed_shape = jax.ShapeDtypeStruct((rows, columns), jnp.bfloat16)

    layer_input, stream, w_kv = [
        pltpu.with_memory_space_constraint(x, pltpu.HBM) for x in (layer_input, stream, w_kv)
    ]

    rows_out, token = whole_call(opening_kernel, [row_shape], [stream, moe_norm[None]])
    lane, crossed = [rows_out, along(rows_out)], [across(rows_out)]
    where, expert_ids, kv_owner, attn_gain, key_gain, token = tied(
        [where, expert_ids, kv_owner, attn_norm[None], k_norm[None]], token
    )

    small, token = whole_call(
        stats_kernel, [small_shape], [layer_input, stream, rows_out, router], token
    )
    small_other = across(small)
    gate_held, token = loaded(w_gate, token)
    lane[1], crossed[0], small_other, token = tied([lane[1], crossed[0], small_other], token)
    lane.append(along(lane[1]))
    crossed.append(across(lane[1]))
    side, scale, token = whole_call(
        sides_kernel, [small_shape, scale_shape], [small, small_other, expert_ids], token
    )
    side_other = beside(side)
    up_held, token = loaded(w_up, token)
    side, token = whole_call(joined_kernel, [pair_shape], [side, side_other], token)
    sides = [side]
    for _ in range(chips - 1):
        sides.append(along(sides[-1]))

    hidden, own, back, swapped = [[None] * chips for _ in range(4)]

    def up(s, after):
        chunks = (lane[s], crossed[s], beside(lane[s]), beside(crossed[s]))
        hidden[s], after = block_hidden(where, chunks, sides[s], gate_held, up_held, after)
        return after

    def down(s, after):
        own[s], back[s], after = block_down(where, hidden[s], w_down, after)
        return after

    def exchange(s, arrays, after):
        *arrays, sent, after = tied([*arrays, back[s]], after)
        back[s] = beside(sent)
        return *arrays, after

    def swap(s, after):
        sent, after = summed(1, [own[s], back[s]], after)
        swapped[s] = across(sent)
        return after

    def gather(s, travelling, after):
        terms = [own[s], back[s], swapped[s]] + travelling
        return summed(0, terms, after)

    token = up(0, token)
    kept, sent, token = whole_call(
        rows_kernel,
        [placed_shape, placed_shape],
        [where, layer_input, attn_gain, w_kv, scale, kv_owner],
        token,
        kinds=[pltpu.SMEM] + [pltpu.VMEM] * 5,
        limit=10,
    )
    lane[2], crossed[1], token = tied([lane[2], crossed[1]], token)
    lane.append(along(lane[2]))
    crossed.append(across(lane[2]))
    token = up(1, token)
    token = down(1, token)
    lane[3], crossed[2], token = exchange(1, [lane[3], crossed[2]], token)
    crossed.append(across(lane[3]))
    token = swap(1, token)
    token = up(2, token)
    token = down(2, token)
    passed, token = gather(1, [], token)
    travelling = [along(passed)]
    crossed[3], token = exchange(2, [crossed[3]], token)
    token = swap(2, token)
    token = up(3, token)
    token = down(3, token)
    passed, token = gather(2, travelling, token)
    travelling = [along(passed)]
    arrived, token = exchange(3, [across(sent)], token)
    token = swap(3, token)
    token = down(0, token)
    passed, token = gather(3, travelling, token)
    travelling = [along(passed)]
    (token,) = exchange(0, [], token)
    token = swap(0, token)
    kv_cache, token = whole_call(cache_kernel, [placed_shape], [kept, arrived, key_gain], token)
    moe_out, token = gather(0, travelling, token)
    return moe_out, kv_cache.reshape(1, 1, rows, columns)


def hidden_kernel(x_ref, wg_ref, wu_ref, scale_ref, weight_ref, out_ref):
    blocks, parts, rows, width = x_ref.shape
    gate = up = None
    for part in range(parts):
        x = x_ref[:, part].reshape(blocks * rows, width)
        depth = pl.ds(part * width, width)
        g = jnp.dot(x, wg_ref[0, depth], preferred_element_type=jnp.float32)
        u = jnp.dot(x, wu_ref[0, depth], preferred_element_type=jnp.float32)
        gate = g if gate is None else gate + g
        up = u if up is None else up + u
    out_ref[0] = silu_up(gate, up, scale_ref[...], weight_ref[0])


def hidden_of(x, w_gate, w_up, scale, weight):
    blocks, parts, rows, width = x.shape
    experts, depth, units = w_gate.shape
    tokens = blocks * rows
    tile = tile_of(units, 256)
    tiles = units // tile
    wspec = pl.BlockSpec((1, depth, tile), lambda e, f: (e, 0, f))
    return pl.pallas_call(
        hidden_kernel,
        grid=(experts, tiles),
        in_specs=[
            pl.BlockSpec(x.shape, lambda e, f: (0, 0, 0, 0)),
            wspec,
            wspec,
            pl.BlockSpec((tokens, 1), lambda e, f: (0, 0)),
            pl.BlockSpec((1, tokens, 1), lambda e, f: (e, 0, 0)),
        ],
        out_specs=pl.BlockSpec((1, tokens, tile), lambda e, f: (e, 0, f)),
        out_shape=jax.ShapeDtypeStruct((experts, tokens, units), jnp.bfloat16),
        compiler_params=pltpu.CompilerParams(vmem_limit_bytes=VMEM_LIMIT),
    )(x, w_gate, w_up, scale, weight)


def down_kernel(h_ref, w_ref, out_ref):
    blocks, _, rows, tile = out_ref.shape
    y = None
    for e in range(h_ref.shape[0]):
        term = jnp.dot(h_ref[e], w_ref[e], preferred_element_type=jnp.float32)
        y = term if y is None else y + term
    out_ref[:, 0] = y.astype(jnp.bfloat16).reshape(blocks, rows, tile)


def down_of(hidden, w_down, blocks, parts):
    experts, tokens, units = hidden.shape
    width = w_down.shape[2] // parts
    rows = tokens // blocks
    tile = tile_of(width, 512)
    tiles = width // tile
    return pl.pallas_call(
        down_kernel,
        grid=(parts * tiles,),
        in_specs=[
            pl.BlockSpec((experts, tokens, units), lambda n: (0, 0, 0)),
            pl.BlockSpec((experts, units, tile), lambda n: (0, 0, n)),
        ],
        out_specs=pl.BlockSpec(
            (blocks, 1, rows, tile), lambda n: (0, n // tiles, 0, n % tiles)
        ),
        out_shape=jax.ShapeDtypeStruct((blocks, parts, rows, width), jnp.bfloat16),
        compiler_params=pltpu.CompilerParams(vmem_limit_bytes=VMEM_LIMIT),
    )(hidden, w_down)


def plain_experts(rows_out, side, w_gate, w_up, w_down):
    tp_count, ep_count = lax.axis_size("tp"), lax.axis_size("ep")
    rows, width = rows_out.shape
    exp_local = w_gate.shape[0]
    gathered = lax.all_gather(rows_out, ("ep", "tp"), axis=0, tiled=False)
    gathered = gathered.reshape(ep_count, tp_count, rows, width)
    side = lax.all_gather(side, "ep", axis=1, tiled=True)
    first_expert = 1 + lax.axis_index("ep") * exp_local
    weight = lax.dynamic_slice_in_dim(side, first_expert, exp_local, 0)[:, :, None]
    hidden = hidden_of(gathered, w_gate, w_up, side[0][:, None], weight)
    partial = down_of(hidden, w_down, ep_count, tp_count)
    partial = partial.reshape(ep_count * tp_count, rows, width)
    return lax.psum_scatter(partial, ("ep", "tp"), scatter_dimension=0, tiled=False)


def per_device(
    layer_input,
    stream,
    expert_ids,
    kv_owner,
    attn_norm,
    moe_norm,
    k_norm,
    w_kv,
    router,
    w_gate,
    w_up,
    w_down,
):
    rows = layer_input.shape[0]
    tp_count = lax.axis_size("tp")
    tiled = w_gate.shape[2] % MXU == 0 and stream.shape[1] % (2 * MXU) == 0
    if tp_count == 2 and tiled and rows == 128 and lax.axis_size("ep") == 8:
        return ring_device(
            layer_input, stream, expert_ids, kv_owner, attn_norm, moe_norm, k_norm, w_kv, router,
            w_gate, w_up, w_down,
        )
    columns = 2 * KVH * HD
    expert_count = router.shape[1]
    first = layer_input.astype(jnp.float32)
    second = stream.astype(jnp.float32)

    rows_out = (second * moe_norm.astype(jnp.float32)).astype(jnp.bfloat16)

    logits = lax.dot_general(
        router, rows_out, (((0,), (1,)), ((), ())), preferred_element_type=jnp.float32
    )
    squares = jnp.stack([jnp.sum(first * first, 1), jnp.sum(second * second, 1)], 0)
    small = jnp.concatenate([squares, logits], 0)
    small = lax.psum(small, "tp")
    first_scale = lax.rsqrt(small[0] / D + EPS)
    second_scale = lax.rsqrt(small[1:2] / D + EPS)
    logits = small[2:] * second_scale
    expert_range = jnp.arange(expert_count, dtype=jnp.int32)
    chosen = jnp.any(expert_ids.T[None, :, :] == expert_range[:, None, None], 1)
    top = jnp.max(jnp.where(chosen, logits, -jnp.inf), 0, keepdims=True)
    weights = jnp.where(chosen, jnp.exp(jnp.where(chosen, logits - top, 0.0)), 0.0)
    weights = weights / jnp.sum(weights, 0, keepdims=True)
    fill = jnp.zeros((-(1 + expert_count) % 8, rows), jnp.float32)
    side = jnp.concatenate([second_scale, weights, fill], 0)

    attn_in = (first * attn_norm.astype(jnp.float32)).astype(jnp.bfloat16)
    kv = jnp.dot(attn_in, w_kv, preferred_element_type=jnp.float32) * first_scale[:, None]
    owner_cap = 2 * rows // tp_count
    owner = kv_owner[:, 0]
    owner_hot = (owner[:, None] == jnp.arange(tp_count, dtype=jnp.int32)[None, :]).astype(jnp.int32)
    owner_slot = jnp.sum(
        (jnp.cumsum(owner_hot, 0, dtype=jnp.int32) - owner_hot) * owner_hot, 1, dtype=jnp.int32
    )
    target = owner * owner_cap + owner_slot
    placing = target[None, :] == jnp.arange(tp_count * owner_cap, dtype=jnp.int32)[:, None]
    placed = jnp.dot(
        placing.astype(jnp.bfloat16), kv.astype(jnp.bfloat16), preferred_element_type=jnp.float32
    )
    placed = placed.astype(jnp.bfloat16).reshape(tp_count, owner_cap, columns)
    arrived = lax.all_to_all(placed, "tp", split_axis=0, concat_axis=0, tiled=True)
    heads = jnp.sum(arrived.astype(jnp.float32), 0)
    heads = heads.reshape(owner_cap, 2 * KVH, HD)
    keys = heads[:, :KVH]
    keys = keys * lax.rsqrt(jnp.mean(keys * keys, 2, keepdims=True) + EPS)
    keys = keys * k_norm.astype(jnp.float32)
    kv_cache = jnp.concatenate([keys, heads[:, KVH:]], 1).astype(jnp.bfloat16)
    kv_cache = kv_cache.reshape(1, 1, owner_cap, columns)

    moe_out = plain_experts(rows_out, side, w_gate, w_up, w_down)
    return (moe_out, kv_cache)


def solution(mesh):
    placed = (
        P(("group", "ep"), "tp"),
        P(("group", "ep"), "tp"),
        P(("group", "ep"), None),
        P(("group", "ep"), None),
        P("tp"),
        P("tp"),
        P(),
        P("tp", None),
        P("tp", None),
        P("ep", None, "tp"),
        P("ep", None, "tp"),
        P("ep", "tp", None),
    )
    return jax.shard_map(
        per_device,
        mesh=mesh,
        in_specs=placed,
        out_specs=(P(("group", "ep"), "tp"), P(("group", "ep"), "tp", None, None)),
        check_vma=False,
    )
```

```python
import functools

import jax
import jax.numpy as jnp
from jax import lax
from jax.experimental import pallas as pl
from jax.experimental.pallas import tpu as pltpu
from jax.sharding import PartitionSpec as P

D = 4096
KVH = 4
HD = 128
TOPK = 8


EPS = 1e-06
VMEM_LIMIT = 56 * 1024 * 1024
MXU = 256
SIDE = 8


def weight_work(rows, *weights):
    size = sum(w.size for w in weights)
    return pl.CostEstimate(flops=2 * rows * size, bytes_accessed=2 * size, transcendentals=0)


BRIEF = pl.CostEstimate(flops=1, bytes_accessed=1, transcendentals=0)


def tile_of(size, most):
    for candidate in range(most, 127, -128):
        if size % candidate == 0:
            return candidate
    return size


def silu_up(gate, up, scale, weight):
    gate = gate * scale
    up = up * scale
    return (gate / (1.0 + jnp.exp(-gate)) * up * weight).astype(jnp.bfloat16)


def column_of(side, index):
    lane = lax.broadcasted_iota(jnp.int32, side.shape, 1)
    return jnp.sum(jnp.where(lane == index, side, 0.0), 1, keepdims=True)


def in_vmem(count):
    return [pl.BlockSpec(memory_space=pltpu.VMEM)] * count


def whole_call(body, outs, operands, after=None, kinds=None, scratch=(), limit=6, work=BRIEF):
    kinds = kinds or [pltpu.VMEM] * len(operands)
    count = len(operands)

    token = jax.ShapeDtypeStruct((8, 128), jnp.float32)
    afters = [] if after is None else [after]

    def with_token(*refs):
        inputs, rest = refs[:count], refs[count + len(afters) :]
        results, spare = rest[: len(outs)], rest[len(outs) + 1 :]
        rest[len(outs)][...] = jnp.zeros((8, 128), jnp.float32)
        body(*inputs, *results, *spare)

    return pl.pallas_call(
        with_token,
        in_specs=[pl.BlockSpec(memory_space=kind) for kind in kinds]
        + [pl.BlockSpec(memory_space=pl.ANY)] * len(afters),
        out_specs=in_vmem(len(outs) + 1),
        out_shape=[*outs, token],
        scratch_shapes=scratch,
        compiler_params=pltpu.CompilerParams(vmem_limit_bytes=limit * 1024 * 1024),
        cost_estimate=work,
    )(*operands, *afters)


def row_of(gain_ref):
    return gain_ref[...].astype(jnp.float32).reshape(1, -1)


def opening_kernel(x_ref, gain_ref, out_ref):
    out_ref[...] = (x_ref[...].astype(jnp.float32) * row_of(gain_ref)).astype(jnp.bfloat16)


def stats_kernel(first_ref, second_ref, rows_ref, router_ref, small_ref):
    tokens = first_ref.shape[0]
    squares = []
    for ref in (first_ref, second_ref):
        x = ref[...].astype(jnp.float32)
        squares.append(jnp.sum(x * x, 1, keepdims=True))
    squares = jnp.concatenate(squares + [jnp.zeros((tokens, 126), jnp.float32)], 1)
    small_ref[0:SIDE] = jnp.transpose(squares)[0:SIDE]
    small_ref[SIDE:] = lax.dot_general(
        router_ref[...],
        rows_ref[...],
        (((1,), (1,)), ((), ())),
        preferred_element_type=jnp.float32,
    )


def sides_kernel(mine_ref, other_ref, ids_ref, side_ref):
    small = mine_ref[...] + other_ref[...]
    scales = lax.rsqrt(small[0:SIDE] / D + EPS)
    logits = small[SIDE:] * scales[1:2]
    expert = lax.broadcasted_iota(jnp.int32, logits.shape, 0)
    ids = ids_ref[...]
    chosen = expert == ids[0:1]
    for k in range(1, ids.shape[0]):
        chosen = chosen | (expert == ids[k : k + 1])
    top = jnp.max(jnp.where(chosen, logits, -jnp.inf), 0, keepdims=True)
    weights = jnp.where(chosen, jnp.exp(jnp.where(chosen, logits - top, 0.0)), 0.0)
    side_ref[0:SIDE] = scales
    side_ref[SIDE:] = weights / jnp.sum(weights, 0, keepdims=True)


def rows_kernel(first_ref, gain_ref, w_ref, side_ref, owner_ref, kept_ref, sent_ref):
    tokens = first_ref.shape[0]
    attn_in = (first_ref[...].astype(jnp.float32) * row_of(gain_ref)).astype(jnp.bfloat16)
    kv = jnp.dot(attn_in, w_ref[...], preferred_element_type=jnp.float32)
    fill = jnp.zeros((tokens - SIDE, tokens), jnp.float32)
    scales = jnp.transpose(jnp.concatenate([side_ref[0:SIDE], fill], 0))
    kv = (kv * scales[:, 0:1]).astype(jnp.bfloat16)
    theirs = jnp.where(owner_ref[...] == lax.axis_index("tp"), 0, 1)
    hot = lax.broadcasted_iota(jnp.int32, (SIDE, tokens), 0) == theirs
    hot = jnp.where(hot, 1.0, 0.0)
    row = lax.broadcasted_iota(jnp.int32, (tokens, tokens), 0)
    column = lax.broadcasted_iota(jnp.int32, (tokens, tokens), 1)
    before = jnp.where(row < column, 1.0, 0.0).astype(jnp.bfloat16)
    earlier = jnp.dot(hot.astype(jnp.bfloat16), before, preferred_element_type=jnp.float32)
    slot = jnp.sum(earlier * hot, 0, keepdims=True).astype(jnp.int32)
    for side, out_ref in enumerate((kept_ref, sent_ref)):
        placing = jnp.where((slot == row) & (theirs == side), 1.0, 0.0).astype(jnp.bfloat16)
        out = jnp.dot(placing, kv, preferred_element_type=jnp.float32)
        out_ref[...] = out.astype(jnp.bfloat16)


def cache_kernel(kept_ref, arrived_ref, gain_ref, out_ref):
    gain = row_of(gain_ref)
    for head in range(2 * KVH):
        columns = slice(head * HD, (head + 1) * HD)
        x = kept_ref[:, columns].astype(jnp.float32) + arrived_ref[:, columns].astype(jnp.float32)
        if head < KVH:
            x = x * lax.rsqrt(jnp.mean(x * x, 1, keepdims=True) + EPS) * gain
        out_ref[:, columns] = x.astype(jnp.bfloat16)


def joined_kernel(first_ref, second_ref, out_ref):
    tokens = first_ref.shape[1]
    out_ref[:, :tokens] = first_ref[...]
    out_ref[:, tokens:] = second_ref[...]


def tied(arrays, after):
    count = len(arrays)
    anywhere = pl.BlockSpec(memory_space=pl.ANY)

    def kernel(*refs):
        refs[-1][...] = jnp.zeros((8, 128), jnp.float32)

    shapes = [jax.ShapeDtypeStruct(x.shape, x.dtype) for x in arrays]
    return pl.pallas_call(
        kernel,
        in_specs=[anywhere] * (count + 1),
        out_specs=[anywhere] * count + in_vmem(1),
        out_shape=[*shapes, jax.ShapeDtypeStruct((8, 128), jnp.float32)],
        input_output_aliases={n: n for n in range(count)},
        compiler_params=pltpu.CompilerParams(vmem_limit_bytes=1024 * 1024),
        cost_estimate=BRIEF,
    )(*arrays, after)


def sum_kernel(*refs):
    refs[-1][...] = total(*[ref[...] for ref in refs[:-1]])


def summed(terms, after):
    return whole_call(
        sum_kernel, [jax.ShapeDtypeStruct(terms[0].shape, jnp.bfloat16)], terms, after, limit=4
    )


def paired_products(rows, steps):
    def stage(index):
        _, first_tile, second_tile = steps[index]
        pltpu.matmul_push_rhs(first_tile(), index % 2, 0)
        pltpu.matmul_push_rhs(second_tile(), index % 2, 1)

    def run(first_acc, second_acc):
        stage(0)
        for index, (lhs, _, _) in enumerate(steps):
            if index + 1 < len(steps):
                stage(index + 1)
            left = lhs()
            pltpu.matmul_acc_lhs(first_acc, left, index % 2)
            pltpu.matmul_acc_lhs(second_acc, left, index % 2)
        return pltpu.matmul_pop(first_acc), pltpu.matmul_pop(second_acc)

    return pl.run_scoped(
        run, pltpu.ACC(0)((rows, MXU), jnp.float32), pltpu.ACC(1)((rows, MXU), jnp.float32)
    )


def load_kernel(source_ref, held_ref, sem):
    copies = [
        pltpu.make_async_copy(source_ref.at[e], held_ref.at[e], sem.at[e])
        for e in range(source_ref.shape[0])
    ]
    for copy in copies:
        copy.start()
    for copy in copies:
        copy.wait()


def loaded(w, after):
    return whole_call(
        load_kernel,
        [pltpu.VMEM(w.shape, w.dtype)],
        [pltpu.with_memory_space_constraint(w, pltpu.HBM)],
        after,
        kinds=[pl.ANY],
        scratch=[pltpu.SemaphoreType.DMA((w.shape[0],))],
        limit=1,
        work=weight_work(1, w),
    )


def block_hidden_kernel(
    own_ref, other_ref, sib_own_ref, sib_other_ref, side_ref, wg_ref, wu_ref, out_ref, x_ref
):
    rows, width = own_ref.shape
    experts, depth, units = wg_ref.shape
    half = lax.axis_index("tp")
    first_expert = SIDE + lax.axis_index("ep") * experts
    mine = pl.ds(pl.multiple_of(half * width, width), width)
    theirs = pl.ds(pl.multiple_of((1 - half) * width, width), width)
    x_ref[0:rows, mine] = own_ref[...]
    x_ref[0:rows, theirs] = other_ref[...]
    x_ref[rows : 2 * rows, mine] = sib_own_ref[...]
    x_ref[rows : 2 * rows, theirs] = sib_other_ref[...]
    side = jnp.transpose(side_ref[...])
    scale = column_of(side, 1)

    @pl.loop(0, experts)
    def _(e):
        weight = column_of(side, first_expert + e)
        for tile in range(units // MXU):
            columns = pl.ds(tile * MXU, MXU)

            def step(k):
                part = pl.ds(k * MXU, MXU)
                return (
                    lambda: x_ref[:, part],
                    lambda: wg_ref[e, part, columns],
                    lambda: wu_ref[e, part, columns],
                )

            steps = [step(k) for k in range(depth // MXU)]
            gate, up = paired_products(2 * rows, steps)
            out_ref[e, :, columns] = silu_up(gate, up, scale, weight)


def block_hidden(chunks, side, w_gate, w_up, after):
    rows, _ = chunks[0].shape
    experts, depth, units = w_gate.shape
    return whole_call(
        block_hidden_kernel,
        [jax.ShapeDtypeStruct((experts, 2 * rows, units), jnp.bfloat16)],
        [*chunks, side, w_gate, w_up],
        after,
        scratch=[pltpu.VMEM((2 * rows, depth), jnp.bfloat16)],
        work=weight_work(2 * rows, w_gate, w_up),
    )


def block_down_kernel(half, h_ref, w_ref, own_ref, sib_ref):
    rows, width = own_ref.shape
    experts, _, units = h_ref.shape
    here = lax.axis_index("tp")
    first = (here + half - 2 * half * here) * width

    @pl.loop(0, width // (2 * MXU))
    def _(tile):
        start = pl.multiple_of(tile * (2 * MXU), 2 * MXU)

        def step(e, k):
            part = pl.ds(k * MXU, MXU)
            at = [pl.ds(pl.multiple_of(first + start + MXU * n, MXU), MXU) for n in (0, 1)]
            return (
                lambda: h_ref[e, :, part],
                lambda: w_ref[e, part, at[0]],
                lambda: w_ref[e, part, at[1]],
            )

        steps = [step(e, k) for e in range(experts) for k in range(units // MXU)]
        for n, y in enumerate(paired_products(2 * rows, steps)):
            columns = pl.ds(pl.multiple_of(start + n * MXU, MXU), MXU)
            own_ref[:, columns] = y[:rows].astype(jnp.bfloat16)
            sib_ref[:, columns] = y[rows:].astype(jnp.bfloat16)


def block_down(half, hidden, w_down, after):
    _, tokens, _ = hidden.shape
    out = jax.ShapeDtypeStruct((tokens // 2, w_down.shape[2] // 2), jnp.bfloat16)
    return whole_call(
        functools.partial(block_down_kernel, half),
        [out, out],
        [hidden, w_down],
        after,
        work=weight_work(tokens // 2, w_down),
    )


def total(*terms):
    return sum(term.astype(jnp.float32) for term in terms).astype(jnp.bfloat16)


def ring_device(
    layer_input,
    stream,
    expert_ids,
    kv_owner,
    attn_norm,
    moe_norm,
    k_norm,
    w_kv,
    router,
    w_gate,
    w_up,
    w_down,
):
    ep_count = lax.axis_size("ep")
    chips = ep_count // 2
    forward = [(d, (d + 2) % ep_count) for d in range(ep_count)]
    siblings = [(d, d ^ 1) for d in range(ep_count)]
    along = functools.partial(lax.ppermute, axis_name="ep", perm=forward)
    beside = functools.partial(lax.ppermute, axis_name="ep", perm=siblings)
    across = functools.partial(lax.ppermute, axis_name="tp", perm=[(0, 1), (1, 0)])
    rows = stream.shape[0]
    columns = w_kv.shape[1]
    side_rows = SIDE + router.shape[1]
    row_shape = jax.ShapeDtypeStruct(stream.shape, jnp.bfloat16)
    small_shape = jax.ShapeDtypeStruct((side_rows, rows), jnp.float32)
    pair_shape = jax.ShapeDtypeStruct((side_rows, 2 * rows), jnp.float32)
    placed_shape = jax.ShapeDtypeStruct((rows, columns), jnp.bfloat16)
    layer_input, stream, w_kv = [
        pltpu.with_memory_space_constraint(x, pltpu.HBM) for x in (layer_input, stream, w_kv)
    ]

    rows_out, token = whole_call(opening_kernel, [row_shape], [stream, moe_norm])
    lane, crossed = [rows_out, along(rows_out)], [across(rows_out)]

    small, token = whole_call(
        stats_kernel, [small_shape], [layer_input, stream, rows_out, router.T], token
    )
    small_other = across(small)
    gate_held, token = loaded(w_gate, token)
    up_held, token = loaded(w_up, token)
    lane[1], crossed[0], small_other, token = tied([lane[1], crossed[0], small_other], token)
    lane.append(along(lane[1]))
    crossed.append(across(lane[1]))
    side, token = whole_call(
        sides_kernel, [small_shape], [small, small_other, expert_ids.T], token
    )
    side_other = beside(side)
    down_held, token = loaded(w_down, token)
    pair, token = whole_call(joined_kernel, [pair_shape], [side, side_other], token)
    sides = [pair]
    for _ in range(chips - 1):
        sides.append(along(sides[-1]))

    hidden, own, back, swapped = [[None] * chips for _ in range(4)]

    def up(s, after):
        chunks = (lane[s], crossed[s], beside(lane[s]), beside(crossed[s]))
        hidden[s], after = block_hidden(chunks, sides[s], gate_held, up_held, after)
        return after

    def down(s, arrays, after, meanwhile=lambda after: after):
        kept, sent, after = block_down(1, hidden[s], down_held, after)
        *arrays, sent, after = tied([*arrays, sent], after)
        own[s], back[s], after = block_down(0, hidden[s], down_held, after)
        after = meanwhile(after)
        passed, after = summed([kept, beside(sent)], after)
        swapped[s] = across(passed)
        return *arrays, after

    def exchange(s, after):
        sent, after = tied([back[s]], after)
        back[s] = beside(sent)
        return after

    def gather(s, after):
        passed, after = summed([own[s], back[s], swapped[s]] + travelling, after)
        travelling[:] = [along(passed)]
        return after

    travelling = []
    token = up(0, token)
    lane[2], crossed[1], token = tied([lane[2], crossed[1]], token)
    lane.append(along(lane[2]))
    crossed.append(across(lane[2]))
    kept, sent, token = whole_call(
        rows_kernel,
        [placed_shape, placed_shape],
        [layer_input, attn_norm, w_kv, side, kv_owner.T],
        token,
        limit=10,
    )
    token = up(1, token)
    lane[3], crossed[2], token = down(1, [lane[3], crossed[2]], token)
    crossed.append(across(lane[3]))
    token = exchange(1, token)
    token = up(2, token)
    crossed[3], token = down(2, [crossed[3]], token, functools.partial(gather, 1))
    token = exchange(2, token)
    token = up(3, token)
    arrived, token = down(3, [across(sent)], token, functools.partial(gather, 2))
    token = exchange(3, token)
    kv_cache, token = whole_call(cache_kernel, [placed_shape], [kept, arrived, k_norm], token)
    (token,) = down(0, [], token, functools.partial(gather, 3))
    token = exchange(0, token)
    moe_out, _ = summed([own[0], back[0], swapped[0], *travelling], token)
    return moe_out, kv_cache.reshape(1, 1, rows, columns)


def hidden_kernel(x_ref, wg_ref, wu_ref, scale_ref, weight_ref, out_ref):
    blocks, parts, rows, width = x_ref.shape
    gate = up = None
    for part in range(parts):
        x = x_ref[:, part].reshape(blocks * rows, width)
        depth = pl.ds(part * width, width)
        g = jnp.dot(x, wg_ref[0, depth], preferred_element_type=jnp.float32)
        u = jnp.dot(x, wu_ref[0, depth], preferred_element_type=jnp.float32)
        gate = g if gate is None else gate + g
        up = u if up is None else up + u
    out_ref[0] = silu_up(gate, up, scale_ref[...], weight_ref[0])


def hidden_of(x, w_gate, w_up, scale, weight):
    blocks, parts, rows, width = x.shape
    experts, depth, units = w_gate.shape
    tokens = blocks * rows
    tile = tile_of(units, 256)
    tiles = units // tile
    wspec = pl.BlockSpec((1, depth, tile), lambda e, f: (e, 0, f))
    return pl.pallas_call(
        hidden_kernel,
        grid=(experts, tiles),
        in_specs=[
            pl.BlockSpec(x.shape, lambda e, f: (0, 0, 0, 0)),
            wspec,
            wspec,
            pl.BlockSpec((tokens, 1), lambda e, f: (0, 0)),
            pl.BlockSpec((1, tokens, 1), lambda e, f: (e, 0, 0)),
        ],
        out_specs=pl.BlockSpec((1, tokens, tile), lambda e, f: (e, 0, f)),
        out_shape=jax.ShapeDtypeStruct((experts, tokens, units), jnp.bfloat16),
        compiler_params=pltpu.CompilerParams(vmem_limit_bytes=VMEM_LIMIT),
    )(x, w_gate, w_up, scale, weight)


def down_kernel(h_ref, w_ref, out_ref):
    blocks, _, rows, tile = out_ref.shape
    y = None
    for e in range(h_ref.shape[0]):
        term = jnp.dot(h_ref[e], w_ref[e], preferred_element_type=jnp.float32)
        y = term if y is None else y + term
    out_ref[:, 0] = y.astype(jnp.bfloat16).reshape(blocks, rows, tile)


def down_of(hidden, w_down, blocks, parts):
    experts, tokens, units = hidden.shape
    width = w_down.shape[2] // parts
    rows = tokens // blocks
    tile = tile_of(width, 512)
    tiles = width // tile
    return pl.pallas_call(
        down_kernel,
        grid=(parts * tiles,),
        in_specs=[
            pl.BlockSpec((experts, tokens, units), lambda n: (0, 0, 0)),
            pl.BlockSpec((experts, units, tile), lambda n: (0, 0, n)),
        ],
        out_specs=pl.BlockSpec(
            (blocks, 1, rows, tile), lambda n: (0, n // tiles, 0, n % tiles)
        ),
        out_shape=jax.ShapeDtypeStruct((blocks, parts, rows, width), jnp.bfloat16),
        compiler_params=pltpu.CompilerParams(vmem_limit_bytes=VMEM_LIMIT),
    )(hidden, w_down)


def plain_experts(rows_out, side, w_gate, w_up, w_down):
    tp_count, ep_count = lax.axis_size("tp"), lax.axis_size("ep")
    rows, width = rows_out.shape
    exp_local = w_gate.shape[0]
    gathered = lax.all_gather(rows_out, ("ep", "tp"), axis=0, tiled=False)
    gathered = gathered.reshape(ep_count, tp_count, rows, width)
    side = lax.all_gather(side, "ep", axis=1, tiled=True)
    first_expert = 1 + lax.axis_index("ep") * exp_local
    weight = lax.dynamic_slice_in_dim(side, first_expert, exp_local, 0)[:, :, None]
    hidden = hidden_of(gathered, w_gate, w_up, side[0][:, None], weight)
    partial = down_of(hidden, w_down, ep_count, tp_count)
    partial = partial.reshape(ep_count * tp_count, rows, width)
    return lax.psum_scatter(partial, ("ep", "tp"), scatter_dimension=0, tiled=False)


def per_device(
    layer_input,
    stream,
    expert_ids,
    kv_owner,
    attn_norm,
    moe_norm,
    k_norm,
    w_kv,
    router,
    w_gate,
    w_up,
    w_down,
):
    rows = layer_input.shape[0]
    tp_count = lax.axis_size("tp")
    tiled = w_gate.shape[2] % MXU == 0 and stream.shape[1] % (2 * MXU) == 0
    if tp_count == 2 and tiled and rows == 128 and lax.axis_size("ep") == 8:
        return ring_device(
            layer_input, stream, expert_ids, kv_owner, attn_norm, moe_norm, k_norm, w_kv, router,
            w_gate, w_up, w_down,
        )
    columns = 2 * KVH * HD
    expert_count = router.shape[1]
    first = layer_input.astype(jnp.float32)
    second = stream.astype(jnp.float32)

    rows_out = (second * moe_norm.astype(jnp.float32)).astype(jnp.bfloat16)

    logits = lax.dot_general(
        router, rows_out, (((0,), (1,)), ((), ())), preferred_element_type=jnp.float32
    )
    squares = jnp.stack([jnp.sum(first * first, 1), jnp.sum(second * second, 1)], 0)
    small = jnp.concatenate([squares, logits], 0)
    small = lax.psum(small, "tp")
    first_scale = lax.rsqrt(small[0] / D + EPS)
    second_scale = lax.rsqrt(small[1:2] / D + EPS)
    logits = small[2:] * second_scale
    expert_range = jnp.arange(expert_count, dtype=jnp.int32)
    chosen = jnp.any(expert_ids.T[None, :, :] == expert_range[:, None, None], 1)
    top = jnp.max(jnp.where(chosen, logits, -jnp.inf), 0, keepdims=True)
    weights = jnp.where(chosen, jnp.exp(jnp.where(chosen, logits - top, 0.0)), 0.0)
    weights = weights / jnp.sum(weights, 0, keepdims=True)
    fill = jnp.zeros((-(1 + expert_count) % 8, rows), jnp.float32)
    side = jnp.concatenate([second_scale, weights, fill], 0)

    attn_in = (first * attn_norm.astype(jnp.float32)).astype(jnp.bfloat16)
    kv = jnp.dot(attn_in, w_kv, preferred_element_type=jnp.float32) * first_scale[:, None]
    owner_cap = 2 * rows // tp_count
    owner = kv_owner[:, 0]
    owner_hot = (owner[:, None] == jnp.arange(tp_count, dtype=jnp.int32)[None, :]).astype(jnp.int32)
    owner_slot = jnp.sum(
        (jnp.cumsum(owner_hot, 0, dtype=jnp.int32) - owner_hot) * owner_hot, 1, dtype=jnp.int32
    )
    target = owner * owner_cap + owner_slot
    placing = target[None, :] == jnp.arange(tp_count * owner_cap, dtype=jnp.int32)[:, None]
    placed = jnp.dot(
        placing.astype(jnp.bfloat16), kv.astype(jnp.bfloat16), preferred_element_type=jnp.float32
    )
    placed = placed.astype(jnp.bfloat16).reshape(tp_count, owner_cap, columns)
    arrived = lax.all_to_all(placed, "tp", split_axis=0, concat_axis=0, tiled=True)
    heads = jnp.sum(arrived.astype(jnp.float32), 0)
    heads = heads.reshape(owner_cap, 2 * KVH, HD)
    keys = heads[:, :KVH]
    keys = keys * lax.rsqrt(jnp.mean(keys * keys, 2, keepdims=True) + EPS)
    keys = keys * k_norm.astype(jnp.float32)
    kv_cache = jnp.concatenate([keys, heads[:, KVH:]], 1).astype(jnp.bfloat16)
    kv_cache = kv_cache.reshape(1, 1, owner_cap, columns)

    moe_out = plain_experts(rows_out, side, w_gate, w_up, w_down)
    return (moe_out, kv_cache)


def solution(mesh):
    placed = (
        P(("group", "ep"), "tp"),
        P(("group", "ep"), "tp"),
        P(("group", "ep"), None),
        P(("group", "ep"), None),
        P("tp"),
        P("tp"),
        P(),
        P("tp", None),
        P("tp", None),
        P("ep", None, "tp"),
        P("ep", None, "tp"),
        P("ep", "tp", None),
    )
    return jax.shard_map(
        per_device,
        mesh=mesh,
        in_specs=placed,
        out_specs=(P(("group", "ep"), "tp"), P(("group", "ep"), "tp", None, None)),
        check_vma=False,
    )
```

```python
import functools

import jax
import jax.numpy as jnp
from jax import lax
from jax.experimental import pallas as pl
from jax.experimental.pallas import tpu as pltpu
from jax.sharding import PartitionSpec as P

D = 4096
KVH = 4
HD = 128
TOPK = 8


EPS = 1e-06
VMEM_LIMIT = 56 * 1024 * 1024
MXU = 256
SIDE = 8


def weight_work(rows, *weights):
    size = sum(w.size for w in weights)
    return pl.CostEstimate(flops=2 * rows * size, bytes_accessed=2 * size, transcendentals=0)


BRIEF = pl.CostEstimate(flops=1, bytes_accessed=1, transcendentals=0)


def tile_of(size, most):
    for candidate in range(most, 127, -128):
        if size % candidate == 0:
            return candidate
    return size


def silu_up(gate, up, scale, weight):
    gate = gate * scale
    up = up * scale
    return (gate / (1.0 + jnp.exp(-gate)) * up * weight).astype(jnp.bfloat16)


def column_of(side, index):
    lane = lax.broadcasted_iota(jnp.int32, side.shape, 1)
    return jnp.sum(jnp.where(lane == index, side, 0.0), 1, keepdims=True)


def in_vmem(count):
    return [pl.BlockSpec(memory_space=pltpu.VMEM)] * count


def whole_call(body, outs, operands, after=None, kinds=None, scratch=(), limit=2, work=BRIEF):
    kinds = kinds or [pltpu.VMEM] * len(operands)
    count = len(operands)

    token = jax.ShapeDtypeStruct((8, 128), jnp.float32)
    afters = [] if after is None else [after]

    def with_token(*refs):
        inputs, rest = refs[:count], refs[count + len(afters) :]
        results, spare = rest[: len(outs)], rest[len(outs) + 1 :]
        rest[len(outs)][...] = jnp.zeros((8, 128), jnp.float32)
        body(*inputs, *results, *spare)

    return pl.pallas_call(
        with_token,
        in_specs=[pl.BlockSpec(memory_space=kind) for kind in kinds]
        + [pl.BlockSpec(memory_space=pl.ANY)] * len(afters),
        out_specs=in_vmem(len(outs) + 1),
        out_shape=[*outs, token],
        scratch_shapes=scratch,
        compiler_params=pltpu.CompilerParams(vmem_limit_bytes=limit * 1024 * 1024),
        cost_estimate=work,
    )(*operands, *afters)


def copies_of(source_ref, held_ref, sem):
    return [
        pltpu.make_async_copy(source_ref.at[e], held_ref.at[e], sem.at[e])
        for e in range(source_ref.shape[0])
    ]


def row_of(gain_ref):
    return gain_ref[...].astype(jnp.float32).reshape(1, -1)


def opening_kernel(x_ref, gain_ref, out_ref):
    out_ref[...] = (x_ref[...].astype(jnp.float32) * row_of(gain_ref)).astype(jnp.bfloat16)


def stats_kernel(first_ref, second_ref, rows_ref, router_ref, small_ref):
    tokens = first_ref.shape[0]
    squares = []
    for ref in (first_ref, second_ref):
        x = ref[...].astype(jnp.float32)
        squares.append(jnp.sum(x * x, 1, keepdims=True))
    squares = jnp.concatenate(squares + [jnp.zeros((tokens, 126), jnp.float32)], 1)
    small_ref[0:SIDE] = jnp.transpose(squares)[0:SIDE]
    small_ref[SIDE:] = lax.dot_general(
        router_ref[...],
        rows_ref[...],
        (((1,), (1,)), ((), ())),
        preferred_element_type=jnp.float32,
    )


def sides_kernel(mine_ref, other_ref, ids_ref, side_ref):
    small = mine_ref[...] + other_ref[...]
    scales = lax.rsqrt(small[0:SIDE] / D + EPS)
    logits = small[SIDE:] * scales[1:2]
    expert = lax.broadcasted_iota(jnp.int32, logits.shape, 0)
    ids = ids_ref[...]
    chosen = expert == ids[0:1]
    for k in range(1, ids.shape[0]):
        chosen = chosen | (expert == ids[k : k + 1])
    top = jnp.max(jnp.where(chosen, logits, -jnp.inf), 0, keepdims=True)
    weights = jnp.where(chosen, jnp.exp(jnp.where(chosen, logits - top, 0.0)), 0.0)
    side_ref[0:SIDE] = scales
    side_ref[SIDE:] = weights / jnp.sum(weights, 0, keepdims=True)


def rows_kernel(
    first_ref, gain_ref, w_ref, side_ref, owner_ref, source_ref, kept_ref, sent_ref, held_ref, sem
):
    tokens = first_ref.shape[0]
    copies = copies_of(source_ref, held_ref, sem)
    for copy in copies:
        copy.start()
    attn_in = (first_ref[...].astype(jnp.float32) * row_of(gain_ref)).astype(jnp.bfloat16)
    kv = jnp.dot(attn_in, w_ref[...], preferred_element_type=jnp.float32)
    fill = jnp.zeros((tokens - SIDE, tokens), jnp.float32)
    scales = jnp.transpose(jnp.concatenate([side_ref[0:SIDE], fill], 0))
    kv = (kv * scales[:, 0:1]).astype(jnp.bfloat16)
    theirs = jnp.where(owner_ref[...] == lax.axis_index("tp"), 0, 1)
    hot = lax.broadcasted_iota(jnp.int32, (SIDE, tokens), 0) == theirs
    hot = jnp.where(hot, 1.0, 0.0)
    row = lax.broadcasted_iota(jnp.int32, (tokens, tokens), 0)
    column = lax.broadcasted_iota(jnp.int32, (tokens, tokens), 1)
    before = jnp.where(row < column, 1.0, 0.0).astype(jnp.bfloat16)
    earlier = jnp.dot(hot.astype(jnp.bfloat16), before, preferred_element_type=jnp.float32)
    slot = jnp.sum(earlier * hot, 0, keepdims=True).astype(jnp.int32)
    for side, out_ref in enumerate((kept_ref, sent_ref)):
        placing = jnp.where((slot == row) & (theirs == side), 1.0, 0.0).astype(jnp.bfloat16)
        out = jnp.dot(placing, kv, preferred_element_type=jnp.float32)
        out_ref[...] = out.astype(jnp.bfloat16)
    for copy in copies:
        copy.wait()


def cache_kernel(kept_ref, arrived_ref, gain_ref, out_ref):
    gain = row_of(gain_ref)
    for head in range(2 * KVH):
        columns = slice(head * HD, (head + 1) * HD)
        x = kept_ref[:, columns].astype(jnp.float32) + arrived_ref[:, columns].astype(jnp.float32)
        if head < KVH:
            x = x * lax.rsqrt(jnp.mean(x * x, 1, keepdims=True) + EPS) * gain
        out_ref[:, columns] = x.astype(jnp.bfloat16)


def joined_kernel(first_ref, second_ref, out_ref):
    tokens = first_ref.shape[1]
    out_ref[:, :tokens] = first_ref[...]
    out_ref[:, tokens:] = second_ref[...]


def tied(arrays, after):
    count = len(arrays)
    anywhere = pl.BlockSpec(memory_space=pl.ANY)

    def kernel(*refs):
        refs[-1][...] = jnp.zeros((8, 128), jnp.float32)

    shapes = [jax.ShapeDtypeStruct(x.shape, x.dtype) for x in arrays]
    return pl.pallas_call(
        kernel,
        in_specs=[anywhere] * (count + 1),
        out_specs=[anywhere] * count + in_vmem(1),
        out_shape=[*shapes, jax.ShapeDtypeStruct((8, 128), jnp.float32)],
        input_output_aliases={n: n for n in range(count)},
        compiler_params=pltpu.CompilerParams(vmem_limit_bytes=1024 * 1024),
        cost_estimate=BRIEF,
    )(*arrays, after)


def sum_kernel(first, *refs):
    *terms, out_ref = refs
    rows = out_ref.shape[0]
    at = [pl.ds(first if ref.shape[0] > rows else 0, rows) for ref in terms]
    out_ref[...] = total(*[ref[part] for ref, part in zip(terms, at)])


def summed(terms, after, first=0, rows=None, work=BRIEF):
    rows = rows or terms[0].shape[0]
    out = jax.ShapeDtypeStruct((rows, terms[0].shape[1]), jnp.bfloat16)
    return whole_call(functools.partial(sum_kernel, first), [out], terms, after, work=work)


def final_kernel(*refs):
    *terms, out_ref = refs
    rows = out_ref.shape[0] // 2
    for n in range(2):
        part = pl.ds(n * rows, rows)
        whole = [ref[part] for ref in terms if ref.shape[0] > rows]
        halves = [ref[...] for ref in terms if ref.shape[0] == rows][n::2]
        out_ref[part] = total(*whole, *halves)


def paired_products(rows, tiles):
    flat = [(t, k) for t, (steps, _) in enumerate(tiles) for k in range(len(steps))]

    def stage(index):
        t, k = flat[index]
        _, first_tile, second_tile = tiles[t][0][k]
        pltpu.matmul_push_rhs(first_tile(), index % 2, 0)
        pltpu.matmul_push_rhs(second_tile(), index % 2, 1)

    def run(*accs):
        def finish(t):
            first, second = accs[t % 2], accs[2 + t % 2]
            tiles[t][1](pltpu.matmul_pop(first), pltpu.matmul_pop(second))

        stage(0)
        for index, (t, k) in enumerate(flat):
            if index + 1 < len(flat):
                stage(index + 1)
            left = tiles[t][0][k][0]()
            pltpu.matmul_acc_lhs(accs[t % 2], left, index % 2)
            pltpu.matmul_acc_lhs(accs[2 + t % 2], left, index % 2)
            if t and k == 1:
                finish(t - 1)
        finish(len(tiles) - 1)

    kinds = [pltpu.ACC(unit)((rows, MXU), jnp.float32) for unit in (0, 0, 1, 1)]
    pl.run_scoped(run, *kinds)


def load_kernel(source_ref, held_ref, sem):
    copies = copies_of(source_ref, held_ref, sem)
    for copy in copies:
        copy.start()
    for copy in copies:
        copy.wait()


def loaded(w, after):
    return whole_call(
        load_kernel,
        [pltpu.VMEM(w.shape, w.dtype)],
        [pltpu.with_memory_space_constraint(w, pltpu.HBM)],
        after,
        kinds=[pl.ANY],
        scratch=[pltpu.SemaphoreType.DMA((w.shape[0],))],
        limit=1,
        work=weight_work(1, w),
    )


def block_hidden_kernel(
    own_ref, other_ref, sib_own_ref, sib_other_ref, side_ref, wg_ref, wu_ref, out_ref, x_ref
):
    rows, width = own_ref.shape
    experts, depth, units = wg_ref.shape
    half = lax.axis_index("tp")
    first_expert = SIDE + lax.axis_index("ep") * experts
    mine = pl.ds(pl.multiple_of(half * width, width), width)
    theirs = pl.ds(pl.multiple_of((1 - half) * width, width), width)
    x_ref[0:rows, mine] = own_ref[...]
    x_ref[0:rows, theirs] = other_ref[...]
    x_ref[rows : 2 * rows, mine] = sib_own_ref[...]
    x_ref[rows : 2 * rows, theirs] = sib_other_ref[...]
    side = jnp.transpose(side_ref[...])
    scale = column_of(side, 1)

    @pl.loop(0, experts)
    def _(e):
        weight = column_of(side, first_expert + e)

        def tile_of_units(tile):
            columns = pl.ds(tile * MXU, MXU)

            def step(k):
                part = pl.ds(k * MXU, MXU)
                return (
                    lambda: x_ref[:, part],
                    lambda: wg_ref[e, part, columns],
                    lambda: wu_ref[e, part, columns],
                )

            def finish(gate, up):
                out_ref[e, :, columns] = silu_up(gate, up, scale, weight)

            return [step(k) for k in range(depth // MXU)], finish

        paired_products(2 * rows, [tile_of_units(tile) for tile in range(units // MXU)])


def block_hidden(chunks, side, w_gate, w_up, after):
    rows, _ = chunks[0].shape
    experts, depth, units = w_gate.shape
    return whole_call(
        block_hidden_kernel,
        [jax.ShapeDtypeStruct((experts, 2 * rows, units), jnp.bfloat16)],
        [*chunks, side, w_gate, w_up],
        after,
        scratch=[pltpu.VMEM((2 * rows, depth), jnp.bfloat16)],
        limit=4,
        work=weight_work(2 * rows, w_gate, w_up),
    )


def block_down_kernel(half, h_ref, w_ref, own_ref, *sib_refs):
    rows, width = own_ref.shape
    count = rows // len(sib_refs)
    experts, _, units = h_ref.shape
    here = lax.axis_index("tp")
    first = (here + half - 2 * half * here) * width

    def tile_of_columns(tile):
        start = tile * (2 * MXU)

        def step(e, k):
            part = pl.ds(k * MXU, MXU)
            at = [pl.ds(pl.multiple_of(first + start + MXU * n, MXU), MXU) for n in (0, 1)]
            return (
                lambda: h_ref[e, :, part],
                lambda: w_ref[e, part, at[0]],
                lambda: w_ref[e, part, at[1]],
            )

        def finish(*products):
            for n, y in enumerate(products):
                columns = pl.ds(start + n * MXU, MXU)
                own_ref[:, columns] = y[:rows].astype(jnp.bfloat16)
                for m, sib_ref in enumerate(sib_refs):
                    part = y[rows + m * count : rows + (m + 1) * count]
                    sib_ref[:, columns] = part.astype(jnp.bfloat16)

        return [step(e, k) for e in range(experts) for k in range(units // MXU)], finish

    paired_products(2 * rows, [tile_of_columns(n) for n in range(width // (2 * MXU))])


def block_down(half, hidden, w_down, after, parts=1):
    _, tokens, _ = hidden.shape
    rows, width = tokens // 2, w_down.shape[2] // 2
    out = jax.ShapeDtypeStruct((rows, width), jnp.bfloat16)
    part = jax.ShapeDtypeStruct((rows // parts, width), jnp.bfloat16)
    return whole_call(
        functools.partial(block_down_kernel, half),
        [out] + [part] * parts,
        [hidden, w_down],
        after,
        work=weight_work(rows, w_down),
    )


def total(*terms):
    return sum(term.astype(jnp.float32) for term in terms).astype(jnp.bfloat16)


def ring_device(
    layer_input,
    stream,
    expert_ids,
    kv_owner,
    attn_norm,
    moe_norm,
    k_norm,
    w_kv,
    router,
    w_gate,
    w_up,
    w_down,
):
    ep_count = lax.axis_size("ep")
    chips = ep_count // 2
    forward = [(d, (d + 2) % ep_count) for d in range(ep_count)]
    siblings = [(d, d ^ 1) for d in range(ep_count)]
    along = functools.partial(lax.ppermute, axis_name="ep", perm=forward)
    beside = functools.partial(lax.ppermute, axis_name="ep", perm=siblings)
    across = functools.partial(lax.ppermute, axis_name="tp", perm=[(0, 1), (1, 0)])
    rows = stream.shape[0]
    columns = w_kv.shape[1]
    side_rows = SIDE + router.shape[1]
    row_shape = jax.ShapeDtypeStruct(stream.shape, jnp.bfloat16)
    small_shape = jax.ShapeDtypeStruct((side_rows, rows), jnp.float32)
    pair_shape = jax.ShapeDtypeStruct((side_rows, 2 * rows), jnp.float32)
    placed_shape = jax.ShapeDtypeStruct((rows, columns), jnp.bfloat16)
    layer_input, stream, w_kv, w_down = [
        pltpu.with_memory_space_constraint(x, pltpu.HBM)
        for x in (layer_input, stream, w_kv, w_down)
    ]

    rows_out, token = whole_call(
        opening_kernel, [row_shape], [stream, moe_norm], limit=8
    )
    lane, crossed = [rows_out, along(rows_out)], [across(rows_out)]

    small, token = whole_call(
        stats_kernel, [small_shape], [layer_input, stream, rows_out, router.T], token, limit=8
    )
    small_other = across(small)
    gate_held, token = loaded(w_gate, token)
    up_held, token = loaded(w_up, token)
    lane[1], crossed[0], small_other, token = tied([lane[1], crossed[0], small_other], token)
    lane.append(along(lane[1]))
    crossed.append(across(lane[1]))
    side, token = whole_call(
        sides_kernel, [small_shape], [small, small_other, expert_ids.T], token
    )
    side_other = beside(side)
    kept, sent, down_held, token = whole_call(
        rows_kernel,
        [placed_shape, placed_shape, pltpu.VMEM(w_down.shape, w_down.dtype)],
        [layer_input, attn_norm, w_kv, side, kv_owner.T, w_down],
        token,
        kinds=[pltpu.VMEM] * 5 + [pl.ANY],
        scratch=[pltpu.SemaphoreType.DMA((w_down.shape[0],))],
        limit=7,
    )
    pair, token = whole_call(joined_kernel, [pair_shape], [side, side_other], token)
    sides = [pair]
    for s in range(1, chips):
        ahead = [(d, (d + 2 * s) % ep_count) for d in range(ep_count)]
        sides.append(lax.ppermute(pair, "ep", ahead))

    hidden, own, back, swapped = [[None] * chips for _ in range(4)]

    def chunks(s):
        return (lane[s], crossed[s], beside(lane[s]), beside(crossed[s]))

    def up(s, after):
        hidden[s], after = block_hidden(chunks(s), sides[s], gate_held, up_held, after)
        return after

    def down(s, arrays, after, meanwhile=lambda after: after, parts=1):
        sent_parts = 1 if s else 2
        kept, *sent, after = block_down(1, hidden[s], down_held, after, sent_parts)
        *taken, after = tied([*arrays, *sent], after)
        own[s], back[s], after = block_down(0, hidden[s], down_held, after)
        after = meanwhile(after)
        returned, swapped[s] = [beside(x) for x in taken[len(arrays) :]], []
        if s == 0:
            passed, after = whole_call(final_kernel, [row_shape], [kept, *returned], after)
            swapped[s].append(across(passed))
            return after
        for n in range(parts):
            count = rows // parts
            passed, after = summed([kept, *returned], after, n * count, count)
            swapped[s].append(across(passed))
        return *taken[: len(arrays)], after

    def exchange(s, after):
        sent, after = tied([back[s]], after)
        back[s] = beside(sent)
        return after

    def gather(s, after, part=0):
        count = swapped[s][part].shape[0]
        terms = [own[s], back[s], swapped[s][part], *travelling[s]]
        passed, after = summed(terms, after, part * count, count, weight_work(1, w_gate, w_up))
        travelling[(s + 1) % chips].append(along(passed))
        return after

    travelling = [[] for _ in range(chips)]
    token = up(0, token)
    lane[2], crossed[1], *sides[1:], token = tied([lane[2], crossed[1], *sides[1:]], token)
    lane.append(along(lane[2]))
    crossed.append(across(lane[2]))
    token = up(1, token)
    lane[3], crossed[2], token = down(1, [lane[3], crossed[2]], token)
    crossed.append(along(crossed[2]))
    token = exchange(1, token)
    token = up(2, token)
    crossed[3], token = down(2, [crossed[3]], token, functools.partial(gather, 1))
    token = exchange(2, token)
    token = up(3, token)
    arrived, token = down(3, [across(sent)], token, functools.partial(gather, 2), 2)
    token = exchange(3, token)
    kv_cache, token = whole_call(cache_kernel, [placed_shape], [kept, arrived, k_norm], token)
    token = down(0, [], token, functools.partial(gather, 3))
    token = gather(3, token, 1)
    token = exchange(0, token)
    moe_out, _ = whole_call(
        final_kernel,
        [row_shape],
        [own[0], back[0], *swapped[0], *travelling[0]],
        token,
        limit=4,
    )
    return moe_out, kv_cache.reshape(1, 1, rows, columns)


def hidden_kernel(x_ref, wg_ref, wu_ref, scale_ref, weight_ref, out_ref):
    blocks, parts, rows, width = x_ref.shape
    gate = up = None
    for part in range(parts):
        x = x_ref[:, part].reshape(blocks * rows, width)
        depth = pl.ds(part * width, width)
        g = jnp.dot(x, wg_ref[0, depth], preferred_element_type=jnp.float32)
        u = jnp.dot(x, wu_ref[0, depth], preferred_element_type=jnp.float32)
        gate = g if gate is None else gate + g
        up = u if up is None else up + u
    out_ref[0] = silu_up(gate, up, scale_ref[...], weight_ref[0])


def hidden_of(x, w_gate, w_up, scale, weight):
    blocks, parts, rows, width = x.shape
    experts, depth, units = w_gate.shape
    tokens = blocks * rows
    tile = tile_of(units, 256)
    tiles = units // tile
    wspec = pl.BlockSpec((1, depth, tile), lambda e, f: (e, 0, f))
    return pl.pallas_call(
        hidden_kernel,
        grid=(experts, tiles),
        in_specs=[
            pl.BlockSpec(x.shape, lambda e, f: (0, 0, 0, 0)),
            wspec,
            wspec,
            pl.BlockSpec((tokens, 1), lambda e, f: (0, 0)),
            pl.BlockSpec((1, tokens, 1), lambda e, f: (e, 0, 0)),
        ],
        out_specs=pl.BlockSpec((1, tokens, tile), lambda e, f: (e, 0, f)),
        out_shape=jax.ShapeDtypeStruct((experts, tokens, units), jnp.bfloat16),
        compiler_params=pltpu.CompilerParams(vmem_limit_bytes=VMEM_LIMIT),
    )(x, w_gate, w_up, scale, weight)


def down_kernel(h_ref, w_ref, out_ref):
    blocks, _, rows, tile = out_ref.shape
    y = None
    for e in range(h_ref.shape[0]):
        term = jnp.dot(h_ref[e], w_ref[e], preferred_element_type=jnp.float32)
        y = term if y is None else y + term
    out_ref[:, 0] = y.astype(jnp.bfloat16).reshape(blocks, rows, tile)


def down_of(hidden, w_down, blocks, parts):
    experts, tokens, units = hidden.shape
    width = w_down.shape[2] // parts
    rows = tokens // blocks
    tile = tile_of(width, 512)
    tiles = width // tile
    return pl.pallas_call(
        down_kernel,
        grid=(parts * tiles,),
        in_specs=[
            pl.BlockSpec((experts, tokens, units), lambda n: (0, 0, 0)),
            pl.BlockSpec((experts, units, tile), lambda n: (0, 0, n)),
        ],
        out_specs=pl.BlockSpec(
            (blocks, 1, rows, tile), lambda n: (0, n // tiles, 0, n % tiles)
        ),
        out_shape=jax.ShapeDtypeStruct((blocks, parts, rows, width), jnp.bfloat16),
        compiler_params=pltpu.CompilerParams(vmem_limit_bytes=VMEM_LIMIT),
    )(hidden, w_down)


def plain_experts(rows_out, side, w_gate, w_up, w_down):
    tp_count, ep_count = lax.axis_size("tp"), lax.axis_size("ep")
    rows, width = rows_out.shape
    exp_local = w_gate.shape[0]
    gathered = lax.all_gather(rows_out, ("ep", "tp"), axis=0, tiled=False)
    gathered = gathered.reshape(ep_count, tp_count, rows, width)
    side = lax.all_gather(side, "ep", axis=1, tiled=True)
    first_expert = 1 + lax.axis_index("ep") * exp_local
    weight = lax.dynamic_slice_in_dim(side, first_expert, exp_local, 0)[:, :, None]
    hidden = hidden_of(gathered, w_gate, w_up, side[0][:, None], weight)
    partial = down_of(hidden, w_down, ep_count, tp_count)
    partial = partial.reshape(ep_count * tp_count, rows, width)
    return lax.psum_scatter(partial, ("ep", "tp"), scatter_dimension=0, tiled=False)


def per_device(
    layer_input,
    stream,
    expert_ids,
    kv_owner,
    attn_norm,
    moe_norm,
    k_norm,
    w_kv,
    router,
    w_gate,
    w_up,
    w_down,
):
    rows = layer_input.shape[0]
    tp_count = lax.axis_size("tp")
    tiled = w_gate.shape[2] % MXU == 0 and stream.shape[1] % (2 * MXU) == 0
    if tp_count == 2 and tiled and rows == 128 and lax.axis_size("ep") == 8:
        return ring_device(
            layer_input, stream, expert_ids, kv_owner, attn_norm, moe_norm, k_norm, w_kv, router,
            w_gate, w_up, w_down,
        )
    columns = 2 * KVH * HD
    expert_count = router.shape[1]
    first = layer_input.astype(jnp.float32)
    second = stream.astype(jnp.float32)

    rows_out = (second * moe_norm.astype(jnp.float32)).astype(jnp.bfloat16)

    logits = lax.dot_general(
        router, rows_out, (((0,), (1,)), ((), ())), preferred_element_type=jnp.float32
    )
    squares = jnp.stack([jnp.sum(first * first, 1), jnp.sum(second * second, 1)], 0)
    small = jnp.concatenate([squares, logits], 0)
    small = lax.psum(small, "tp")
    first_scale = lax.rsqrt(small[0] / D + EPS)
    second_scale = lax.rsqrt(small[1:2] / D + EPS)
    logits = small[2:] * second_scale
    expert_range = jnp.arange(expert_count, dtype=jnp.int32)
    chosen = jnp.any(expert_ids.T[None, :, :] == expert_range[:, None, None], 1)
    top = jnp.max(jnp.where(chosen, logits, -jnp.inf), 0, keepdims=True)
    weights = jnp.where(chosen, jnp.exp(jnp.where(chosen, logits - top, 0.0)), 0.0)
    weights = weights / jnp.sum(weights, 0, keepdims=True)
    fill = jnp.zeros((-(1 + expert_count) % 8, rows), jnp.float32)
    side = jnp.concatenate([second_scale, weights, fill], 0)

    attn_in = (first * attn_norm.astype(jnp.float32)).astype(jnp.bfloat16)
    kv = jnp.dot(attn_in, w_kv, preferred_element_type=jnp.float32) * first_scale[:, None]
    owner_cap = 2 * rows // tp_count
    owner = kv_owner[:, 0]
    owner_hot = (owner[:, None] == jnp.arange(tp_count, dtype=jnp.int32)[None, :]).astype(jnp.int32)
    owner_slot = jnp.sum(
        (jnp.cumsum(owner_hot, 0, dtype=jnp.int32) - owner_hot) * owner_hot, 1, dtype=jnp.int32
    )
    target = owner * owner_cap + owner_slot
    placing = target[None, :] == jnp.arange(tp_count * owner_cap, dtype=jnp.int32)[:, None]
    placed = jnp.dot(
        placing.astype(jnp.bfloat16), kv.astype(jnp.bfloat16), preferred_element_type=jnp.float32
    )
    placed = placed.astype(jnp.bfloat16).reshape(tp_count, owner_cap, columns)
    arrived = lax.all_to_all(placed, "tp", split_axis=0, concat_axis=0, tiled=True)
    heads = jnp.sum(arrived.astype(jnp.float32), 0)
    heads = heads.reshape(owner_cap, 2 * KVH, HD)
    keys = heads[:, :KVH]
    keys = keys * lax.rsqrt(jnp.mean(keys * keys, 2, keepdims=True) + EPS)
    keys = keys * k_norm.astype(jnp.float32)
    kv_cache = jnp.concatenate([keys, heads[:, KVH:]], 1).astype(jnp.bfloat16)
    kv_cache = kv_cache.reshape(1, 1, owner_cap, columns)

    moe_out = plain_experts(rows_out, side, w_gate, w_up, w_down)
    return (moe_out, kv_cache)


def solution(mesh):
    placed = (
        P(("group", "ep"), "tp"),
        P(("group", "ep"), "tp"),
        P(("group", "ep"), None),
        P(("group", "ep"), None),
        P("tp"),
        P("tp"),
        P(),
        P("tp", None),
        P("tp", None),
        P("ep", None, "tp"),
        P("ep", None, "tp"),
        P("ep", "tp", None),
    )
    return jax.shard_map(
        per_device,
        mesh=mesh,
        in_specs=placed,
        out_specs=(P(("group", "ep"), "tp"), P(("group", "ep"), "tp", None, None)),
        check_vma=False,
    )
```

```python
import functools

import jax
import jax.numpy as jnp
from jax import lax
from jax.experimental import pallas as pl
from jax.experimental.pallas import tpu as pltpu
from jax.sharding import PartitionSpec as P

D = 4096
KVH = 4
HD = 128
TOPK = 8


EPS = 1e-06
VMEM_LIMIT = 56 * 1024 * 1024
MXU = 256
SIDE = 8


def weight_work(rows, *weights):
    size = sum(w.size for w in weights)
    return pl.CostEstimate(flops=2 * rows * size, bytes_accessed=2 * size, transcendentals=0)


BRIEF = pl.CostEstimate(flops=1, bytes_accessed=1, transcendentals=0)


def tile_of(size, most):
    for candidate in range(most, 127, -128):
        if size % candidate == 0:
            return candidate
    return size


def silu_up(gate, up, scale, weight):
    gate = gate * scale
    up = up * scale
    return (gate / (1.0 + jnp.exp(-gate)) * up * weight).astype(jnp.bfloat16)


def column_of(side, index):
    lane = lax.broadcasted_iota(jnp.int32, side.shape, 1)
    return jnp.sum(jnp.where(lane == index, side, 0.0), 1, keepdims=True)


def in_vmem(count):
    return [pl.BlockSpec(memory_space=pltpu.VMEM)] * count


def whole_call(body, outs, operands, after=None, kinds=None, scratch=(), limit=2, work=BRIEF, same=None):
    kinds = kinds or [pltpu.VMEM] * len(operands)
    count = len(operands)

    token = jax.ShapeDtypeStruct((8, 128), jnp.float32)
    afters = [] if after is None else [after]

    def with_token(*refs):
        inputs, rest = refs[:count], refs[count + len(afters) :]
        results, spare = rest[: len(outs)], rest[len(outs) + 1 :]
        rest[len(outs)][...] = jnp.zeros((8, 128), jnp.float32)
        body(*inputs, *results, *spare)

    return pl.pallas_call(
        with_token,
        in_specs=[pl.BlockSpec(memory_space=kind) for kind in kinds]
        + [pl.BlockSpec(memory_space=pl.ANY)] * len(afters),
        out_specs=in_vmem(len(outs) + 1),
        out_shape=[*outs, token],
        scratch_shapes=scratch,
        compiler_params=pltpu.CompilerParams(vmem_limit_bytes=limit * 1024 * 1024),
        cost_estimate=work,
        input_output_aliases=same or {},
    )(*operands, *afters)


def copies_of(source_ref, held_refs, sem):
    return [
        pltpu.make_async_copy(source_ref.at[e], held_ref, sem.at[e])
        for e, held_ref in enumerate(held_refs)
    ]


def row_of(gain_ref):
    return gain_ref[...].astype(jnp.float32).reshape(1, -1)


def opening_kernel(x_ref, gain_ref, out_ref):
    out_ref[...] = (x_ref[...].astype(jnp.float32) * row_of(gain_ref)).astype(jnp.bfloat16)


def stats_kernel(first_ref, second_ref, rows_ref, router_ref, small_ref):
    tokens = first_ref.shape[0]
    squares = []
    for ref in (first_ref, second_ref):
        x = ref[...].astype(jnp.float32)
        squares.append(jnp.sum(x * x, 1, keepdims=True))
    squares = jnp.concatenate(squares + [jnp.zeros((tokens, 126), jnp.float32)], 1)
    small_ref[0:SIDE] = jnp.transpose(squares)[0:SIDE]
    small_ref[SIDE:] = lax.dot_general(
        router_ref[...],
        rows_ref[...],
        (((1,), (1,)), ((), ())),
        preferred_element_type=jnp.float32,
    )


def sides_kernel(mine_ref, other_ref, ids_ref, side_ref):
    small = mine_ref[...] + other_ref[...]
    scales = lax.rsqrt(small[0:SIDE] / D + EPS)
    logits = small[SIDE:] * scales[1:2]
    expert = lax.broadcasted_iota(jnp.int32, logits.shape, 0)
    ids = ids_ref[...]
    chosen = expert == ids[0:1]
    for k in range(1, ids.shape[0]):
        chosen = chosen | (expert == ids[k : k + 1])
    top = jnp.max(jnp.where(chosen, logits, -jnp.inf), 0, keepdims=True)
    weights = jnp.where(chosen, jnp.exp(jnp.where(chosen, logits - top, 0.0)), 0.0)
    side_ref[0:SIDE] = scales
    side_ref[SIDE:] = weights / jnp.sum(weights, 0, keepdims=True)


def rows_kernel(
    first_ref, gain_ref, side_ref, owner_ref, w_ref, kept_ref, sent_ref, piece_ref, piece_sem
):
    tokens = first_ref.shape[0]
    slots, depth, _ = piece_ref.shape
    pieces = w_ref.shape[0] // depth

    def fetch(n):
        return pltpu.make_async_copy(
            w_ref.at[pl.ds(n * depth, depth)], piece_ref.at[n % slots], piece_sem.at[n % slots]
        )

    for n in range(slots):
        fetch(n).start()
    attn_in = (first_ref[...].astype(jnp.float32) * row_of(gain_ref)).astype(jnp.bfloat16)
    kv = None
    for n in range(pieces):
        fetch(n).wait()
        term = jnp.dot(
            attn_in[:, n * depth : (n + 1) * depth],
            piece_ref[n % slots],
            preferred_element_type=jnp.float32,
        )
        kv = term if kv is None else kv + term
        if n + slots < pieces:
            fetch(n + slots).start()
    fill = jnp.zeros((tokens - SIDE, tokens), jnp.float32)
    scales = jnp.transpose(jnp.concatenate([side_ref[0:SIDE], fill], 0))
    kv = (kv * scales[:, 0:1]).astype(jnp.bfloat16)
    theirs = jnp.where(owner_ref[...] == lax.axis_index("tp"), 0, 1)
    hot = lax.broadcasted_iota(jnp.int32, (SIDE, tokens), 0) == theirs
    hot = jnp.where(hot, 1.0, 0.0)
    row = lax.broadcasted_iota(jnp.int32, (tokens, tokens), 0)
    column = lax.broadcasted_iota(jnp.int32, (tokens, tokens), 1)
    before = jnp.where(row < column, 1.0, 0.0).astype(jnp.bfloat16)
    earlier = jnp.dot(hot.astype(jnp.bfloat16), before, preferred_element_type=jnp.float32)
    slot = jnp.sum(earlier * hot, 0, keepdims=True).astype(jnp.int32)
    for side, out_ref in enumerate((kept_ref, sent_ref)):
        placing = jnp.where((slot == row) & (theirs == side), 1.0, 0.0).astype(jnp.bfloat16)
        out = jnp.dot(placing, kv, preferred_element_type=jnp.float32)
        out_ref[...] = out.astype(jnp.bfloat16)


def cache_kernel(kept_ref, arrived_ref, gain_ref, out_ref):
    gain = row_of(gain_ref)
    for head in range(2 * KVH):
        columns = slice(head * HD, (head + 1) * HD)
        x = kept_ref[:, columns].astype(jnp.float32) + arrived_ref[:, columns].astype(jnp.float32)
        if head < KVH:
            x = x * lax.rsqrt(jnp.mean(x * x, 1, keepdims=True) + EPS) * gain
        out_ref[:, columns] = x.astype(jnp.bfloat16)


def joined_kernel(first_ref, second_ref, out_ref):
    tokens = first_ref.shape[1]
    out_ref[:, :tokens] = first_ref[...]
    out_ref[:, tokens:] = second_ref[...]


def tied(arrays, after):
    count = len(arrays)
    anywhere = pl.BlockSpec(memory_space=pl.ANY)

    def kernel(*refs):
        refs[-1][...] = jnp.zeros((8, 128), jnp.float32)

    shapes = [jax.ShapeDtypeStruct(x.shape, x.dtype) for x in arrays]
    return pl.pallas_call(
        kernel,
        in_specs=[anywhere] * (count + 1),
        out_specs=[anywhere] * count + in_vmem(1),
        out_shape=[*shapes, jax.ShapeDtypeStruct((8, 128), jnp.float32)],
        input_output_aliases={n: n for n in range(count)},
        compiler_params=pltpu.CompilerParams(vmem_limit_bytes=1024 * 1024),
        cost_estimate=BRIEF,
    )(*arrays, after)


def sum_kernel(first, *refs):
    *terms, out_ref = refs
    rows = out_ref.shape[0]
    at = [pl.ds(first if ref.shape[0] > rows else 0, rows) for ref in terms]
    out_ref[...] = total(*[ref[part] for ref, part in zip(terms, at)])


def summed(terms, after, first=0, rows=None, work=BRIEF):
    rows = rows or terms[0].shape[0]
    out = jax.ShapeDtypeStruct((rows, terms[0].shape[1]), jnp.bfloat16)
    return whole_call(functools.partial(sum_kernel, first), [out], terms, after, work=work)


def final_kernel(*refs):
    *terms, out_ref = refs
    rows = out_ref.shape[0] // 2
    for n in range(2):
        part = pl.ds(n * rows, rows)
        whole = [ref[part] for ref in terms if ref.shape[0] > rows]
        halves = [ref[...] for ref in terms if ref.shape[0] == rows][n::2]
        out_ref[part] = total(*whole, *halves)


def paired_products(rows, tiles):
    flat = [(t, k) for t, (steps, _) in enumerate(tiles) for k in range(len(steps))]

    def stage(index):
        t, k = flat[index]
        _, first_tile, second_tile = tiles[t][0][k]
        pltpu.matmul_push_rhs(first_tile(), index % 2, 0)
        pltpu.matmul_push_rhs(second_tile(), index % 2, 1)

    def run(*accs):
        def finish(t):
            first, second = accs[t % 2], accs[2 + t % 2]
            tiles[t][1](pltpu.matmul_pop(first), pltpu.matmul_pop(second))

        stage(0)
        for index, (t, k) in enumerate(flat):
            if index + 1 < len(flat):
                stage(index + 1)
            left = tiles[t][0][k][0]()
            pltpu.matmul_acc_lhs(accs[t % 2], left, index % 2)
            pltpu.matmul_acc_lhs(accs[2 + t % 2], left, index % 2)
            if t and k == 1:
                finish(t - 1)
        finish(len(tiles) - 1)

    kinds = [pltpu.ACC(unit)((rows, MXU), jnp.float32) for unit in (0, 0, 1, 1)]
    pl.run_scoped(run, *kinds)


def load_kernel(source_ref, *refs):
    *held_refs, sem = refs
    copies = copies_of(source_ref, held_refs, sem)
    for copy in copies:
        copy.start()
    for copy in copies:
        copy.wait()


def experts_in_vmem(w):
    return [pltpu.VMEM(w.shape[1:], w.dtype)] * w.shape[0]


def loaded(w, after):
    *held, after = whole_call(
        load_kernel,
        experts_in_vmem(w),
        [pltpu.with_memory_space_constraint(w, pltpu.HBM)],
        after,
        kinds=[pl.ANY],
        scratch=[pltpu.SemaphoreType.DMA((w.shape[0],))],
        limit=1,
        work=weight_work(1, w),
    )
    return held, after


def block_hidden_kernel(experts, *refs):
    own_ref, other_ref, sib_own_ref, sib_other_ref, side_ref, *refs = refs
    w_refs, refs = refs[: 2 * experts], refs[2 * experts :]
    copies = []
    if len(refs) > 2:
        source_ref, out_ref, *held_refs, x_ref, sem = refs
        copies = copies_of(source_ref, held_refs, sem)
    else:
        out_ref, x_ref = refs
    for copy in copies:
        copy.start()
    rows, width = own_ref.shape
    depth, units = w_refs[0].shape
    half = lax.axis_index("tp")
    first_expert = SIDE + lax.axis_index("ep") * experts
    mine = pl.ds(pl.multiple_of(half * width, width), width)
    theirs = pl.ds(pl.multiple_of((1 - half) * width, width), width)
    x_ref[0:rows, mine] = own_ref[...]
    x_ref[0:rows, theirs] = other_ref[...]
    x_ref[rows : 2 * rows, mine] = sib_own_ref[...]
    x_ref[rows : 2 * rows, theirs] = sib_other_ref[...]
    side = jnp.transpose(side_ref[...])
    scale = column_of(side, 1)

    def tile_of_units(e, tile):
        columns = pl.ds(tile * MXU, MXU)

        def step(k):
            part = pl.ds(k * MXU, MXU)
            return (
                lambda: x_ref[:, part],
                lambda: w_refs[e][part, columns],
                lambda: w_refs[experts + e][part, columns],
            )

        def finish(gate, up):
            weight = column_of(side, first_expert + e)
            out_ref[e, :, columns] = silu_up(gate, up, scale, weight)

        return [step(k) for k in range(depth // MXU)], finish

    tiles = [tile_of_units(e, tile) for e in range(experts) for tile in range(units // MXU)]
    paired_products(2 * rows, tiles)
    for copy in copies:
        copy.wait()


def block_hidden(chunks, side, gates, ups, after, w_down=None):
    rows, _ = chunks[0].shape
    experts, (depth, units) = len(gates), gates[0].shape
    outs = [jax.ShapeDtypeStruct((experts, 2 * rows, units), jnp.bfloat16)]
    operands, kinds = [*chunks, side, *gates, *ups], [pltpu.VMEM] * (5 + 2 * experts)
    scratch = [pltpu.VMEM((2 * rows, depth), jnp.bfloat16)]
    if w_down is not None:
        outs += experts_in_vmem(w_down)
        operands, kinds = [*operands, w_down], [*kinds, pl.ANY]
        scratch.append(pltpu.SemaphoreType.DMA((experts,)))
    work = weight_work(2 * rows, *gates, *ups)
    body = functools.partial(block_hidden_kernel, experts)
    return whole_call(body, outs, operands, after, kinds, scratch, 4, work)


def block_down_kernel(half, experts, h_ref, *refs):
    w_refs, (own_ref, *sib_refs) = refs[:experts], refs[experts:]
    rows, width = own_ref.shape
    count = rows // len(sib_refs)
    units = h_ref.shape[2]
    here = lax.axis_index("tp")
    first = (here + half - 2 * half * here) * width

    def tile_of_columns(tile):
        start = tile * (2 * MXU)

        def step(e, k):
            part = pl.ds(k * MXU, MXU)
            at = [pl.ds(pl.multiple_of(first + start + MXU * n, MXU), MXU) for n in (0, 1)]
            return (
                lambda: h_ref[e, :, part],
                lambda: w_refs[e][part, at[0]],
                lambda: w_refs[e][part, at[1]],
            )

        def finish(*products):
            for n, y in enumerate(products):
                columns = pl.ds(start + n * MXU, MXU)
                own_ref[:, columns] = y[:rows].astype(jnp.bfloat16)
                for m, sib_ref in enumerate(sib_refs):
                    part = y[rows + m * count : rows + (m + 1) * count]
                    sib_ref[:, columns] = part.astype(jnp.bfloat16)

        return [step(e, k) for e in range(experts) for k in range(units // MXU)], finish

    paired_products(2 * rows, [tile_of_columns(n) for n in range(width // (2 * MXU))])


def block_down(half, hidden, w_down, after, parts=1):
    _, tokens, _ = hidden.shape
    rows, width = tokens // 2, w_down[0].shape[1] // 2
    out = jax.ShapeDtypeStruct((rows, width), jnp.bfloat16)
    part = jax.ShapeDtypeStruct((rows // parts, width), jnp.bfloat16)
    return whole_call(
        functools.partial(block_down_kernel, half, len(w_down)),
        [out] + [part] * parts,
        [hidden, *w_down],
        after,
        work=weight_work(rows, *w_down),
    )


def total(*terms):
    return sum(term.astype(jnp.float32) for term in terms).astype(jnp.bfloat16)


def ring_device(
    layer_input,
    stream,
    expert_ids,
    kv_owner,
    attn_norm,
    moe_norm,
    k_norm,
    w_kv,
    router,
    w_gate,
    w_up,
    w_down,
):
    ep_count = lax.axis_size("ep")
    chips = ep_count // 2
    forward = [(d, (d + 2) % ep_count) for d in range(ep_count)]
    siblings = [(d, d ^ 1) for d in range(ep_count)]
    along = functools.partial(lax.ppermute, axis_name="ep", perm=forward)
    beside = functools.partial(lax.ppermute, axis_name="ep", perm=siblings)
    across = functools.partial(lax.ppermute, axis_name="tp", perm=[(0, 1), (1, 0)])
    rows = stream.shape[0]
    columns = w_kv.shape[1]
    side_rows = SIDE + router.shape[1]
    row_shape = jax.ShapeDtypeStruct(stream.shape, jnp.bfloat16)
    small_shape = jax.ShapeDtypeStruct((side_rows, rows), jnp.float32)
    pair_shape = jax.ShapeDtypeStruct((side_rows, 2 * rows), jnp.float32)
    placed_shape = jax.ShapeDtypeStruct((rows, columns), jnp.bfloat16)
    layer_input, stream, w_kv, w_down = [
        pltpu.with_memory_space_constraint(x, pltpu.HBM)
        for x in (layer_input, stream, w_kv, w_down)
    ]

    rows_out, token = whole_call(
        opening_kernel, [row_shape], [stream, moe_norm], limit=8
    )
    lane, crossed = [rows_out, along(rows_out)], [across(rows_out)]

    small, token = whole_call(
        stats_kernel, [small_shape], [layer_input, stream, rows_out, router.T], token, limit=8
    )
    small_other = across(small)
    gate_held, token = loaded(w_gate, token)
    up_held, token = loaded(w_up, token)
    lane[1], crossed[0], small_other, token = tied([lane[1], crossed[0], small_other], token)
    lane.append(along(lane[1]))
    crossed.append(across(lane[1]))
    side, token = whole_call(
        sides_kernel, [small_shape], [small, small_other, expert_ids.T], token
    )
    side_other = beside(side)
    pair, token = whole_call(joined_kernel, [pair_shape], [side, side_other], token)

    def side_at(pair, s):
        ahead = [(d, (d + 2 * s) % ep_count) for d in range(ep_count)]
        return lax.ppermute(pair, "ep", ahead)

    sides = [pair, side_at(pair, 1), None, None]

    down_held = []
    hidden, own, back, swapped = [[None] * chips for _ in range(4)]

    def chunks(s):
        return (lane[s], crossed[s], beside(lane[s]), beside(crossed[s]))

    def up(s, after):
        given = w_down if s else None
        hidden[s], *down_held[:], after = block_hidden(
            chunks(s), sides[s], gate_held, up_held, after, given
        )
        return after

    def down(s, arrays, after, meanwhile=lambda after: after, parts=1):
        sent_parts = 1 if s else 2
        kept, *sent, after = block_down(1, hidden[s], down_held, after, sent_parts)
        *taken, after = tied([*arrays, *sent], after)
        own[s], back[s], after = block_down(0, hidden[s], down_held, after)
        after = meanwhile(after)
        returned, swapped[s] = [beside(x) for x in taken[len(arrays) :]], []
        if s == 0:
            passed, after = whole_call(final_kernel, [row_shape], [kept, *returned], after)
            swapped[s].append(across(passed))
            return after
        for n in range(parts):
            count = rows // parts
            passed, after = summed([kept, *returned], after, n * count, count)
            swapped[s].append(across(passed))
        return (*taken[: len(arrays)], after) if arrays else after

    def exchange(s, after):
        sent, after = tied([back[s]], after)
        back[s] = beside(sent)
        return after

    def gather(s, after, part=0):
        count = swapped[s][part].shape[0]
        terms = [own[s], back[s], swapped[s][part], *travelling[s]]
        passed, after = summed(terms, after, part * count, count, weight_work(1, w_gate, w_up))
        travelling[(s + 1) % chips].append(along(passed))
        return after

    travelling = [[] for _ in range(chips)]
    token = up(0, token)
    lane[2], crossed[1], sides[1], token = tied([lane[2], crossed[1], sides[1]], token)
    lane.append(along(lane[2]))
    crossed.append(across(lane[2]))
    depth = stream.shape[1] // 4
    kept, sent, token = whole_call(
        rows_kernel,
        [placed_shape, placed_shape],
        [layer_input, attn_norm, side, kv_owner.T, w_kv],
        token,
        kinds=[pltpu.VMEM] * 4 + [pl.ANY],
        scratch=[
            pltpu.VMEM((2, depth, columns), jnp.bfloat16),
            pltpu.SemaphoreType.DMA((2,)),
        ],
        limit=5,
    )
    token = up(1, token)
    lane[3], crossed[2], sent, pair, token = down(1, [lane[3], crossed[2], sent, pair], token)
    arrived, sides[2] = across(sent), side_at(pair, 2)
    crossed.append(along(crossed[2]))
    token = exchange(1, token)
    token = up(2, token)
    crossed[3], arrived, pair, token = down(
        2, [crossed[3], arrived, pair], token, functools.partial(gather, 1)
    )
    sides[3] = side_at(pair, 3)
    token = exchange(2, token)
    token = up(3, token)
    token = down(3, [], token, functools.partial(gather, 2), 2)
    token = exchange(3, token)
    kv_cache, token = whole_call(cache_kernel, [placed_shape], [kept, arrived, k_norm], token)
    token = down(0, [], token, functools.partial(gather, 3))
    token = gather(3, token, 1)
    token = exchange(0, token)
    moe_out, _ = whole_call(
        final_kernel,
        [row_shape],
        [own[0], back[0], *swapped[0], *travelling[0]],
        token,
        limit=4,
    )
    return moe_out, kv_cache.reshape(1, 1, rows, columns)


def hidden_kernel(x_ref, wg_ref, wu_ref, scale_ref, weight_ref, out_ref):
    blocks, parts, rows, width = x_ref.shape
    gate = up = None
    for part in range(parts):
        x = x_ref[:, part].reshape(blocks * rows, width)
        depth = pl.ds(part * width, width)
        g = jnp.dot(x, wg_ref[0, depth], preferred_element_type=jnp.float32)
        u = jnp.dot(x, wu_ref[0, depth], preferred_element_type=jnp.float32)
        gate = g if gate is None else gate + g
        up = u if up is None else up + u
    out_ref[0] = silu_up(gate, up, scale_ref[...], weight_ref[0])


def hidden_of(x, w_gate, w_up, scale, weight):
    blocks, parts, rows, width = x.shape
    experts, depth, units = w_gate.shape
    tokens = blocks * rows
    tile = tile_of(units, 256)
    tiles = units // tile
    wspec = pl.BlockSpec((1, depth, tile), lambda e, f: (e, 0, f))
    return pl.pallas_call(
        hidden_kernel,
        grid=(experts, tiles),
        in_specs=[
            pl.BlockSpec(x.shape, lambda e, f: (0, 0, 0, 0)),
            wspec,
            wspec,
            pl.BlockSpec((tokens, 1), lambda e, f: (0, 0)),
            pl.BlockSpec((1, tokens, 1), lambda e, f: (e, 0, 0)),
        ],
        out_specs=pl.BlockSpec((1, tokens, tile), lambda e, f: (e, 0, f)),
        out_shape=jax.ShapeDtypeStruct((experts, tokens, units), jnp.bfloat16),
        compiler_params=pltpu.CompilerParams(vmem_limit_bytes=VMEM_LIMIT),
    )(x, w_gate, w_up, scale, weight)


def down_kernel(h_ref, w_ref, out_ref):
    blocks, _, rows, tile = out_ref.shape
    y = None
    for e in range(h_ref.shape[0]):
        term = jnp.dot(h_ref[e], w_ref[e], preferred_element_type=jnp.float32)
        y = term if y is None else y + term
    out_ref[:, 0] = y.astype(jnp.bfloat16).reshape(blocks, rows, tile)


def down_of(hidden, w_down, blocks, parts):
    experts, tokens, units = hidden.shape
    width = w_down.shape[2] // parts
    rows = tokens // blocks
    tile = tile_of(width, 512)
    tiles = width // tile
    return pl.pallas_call(
        down_kernel,
        grid=(parts * tiles,),
        in_specs=[
            pl.BlockSpec((experts, tokens, units), lambda n: (0, 0, 0)),
            pl.BlockSpec((experts, units, tile), lambda n: (0, 0, n)),
        ],
        out_specs=pl.BlockSpec(
            (blocks, 1, rows, tile), lambda n: (0, n // tiles, 0, n % tiles)
        ),
        out_shape=jax.ShapeDtypeStruct((blocks, parts, rows, width), jnp.bfloat16),
        compiler_params=pltpu.CompilerParams(vmem_limit_bytes=VMEM_LIMIT),
    )(hidden, w_down)


def plain_experts(rows_out, side, w_gate, w_up, w_down):
    tp_count, ep_count = lax.axis_size("tp"), lax.axis_size("ep")
    rows, width = rows_out.shape
    exp_local = w_gate.shape[0]
    gathered = lax.all_gather(rows_out, ("ep", "tp"), axis=0, tiled=False)
    gathered = gathered.reshape(ep_count, tp_count, rows, width)
    side = lax.all_gather(side, "ep", axis=1, tiled=True)
    first_expert = 1 + lax.axis_index("ep") * exp_local
    weight = lax.dynamic_slice_in_dim(side, first_expert, exp_local, 0)[:, :, None]
    hidden = hidden_of(gathered, w_gate, w_up, side[0][:, None], weight)
    partial = down_of(hidden, w_down, ep_count, tp_count)
    partial = partial.reshape(ep_count * tp_count, rows, width)
    return lax.psum_scatter(partial, ("ep", "tp"), scatter_dimension=0, tiled=False)


def per_device(
    layer_input,
    stream,
    expert_ids,
    kv_owner,
    attn_norm,
    moe_norm,
    k_norm,
    w_kv,
    router,
    w_gate,
    w_up,
    w_down,
):
    rows = layer_input.shape[0]
    tp_count = lax.axis_size("tp")
    tiled = w_gate.shape[2] % MXU == 0 and stream.shape[1] % (2 * MXU) == 0
    if tp_count == 2 and tiled and rows == 128 and lax.axis_size("ep") == 8:
        return ring_device(
            layer_input, stream, expert_ids, kv_owner, attn_norm, moe_norm, k_norm, w_kv, router,
            w_gate, w_up, w_down,
        )
    columns = 2 * KVH * HD
    expert_count = router.shape[1]
    first = layer_input.astype(jnp.float32)
    second = stream.astype(jnp.float32)

    rows_out = (second * moe_norm.astype(jnp.float32)).astype(jnp.bfloat16)

    logits = lax.dot_general(
        router, rows_out, (((0,), (1,)), ((), ())), preferred_element_type=jnp.float32
    )
    squares = jnp.stack([jnp.sum(first * first, 1), jnp.sum(second * second, 1)], 0)
    small = jnp.concatenate([squares, logits], 0)
    small = lax.psum(small, "tp")
    first_scale = lax.rsqrt(small[0] / D + EPS)
    second_scale = lax.rsqrt(small[1:2] / D + EPS)
    logits = small[2:] * second_scale
    expert_range = jnp.arange(expert_count, dtype=jnp.int32)
    chosen = jnp.any(expert_ids.T[None, :, :] == expert_range[:, None, None], 1)
    top = jnp.max(jnp.where(chosen, logits, -jnp.inf), 0, keepdims=True)
    weights = jnp.where(chosen, jnp.exp(jnp.where(chosen, logits - top, 0.0)), 0.0)
    weights = weights / jnp.sum(weights, 0, keepdims=True)
    fill = jnp.zeros((-(1 + expert_count) % 8, rows), jnp.float32)
    side = jnp.concatenate([second_scale, weights, fill], 0)

    attn_in = (first * attn_norm.astype(jnp.float32)).astype(jnp.bfloat16)
    kv = jnp.dot(attn_in, w_kv, preferred_element_type=jnp.float32) * first_scale[:, None]
    owner_cap = 2 * rows // tp_count
    owner = kv_owner[:, 0]
    owner_hot = (owner[:, None] == jnp.arange(tp_count, dtype=jnp.int32)[None, :]).astype(jnp.int32)
    owner_slot = jnp.sum(
        (jnp.cumsum(owner_hot, 0, dtype=jnp.int32) - owner_hot) * owner_hot, 1, dtype=jnp.int32
    )
    target = owner * owner_cap + owner_slot
    placing = target[None, :] == jnp.arange(tp_count * owner_cap, dtype=jnp.int32)[:, None]
    placed = jnp.dot(
        placing.astype(jnp.bfloat16), kv.astype(jnp.bfloat16), preferred_element_type=jnp.float32
    )
    placed = placed.astype(jnp.bfloat16).reshape(tp_count, owner_cap, columns)
    arrived = lax.all_to_all(placed, "tp", split_axis=0, concat_axis=0, tiled=True)
    heads = jnp.sum(arrived.astype(jnp.float32), 0)
    heads = heads.reshape(owner_cap, 2 * KVH, HD)
    keys = heads[:, :KVH]
    keys = keys * lax.rsqrt(jnp.mean(keys * keys, 2, keepdims=True) + EPS)
    keys = keys * k_norm.astype(jnp.float32)
    kv_cache = jnp.concatenate([keys, heads[:, KVH:]], 1).astype(jnp.bfloat16)
    kv_cache = kv_cache.reshape(1, 1, owner_cap, columns)

    moe_out = plain_experts(rows_out, side, w_gate, w_up, w_down)
    return (moe_out, kv_cache)


def solution(mesh):
    placed = (
        P(("group", "ep"), "tp"),
        P(("group", "ep"), "tp"),
        P(("group", "ep"), None),
        P(("group", "ep"), None),
        P("tp"),
        P("tp"),
        P(),
        P("tp", None),
        P("tp", None),
        P("ep", None, "tp"),
        P("ep", None, "tp"),
        P("ep", "tp", None),
    )
    return jax.shard_map(
        per_device,
        mesh=mesh,
        in_specs=placed,
        out_specs=(P(("group", "ep"), "tp"), P(("group", "ep"), "tp", None, None)),
        check_vma=False,
    )
```

```python
import functools

import jax
import jax.numpy as jnp
from jax import lax
from jax.experimental import pallas as pl
from jax.experimental.pallas import tpu as pltpu
from jax.sharding import PartitionSpec as P

D = 4096
KVH = 4
HD = 128
TOPK = 8


EPS = 1e-06
VMEM_LIMIT = 56 * 1024 * 1024
MXU = 256
SIDE = 8


def weight_work(rows, *weights):
    size = sum(w.size for w in weights)
    return pl.CostEstimate(flops=2 * rows * size, bytes_accessed=2 * size, transcendentals=0)


BRIEF = pl.CostEstimate(flops=1, bytes_accessed=1, transcendentals=0)


def tile_of(size, most):
    for candidate in range(most, 127, -128):
        if size % candidate == 0:
            return candidate
    return size


def silu_up(gate, up, scale, weight):
    gate = gate * scale
    up = up * scale
    return (gate / (1.0 + jnp.exp(-gate)) * up * weight).astype(jnp.bfloat16)


def column_of(side, index):
    lane = lax.broadcasted_iota(jnp.int32, side.shape, 1)
    return jnp.sum(jnp.where(lane == index, side, 0.0), 1, keepdims=True)


def in_vmem(count):
    return [pl.BlockSpec(memory_space=pltpu.VMEM)] * count


def whole_call(body, outs, operands, after=None, kinds=None, scratch=(), limit=2, work=BRIEF, same=None):
    kinds = kinds or [pltpu.VMEM] * len(operands)
    count = len(operands)

    token = jax.ShapeDtypeStruct((8, 128), jnp.float32)
    afters = [] if after is None else [after]

    def with_token(*refs):
        inputs, rest = refs[:count], refs[count + len(afters) :]
        results, spare = rest[: len(outs)], rest[len(outs) + 1 :]
        rest[len(outs)][...] = jnp.zeros((8, 128), jnp.float32)
        body(*inputs, *results, *spare)

    return pl.pallas_call(
        with_token,
        in_specs=[pl.BlockSpec(memory_space=kind) for kind in kinds]
        + [pl.BlockSpec(memory_space=pl.ANY)] * len(afters),
        out_specs=in_vmem(len(outs) + 1),
        out_shape=[*outs, token],
        scratch_shapes=scratch,
        compiler_params=pltpu.CompilerParams(vmem_limit_bytes=limit * 1024 * 1024),
        cost_estimate=work,
        input_output_aliases=same or {},
    )(*operands, *afters)


def copies_of(source_ref, held_refs, sem):
    return [
        pltpu.make_async_copy(source_ref.at[e], held_ref, sem.at[e])
        for e, held_ref in enumerate(held_refs)
    ]


def row_of(gain_ref):
    return gain_ref[...].astype(jnp.float32).reshape(1, -1)


def opening_kernel(x_ref, gain_ref, out_ref):
    out_ref[...] = (x_ref[...].astype(jnp.float32) * row_of(gain_ref)).astype(jnp.bfloat16)


def stats_kernel(first_ref, second_ref, rows_ref, router_ref, small_ref):
    tokens = first_ref.shape[0]
    squares = []
    for ref in (first_ref, second_ref):
        x = ref[...].astype(jnp.float32)
        squares.append(jnp.sum(x * x, 1, keepdims=True))
    squares = jnp.concatenate(squares + [jnp.zeros((tokens, 126), jnp.float32)], 1)
    small_ref[0:SIDE] = jnp.transpose(squares)[0:SIDE]
    small_ref[SIDE:] = lax.dot_general(
        router_ref[...],
        rows_ref[...],
        (((1,), (1,)), ((), ())),
        preferred_element_type=jnp.float32,
    )


def sides_kernel(mine_ref, other_ref, ids_ref, side_ref):
    small = mine_ref[...] + other_ref[...]
    scales = lax.rsqrt(small[0:SIDE] / D + EPS)
    logits = small[SIDE:] * scales[1:2]
    expert = lax.broadcasted_iota(jnp.int32, logits.shape, 0)
    ids = ids_ref[...]
    chosen = expert == ids[0:1]
    for k in range(1, ids.shape[0]):
        chosen = chosen | (expert == ids[k : k + 1])
    top = jnp.max(jnp.where(chosen, logits, -jnp.inf), 0, keepdims=True)
    weights = jnp.where(chosen, jnp.exp(jnp.where(chosen, logits - top, 0.0)), 0.0)
    side_ref[0:SIDE] = scales
    side_ref[SIDE:] = weights / jnp.sum(weights, 0, keepdims=True)


def rows_kernel(
    first_ref, gain_ref, side_ref, owner_ref, w_ref, kept_ref, sent_ref, piece_ref, piece_sem
):
    tokens = first_ref.shape[0]
    slots, depth, _ = piece_ref.shape
    pieces = w_ref.shape[0] // depth

    def fetch(n):
        return pltpu.make_async_copy(
            w_ref.at[pl.ds(n * depth, depth)], piece_ref.at[n % slots], piece_sem.at[n % slots]
        )

    for n in range(slots):
        fetch(n).start()
    attn_in = (first_ref[...].astype(jnp.float32) * row_of(gain_ref)).astype(jnp.bfloat16)
    kv = None
    for n in range(pieces):
        fetch(n).wait()
        term = jnp.dot(
            attn_in[:, n * depth : (n + 1) * depth],
            piece_ref[n % slots],
            preferred_element_type=jnp.float32,
        )
        kv = term if kv is None else kv + term
        if n + slots < pieces:
            fetch(n + slots).start()
    fill = jnp.zeros((tokens - SIDE, tokens), jnp.float32)
    scales = jnp.transpose(jnp.concatenate([side_ref[0:SIDE], fill], 0))
    kv = (kv * scales[:, 0:1]).astype(jnp.bfloat16)
    theirs = jnp.where(owner_ref[...] == lax.axis_index("tp"), 0, 1)
    hot = lax.broadcasted_iota(jnp.int32, (SIDE, tokens), 0) == theirs
    hot = jnp.where(hot, 1.0, 0.0)
    row = lax.broadcasted_iota(jnp.int32, (tokens, tokens), 0)
    column = lax.broadcasted_iota(jnp.int32, (tokens, tokens), 1)
    before = jnp.where(row < column, 1.0, 0.0).astype(jnp.bfloat16)
    earlier = jnp.dot(hot.astype(jnp.bfloat16), before, preferred_element_type=jnp.float32)
    slot = jnp.sum(earlier * hot, 0, keepdims=True).astype(jnp.int32)
    for side, out_ref in enumerate((kept_ref, sent_ref)):
        placing = jnp.where((slot == row) & (theirs == side), 1.0, 0.0).astype(jnp.bfloat16)
        out = jnp.dot(placing, kv, preferred_element_type=jnp.float32)
        out_ref[...] = out.astype(jnp.bfloat16)


def cache_kernel(kept_ref, arrived_ref, gain_ref, out_ref):
    gain = row_of(gain_ref)
    for head in range(2 * KVH):
        columns = slice(head * HD, (head + 1) * HD)
        x = kept_ref[:, columns].astype(jnp.float32) + arrived_ref[:, columns].astype(jnp.float32)
        if head < KVH:
            x = x * lax.rsqrt(jnp.mean(x * x, 1, keepdims=True) + EPS) * gain
        out_ref[:, columns] = x.astype(jnp.bfloat16)


def joined_kernel(first_ref, second_ref, out_ref):
    tokens = first_ref.shape[1]
    out_ref[:, :tokens] = first_ref[...]
    out_ref[:, tokens:] = second_ref[...]


def tied(arrays, after):
    count = len(arrays)
    anywhere = pl.BlockSpec(memory_space=pl.ANY)

    def kernel(*refs):
        refs[-1][...] = jnp.zeros((8, 128), jnp.float32)

    shapes = [jax.ShapeDtypeStruct(x.shape, x.dtype) for x in arrays]
    return pl.pallas_call(
        kernel,
        in_specs=[anywhere] * (count + 1),
        out_specs=[anywhere] * count + in_vmem(1),
        out_shape=[*shapes, jax.ShapeDtypeStruct((8, 128), jnp.float32)],
        input_output_aliases={n: n for n in range(count)},
        compiler_params=pltpu.CompilerParams(vmem_limit_bytes=1024 * 1024),
        cost_estimate=BRIEF,
    )(*arrays, after)


def sum_kernel(*refs):
    refs[-1][...] = total(*[ref[...] for ref in refs[:-1]])


def summed(terms, after, work=BRIEF):
    out = jax.ShapeDtypeStruct(terms[0].shape, jnp.bfloat16)
    return whole_call(sum_kernel, [out], terms, after, work=work)


def paired_products(rows, tiles):
    flat = [(t, k) for t, (steps, _) in enumerate(tiles) for k in range(len(steps))]

    def stage(index):
        t, k = flat[index]
        _, first_tile, second_tile = tiles[t][0][k]
        pltpu.matmul_push_rhs(first_tile(), index % 2, 0)
        pltpu.matmul_push_rhs(second_tile(), index % 2, 1)

    def run(*accs):
        def finish(t):
            first, second = accs[t % 2], accs[2 + t % 2]
            tiles[t][1](pltpu.matmul_pop(first), pltpu.matmul_pop(second))

        stage(0)
        for index, (t, k) in enumerate(flat):
            if index + 1 < len(flat):
                stage(index + 1)
            left = tiles[t][0][k][0]()
            pltpu.matmul_acc_lhs(accs[t % 2], left, index % 2)
            pltpu.matmul_acc_lhs(accs[2 + t % 2], left, index % 2)
            if t and k == 1:
                finish(t - 1)
        finish(len(tiles) - 1)

    kinds = [pltpu.ACC(unit)((rows, MXU), jnp.float32) for unit in (0, 0, 1, 1)]
    pl.run_scoped(run, *kinds)


def load_kernel(source_ref, *refs):
    *held_refs, sem = refs
    copies = copies_of(source_ref, held_refs, sem)
    for copy in copies:
        copy.start()
    for copy in copies:
        copy.wait()


def experts_in_vmem(w):
    return [pltpu.VMEM(w.shape[1:], w.dtype)] * w.shape[0]


def loaded(w, after):
    *held, after = whole_call(
        load_kernel,
        experts_in_vmem(w),
        [pltpu.with_memory_space_constraint(w, pltpu.HBM)],
        after,
        kinds=[pl.ANY],
        scratch=[pltpu.SemaphoreType.DMA((w.shape[0],))],
        limit=1,
        work=weight_work(1, w),
    )
    return held, after


def block_hidden_kernel(experts, *refs):
    own_ref, other_ref, sib_own_ref, sib_other_ref, side_ref, *refs = refs
    w_refs, refs = refs[: 2 * experts], refs[2 * experts :]
    copies = []
    if len(refs) > 2:
        source_ref, out_ref, *held_refs, x_ref, sem = refs
        copies = copies_of(source_ref, held_refs, sem)
    else:
        out_ref, x_ref = refs
    for copy in copies:
        copy.start()
    rows, width = own_ref.shape
    depth, units = w_refs[0].shape
    half = lax.axis_index("tp")
    first_expert = SIDE + lax.axis_index("ep") * experts
    mine = pl.ds(pl.multiple_of(half * width, width), width)
    theirs = pl.ds(pl.multiple_of((1 - half) * width, width), width)
    x_ref[0:rows, mine] = own_ref[...]
    x_ref[0:rows, theirs] = other_ref[...]
    x_ref[rows : 2 * rows, mine] = sib_own_ref[...]
    x_ref[rows : 2 * rows, theirs] = sib_other_ref[...]
    side = jnp.transpose(side_ref[...])
    scale = column_of(side, 1)

    def tile_of_units(e, tile):
        columns = pl.ds(tile * MXU, MXU)

        def step(k):
            part = pl.ds(k * MXU, MXU)
            return (
                lambda: x_ref[:, part],
                lambda: w_refs[e][part, columns],
                lambda: w_refs[experts + e][part, columns],
            )

        def finish(gate, up):
            weight = column_of(side, first_expert + e)
            out_ref[e, :, columns] = silu_up(gate, up, scale, weight)

        return [step(k) for k in range(depth // MXU)], finish

    tiles = [tile_of_units(e, tile) for e in range(experts) for tile in range(units // MXU)]
    paired_products(2 * rows, tiles)
    for copy in copies:
        copy.wait()


def block_hidden(chunks, side, gates, ups, after, w_down=None):
    rows, _ = chunks[0].shape
    experts, (depth, units) = len(gates), gates[0].shape
    outs = [jax.ShapeDtypeStruct((experts, 2 * rows, units), jnp.bfloat16)]
    operands, kinds = [*chunks, side, *gates, *ups], [pltpu.VMEM] * (5 + 2 * experts)
    scratch = [pltpu.VMEM((2 * rows, depth), jnp.bfloat16)]
    if w_down is not None:
        outs += experts_in_vmem(w_down)
        operands, kinds = [*operands, w_down], [*kinds, pl.ANY]
        scratch.append(pltpu.SemaphoreType.DMA((experts,)))
    work = weight_work(2 * rows, *gates, *ups)
    body = functools.partial(block_hidden_kernel, experts)
    return whole_call(body, outs, operands, after, kinds, scratch, 4, work)


def block_down_kernel(half, experts, h_ref, *refs):
    w_refs, (own_ref, sib_ref) = refs[:experts], refs[experts:]
    rows, width = own_ref.shape
    units = h_ref.shape[2]
    here = lax.axis_index("tp")
    first = (here + half - 2 * half * here) * width

    def tile_of_columns(tile):
        start = tile * (2 * MXU)

        def step(e, k):
            part = pl.ds(k * MXU, MXU)
            at = [pl.ds(pl.multiple_of(first + start + MXU * n, MXU), MXU) for n in (0, 1)]
            return (
                lambda: h_ref[e, :, part],
                lambda: w_refs[e][part, at[0]],
                lambda: w_refs[e][part, at[1]],
            )

        def finish(*products):
            for n, y in enumerate(products):
                columns = pl.ds(start + n * MXU, MXU)
                own_ref[:, columns] = y[:rows].astype(jnp.bfloat16)
                sib_ref[:, columns] = y[rows:].astype(jnp.bfloat16)

        return [step(e, k) for e in range(experts) for k in range(units // MXU)], finish

    paired_products(2 * rows, [tile_of_columns(n) for n in range(width // (2 * MXU))])


def block_down(half, hidden, w_down, after):
    _, tokens, _ = hidden.shape
    rows, width = tokens // 2, w_down[0].shape[1] // 2
    out = jax.ShapeDtypeStruct((rows, width), jnp.bfloat16)
    return whole_call(
        functools.partial(block_down_kernel, half, len(w_down)),
        [out, out],
        [hidden, *w_down],
        after,
        work=weight_work(rows, *w_down),
    )


def total(*terms):
    return sum(term.astype(jnp.float32) for term in terms).astype(jnp.bfloat16)


def ring_device(
    layer_input,
    stream,
    expert_ids,
    kv_owner,
    attn_norm,
    moe_norm,
    k_norm,
    w_kv,
    router,
    w_gate,
    w_up,
    w_down,
):
    ep_count = lax.axis_size("ep")
    chips = ep_count // 2
    forward = [(d, (d + 2) % ep_count) for d in range(ep_count)]
    siblings = [(d, d ^ 1) for d in range(ep_count)]
    along = functools.partial(lax.ppermute, axis_name="ep", perm=forward)
    beside = functools.partial(lax.ppermute, axis_name="ep", perm=siblings)
    across = functools.partial(lax.ppermute, axis_name="tp", perm=[(0, 1), (1, 0)])
    rows = stream.shape[0]
    columns = w_kv.shape[1]
    side_rows = SIDE + router.shape[1]
    row_shape = jax.ShapeDtypeStruct(stream.shape, jnp.bfloat16)
    small_shape = jax.ShapeDtypeStruct((side_rows, rows), jnp.float32)
    pair_shape = jax.ShapeDtypeStruct((side_rows, 2 * rows), jnp.float32)
    placed_shape = jax.ShapeDtypeStruct((rows, columns), jnp.bfloat16)
    layer_input, stream, w_kv, w_down = [
        pltpu.with_memory_space_constraint(x, pltpu.HBM)
        for x in (layer_input, stream, w_kv, w_down)
    ]

    rows_out, token = whole_call(
        opening_kernel, [row_shape], [stream, moe_norm], limit=8
    )
    lane, crossed = [rows_out, along(rows_out)], [across(rows_out)]

    small, token = whole_call(
        stats_kernel, [small_shape], [layer_input, stream, rows_out, router.T], token, limit=8
    )
    small_other = across(small)
    gate_held, token = loaded(w_gate, token)
    up_held, token = loaded(w_up, token)
    lane[1], crossed[0], small_other, token = tied([lane[1], crossed[0], small_other], token)
    lane.append(along(lane[1]))
    crossed.append(across(lane[1]))
    side, token = whole_call(
        sides_kernel, [small_shape], [small, small_other, expert_ids.T], token
    )
    side_other = beside(side)
    pair, token = whole_call(joined_kernel, [pair_shape], [side, side_other], token)

    def side_at(pair, s):
        ahead = [(d, (d + 2 * s) % ep_count) for d in range(ep_count)]
        return lax.ppermute(pair, "ep", ahead)

    sides = [pair, side_at(pair, 1), None, None]

    down_held = []
    hidden, own, back, swapped = [[None] * chips for _ in range(4)]

    def chunks(s):
        return (lane[s], crossed[s], beside(lane[s]), beside(crossed[s]))

    def up(s, after):
        given = w_down if s else None
        hidden[s], *down_held[:], after = block_hidden(
            chunks(s), sides[s], gate_held, up_held, after, given
        )
        return after

    def down(s, arrays, after, meanwhile=lambda after: after):
        kept, sent, after = block_down(1, hidden[s], down_held, after)
        *arrays, sent, after = tied([*arrays, sent], after)
        own[s], back[s], after = block_down(0, hidden[s], down_held, after)
        after = meanwhile(after)
        passed, after = summed([kept, beside(sent)], after)
        swapped[s] = across(passed)
        return (*arrays, after) if arrays else after

    def exchange(s, after):
        sent, after = tied([back[s]], after)
        back[s] = beside(sent)
        return after

    def gather(s, after):
        terms = [*travelling, swapped[s], back[s], own[s]]
        passed, after = summed(terms, after, weight_work(1, w_gate, w_up))
        travelling[:] = [along(passed)]
        return after

    travelling = []
    token = up(0, token)
    lane[2], crossed[1], sides[1], pair, token = tied([lane[2], crossed[1], sides[1], pair], token)
    sides[2:] = [side_at(pair, 2), side_at(pair, 3)]
    lane.append(along(lane[2]))
    crossed.append(across(lane[2]))
    depth = stream.shape[1] // 4
    kept, sent, token = whole_call(
        rows_kernel,
        [placed_shape, placed_shape],
        [layer_input, attn_norm, side, kv_owner.T, w_kv],
        token,
        kinds=[pltpu.VMEM] * 4 + [pl.ANY],
        scratch=[
            pltpu.VMEM((2, depth, columns), jnp.bfloat16),
            pltpu.SemaphoreType.DMA((2,)),
        ],
        limit=5,
    )
    token = up(1, token)
    lane[3], crossed[2], sent, *sides[2:], token = down(
        1, [lane[3], crossed[2], sent, *sides[2:]], token
    )
    arrived = across(sent)
    crossed.append(along(crossed[2]))
    token = exchange(1, token)
    token = up(2, token)
    crossed[3], arrived, token = down(
        2, [crossed[3], arrived], token, functools.partial(gather, 1)
    )
    token = exchange(2, token)
    token = up(3, token)
    token = down(3, [], token, functools.partial(gather, 2))
    token = exchange(3, token)
    kv_cache, token = whole_call(cache_kernel, [placed_shape], [kept, arrived, k_norm], token)
    token = down(0, [], token, functools.partial(gather, 3))
    token = exchange(0, token)
    moe_out, _ = summed([*travelling, swapped[0], back[0], own[0]], token)
    return moe_out, kv_cache.reshape(1, 1, rows, columns)


def hidden_kernel(x_ref, wg_ref, wu_ref, scale_ref, weight_ref, out_ref):
    blocks, parts, rows, width = x_ref.shape
    gate = up = None
    for part in range(parts):
        x = x_ref[:, part].reshape(blocks * rows, width)
        depth = pl.ds(part * width, width)
        g = jnp.dot(x, wg_ref[0, depth], preferred_element_type=jnp.float32)
        u = jnp.dot(x, wu_ref[0, depth], preferred_element_type=jnp.float32)
        gate = g if gate is None else gate + g
        up = u if up is None else up + u
    out_ref[0] = silu_up(gate, up, scale_ref[...], weight_ref[0])


def hidden_of(x, w_gate, w_up, scale, weight):
    blocks, parts, rows, width = x.shape
    experts, depth, units = w_gate.shape
    tokens = blocks * rows
    tile = tile_of(units, 256)
    tiles = units // tile
    wspec = pl.BlockSpec((1, depth, tile), lambda e, f: (e, 0, f))
    return pl.pallas_call(
        hidden_kernel,
        grid=(experts, tiles),
        in_specs=[
            pl.BlockSpec(x.shape, lambda e, f: (0, 0, 0, 0)),
            wspec,
            wspec,
            pl.BlockSpec((tokens, 1), lambda e, f: (0, 0)),
            pl.BlockSpec((1, tokens, 1), lambda e, f: (e, 0, 0)),
        ],
        out_specs=pl.BlockSpec((1, tokens, tile), lambda e, f: (e, 0, f)),
        out_shape=jax.ShapeDtypeStruct((experts, tokens, units), jnp.bfloat16),
        compiler_params=pltpu.CompilerParams(vmem_limit_bytes=VMEM_LIMIT),
    )(x, w_gate, w_up, scale, weight)


def down_kernel(h_ref, w_ref, out_ref):
    blocks, _, rows, tile = out_ref.shape
    y = None
    for e in range(h_ref.shape[0]):
        term = jnp.dot(h_ref[e], w_ref[e], preferred_element_type=jnp.float32)
        y = term if y is None else y + term
    out_ref[:, 0] = y.astype(jnp.bfloat16).reshape(blocks, rows, tile)


def down_of(hidden, w_down, blocks, parts):
    experts, tokens, units = hidden.shape
    width = w_down.shape[2] // parts
    rows = tokens // blocks
    tile = tile_of(width, 512)
    tiles = width // tile
    return pl.pallas_call(
        down_kernel,
        grid=(parts * tiles,),
        in_specs=[
            pl.BlockSpec((experts, tokens, units), lambda n: (0, 0, 0)),
            pl.BlockSpec((experts, units, tile), lambda n: (0, 0, n)),
        ],
        out_specs=pl.BlockSpec(
            (blocks, 1, rows, tile), lambda n: (0, n // tiles, 0, n % tiles)
        ),
        out_shape=jax.ShapeDtypeStruct((blocks, parts, rows, width), jnp.bfloat16),
        compiler_params=pltpu.CompilerParams(vmem_limit_bytes=VMEM_LIMIT),
    )(hidden, w_down)


def plain_experts(rows_out, side, w_gate, w_up, w_down):
    tp_count, ep_count = lax.axis_size("tp"), lax.axis_size("ep")
    rows, width = rows_out.shape
    exp_local = w_gate.shape[0]
    gathered = lax.all_gather(rows_out, ("ep", "tp"), axis=0, tiled=False)
    gathered = gathered.reshape(ep_count, tp_count, rows, width)
    side = lax.all_gather(side, "ep", axis=1, tiled=True)
    first_expert = 1 + lax.axis_index("ep") * exp_local
    weight = lax.dynamic_slice_in_dim(side, first_expert, exp_local, 0)[:, :, None]
    hidden = hidden_of(gathered, w_gate, w_up, side[0][:, None], weight)
    partial = down_of(hidden, w_down, ep_count, tp_count)
    partial = partial.reshape(ep_count * tp_count, rows, width)
    return lax.psum_scatter(partial, ("ep", "tp"), scatter_dimension=0, tiled=False)


def per_device(
    layer_input,
    stream,
    expert_ids,
    kv_owner,
    attn_norm,
    moe_norm,
    k_norm,
    w_kv,
    router,
    w_gate,
    w_up,
    w_down,
):
    rows = layer_input.shape[0]
    tp_count = lax.axis_size("tp")
    tiled = w_gate.shape[2] % MXU == 0 and stream.shape[1] % (2 * MXU) == 0
    if tp_count == 2 and tiled and rows == 128 and lax.axis_size("ep") == 8:
        return ring_device(
            layer_input, stream, expert_ids, kv_owner, attn_norm, moe_norm, k_norm, w_kv, router,
            w_gate, w_up, w_down,
        )
    columns = 2 * KVH * HD
    expert_count = router.shape[1]
    first = layer_input.astype(jnp.float32)
    second = stream.astype(jnp.float32)

    rows_out = (second * moe_norm.astype(jnp.float32)).astype(jnp.bfloat16)

    logits = lax.dot_general(
        router, rows_out, (((0,), (1,)), ((), ())), preferred_element_type=jnp.float32
    )
    squares = jnp.stack([jnp.sum(first * first, 1), jnp.sum(second * second, 1)], 0)
    small = jnp.concatenate([squares, logits], 0)
    small = lax.psum(small, "tp")
    first_scale = lax.rsqrt(small[0] / D + EPS)
    second_scale = lax.rsqrt(small[1:2] / D + EPS)
    logits = small[2:] * second_scale
    expert_range = jnp.arange(expert_count, dtype=jnp.int32)
    chosen = jnp.any(expert_ids.T[None, :, :] == expert_range[:, None, None], 1)
    top = jnp.max(jnp.where(chosen, logits, -jnp.inf), 0, keepdims=True)
    weights = jnp.where(chosen, jnp.exp(jnp.where(chosen, logits - top, 0.0)), 0.0)
    weights = weights / jnp.sum(weights, 0, keepdims=True)
    fill = jnp.zeros((-(1 + expert_count) % 8, rows), jnp.float32)
    side = jnp.concatenate([second_scale, weights, fill], 0)

    attn_in = (first * attn_norm.astype(jnp.float32)).astype(jnp.bfloat16)
    kv = jnp.dot(attn_in, w_kv, preferred_element_type=jnp.float32) * first_scale[:, None]
    owner_cap = 2 * rows // tp_count
    owner = kv_owner[:, 0]
    owner_hot = (owner[:, None] == jnp.arange(tp_count, dtype=jnp.int32)[None, :]).astype(jnp.int32)
    owner_slot = jnp.sum(
        (jnp.cumsum(owner_hot, 0, dtype=jnp.int32) - owner_hot) * owner_hot, 1, dtype=jnp.int32
    )
    target = owner * owner_cap + owner_slot
    placing = target[None, :] == jnp.arange(tp_count * owner_cap, dtype=jnp.int32)[:, None]
    placed = jnp.dot(
        placing.astype(jnp.bfloat16), kv.astype(jnp.bfloat16), preferred_element_type=jnp.float32
    )
    placed = placed.astype(jnp.bfloat16).reshape(tp_count, owner_cap, columns)
    arrived = lax.all_to_all(placed, "tp", split_axis=0, concat_axis=0, tiled=True)
    heads = jnp.sum(arrived.astype(jnp.float32), 0)
    heads = heads.reshape(owner_cap, 2 * KVH, HD)
    keys = heads[:, :KVH]
    keys = keys * lax.rsqrt(jnp.mean(keys * keys, 2, keepdims=True) + EPS)
    keys = keys * k_norm.astype(jnp.float32)
    kv_cache = jnp.concatenate([keys, heads[:, KVH:]], 1).astype(jnp.bfloat16)
    kv_cache = kv_cache.reshape(1, 1, owner_cap, columns)

    moe_out = plain_experts(rows_out, side, w_gate, w_up, w_down)
    return (moe_out, kv_cache)


def solution(mesh):
    placed = (
        P(("group", "ep"), "tp"),
        P(("group", "ep"), "tp"),
        P(("group", "ep"), None),
        P(("group", "ep"), None),
        P("tp"),
        P("tp"),
        P(),
        P("tp", None),
        P("tp", None),
        P("ep", None, "tp"),
        P("ep", None, "tp"),
        P("ep", "tp", None),
    )
    return jax.shard_map(
        per_device,
        mesh=mesh,
        in_specs=placed,
        out_specs=(P(("group", "ep"), "tp"), P(("group", "ep"), "tp", None, None)),
        check_vma=False,
    )
```

```python
import functools

import jax
import jax.numpy as jnp
from jax import lax
from jax.experimental import pallas as pl
from jax.experimental.pallas import tpu as pltpu
from jax.sharding import PartitionSpec as P

D = 4096
KVH = 4
HD = 128
TOPK = 8


EPS = 1e-06
VMEM_LIMIT = 56 * 1024 * 1024
MXU = 256
SIDE = 8


def weight_work(rows, *weights):
    size = sum(w.size for w in weights)
    return pl.CostEstimate(flops=2 * rows * size, bytes_accessed=2 * size, transcendentals=0)


BRIEF = pl.CostEstimate(flops=1, bytes_accessed=1, transcendentals=0)


def tile_of(size, most):
    for candidate in range(most, 127, -128):
        if size % candidate == 0:
            return candidate
    return size


def silu_up(gate, up, scale, weight):
    gate = gate * scale
    up = up * scale
    return (gate / (1.0 + jnp.exp(-gate)) * up * weight).astype(jnp.bfloat16)


def column_of(side, index):
    lane = lax.broadcasted_iota(jnp.int32, side.shape, 1)
    return jnp.sum(jnp.where(lane == index, side, 0.0), 1, keepdims=True)


def in_vmem(count):
    return [pl.BlockSpec(memory_space=pltpu.VMEM)] * count


def whole_call(body, outs, operands, after=None, kinds=None, scratch=(), limit=2, work=BRIEF, same=None):
    kinds = kinds or [pltpu.VMEM] * len(operands)
    count = len(operands)

    token = jax.ShapeDtypeStruct((8, 128), jnp.float32)
    afters = [] if after is None else [after]

    def with_token(*refs):
        inputs, rest = refs[:count], refs[count + len(afters) :]
        results, spare = rest[: len(outs)], rest[len(outs) + 1 :]
        rest[len(outs)][...] = jnp.zeros((8, 128), jnp.float32)
        body(*inputs, *results, *spare)

    return pl.pallas_call(
        with_token,
        in_specs=[pl.BlockSpec(memory_space=kind) for kind in kinds]
        + [pl.BlockSpec(memory_space=pl.ANY)] * len(afters),
        out_specs=in_vmem(len(outs) + 1),
        out_shape=[*outs, token],
        scratch_shapes=scratch,
        compiler_params=pltpu.CompilerParams(vmem_limit_bytes=limit * 1024 * 1024),
        cost_estimate=work,
        input_output_aliases=same or {},
    )(*operands, *afters)


def copies_of(source_ref, held_refs, sem):
    return [
        pltpu.make_async_copy(source_ref.at[e], held_ref, sem.at[e])
        for e, held_ref in enumerate(held_refs)
    ]


def row_of(gain_ref):
    return gain_ref[...].astype(jnp.float32).reshape(1, -1)


def opening_kernel(x_ref, gain_ref, out_ref):
    out_ref[...] = (x_ref[...].astype(jnp.float32) * row_of(gain_ref)).astype(jnp.bfloat16)


def stats_kernel(first_ref, second_ref, rows_ref, router_ref, small_ref):
    tokens = first_ref.shape[0]
    squares = []
    for ref in (first_ref, second_ref):
        x = ref[...].astype(jnp.float32)
        squares.append(jnp.sum(x * x, 1, keepdims=True))
    squares = jnp.concatenate(squares + [jnp.zeros((tokens, 126), jnp.float32)], 1)
    small_ref[0:SIDE] = jnp.transpose(squares)[0:SIDE]
    small_ref[SIDE:] = lax.dot_general(
        router_ref[...],
        rows_ref[...],
        (((1,), (1,)), ((), ())),
        preferred_element_type=jnp.float32,
    )


def sides_kernel(mine_ref, other_ref, ids_ref, side_ref):
    small = mine_ref[...] + other_ref[...]
    scales = lax.rsqrt(small[0:SIDE] / D + EPS)
    logits = small[SIDE:] * scales[1:2]
    expert = lax.broadcasted_iota(jnp.int32, logits.shape, 0)
    ids = ids_ref[...]
    chosen = expert == ids[0:1]
    for k in range(1, ids.shape[0]):
        chosen = chosen | (expert == ids[k : k + 1])
    top = jnp.max(jnp.where(chosen, logits, -jnp.inf), 0, keepdims=True)
    weights = jnp.where(chosen, jnp.exp(jnp.where(chosen, logits - top, 0.0)), 0.0)
    side_ref[0:SIDE] = scales
    side_ref[SIDE:] = weights / jnp.sum(weights, 0, keepdims=True)


def rows_kernel(
    first_ref, gain_ref, side_ref, owner_ref, w_ref, kept_ref, sent_ref, piece_ref, piece_sem
):
    tokens = first_ref.shape[0]
    slots, depth, _ = piece_ref.shape
    pieces = w_ref.shape[0] // depth

    def fetch(n):
        return pltpu.make_async_copy(
            w_ref.at[pl.ds(n * depth, depth)], piece_ref.at[n % slots], piece_sem.at[n % slots]
        )

    for n in range(slots):
        fetch(n).start()
    attn_in = (first_ref[...].astype(jnp.float32) * row_of(gain_ref)).astype(jnp.bfloat16)
    kv = None
    for n in range(pieces):
        fetch(n).wait()
        term = jnp.dot(
            attn_in[:, n * depth : (n + 1) * depth],
            piece_ref[n % slots],
            preferred_element_type=jnp.float32,
        )
        kv = term if kv is None else kv + term
        if n + slots < pieces:
            fetch(n + slots).start()
    fill = jnp.zeros((tokens - SIDE, tokens), jnp.float32)
    scales = jnp.transpose(jnp.concatenate([side_ref[0:SIDE], fill], 0))
    kv = (kv * scales[:, 0:1]).astype(jnp.bfloat16)
    theirs = jnp.where(owner_ref[...] == lax.axis_index("tp"), 0, 1)
    hot = lax.broadcasted_iota(jnp.int32, (SIDE, tokens), 0) == theirs
    hot = jnp.where(hot, 1.0, 0.0)
    row = lax.broadcasted_iota(jnp.int32, (tokens, tokens), 0)
    column = lax.broadcasted_iota(jnp.int32, (tokens, tokens), 1)
    before = jnp.where(row < column, 1.0, 0.0).astype(jnp.bfloat16)
    earlier = jnp.dot(hot.astype(jnp.bfloat16), before, preferred_element_type=jnp.float32)
    slot = jnp.sum(earlier * hot, 0, keepdims=True).astype(jnp.int32)
    for side, out_ref in enumerate((kept_ref, sent_ref)):
        placing = jnp.where((slot == row) & (theirs == side), 1.0, 0.0).astype(jnp.bfloat16)
        out = jnp.dot(placing, kv, preferred_element_type=jnp.float32)
        out_ref[...] = out.astype(jnp.bfloat16)


def cache_kernel(kept_ref, arrived_ref, gain_ref, out_ref):
    gain = row_of(gain_ref)
    for head in range(2 * KVH):
        columns = slice(head * HD, (head + 1) * HD)
        x = kept_ref[:, columns].astype(jnp.float32) + arrived_ref[:, columns].astype(jnp.float32)
        if head < KVH:
            x = x * lax.rsqrt(jnp.mean(x * x, 1, keepdims=True) + EPS) * gain
        out_ref[:, columns] = x.astype(jnp.bfloat16)


def joined_kernel(first_ref, second_ref, out_ref):
    tokens = first_ref.shape[1]
    out_ref[:, :tokens] = first_ref[...]
    out_ref[:, tokens:] = second_ref[...]


def tied(arrays, after):
    count = len(arrays)
    anywhere = pl.BlockSpec(memory_space=pl.ANY)

    def kernel(*refs):
        refs[-1][...] = jnp.zeros((8, 128), jnp.float32)

    shapes = [jax.ShapeDtypeStruct(x.shape, x.dtype) for x in arrays]
    return pl.pallas_call(
        kernel,
        in_specs=[anywhere] * (count + 1),
        out_specs=[anywhere] * count + in_vmem(1),
        out_shape=[*shapes, jax.ShapeDtypeStruct((8, 128), jnp.float32)],
        input_output_aliases={n: n for n in range(count)},
        compiler_params=pltpu.CompilerParams(vmem_limit_bytes=1024 * 1024),
        cost_estimate=BRIEF,
    )(*arrays, after)


def sum_kernel(*refs):
    refs[-1][...] = total(*[ref[...] for ref in refs[:-1]])


def summed(terms, after, work=BRIEF):
    out = jax.ShapeDtypeStruct(terms[0].shape, jnp.bfloat16)
    return whole_call(sum_kernel, [out], terms, after, work=work)


def paired_products(rows, tiles):
    flat = [(t, k) for t, (steps, _) in enumerate(tiles) for k in range(len(steps))]

    def stage(index):
        t, k = flat[index]
        _, first_tile, second_tile = tiles[t][0][k]
        pltpu.matmul_push_rhs(first_tile(), index % 2, 0)
        pltpu.matmul_push_rhs(second_tile(), index % 2, 1)

    def run(*accs):
        def finish(t):
            first, second = accs[t % 2], accs[2 + t % 2]
            tiles[t][1](pltpu.matmul_pop(first), pltpu.matmul_pop(second))

        stage(0)
        for index, (t, k) in enumerate(flat):
            if index + 1 < len(flat):
                stage(index + 1)
            left = tiles[t][0][k][0]()
            pltpu.matmul_acc_lhs(accs[t % 2], left, index % 2)
            pltpu.matmul_acc_lhs(accs[2 + t % 2], left, index % 2)
            if t and k == 1:
                finish(t - 1)
        finish(len(tiles) - 1)

    kinds = [pltpu.ACC(unit)((rows, MXU), jnp.float32) for unit in (0, 0, 1, 1)]
    pl.run_scoped(run, *kinds)


def load_kernel(source_ref, *refs):
    *held_refs, sem = refs
    copies = copies_of(source_ref, held_refs, sem)
    for copy in copies:
        copy.start()
    for copy in copies:
        copy.wait()


def experts_in_vmem(w):
    return [pltpu.VMEM(w.shape[1:], w.dtype)] * w.shape[0]


def loaded(w, after):
    *held, after = whole_call(
        load_kernel,
        experts_in_vmem(w),
        [pltpu.with_memory_space_constraint(w, pltpu.HBM)],
        after,
        kinds=[pl.ANY],
        scratch=[pltpu.SemaphoreType.DMA((w.shape[0],))],
        limit=1,
        work=weight_work(1, w),
    )
    return held, after


def block_hidden_kernel(experts, *refs):
    own_ref, other_ref, sib_own_ref, sib_other_ref, side_ref, *refs = refs
    w_refs, refs = refs[: 2 * experts], refs[2 * experts :]
    copies = []
    if len(refs) > 2:
        source_ref, out_ref, *held_refs, x_ref, sem = refs
        copies = copies_of(source_ref, held_refs, sem)
    else:
        out_ref, x_ref = refs
    for copy in copies:
        copy.start()
    rows, width = own_ref.shape
    depth, units = w_refs[0].shape
    half = lax.axis_index("tp")
    first_expert = SIDE + lax.axis_index("ep") * experts
    mine = pl.ds(pl.multiple_of(half * width, width), width)
    theirs = pl.ds(pl.multiple_of((1 - half) * width, width), width)
    x_ref[0:rows, mine] = own_ref[...]
    x_ref[0:rows, theirs] = other_ref[...]
    x_ref[rows : 2 * rows, mine] = sib_own_ref[...]
    x_ref[rows : 2 * rows, theirs] = sib_other_ref[...]
    side = jnp.transpose(side_ref[...])
    scale = column_of(side, 1)

    def tile_of_units(e, tile):
        columns = pl.ds(tile * MXU, MXU)

        def step(k):
            part = pl.ds(k * MXU, MXU)
            return (
                lambda: x_ref[:, part],
                lambda: w_refs[e][part, columns],
                lambda: w_refs[experts + e][part, columns],
            )

        def finish(gate, up):
            weight = column_of(side, first_expert + e)
            out_ref[e, :, columns] = silu_up(gate, up, scale, weight)

        return [step(k) for k in range(depth // MXU)], finish

    tiles = [tile_of_units(e, tile) for e in range(experts) for tile in range(units // MXU)]
    paired_products(2 * rows, tiles)
    for copy in copies:
        copy.wait()


def block_hidden(chunks, side, gates, ups, after, w_down=None):
    rows, _ = chunks[0].shape
    experts, (depth, units) = len(gates), gates[0].shape
    outs = [jax.ShapeDtypeStruct((experts, 2 * rows, units), jnp.bfloat16)]
    operands, kinds = [*chunks, side, *gates, *ups], [pltpu.VMEM] * (5 + 2 * experts)
    scratch = [pltpu.VMEM((2 * rows, depth), jnp.bfloat16)]
    if w_down is not None:
        outs += experts_in_vmem(w_down)
        operands, kinds = [*operands, w_down], [*kinds, pl.ANY]
        scratch.append(pltpu.SemaphoreType.DMA((experts,)))
    work = weight_work(2 * rows, *gates, *ups)
    body = functools.partial(block_hidden_kernel, experts)
    return whole_call(body, outs, operands, after, kinds, scratch, 4, work)


def block_down_kernel(half, experts, h_ref, *refs):
    w_refs, (own_ref, sib_ref) = refs[:experts], refs[experts:]
    rows, width = own_ref.shape
    units = h_ref.shape[2]
    here = lax.axis_index("tp")
    first = (here + half - 2 * half * here) * width

    def tile_of_columns(tile):
        start = tile * (2 * MXU)

        def step(e, k):
            part = pl.ds(k * MXU, MXU)
            at = [pl.ds(pl.multiple_of(first + start + MXU * n, MXU), MXU) for n in (0, 1)]
            return (
                lambda: h_ref[e, :, part],
                lambda: w_refs[e][part, at[0]],
                lambda: w_refs[e][part, at[1]],
            )

        def finish(*products):
            for n, y in enumerate(products):
                columns = pl.ds(start + n * MXU, MXU)
                own_ref[:, columns] = y[:rows].astype(jnp.bfloat16)
                sib_ref[:, columns] = y[rows:].astype(jnp.bfloat16)

        return [step(e, k) for e in range(experts) for k in range(units // MXU)], finish

    paired_products(2 * rows, [tile_of_columns(n) for n in range(width // (2 * MXU))])


def block_down(half, hidden, w_down, after):
    _, tokens, _ = hidden.shape
    rows, width = tokens // 2, w_down[0].shape[1] // 2
    out = jax.ShapeDtypeStruct((rows, width), jnp.bfloat16)
    return whole_call(
        functools.partial(block_down_kernel, half, len(w_down)),
        [out, out],
        [hidden, *w_down],
        after,
        work=weight_work(rows, *w_down),
    )


def total(*terms):
    return sum(term.astype(jnp.float32) for term in terms).astype(jnp.bfloat16)


def ring_device(
    layer_input,
    stream,
    expert_ids,
    kv_owner,
    attn_norm,
    moe_norm,
    k_norm,
    w_kv,
    router,
    w_gate,
    w_up,
    w_down,
):
    ep_count = lax.axis_size("ep")
    chips = ep_count // 2
    forward = [(d, (d + 2) % ep_count) for d in range(ep_count)]
    siblings = [(d, d ^ 1) for d in range(ep_count)]
    along = functools.partial(lax.ppermute, axis_name="ep", perm=forward)
    beside = functools.partial(lax.ppermute, axis_name="ep", perm=siblings)
    across = functools.partial(lax.ppermute, axis_name="tp", perm=[(0, 1), (1, 0)])
    rows = stream.shape[0]
    columns = w_kv.shape[1]
    side_rows = SIDE + router.shape[1]
    row_shape = jax.ShapeDtypeStruct(stream.shape, jnp.bfloat16)
    small_shape = jax.ShapeDtypeStruct((side_rows, rows), jnp.float32)
    pair_shape = jax.ShapeDtypeStruct((side_rows, 2 * rows), jnp.float32)
    placed_shape = jax.ShapeDtypeStruct((rows, columns), jnp.bfloat16)
    layer_input, stream, w_kv, w_down = [
        pltpu.with_memory_space_constraint(x, pltpu.HBM)
        for x in (layer_input, stream, w_kv, w_down)
    ]

    rows_out, token = whole_call(
        opening_kernel, [row_shape], [stream, moe_norm], limit=8
    )
    lane, crossed = [rows_out, along(rows_out)], [across(rows_out)]

    small, token = whole_call(
        stats_kernel, [small_shape], [layer_input, stream, rows_out, router.T], token, limit=8
    )
    small_other = across(small)
    gate_held, token = loaded(w_gate, token)
    up_held, token = loaded(w_up, token)
    lane[1], crossed[0], small_other, token = tied([lane[1], crossed[0], small_other], token)
    lane.append(along(lane[1]))
    crossed.append(across(lane[1]))
    side, token = whole_call(
        sides_kernel, [small_shape], [small, small_other, expert_ids.T], token
    )
    side_other = beside(side)
    pair, token = whole_call(joined_kernel, [pair_shape], [side, side_other], token)

    def side_at(pair, s):
        ahead = [(d, (d + 2 * s) % ep_count) for d in range(ep_count)]
        return lax.ppermute(pair, "ep", ahead)

    sides = [pair, side_at(pair, 1), None, None]

    down_held = []
    hidden, own, back, swapped = [[None] * chips for _ in range(4)]

    def chunks(s):
        return (lane[s], crossed[s], beside(lane[s]), beside(crossed[s]))

    def up(s, after):
        given = w_down if s else None
        hidden[s], *down_held[:], after = block_hidden(
            chunks(s), sides[s], gate_held, up_held, after, given
        )
        return after

    def down(s, arrays, after, meanwhile=lambda after: after):
        kept, sent, after = block_down(1, hidden[s], down_held, after)
        *arrays, sent, after = tied([*arrays, sent], after)
        own[s], back[s], after = block_down(0, hidden[s], down_held, after)
        after = meanwhile(after)
        passed, after = summed([kept, beside(sent)], after)
        swapped[s] = across(passed)
        return (*arrays, after) if arrays else after

    def exchange(s, after):
        sent, after = tied([back[s]], after)
        back[s] = beside(sent)
        return after

    def gather(s, after):
        terms = [*travelling, swapped[s], back[s], own[s]]
        passed, after = summed(terms, after, weight_work(1, w_gate, w_up))
        travelling[:] = [along(passed)]
        return after

    travelling = []
    token = up(0, token)
    depth = stream.shape[1] // 4
    kept, sent, token = whole_call(
        rows_kernel,
        [placed_shape, placed_shape],
        [layer_input, attn_norm, side, kv_owner.T, w_kv],
        token,
        kinds=[pltpu.VMEM] * 4 + [pl.ANY],
        scratch=[
            pltpu.VMEM((2, depth, columns), jnp.bfloat16),
            pltpu.SemaphoreType.DMA((2,)),
        ],
        limit=5,
    )
    lane[2], crossed[1], sides[1], pair, token = tied([lane[2], crossed[1], sides[1], pair], token)
    sides[2:] = [side_at(pair, 2), side_at(pair, 3)]
    lane.append(along(lane[2]))
    crossed.append(across(lane[2]))
    token = up(1, token)
    lane[3], crossed[2], sent, *sides[2:], token = down(
        1, [lane[3], crossed[2], sent, *sides[2:]], token
    )
    arrived = across(sent)
    crossed.append(along(crossed[2]))
    token = exchange(1, token)
    token = up(2, token)
    crossed[3], arrived, token = down(
        2, [crossed[3], arrived], token, functools.partial(gather, 1)
    )
    token = exchange(2, token)
    token = up(3, token)
    token = down(3, [], token, functools.partial(gather, 2))
    token = exchange(3, token)
    kv_cache, token = whole_call(cache_kernel, [placed_shape], [kept, arrived, k_norm], token)
    token = down(0, [], token, functools.partial(gather, 3))
    token = exchange(0, token)
    moe_out, _ = summed([*travelling, swapped[0], back[0], own[0]], token)
    return moe_out, kv_cache.reshape(1, 1, rows, columns)


def hidden_kernel(x_ref, wg_ref, wu_ref, scale_ref, weight_ref, out_ref):
    blocks, parts, rows, width = x_ref.shape
    gate = up = None
    for part in range(parts):
        x = x_ref[:, part].reshape(blocks * rows, width)
        depth = pl.ds(part * width, width)
        g = jnp.dot(x, wg_ref[0, depth], preferred_element_type=jnp.float32)
        u = jnp.dot(x, wu_ref[0, depth], preferred_element_type=jnp.float32)
        gate = g if gate is None else gate + g
        up = u if up is None else up + u
    out_ref[0] = silu_up(gate, up, scale_ref[...], weight_ref[0])


def hidden_of(x, w_gate, w_up, scale, weight):
    blocks, parts, rows, width = x.shape
    experts, depth, units = w_gate.shape
    tokens = blocks * rows
    tile = tile_of(units, 256)
    tiles = units // tile
    wspec = pl.BlockSpec((1, depth, tile), lambda e, f: (e, 0, f))
    return pl.pallas_call(
        hidden_kernel,
        grid=(experts, tiles),
        in_specs=[
            pl.BlockSpec(x.shape, lambda e, f: (0, 0, 0, 0)),
            wspec,
            wspec,
            pl.BlockSpec((tokens, 1), lambda e, f: (0, 0)),
            pl.BlockSpec((1, tokens, 1), lambda e, f: (e, 0, 0)),
        ],
        out_specs=pl.BlockSpec((1, tokens, tile), lambda e, f: (e, 0, f)),
        out_shape=jax.ShapeDtypeStruct((experts, tokens, units), jnp.bfloat16),
        compiler_params=pltpu.CompilerParams(vmem_limit_bytes=VMEM_LIMIT),
    )(x, w_gate, w_up, scale, weight)


def down_kernel(h_ref, w_ref, out_ref):
    blocks, _, rows, tile = out_ref.shape
    y = None
    for e in range(h_ref.shape[0]):
        term = jnp.dot(h_ref[e], w_ref[e], preferred_element_type=jnp.float32)
        y = term if y is None else y + term
    out_ref[:, 0] = y.astype(jnp.bfloat16).reshape(blocks, rows, tile)


def down_of(hidden, w_down, blocks, parts):
    experts, tokens, units = hidden.shape
    width = w_down.shape[2] // parts
    rows = tokens // blocks
    tile = tile_of(width, 512)
    tiles = width // tile
    return pl.pallas_call(
        down_kernel,
        grid=(parts * tiles,),
        in_specs=[
            pl.BlockSpec((experts, tokens, units), lambda n: (0, 0, 0)),
            pl.BlockSpec((experts, units, tile), lambda n: (0, 0, n)),
        ],
        out_specs=pl.BlockSpec(
            (blocks, 1, rows, tile), lambda n: (0, n // tiles, 0, n % tiles)
        ),
        out_shape=jax.ShapeDtypeStruct((blocks, parts, rows, width), jnp.bfloat16),
        compiler_params=pltpu.CompilerParams(vmem_limit_bytes=VMEM_LIMIT),
    )(hidden, w_down)


def plain_experts(rows_out, side, w_gate, w_up, w_down):
    tp_count, ep_count = lax.axis_size("tp"), lax.axis_size("ep")
    rows, width = rows_out.shape
    exp_local = w_gate.shape[0]
    gathered = lax.all_gather(rows_out, ("ep", "tp"), axis=0, tiled=False)
    gathered = gathered.reshape(ep_count, tp_count, rows, width)
    side = lax.all_gather(side, "ep", axis=1, tiled=True)
    first_expert = 1 + lax.axis_index("ep") * exp_local
    weight = lax.dynamic_slice_in_dim(side, first_expert, exp_local, 0)[:, :, None]
    hidden = hidden_of(gathered, w_gate, w_up, side[0][:, None], weight)
    partial = down_of(hidden, w_down, ep_count, tp_count)
    partial = partial.reshape(ep_count * tp_count, rows, width)
    return lax.psum_scatter(partial, ("ep", "tp"), scatter_dimension=0, tiled=False)


def per_device(
    layer_input,
    stream,
    expert_ids,
    kv_owner,
    attn_norm,
    moe_norm,
    k_norm,
    w_kv,
    router,
    w_gate,
    w_up,
    w_down,
):
    rows = layer_input.shape[0]
    tp_count = lax.axis_size("tp")
    tiled = w_gate.shape[2] % MXU == 0 and stream.shape[1] % (2 * MXU) == 0
    if tp_count == 2 and tiled and rows == 128 and lax.axis_size("ep") == 8:
        return ring_device(
            layer_input, stream, expert_ids, kv_owner, attn_norm, moe_norm, k_norm, w_kv, router,
            w_gate, w_up, w_down,
        )
    columns = 2 * KVH * HD
    expert_count = router.shape[1]
    first = layer_input.astype(jnp.float32)
    second = stream.astype(jnp.float32)

    rows_out = (second * moe_norm.astype(jnp.float32)).astype(jnp.bfloat16)

    logits = lax.dot_general(
        router, rows_out, (((0,), (1,)), ((), ())), preferred_element_type=jnp.float32
    )
    squares = jnp.stack([jnp.sum(first * first, 1), jnp.sum(second * second, 1)], 0)
    small = jnp.concatenate([squares, logits], 0)
    small = lax.psum(small, "tp")
    first_scale = lax.rsqrt(small[0] / D + EPS)
    second_scale = lax.rsqrt(small[1:2] / D + EPS)
    logits = small[2:] * second_scale
    expert_range = jnp.arange(expert_count, dtype=jnp.int32)
    chosen = jnp.any(expert_ids.T[None, :, :] == expert_range[:, None, None], 1)
    top = jnp.max(jnp.where(chosen, logits, -jnp.inf), 0, keepdims=True)
    weights = jnp.where(chosen, jnp.exp(jnp.where(chosen, logits - top, 0.0)), 0.0)
    weights = weights / jnp.sum(weights, 0, keepdims=True)
    fill = jnp.zeros((-(1 + expert_count) % 8, rows), jnp.float32)
    side = jnp.concatenate([second_scale, weights, fill], 0)

    attn_in = (first * attn_norm.astype(jnp.float32)).astype(jnp.bfloat16)
    kv = jnp.dot(attn_in, w_kv, preferred_element_type=jnp.float32) * first_scale[:, None]
    owner_cap = 2 * rows // tp_count
    owner = kv_owner[:, 0]
    owner_hot = (owner[:, None] == jnp.arange(tp_count, dtype=jnp.int32)[None, :]).astype(jnp.int32)
    owner_slot = jnp.sum(
        (jnp.cumsum(owner_hot, 0, dtype=jnp.int32) - owner_hot) * owner_hot, 1, dtype=jnp.int32
    )
    target = owner * owner_cap + owner_slot
    placing = target[None, :] == jnp.arange(tp_count * owner_cap, dtype=jnp.int32)[:, None]
    placed = jnp.dot(
        placing.astype(jnp.bfloat16), kv.astype(jnp.bfloat16), preferred_element_type=jnp.float32
    )
    placed = placed.astype(jnp.bfloat16).reshape(tp_count, owner_cap, columns)
    arrived = lax.all_to_all(placed, "tp", split_axis=0, concat_axis=0, tiled=True)
    heads = jnp.sum(arrived.astype(jnp.float32), 0)
    heads = heads.reshape(owner_cap, 2 * KVH, HD)
    keys = heads[:, :KVH]
    keys = keys * lax.rsqrt(jnp.mean(keys * keys, 2, keepdims=True) + EPS)
    keys = keys * k_norm.astype(jnp.float32)
    kv_cache = jnp.concatenate([keys, heads[:, KVH:]], 1).astype(jnp.bfloat16)
    kv_cache = kv_cache.reshape(1, 1, owner_cap, columns)

    moe_out = plain_experts(rows_out, side, w_gate, w_up, w_down)
    return (moe_out, kv_cache)


def solution(mesh):
    placed = (
        P(("group", "ep"), "tp"),
        P(("group", "ep"), "tp"),
        P(("group", "ep"), None),
        P(("group", "ep"), None),
        P("tp"),
        P("tp"),
        P(),
        P("tp", None),
        P("tp", None),
        P("ep", None, "tp"),
        P("ep", None, "tp"),
        P("ep", "tp", None),
    )
    return jax.shard_map(
        per_device,
        mesh=mesh,
        in_specs=placed,
        out_specs=(P(("group", "ep"), "tp"), P(("group", "ep"), "tp", None, None)),
        check_vma=False,
    )
```

```python
import functools

import jax
import jax.numpy as jnp
from jax import lax
from jax.experimental import pallas as pl
from jax.experimental.pallas import tpu as pltpu
from jax.sharding import PartitionSpec as P

D = 4096
KVH = 4
HD = 128
TOPK = 8


EPS = 1e-06
VMEM_LIMIT = 56 * 1024 * 1024
MXU = 256
SIDE = 8


def weight_work(rows, *weights):
    size = sum(w.size for w in weights)
    return pl.CostEstimate(flops=2 * rows * size, bytes_accessed=2 * size, transcendentals=0)


BRIEF = pl.CostEstimate(flops=1, bytes_accessed=1, transcendentals=0)


def tile_of(size, most):
    for candidate in range(most, 127, -128):
        if size % candidate == 0:
            return candidate
    return size


def silu_up(gate, up, scale, weight):
    gate = gate * scale
    up = up * scale
    return (gate / (1.0 + jnp.exp(-gate)) * up * weight).astype(jnp.bfloat16)


def column_of(side, index):
    lane = lax.broadcasted_iota(jnp.int32, side.shape, 1)
    return jnp.sum(jnp.where(lane == index, side, 0.0), 1, keepdims=True)


def in_vmem(count):
    return [pl.BlockSpec(memory_space=pltpu.VMEM)] * count


def whole_call(body, outs, operands, after=None, kinds=None, scratch=(), limit=2, work=BRIEF, same=None):
    kinds = kinds or [pltpu.VMEM] * len(operands)
    count = len(operands)

    token = jax.ShapeDtypeStruct((8, 128), jnp.float32)
    afters = [] if after is None else [after]

    def with_token(*refs):
        inputs, rest = refs[:count], refs[count + len(afters) :]
        results, spare = rest[: len(outs)], rest[len(outs) + 1 :]
        rest[len(outs)][...] = jnp.zeros((8, 128), jnp.float32)
        body(*inputs, *results, *spare)

    return pl.pallas_call(
        with_token,
        in_specs=[pl.BlockSpec(memory_space=kind) for kind in kinds]
        + [pl.BlockSpec(memory_space=pl.ANY)] * len(afters),
        out_specs=in_vmem(len(outs) + 1),
        out_shape=[*outs, token],
        scratch_shapes=scratch,
        compiler_params=pltpu.CompilerParams(vmem_limit_bytes=limit * 1024 * 1024),
        cost_estimate=work,
        input_output_aliases=same or {},
    )(*operands, *afters)


def copies_of(source_ref, held_refs, sem):
    return [
        pltpu.make_async_copy(source_ref.at[e], held_ref, sem.at[e])
        for e, held_ref in enumerate(held_refs)
    ]


def row_of(gain_ref):
    return gain_ref[...].astype(jnp.float32).reshape(1, -1)


def opening_kernel(x_ref, gain_ref, out_ref):
    out_ref[...] = (x_ref[...].astype(jnp.float32) * row_of(gain_ref)).astype(jnp.bfloat16)


def stats_kernel(first_ref, second_ref, rows_ref, router_ref, small_ref):
    tokens = first_ref.shape[0]
    squares = []
    for ref in (first_ref, second_ref):
        x = ref[...].astype(jnp.float32)
        squares.append(jnp.sum(x * x, 1, keepdims=True))
    squares = jnp.concatenate(squares + [jnp.zeros((tokens, 126), jnp.float32)], 1)
    small_ref[0:SIDE] = jnp.transpose(squares)[0:SIDE]
    small_ref[SIDE:] = lax.dot_general(
        router_ref[...],
        rows_ref[...],
        (((1,), (1,)), ((), ())),
        preferred_element_type=jnp.float32,
    )


def sides_kernel(mine_ref, other_ref, ids_ref, side_ref):
    small = mine_ref[...] + other_ref[...]
    scales = lax.rsqrt(small[0:SIDE] / D + EPS)
    logits = small[SIDE:] * scales[1:2]
    expert = lax.broadcasted_iota(jnp.int32, logits.shape, 0)
    ids = ids_ref[...]
    chosen = expert == ids[0:1]
    for k in range(1, ids.shape[0]):
        chosen = chosen | (expert == ids[k : k + 1])
    top = jnp.max(jnp.where(chosen, logits, -jnp.inf), 0, keepdims=True)
    weights = jnp.where(chosen, jnp.exp(jnp.where(chosen, logits - top, 0.0)), 0.0)
    side_ref[0:SIDE] = scales
    side_ref[SIDE:] = weights / jnp.sum(weights, 0, keepdims=True)


def rows_kernel(
    first_ref, gain_ref, side_ref, owner_ref, w_ref, kept_ref, sent_ref, piece_ref, piece_sem
):
    tokens = first_ref.shape[0]
    slots, depth, _ = piece_ref.shape
    pieces = w_ref.shape[0] // depth

    def fetch(n):
        return pltpu.make_async_copy(
            w_ref.at[pl.ds(n * depth, depth)], piece_ref.at[n % slots], piece_sem.at[n % slots]
        )

    for n in range(slots):
        fetch(n).start()
    attn_in = (first_ref[...].astype(jnp.float32) * row_of(gain_ref)).astype(jnp.bfloat16)
    kv = None
    for n in range(pieces):
        fetch(n).wait()
        term = jnp.dot(
            attn_in[:, n * depth : (n + 1) * depth],
            piece_ref[n % slots],
            preferred_element_type=jnp.float32,
        )
        kv = term if kv is None else kv + term
        if n + slots < pieces:
            fetch(n + slots).start()
    fill = jnp.zeros((tokens - SIDE, tokens), jnp.float32)
    scales = jnp.transpose(jnp.concatenate([side_ref[0:SIDE], fill], 0))
    kv = (kv * scales[:, 0:1]).astype(jnp.bfloat16)
    theirs = jnp.where(owner_ref[...] == lax.axis_index("tp"), 0, 1)
    hot = lax.broadcasted_iota(jnp.int32, (SIDE, tokens), 0) == theirs
    hot = jnp.where(hot, 1.0, 0.0)
    row = lax.broadcasted_iota(jnp.int32, (tokens, tokens), 0)
    column = lax.broadcasted_iota(jnp.int32, (tokens, tokens), 1)
    before = jnp.where(row < column, 1.0, 0.0).astype(jnp.bfloat16)
    earlier = jnp.dot(hot.astype(jnp.bfloat16), before, preferred_element_type=jnp.float32)
    slot = jnp.sum(earlier * hot, 0, keepdims=True).astype(jnp.int32)
    for side, out_ref in enumerate((kept_ref, sent_ref)):
        placing = jnp.where((slot == row) & (theirs == side), 1.0, 0.0).astype(jnp.bfloat16)
        out = jnp.dot(placing, kv, preferred_element_type=jnp.float32)
        out_ref[...] = out.astype(jnp.bfloat16)


def cache_kernel(kept_ref, arrived_ref, gain_ref, out_ref):
    gain = row_of(gain_ref)
    for head in range(2 * KVH):
        columns = slice(head * HD, (head + 1) * HD)
        x = kept_ref[:, columns].astype(jnp.float32) + arrived_ref[:, columns].astype(jnp.float32)
        if head < KVH:
            x = x * lax.rsqrt(jnp.mean(x * x, 1, keepdims=True) + EPS) * gain
        out_ref[:, columns] = x.astype(jnp.bfloat16)


def joined_kernel(first_ref, second_ref, out_ref):
    tokens = first_ref.shape[1]
    out_ref[:, :tokens] = first_ref[...]
    out_ref[:, tokens:] = second_ref[...]


def tied(arrays, after):
    count = len(arrays)
    anywhere = pl.BlockSpec(memory_space=pl.ANY)

    def kernel(*refs):
        refs[-1][...] = jnp.zeros((8, 128), jnp.float32)

    shapes = [jax.ShapeDtypeStruct(x.shape, x.dtype) for x in arrays]
    return pl.pallas_call(
        kernel,
        in_specs=[anywhere] * (count + 1),
        out_specs=[anywhere] * count + in_vmem(1),
        out_shape=[*shapes, jax.ShapeDtypeStruct((8, 128), jnp.float32)],
        input_output_aliases={n: n for n in range(count)},
        compiler_params=pltpu.CompilerParams(vmem_limit_bytes=1024 * 1024),
        cost_estimate=BRIEF,
    )(*arrays, after)


def sum_kernel(counts, outs, *refs):
    term_refs, out_refs = refs[: sum(counts)], refs[sum(counts) :]
    rows = sum(ref.shape[0] for ref in out_refs)
    step = rows // max(*counts, outs)
    for first in range(0, rows, step):
        taken, at = [], 0
        for count in counts:
            size = rows // count
            taken.append(term_refs[at + first // size][pl.ds(first % size, step)])
            at += count
        size = rows // outs
        out_refs[first // size][pl.ds(first % size, step)] = total(*taken)


def summed(terms, after, outs=1, work=BRIEF):
    rows = sum(part.shape[0] for part in terms[0])
    out = jax.ShapeDtypeStruct((rows // outs, terms[0][0].shape[1]), jnp.bfloat16)
    body = functools.partial(sum_kernel, [len(term) for term in terms], outs)
    *results, after = whole_call(body, [out] * outs, sum(terms, []), after, work=work)
    return results, after


def half_kernel(n, *refs):
    *term_refs, out_ref = refs
    rows = out_ref.shape[0]
    part = pl.ds(n * rows, rows)
    out_ref[...] = total(*[ref[part] if ref.shape[0] > rows else ref[...] for ref in term_refs])


def half_summed(n, terms, after):
    terms = [part for term in terms for part in term]
    out = jax.ShapeDtypeStruct(terms[0].shape, jnp.bfloat16)
    return whole_call(functools.partial(half_kernel, n), [out], terms, after)


def paired_products(rows, tiles):
    flat = [(t, k) for t, (steps, _) in enumerate(tiles) for k in range(len(steps))]

    def stage(index):
        t, k = flat[index]
        _, first_tile, second_tile = tiles[t][0][k]
        pltpu.matmul_push_rhs(first_tile(), index % 2, 0)
        pltpu.matmul_push_rhs(second_tile(), index % 2, 1)

    def run(*accs):
        def finish(t):
            first, second = accs[t % 2], accs[2 + t % 2]
            tiles[t][1](pltpu.matmul_pop(first), pltpu.matmul_pop(second))

        stage(0)
        for index, (t, k) in enumerate(flat):
            if index + 1 < len(flat):
                stage(index + 1)
            left = tiles[t][0][k][0]()
            pltpu.matmul_acc_lhs(accs[t % 2], left, index % 2)
            pltpu.matmul_acc_lhs(accs[2 + t % 2], left, index % 2)
            if t and k == 1:
                finish(t - 1)
        finish(len(tiles) - 1)

    kinds = [pltpu.ACC(unit)((rows, MXU), jnp.float32) for unit in (0, 0, 1, 1)]
    pl.run_scoped(run, *kinds)


def load_kernel(source_ref, *refs):
    *held_refs, sem = refs
    copies = copies_of(source_ref, held_refs, sem)
    for copy in copies:
        copy.start()
    for copy in copies:
        copy.wait()


def experts_in_vmem(w):
    return [pltpu.VMEM(w.shape[1:], w.dtype)] * w.shape[0]


def loaded(w, after):
    *held, after = whole_call(
        load_kernel,
        experts_in_vmem(w),
        [pltpu.with_memory_space_constraint(w, pltpu.HBM)],
        after,
        kinds=[pl.ANY],
        scratch=[pltpu.SemaphoreType.DMA((w.shape[0],))],
        limit=1,
        work=weight_work(1, w),
    )
    return held, after


def block_hidden_kernel(experts, *refs):
    own_ref, other_ref, sib_own_ref, sib_other_ref, side_ref, *refs = refs
    w_refs, refs = refs[: 2 * experts], refs[2 * experts :]
    copies = []
    if len(refs) > 2:
        source_ref, out_ref, *held_refs, x_ref, sem = refs
        copies = copies_of(source_ref, held_refs, sem)
    else:
        out_ref, x_ref = refs
    for copy in copies:
        copy.start()
    rows, width = own_ref.shape
    depth, units = w_refs[0].shape
    half = lax.axis_index("tp")
    first_expert = SIDE + lax.axis_index("ep") * experts
    mine = pl.ds(pl.multiple_of(half * width, width), width)
    theirs = pl.ds(pl.multiple_of((1 - half) * width, width), width)
    x_ref[0:rows, mine] = own_ref[...]
    x_ref[0:rows, theirs] = other_ref[...]
    x_ref[rows : 2 * rows, mine] = sib_own_ref[...]
    x_ref[rows : 2 * rows, theirs] = sib_other_ref[...]
    side = jnp.transpose(side_ref[...])
    scale = column_of(side, 1)

    def tile_of_units(e, tile):
        columns = pl.ds(tile * MXU, MXU)

        def step(k):
            part = pl.ds(k * MXU, MXU)
            return (
                lambda: x_ref[:, part],
                lambda: w_refs[e][part, columns],
                lambda: w_refs[experts + e][part, columns],
            )

        def finish(gate, up):
            weight = column_of(side, first_expert + e)
            out_ref[e, :, columns] = silu_up(gate, up, scale, weight)

        return [step(k) for k in range(depth // MXU)], finish

    tiles = [tile_of_units(e, tile) for e in range(experts) for tile in range(units // MXU)]
    paired_products(2 * rows, tiles)
    for copy in copies:
        copy.wait()


def block_hidden(chunks, side, gates, ups, after, w_down=None):
    rows, _ = chunks[0].shape
    experts, (depth, units) = len(gates), gates[0].shape
    outs = [jax.ShapeDtypeStruct((experts, 2 * rows, units), jnp.bfloat16)]
    operands, kinds = [*chunks, side, *gates, *ups], [pltpu.VMEM] * (5 + 2 * experts)
    scratch = [pltpu.VMEM((2 * rows, depth), jnp.bfloat16)]
    if w_down is not None:
        outs += experts_in_vmem(w_down)
        operands, kinds = [*operands, w_down], [*kinds, pl.ANY]
        scratch.append(pltpu.SemaphoreType.DMA((experts,)))
    work = weight_work(2 * rows, *gates, *ups)
    body = functools.partial(block_hidden_kernel, experts)
    return whole_call(body, outs, operands, after, kinds, scratch, 4, work)


def block_down_kernel(half, experts, h_ref, *refs):
    w_refs, (own_ref, sib_ref) = refs[:experts], refs[experts:]
    rows, width = own_ref.shape
    units = h_ref.shape[2]
    here = lax.axis_index("tp")
    first = (here + half - 2 * half * here) * width

    def tile_of_columns(tile):
        start = tile * (2 * MXU)

        def step(e, k):
            part = pl.ds(k * MXU, MXU)
            at = [pl.ds(pl.multiple_of(first + start + MXU * n, MXU), MXU) for n in (0, 1)]
            return (
                lambda: h_ref[e, :, part],
                lambda: w_refs[e][part, at[0]],
                lambda: w_refs[e][part, at[1]],
            )

        def finish(*products):
            for n, y in enumerate(products):
                columns = pl.ds(start + n * MXU, MXU)
                own_ref[:, columns] = y[:rows].astype(jnp.bfloat16)
                sib_ref[:, columns] = y[rows:].astype(jnp.bfloat16)

        return [step(e, k) for e in range(experts) for k in range(units // MXU)], finish

    paired_products(2 * rows, [tile_of_columns(n) for n in range(width // (2 * MXU))])


def block_down(half, hidden, w_down, after):
    _, tokens, _ = hidden.shape
    rows, width = tokens // 2, w_down[0].shape[1] // 2
    out = jax.ShapeDtypeStruct((rows, width), jnp.bfloat16)
    return whole_call(
        functools.partial(block_down_kernel, half, len(w_down)),
        [out, out],
        [hidden, *w_down],
        after,
        work=weight_work(rows, *w_down),
    )


def total(*terms):
    return sum(term.astype(jnp.float32) for term in terms).astype(jnp.bfloat16)


def ring_device(
    layer_input,
    stream,
    expert_ids,
    kv_owner,
    attn_norm,
    moe_norm,
    k_norm,
    w_kv,
    router,
    w_gate,
    w_up,
    w_down,
):
    ep_count = lax.axis_size("ep")
    chips = ep_count // 2
    forward = [(d, (d + 2) % ep_count) for d in range(ep_count)]
    siblings = [(d, d ^ 1) for d in range(ep_count)]
    along = functools.partial(lax.ppermute, axis_name="ep", perm=forward)
    beside = functools.partial(lax.ppermute, axis_name="ep", perm=siblings)
    across = functools.partial(lax.ppermute, axis_name="tp", perm=[(0, 1), (1, 0)])
    rows = stream.shape[0]
    columns = w_kv.shape[1]
    side_rows = SIDE + router.shape[1]
    row_shape = jax.ShapeDtypeStruct(stream.shape, jnp.bfloat16)
    small_shape = jax.ShapeDtypeStruct((side_rows, rows), jnp.float32)
    pair_shape = jax.ShapeDtypeStruct((side_rows, 2 * rows), jnp.float32)
    placed_shape = jax.ShapeDtypeStruct((rows, columns), jnp.bfloat16)
    layer_input, stream, w_kv, w_down = [
        pltpu.with_memory_space_constraint(x, pltpu.HBM)
        for x in (layer_input, stream, w_kv, w_down)
    ]

    rows_out, token = whole_call(
        opening_kernel, [row_shape], [stream, moe_norm], limit=8
    )
    lane, crossed = [rows_out, along(rows_out)], [across(rows_out)]

    small, token = whole_call(
        stats_kernel, [small_shape], [layer_input, stream, rows_out, router.T], token, limit=8
    )
    small_other = across(small)
    gate_held, token = loaded(w_gate, token)
    up_held, token = loaded(w_up, token)
    lane[1], crossed[0], small_other, token = tied([lane[1], crossed[0], small_other], token)
    lane.append(along(lane[1]))
    crossed.append(across(lane[1]))
    side, token = whole_call(
        sides_kernel, [small_shape], [small, small_other, expert_ids.T], token
    )
    side_other = beside(side)
    pair, token = whole_call(joined_kernel, [pair_shape], [side, side_other], token)

    def side_at(pair, s):
        ahead = [(d, (d + 2 * s) % ep_count) for d in range(ep_count)]
        return lax.ppermute(pair, "ep", ahead)

    sides = [pair, side_at(pair, 1), None, None]

    down_held = []
    hidden, own, back, swapped = [[None] * chips for _ in range(4)]

    def chunks(s):
        return (lane[s], crossed[s], beside(lane[s]), beside(crossed[s]))

    def up(s, after):
        given = w_down if s else None
        hidden[s], *down_held[:], after = block_hidden(
            chunks(s), sides[s], gate_held, up_held, after, given
        )
        return after

    def down(s, arrays, after, spare=lambda after: after, meanwhile=lambda after: after, outs=1):
        kept[s], sent, after = block_down(1, hidden[s], down_held, after)
        after = spare(after)
        *arrays, sent, after = tied([*arrays, sent], after)
        own[s], back[s], after = block_down(0, hidden[s], down_held, after)
        after = meanwhile(after)
        return *arrays, swap(s, beside(sent), after, outs)

    def swap(s, returned, after, outs=1):
        passed, after = summed([[kept[s]], [returned]], after, outs)
        swapped[s] = [across(part) for part in passed]
        return after

    def exchange(s, after):
        sent, after = tied([back[s]], after)
        back[s] = beside(sent)
        return after

    def gather(s, after, outs=1):
        terms = [*travelling, swapped[s], [back[s]], [own[s]]]
        passed, after = summed(terms, after, outs)
        travelling[:] = [[along(part) for part in passed]]
        return after

    def gather_half(n, after):
        terms = [[travelling[0][n]], [swapped[3][n]], [back[3]], [own[3]]]
        passed, after = half_summed(n, terms, after)
        onward.append(along(passed))
        return after

    def spare_partner(after):
        kept[0], sent, after = block_down(1, hidden[0], down_held, after)
        first_sent[:] = [sent]
        return after

    def spare_own(after):
        own[0], back[0], after = block_down(0, hidden[0], down_held, after)
        return after

    travelling, onward, kept, first_sent = [], [], [None] * chips, []
    token = up(0, token)
    depth = stream.shape[1] // 4
    cache_kept, sent, token = whole_call(
        rows_kernel,
        [placed_shape, placed_shape],
        [layer_input, attn_norm, side, kv_owner.T, w_kv],
        token,
        kinds=[pltpu.VMEM] * 4 + [pl.ANY],
        scratch=[
            pltpu.VMEM((2, depth, columns), jnp.bfloat16),
            pltpu.SemaphoreType.DMA((2,)),
        ],
        limit=5,
    )
    lane[2], crossed[1], sides[1], pair, token = tied([lane[2], crossed[1], sides[1], pair], token)
    sides[2:] = [side_at(pair, 2), side_at(pair, 3)]
    lane.append(along(lane[2]))
    crossed.append(across(lane[2]))
    token = up(1, token)
    lane[3], crossed[2], sent, *sides[2:], token = down(
        1, [lane[3], crossed[2], sent, *sides[2:]], token, spare_partner
    )
    arrived = across(sent)
    crossed.append(along(crossed[2]))
    token = exchange(1, token)
    token = up(2, token)
    crossed[3], arrived, first, token = down(
        2,
        [crossed[3], arrived, *first_sent],
        token,
        spare_own,
        functools.partial(gather, 1),
    )
    token = exchange(2, token)
    token = up(3, token)
    (token,) = down(3, [], token, meanwhile=functools.partial(gather, 2, outs=2), outs=2)
    token = exchange(3, token)
    token = swap(0, beside(first), token)
    token = exchange(0, token)
    kv_cache, token = whole_call(
        cache_kernel, [placed_shape], [cache_kept, arrived, k_norm], token
    )
    token = gather_half(0, token)
    token = gather_half(1, token)
    (moe_out,), _ = summed([onward, swapped[0], [back[0]], [own[0]]], token)
    return moe_out, kv_cache.reshape(1, 1, rows, columns)


def hidden_kernel(x_ref, wg_ref, wu_ref, scale_ref, weight_ref, out_ref):
    blocks, parts, rows, width = x_ref.shape
    gate = up = None
    for part in range(parts):
        x = x_ref[:, part].reshape(blocks * rows, width)
        depth = pl.ds(part * width, width)
        g = jnp.dot(x, wg_ref[0, depth], preferred_element_type=jnp.float32)
        u = jnp.dot(x, wu_ref[0, depth], preferred_element_type=jnp.float32)
        gate = g if gate is None else gate + g
        up = u if up is None else up + u
    out_ref[0] = silu_up(gate, up, scale_ref[...], weight_ref[0])


def hidden_of(x, w_gate, w_up, scale, weight):
    blocks, parts, rows, width = x.shape
    experts, depth, units = w_gate.shape
    tokens = blocks * rows
    tile = tile_of(units, 256)
    tiles = units // tile
    wspec = pl.BlockSpec((1, depth, tile), lambda e, f: (e, 0, f))
    return pl.pallas_call(
        hidden_kernel,
        grid=(experts, tiles),
        in_specs=[
            pl.BlockSpec(x.shape, lambda e, f: (0, 0, 0, 0)),
            wspec,
            wspec,
            pl.BlockSpec((tokens, 1), lambda e, f: (0, 0)),
            pl.BlockSpec((1, tokens, 1), lambda e, f: (e, 0, 0)),
        ],
        out_specs=pl.BlockSpec((1, tokens, tile), lambda e, f: (e, 0, f)),
        out_shape=jax.ShapeDtypeStruct((experts, tokens, units), jnp.bfloat16),
        compiler_params=pltpu.CompilerParams(vmem_limit_bytes=VMEM_LIMIT),
    )(x, w_gate, w_up, scale, weight)


def down_kernel(h_ref, w_ref, out_ref):
    blocks, _, rows, tile = out_ref.shape
    y = None
    for e in range(h_ref.shape[0]):
        term = jnp.dot(h_ref[e], w_ref[e], preferred_element_type=jnp.float32)
        y = term if y is None else y + term
    out_ref[:, 0] = y.astype(jnp.bfloat16).reshape(blocks, rows, tile)


def down_of(hidden, w_down, blocks, parts):
    experts, tokens, units = hidden.shape
    width = w_down.shape[2] // parts
    rows = tokens // blocks
    tile = tile_of(width, 512)
    tiles = width // tile
    return pl.pallas_call(
        down_kernel,
        grid=(parts * tiles,),
        in_specs=[
            pl.BlockSpec((experts, tokens, units), lambda n: (0, 0, 0)),
            pl.BlockSpec((experts, units, tile), lambda n: (0, 0, n)),
        ],
        out_specs=pl.BlockSpec(
            (blocks, 1, rows, tile), lambda n: (0, n // tiles, 0, n % tiles)
        ),
        out_shape=jax.ShapeDtypeStruct((blocks, parts, rows, width), jnp.bfloat16),
        compiler_params=pltpu.CompilerParams(vmem_limit_bytes=VMEM_LIMIT),
    )(hidden, w_down)


def plain_experts(rows_out, side, w_gate, w_up, w_down):
    tp_count, ep_count = lax.axis_size("tp"), lax.axis_size("ep")
    rows, width = rows_out.shape
    exp_local = w_gate.shape[0]
    gathered = lax.all_gather(rows_out, ("ep", "tp"), axis=0, tiled=False)
    gathered = gathered.reshape(ep_count, tp_count, rows, width)
    side = lax.all_gather(side, "ep", axis=1, tiled=True)
    first_expert = 1 + lax.axis_index("ep") * exp_local
    weight = lax.dynamic_slice_in_dim(side, first_expert, exp_local, 0)[:, :, None]
    hidden = hidden_of(gathered, w_gate, w_up, side[0][:, None], weight)
    partial = down_of(hidden, w_down, ep_count, tp_count)
    partial = partial.reshape(ep_count * tp_count, rows, width)
    return lax.psum_scatter(partial, ("ep", "tp"), scatter_dimension=0, tiled=False)


def per_device(
    layer_input,
    stream,
    expert_ids,
    kv_owner,
    attn_norm,
    moe_norm,
    k_norm,
    w_kv,
    router,
    w_gate,
    w_up,
    w_down,
):
    rows = layer_input.shape[0]
    tp_count = lax.axis_size("tp")
    tiled = w_gate.shape[2] % MXU == 0 and stream.shape[1] % (2 * MXU) == 0
    if tp_count == 2 and tiled and rows == 128 and lax.axis_size("ep") == 8:
        return ring_device(
            layer_input, stream, expert_ids, kv_owner, attn_norm, moe_norm, k_norm, w_kv, router,
            w_gate, w_up, w_down,
        )
    columns = 2 * KVH * HD
    expert_count = router.shape[1]
    first = layer_input.astype(jnp.float32)
    second = stream.astype(jnp.float32)

    rows_out = (second * moe_norm.astype(jnp.float32)).astype(jnp.bfloat16)

    logits = lax.dot_general(
        router, rows_out, (((0,), (1,)), ((), ())), preferred_element_type=jnp.float32
    )
    squares = jnp.stack([jnp.sum(first * first, 1), jnp.sum(second * second, 1)], 0)
    small = jnp.concatenate([squares, logits], 0)
    small = lax.psum(small, "tp")
    first_scale = lax.rsqrt(small[0] / D + EPS)
    second_scale = lax.rsqrt(small[1:2] / D + EPS)
    logits = small[2:] * second_scale
    expert_range = jnp.arange(expert_count, dtype=jnp.int32)
    chosen = jnp.any(expert_ids.T[None, :, :] == expert_range[:, None, None], 1)
    top = jnp.max(jnp.where(chosen, logits, -jnp.inf), 0, keepdims=True)
    weights = jnp.where(chosen, jnp.exp(jnp.where(chosen, logits - top, 0.0)), 0.0)
    weights = weights / jnp.sum(weights, 0, keepdims=True)
    fill = jnp.zeros((-(1 + expert_count) % 8, rows), jnp.float32)
    side = jnp.concatenate([second_scale, weights, fill], 0)

    attn_in = (first * attn_norm.astype(jnp.float32)).astype(jnp.bfloat16)
    kv = jnp.dot(attn_in, w_kv, preferred_element_type=jnp.float32) * first_scale[:, None]
    owner_cap = 2 * rows // tp_count
    owner = kv_owner[:, 0]
    owner_hot = (owner[:, None] == jnp.arange(tp_count, dtype=jnp.int32)[None, :]).astype(jnp.int32)
    owner_slot = jnp.sum(
        (jnp.cumsum(owner_hot, 0, dtype=jnp.int32) - owner_hot) * owner_hot, 1, dtype=jnp.int32
    )
    target = owner * owner_cap + owner_slot
    placing = target[None, :] == jnp.arange(tp_count * owner_cap, dtype=jnp.int32)[:, None]
    placed = jnp.dot(
        placing.astype(jnp.bfloat16), kv.astype(jnp.bfloat16), preferred_element_type=jnp.float32
    )
    placed = placed.astype(jnp.bfloat16).reshape(tp_count, owner_cap, columns)
    arrived = lax.all_to_all(placed, "tp", split_axis=0, concat_axis=0, tiled=True)
    heads = jnp.sum(arrived.astype(jnp.float32), 0)
    heads = heads.reshape(owner_cap, 2 * KVH, HD)
    keys = heads[:, :KVH]
    keys = keys * lax.rsqrt(jnp.mean(keys * keys, 2, keepdims=True) + EPS)
    keys = keys * k_norm.astype(jnp.float32)
    kv_cache = jnp.concatenate([keys, heads[:, KVH:]], 1).astype(jnp.bfloat16)
    kv_cache = kv_cache.reshape(1, 1, owner_cap, columns)

    moe_out = plain_experts(rows_out, side, w_gate, w_up, w_down)
    return (moe_out, kv_cache)


def solution(mesh):
    placed = (
        P(("group", "ep"), "tp"),
        P(("group", "ep"), "tp"),
        P(("group", "ep"), None),
        P(("group", "ep"), None),
        P("tp"),
        P("tp"),
        P(),
        P("tp", None),
        P("tp", None),
        P("ep", None, "tp"),
        P("ep", None, "tp"),
        P("ep", "tp", None),
    )
    return jax.shard_map(
        per_device,
        mesh=mesh,
        in_specs=placed,
        out_specs=(P(("group", "ep"), "tp"), P(("group", "ep"), "tp", None, None)),
        check_vma=False,
    )
```

```python
import functools

import jax
import jax.numpy as jnp
from jax import lax
from jax.experimental import pallas as pl
from jax.experimental.pallas import tpu as pltpu
from jax.sharding import PartitionSpec as P

D = 4096
KVH = 4
HD = 128
TOPK = 8


EPS = 1e-06
VMEM_LIMIT = 56 * 1024 * 1024
MXU = 256
SIDE = 8


def weight_work(rows, *weights):
    size = sum(w.size for w in weights)
    return pl.CostEstimate(flops=2 * rows * size, bytes_accessed=2 * size, transcendentals=0)


BRIEF = pl.CostEstimate(flops=1, bytes_accessed=1, transcendentals=0)


def tile_of(size, most):
    for candidate in range(most, 127, -128):
        if size % candidate == 0:
            return candidate
    return size


def silu_up(gate, up, scale, weight):
    gate = gate * scale
    up = up * scale
    return (gate / (1.0 + jnp.exp(-gate)) * up * weight).astype(jnp.bfloat16)


def column_of(side, index):
    lane = lax.broadcasted_iota(jnp.int32, side.shape, 1)
    return jnp.sum(jnp.where(lane == index, side, 0.0), 1, keepdims=True)


def in_vmem(count):
    return [pl.BlockSpec(memory_space=pltpu.VMEM)] * count


def whole_call(body, outs, operands, after=None, kinds=None, scratch=(), limit=2, work=BRIEF, same=None):
    kinds = kinds or [pltpu.VMEM] * len(operands)
    count = len(operands)

    token = jax.ShapeDtypeStruct((8, 128), jnp.float32)
    afters = [] if after is None else [after]

    def with_token(*refs):
        inputs, rest = refs[:count], refs[count + len(afters) :]
        results, spare = rest[: len(outs)], rest[len(outs) + 1 :]
        rest[len(outs)][...] = jnp.zeros((8, 128), jnp.float32)
        body(*inputs, *results, *spare)

    return pl.pallas_call(
        with_token,
        in_specs=[pl.BlockSpec(memory_space=kind) for kind in kinds]
        + [pl.BlockSpec(memory_space=pl.ANY)] * len(afters),
        out_specs=in_vmem(len(outs) + 1),
        out_shape=[*outs, token],
        scratch_shapes=scratch,
        compiler_params=pltpu.CompilerParams(vmem_limit_bytes=limit * 1024 * 1024),
        cost_estimate=work,
        input_output_aliases=same or {},
    )(*operands, *afters)


def copies_of(source_ref, held_refs, sem):
    return [
        pltpu.make_async_copy(source_ref.at[e], held_ref, sem.at[e])
        for e, held_ref in enumerate(held_refs)
    ]


def row_of(gain_ref):
    return gain_ref[...].astype(jnp.float32).reshape(1, -1)


def opening_kernel(x_ref, gain_ref, out_ref):
    out_ref[...] = (x_ref[...].astype(jnp.float32) * row_of(gain_ref)).astype(jnp.bfloat16)


def stats_kernel(first_ref, second_ref, rows_ref, router_ref, small_ref):
    tokens = first_ref.shape[0]
    squares = []
    for ref in (first_ref, second_ref):
        x = ref[...].astype(jnp.float32)
        squares.append(jnp.sum(x * x, 1, keepdims=True))
    squares = jnp.concatenate(squares + [jnp.zeros((tokens, 126), jnp.float32)], 1)
    small_ref[0:SIDE] = jnp.transpose(squares)[0:SIDE]
    small_ref[SIDE:] = lax.dot_general(
        router_ref[...],
        rows_ref[...],
        (((1,), (1,)), ((), ())),
        preferred_element_type=jnp.float32,
    )


def sides_kernel(mine_ref, other_ref, ids_ref, side_ref):
    small = mine_ref[...] + other_ref[...]
    scales = lax.rsqrt(small[0:SIDE] / D + EPS)
    logits = small[SIDE:] * scales[1:2]
    expert = lax.broadcasted_iota(jnp.int32, logits.shape, 0)
    ids = ids_ref[...]
    chosen = expert == ids[0:1]
    for k in range(1, ids.shape[0]):
        chosen = chosen | (expert == ids[k : k + 1])
    top = jnp.max(jnp.where(chosen, logits, -jnp.inf), 0, keepdims=True)
    weights = jnp.where(chosen, jnp.exp(jnp.where(chosen, logits - top, 0.0)), 0.0)
    side_ref[0:SIDE] = scales
    side_ref[SIDE:] = weights / jnp.sum(weights, 0, keepdims=True)


def rows_kernel(
    first_ref, gain_ref, side_ref, owner_ref, w_ref, kept_ref, sent_ref, piece_ref, piece_sem
):
    tokens = first_ref.shape[0]
    slots, depth, _ = piece_ref.shape
    pieces = w_ref.shape[0] // depth

    def fetch(n):
        return pltpu.make_async_copy(
            w_ref.at[pl.ds(n * depth, depth)], piece_ref.at[n % slots], piece_sem.at[n % slots]
        )

    for n in range(slots):
        fetch(n).start()
    attn_in = (first_ref[...].astype(jnp.float32) * row_of(gain_ref)).astype(jnp.bfloat16)
    kv = None
    for n in range(pieces):
        fetch(n).wait()
        term = jnp.dot(
            attn_in[:, n * depth : (n + 1) * depth],
            piece_ref[n % slots],
            preferred_element_type=jnp.float32,
        )
        kv = term if kv is None else kv + term
        if n + slots < pieces:
            fetch(n + slots).start()
    fill = jnp.zeros((tokens - SIDE, tokens), jnp.float32)
    scales = jnp.transpose(jnp.concatenate([side_ref[0:SIDE], fill], 0))
    kv = (kv * scales[:, 0:1]).astype(jnp.bfloat16)
    theirs = jnp.where(owner_ref[...] == lax.axis_index("tp"), 0, 1)
    hot = lax.broadcasted_iota(jnp.int32, (SIDE, tokens), 0) == theirs
    hot = jnp.where(hot, 1.0, 0.0)
    row = lax.broadcasted_iota(jnp.int32, (tokens, tokens), 0)
    column = lax.broadcasted_iota(jnp.int32, (tokens, tokens), 1)
    before = jnp.where(row < column, 1.0, 0.0).astype(jnp.bfloat16)
    earlier = jnp.dot(hot.astype(jnp.bfloat16), before, preferred_element_type=jnp.float32)
    slot = jnp.sum(earlier * hot, 0, keepdims=True).astype(jnp.int32)
    for side, out_ref in enumerate((kept_ref, sent_ref)):
        placing = jnp.where((slot == row) & (theirs == side), 1.0, 0.0).astype(jnp.bfloat16)
        out = jnp.dot(placing, kv, preferred_element_type=jnp.float32)
        out_ref[...] = out.astype(jnp.bfloat16)


def cache_kernel(kept_ref, arrived_ref, gain_ref, out_ref):
    gain = row_of(gain_ref)
    for head in range(2 * KVH):
        columns = slice(head * HD, (head + 1) * HD)
        x = kept_ref[:, columns].astype(jnp.float32) + arrived_ref[:, columns].astype(jnp.float32)
        if head < KVH:
            x = x * lax.rsqrt(jnp.mean(x * x, 1, keepdims=True) + EPS) * gain
        out_ref[:, columns] = x.astype(jnp.bfloat16)


def joined_kernel(first_ref, second_ref, out_ref):
    tokens = first_ref.shape[1]
    out_ref[:, :tokens] = first_ref[...]
    out_ref[:, tokens:] = second_ref[...]


def tied(arrays, after):
    count = len(arrays)
    anywhere = pl.BlockSpec(memory_space=pl.ANY)

    def kernel(*refs):
        refs[-1][...] = jnp.zeros((8, 128), jnp.float32)

    shapes = [jax.ShapeDtypeStruct(x.shape, x.dtype) for x in arrays]
    return pl.pallas_call(
        kernel,
        in_specs=[anywhere] * (count + 1),
        out_specs=[anywhere] * count + in_vmem(1),
        out_shape=[*shapes, jax.ShapeDtypeStruct((8, 128), jnp.float32)],
        input_output_aliases={n: n for n in range(count)},
        compiler_params=pltpu.CompilerParams(vmem_limit_bytes=1024 * 1024),
        cost_estimate=BRIEF,
    )(*arrays, after)


def sum_kernel(counts, outs, *refs):
    term_refs, out_refs = refs[: sum(counts)], refs[sum(counts) :]
    rows = sum(ref.shape[0] for ref in out_refs)
    step = rows // max(*counts, outs)
    for first in range(0, rows, step):
        taken, at = [], 0
        for count in counts:
            size = rows // count
            taken.append(term_refs[at + first // size][pl.ds(first % size, step)])
            at += count
        size = rows // outs
        out_refs[first // size][pl.ds(first % size, step)] = total(*taken)


def summed(terms, after, outs=1, work=BRIEF):
    rows = sum(part.shape[0] for part in terms[0])
    out = jax.ShapeDtypeStruct((rows // outs, terms[0][0].shape[1]), jnp.bfloat16)
    body = functools.partial(sum_kernel, [len(term) for term in terms], outs)
    *results, after = whole_call(body, [out] * outs, sum(terms, []), after, work=work)
    return results, after


def paired_products(rows, tiles):
    flat = [(t, k) for t, (steps, _) in enumerate(tiles) for k in range(len(steps))]

    def stage(index):
        t, k = flat[index]
        _, first_tile, second_tile = tiles[t][0][k]
        pltpu.matmul_push_rhs(first_tile(), index % 2, 0)
        pltpu.matmul_push_rhs(second_tile(), index % 2, 1)

    def run(*accs):
        def finish(t):
            first, second = accs[t % 2], accs[2 + t % 2]
            tiles[t][1](pltpu.matmul_pop(first), pltpu.matmul_pop(second))

        stage(0)
        for index, (t, k) in enumerate(flat):
            if index + 1 < len(flat):
                stage(index + 1)
            left = tiles[t][0][k][0]()
            pltpu.matmul_acc_lhs(accs[t % 2], left, index % 2)
            pltpu.matmul_acc_lhs(accs[2 + t % 2], left, index % 2)
            if t and k == 1:
                finish(t - 1)
        finish(len(tiles) - 1)

    kinds = [pltpu.ACC(unit)((rows, MXU), jnp.float32) for unit in (0, 0, 1, 1)]
    pl.run_scoped(run, *kinds)


def load_kernel(source_ref, *refs):
    *held_refs, sem = refs
    copies = copies_of(source_ref, held_refs, sem)
    for copy in copies:
        copy.start()
    for copy in copies:
        copy.wait()


def experts_in_vmem(w):
    return [pltpu.VMEM(w.shape[1:], w.dtype)] * w.shape[0]


def loaded(w, after):
    *held, after = whole_call(
        load_kernel,
        experts_in_vmem(w),
        [pltpu.with_memory_space_constraint(w, pltpu.HBM)],
        after,
        kinds=[pl.ANY],
        scratch=[pltpu.SemaphoreType.DMA((w.shape[0],))],
        limit=1,
        work=weight_work(1, w),
    )
    return held, after


def block_hidden_kernel(experts, *refs):
    own_ref, other_ref, sib_own_ref, sib_other_ref, side_ref, *refs = refs
    w_refs, refs = refs[: 2 * experts], refs[2 * experts :]
    copies = []
    if len(refs) > 2:
        source_ref, out_ref, *held_refs, x_ref, sem = refs
        copies = copies_of(source_ref, held_refs, sem)
    else:
        out_ref, x_ref = refs
    for copy in copies:
        copy.start()
    rows, width = own_ref.shape
    depth, units = w_refs[0].shape
    half = lax.axis_index("tp")
    first_expert = SIDE + lax.axis_index("ep") * experts
    mine = pl.ds(pl.multiple_of(half * width, width), width)
    theirs = pl.ds(pl.multiple_of((1 - half) * width, width), width)
    x_ref[0:rows, mine] = own_ref[...]
    x_ref[0:rows, theirs] = other_ref[...]
    x_ref[rows : 2 * rows, mine] = sib_own_ref[...]
    x_ref[rows : 2 * rows, theirs] = sib_other_ref[...]
    side = jnp.transpose(side_ref[...])
    scale = column_of(side, 1)

    def tile_of_units(e, tile):
        columns = pl.ds(tile * MXU, MXU)

        def step(k):
            part = pl.ds(k * MXU, MXU)
            return (
                lambda: x_ref[:, part],
                lambda: w_refs[e][part, columns],
                lambda: w_refs[experts + e][part, columns],
            )

        def finish(gate, up):
            weight = column_of(side, first_expert + e)
            out_ref[e, :, columns] = silu_up(gate, up, scale, weight)

        return [step(k) for k in range(depth // MXU)], finish

    tiles = [tile_of_units(e, tile) for e in range(experts) for tile in range(units // MXU)]
    paired_products(2 * rows, tiles)
    for copy in copies:
        copy.wait()


def block_hidden(chunks, side, gates, ups, after, w_down=None):
    rows, _ = chunks[0].shape
    experts, (depth, units) = len(gates), gates[0].shape
    outs = [jax.ShapeDtypeStruct((experts, 2 * rows, units), jnp.bfloat16)]
    operands, kinds = [*chunks, side, *gates, *ups], [pltpu.VMEM] * (5 + 2 * experts)
    scratch = [pltpu.VMEM((2 * rows, depth), jnp.bfloat16)]
    if w_down is not None:
        outs += experts_in_vmem(w_down)
        operands, kinds = [*operands, w_down], [*kinds, pl.ANY]
        scratch.append(pltpu.SemaphoreType.DMA((experts,)))
    work = weight_work(2 * rows, *gates, *ups)
    body = functools.partial(block_hidden_kernel, experts)
    return whole_call(body, outs, operands, after, kinds, scratch, 4, work)


def block_down_kernel(half, experts, h_ref, *refs):
    w_refs, (own_ref, *sib_refs) = refs[:experts], refs[experts:]
    rows, width = own_ref.shape
    count = rows // len(sib_refs)
    units = h_ref.shape[2]
    here = lax.axis_index("tp")
    first = (here + half - 2 * half * here) * width

    def tile_of_columns(tile):
        start = tile * (2 * MXU)

        def step(e, k):
            part = pl.ds(k * MXU, MXU)
            at = [pl.ds(pl.multiple_of(first + start + MXU * n, MXU), MXU) for n in (0, 1)]
            return (
                lambda: h_ref[e, :, part],
                lambda: w_refs[e][part, at[0]],
                lambda: w_refs[e][part, at[1]],
            )

        def finish(*products):
            for n, y in enumerate(products):
                columns = pl.ds(start + n * MXU, MXU)
                own_ref[:, columns] = y[:rows].astype(jnp.bfloat16)
                for m, sib_ref in enumerate(sib_refs):
                    part = y[rows + m * count : rows + (m + 1) * count]
                    sib_ref[:, columns] = part.astype(jnp.bfloat16)

        return [step(e, k) for e in range(experts) for k in range(units // MXU)], finish

    paired_products(2 * rows, [tile_of_columns(n) for n in range(width // (2 * MXU))])


def block_down(half, hidden, w_down, after, parts=1):
    _, tokens, _ = hidden.shape
    rows, width = tokens // 2, w_down[0].shape[1] // 2
    out = jax.ShapeDtypeStruct((rows, width), jnp.bfloat16)
    part = jax.ShapeDtypeStruct((rows // parts, width), jnp.bfloat16)
    return whole_call(
        functools.partial(block_down_kernel, half, len(w_down)),
        [out] + [part] * parts,
        [hidden, *w_down],
        after,
        work=weight_work(rows, *w_down),
    )


def total(*terms):
    return sum(term.astype(jnp.float32) for term in terms).astype(jnp.bfloat16)


def ring_device(
    layer_input,
    stream,
    expert_ids,
    kv_owner,
    attn_norm,
    moe_norm,
    k_norm,
    w_kv,
    router,
    w_gate,
    w_up,
    w_down,
):
    ep_count = lax.axis_size("ep")
    chips = ep_count // 2
    forward = [(d, (d + 2) % ep_count) for d in range(ep_count)]
    siblings = [(d, d ^ 1) for d in range(ep_count)]
    along = functools.partial(lax.ppermute, axis_name="ep", perm=forward)
    beside = functools.partial(lax.ppermute, axis_name="ep", perm=siblings)
    across = functools.partial(lax.ppermute, axis_name="tp", perm=[(0, 1), (1, 0)])
    rows = stream.shape[0]
    columns = w_kv.shape[1]
    side_rows = SIDE + router.shape[1]
    row_shape = jax.ShapeDtypeStruct(stream.shape, jnp.bfloat16)
    small_shape = jax.ShapeDtypeStruct((side_rows, rows), jnp.float32)
    pair_shape = jax.ShapeDtypeStruct((side_rows, 2 * rows), jnp.float32)
    placed_shape = jax.ShapeDtypeStruct((rows, columns), jnp.bfloat16)
    layer_input, stream, w_kv, w_down = [
        pltpu.with_memory_space_constraint(x, pltpu.HBM)
        for x in (layer_input, stream, w_kv, w_down)
    ]

    rows_out, token = whole_call(
        opening_kernel, [row_shape], [stream, moe_norm], limit=8
    )
    lane, crossed = [rows_out, along(rows_out)], [across(rows_out)]

    small, token = whole_call(
        stats_kernel, [small_shape], [layer_input, stream, rows_out, router.T], token, limit=8
    )
    small_other = across(small)
    gate_held, token = loaded(w_gate, token)
    up_held, token = loaded(w_up, token)
    lane[1], crossed[0], small_other, token = tied([lane[1], crossed[0], small_other], token)
    lane.append(along(lane[1]))
    crossed.append(across(lane[1]))
    side, token = whole_call(
        sides_kernel, [small_shape], [small, small_other, expert_ids.T], token
    )
    side_other = beside(side)
    pair, token = whole_call(joined_kernel, [pair_shape], [side, side_other], token)

    def side_at(pair, s):
        ahead = [(d, (d + 2 * s) % ep_count) for d in range(ep_count)]
        return lax.ppermute(pair, "ep", ahead)

    sides = [pair, side_at(pair, 1), None, None]

    down_held = []
    hidden, own, back, swapped = [[None] * chips for _ in range(4)]

    def chunks(s):
        return (lane[s], crossed[s], beside(lane[s]), beside(crossed[s]))

    def up(s, after):
        given = w_down if s else None
        hidden[s], *down_held[:], after = block_hidden(
            chunks(s), sides[s], gate_held, up_held, after, given
        )
        return after

    def down(s, after, arrays=(), meanwhile=lambda after: after, parts=1):
        kept, *sent, after = block_down(1, hidden[s], down_held, after, parts)
        *taken, after = tied([*arrays, *sent], after)
        sent = taken[len(arrays) :]
        own[s], back[s], after = block_down(0, hidden[s], down_held, after)
        after = meanwhile(after)
        (passed,), after = summed([[kept], [beside(part) for part in sent]], after)
        swapped[s] = across(passed)
        return *taken[: len(arrays)], after

    def exchange(s, after, *arrays):
        *arrays, sent, after = tied([*arrays, back[s]], after)
        back[s] = beside(sent)
        return *arrays, after

    def gather(s, after):
        terms = [*travelling, swapped[s], back[s], own[s]]
        (passed,), after = summed([[term] for term in terms], after)
        travelling[:] = [along(passed)]
        return after

    travelling = []
    token = up(0, token)
    depth = stream.shape[1] // 4
    cache_kept, sent, token = whole_call(
        rows_kernel,
        [placed_shape, placed_shape],
        [layer_input, attn_norm, side, kv_owner.T, w_kv],
        token,
        kinds=[pltpu.VMEM] * 4 + [pl.ANY],
        scratch=[
            pltpu.VMEM((2, depth, columns), jnp.bfloat16),
            pltpu.SemaphoreType.DMA((2,)),
        ],
        limit=5,
    )
    lane[2], crossed[1], sides[1], pair, token = tied([lane[2], crossed[1], sides[1], pair], token)
    sides[2] = side_at(pair, 2)
    lane.append(along(lane[2]))
    crossed.append(across(lane[2]))
    token = up(1, token)
    (token,) = down(1, token, parts=2)
    lane[3], crossed[2], sent, sides[2], pair, token = exchange(
        1, token, lane[3], crossed[2], sent, sides[2], pair
    )
    arrived, sides[3] = across(sent), side_at(pair, 3)
    crossed.append(along(crossed[2]))
    token = up(2, token)
    crossed[3], arrived, sides[3], token = down(
        2, token, [crossed[3], arrived, sides[3]], functools.partial(gather, 1)
    )
    (token,) = exchange(2, token)
    token = up(3, token)
    (token,) = down(3, token, meanwhile=functools.partial(gather, 2))
    (token,) = exchange(3, token)
    kv_cache, token = whole_call(
        cache_kernel, [placed_shape], [cache_kept, arrived, k_norm], token
    )
    (token,) = down(0, token, meanwhile=functools.partial(gather, 3))
    (token,) = exchange(0, token)
    terms = [*travelling, swapped[0], back[0], own[0]]
    (moe_out,), _ = summed([[term] for term in terms], token)
    return moe_out, kv_cache.reshape(1, 1, rows, columns)


def hidden_kernel(x_ref, wg_ref, wu_ref, scale_ref, weight_ref, out_ref):
    blocks, parts, rows, width = x_ref.shape
    gate = up = None
    for part in range(parts):
        x = x_ref[:, part].reshape(blocks * rows, width)
        depth = pl.ds(part * width, width)
        g = jnp.dot(x, wg_ref[0, depth], preferred_element_type=jnp.float32)
        u = jnp.dot(x, wu_ref[0, depth], preferred_element_type=jnp.float32)
        gate = g if gate is None else gate + g
        up = u if up is None else up + u
    out_ref[0] = silu_up(gate, up, scale_ref[...], weight_ref[0])


def hidden_of(x, w_gate, w_up, scale, weight):
    blocks, parts, rows, width = x.shape
    experts, depth, units = w_gate.shape
    tokens = blocks * rows
    tile = tile_of(units, 256)
    tiles = units // tile
    wspec = pl.BlockSpec((1, depth, tile), lambda e, f: (e, 0, f))
    return pl.pallas_call(
        hidden_kernel,
        grid=(experts, tiles),
        in_specs=[
            pl.BlockSpec(x.shape, lambda e, f: (0, 0, 0, 0)),
            wspec,
            wspec,
            pl.BlockSpec((tokens, 1), lambda e, f: (0, 0)),
            pl.BlockSpec((1, tokens, 1), lambda e, f: (e, 0, 0)),
        ],
        out_specs=pl.BlockSpec((1, tokens, tile), lambda e, f: (e, 0, f)),
        out_shape=jax.ShapeDtypeStruct((experts, tokens, units), jnp.bfloat16),
        compiler_params=pltpu.CompilerParams(vmem_limit_bytes=VMEM_LIMIT),
    )(x, w_gate, w_up, scale, weight)


def down_kernel(h_ref, w_ref, out_ref):
    blocks, _, rows, tile = out_ref.shape
    y = None
    for e in range(h_ref.shape[0]):
        term = jnp.dot(h_ref[e], w_ref[e], preferred_element_type=jnp.float32)
        y = term if y is None else y + term
    out_ref[:, 0] = y.astype(jnp.bfloat16).reshape(blocks, rows, tile)


def down_of(hidden, w_down, blocks, parts):
    experts, tokens, units = hidden.shape
    width = w_down.shape[2] // parts
    rows = tokens // blocks
    tile = tile_of(width, 512)
    tiles = width // tile
    return pl.pallas_call(
        down_kernel,
        grid=(parts * tiles,),
        in_specs=[
            pl.BlockSpec((experts, tokens, units), lambda n: (0, 0, 0)),
            pl.BlockSpec((experts, units, tile), lambda n: (0, 0, n)),
        ],
        out_specs=pl.BlockSpec(
            (blocks, 1, rows, tile), lambda n: (0, n // tiles, 0, n % tiles)
        ),
        out_shape=jax.ShapeDtypeStruct((blocks, parts, rows, width), jnp.bfloat16),
        compiler_params=pltpu.CompilerParams(vmem_limit_bytes=VMEM_LIMIT),
    )(hidden, w_down)


def plain_experts(rows_out, side, w_gate, w_up, w_down):
    tp_count, ep_count = lax.axis_size("tp"), lax.axis_size("ep")
    rows, width = rows_out.shape
    exp_local = w_gate.shape[0]
    gathered = lax.all_gather(rows_out, ("ep", "tp"), axis=0, tiled=False)
    gathered = gathered.reshape(ep_count, tp_count, rows, width)
    side = lax.all_gather(side, "ep", axis=1, tiled=True)
    first_expert = 1 + lax.axis_index("ep") * exp_local
    weight = lax.dynamic_slice_in_dim(side, first_expert, exp_local, 0)[:, :, None]
    hidden = hidden_of(gathered, w_gate, w_up, side[0][:, None], weight)
    partial = down_of(hidden, w_down, ep_count, tp_count)
    partial = partial.reshape(ep_count * tp_count, rows, width)
    return lax.psum_scatter(partial, ("ep", "tp"), scatter_dimension=0, tiled=False)


def per_device(
    layer_input,
    stream,
    expert_ids,
    kv_owner,
    attn_norm,
    moe_norm,
    k_norm,
    w_kv,
    router,
    w_gate,
    w_up,
    w_down,
):
    rows = layer_input.shape[0]
    tp_count = lax.axis_size("tp")
    tiled = w_gate.shape[2] % MXU == 0 and stream.shape[1] % (2 * MXU) == 0
    if tp_count == 2 and tiled and rows == 128 and lax.axis_size("ep") == 8:
        return ring_device(
            layer_input, stream, expert_ids, kv_owner, attn_norm, moe_norm, k_norm, w_kv, router,
            w_gate, w_up, w_down,
        )
    columns = 2 * KVH * HD
    expert_count = router.shape[1]
    first = layer_input.astype(jnp.float32)
    second = stream.astype(jnp.float32)

    rows_out = (second * moe_norm.astype(jnp.float32)).astype(jnp.bfloat16)

    logits = lax.dot_general(
        router, rows_out, (((0,), (1,)), ((), ())), preferred_element_type=jnp.float32
    )
    squares = jnp.stack([jnp.sum(first * first, 1), jnp.sum(second * second, 1)], 0)
    small = jnp.concatenate([squares, logits], 0)
    small = lax.psum(small, "tp")
    first_scale = lax.rsqrt(small[0] / D + EPS)
    second_scale = lax.rsqrt(small[1:2] / D + EPS)
    logits = small[2:] * second_scale
    expert_range = jnp.arange(expert_count, dtype=jnp.int32)
    chosen = jnp.any(expert_ids.T[None, :, :] == expert_range[:, None, None], 1)
    top = jnp.max(jnp.where(chosen, logits, -jnp.inf), 0, keepdims=True)
    weights = jnp.where(chosen, jnp.exp(jnp.where(chosen, logits - top, 0.0)), 0.0)
    weights = weights / jnp.sum(weights, 0, keepdims=True)
    fill = jnp.zeros((-(1 + expert_count) % 8, rows), jnp.float32)
    side = jnp.concatenate([second_scale, weights, fill], 0)

    attn_in = (first * attn_norm.astype(jnp.float32)).astype(jnp.bfloat16)
    kv = jnp.dot(attn_in, w_kv, preferred_element_type=jnp.float32) * first_scale[:, None]
    owner_cap = 2 * rows // tp_count
    owner = kv_owner[:, 0]
    owner_hot = (owner[:, None] == jnp.arange(tp_count, dtype=jnp.int32)[None, :]).astype(jnp.int32)
    owner_slot = jnp.sum(
        (jnp.cumsum(owner_hot, 0, dtype=jnp.int32) - owner_hot) * owner_hot, 1, dtype=jnp.int32
    )
    target = owner * owner_cap + owner_slot
    placing = target[None, :] == jnp.arange(tp_count * owner_cap, dtype=jnp.int32)[:, None]
    placed = jnp.dot(
        placing.astype(jnp.bfloat16), kv.astype(jnp.bfloat16), preferred_element_type=jnp.float32
    )
    placed = placed.astype(jnp.bfloat16).reshape(tp_count, owner_cap, columns)
    arrived = lax.all_to_all(placed, "tp", split_axis=0, concat_axis=0, tiled=True)
    heads = jnp.sum(arrived.astype(jnp.float32), 0)
    heads = heads.reshape(owner_cap, 2 * KVH, HD)
    keys = heads[:, :KVH]
    keys = keys * lax.rsqrt(jnp.mean(keys * keys, 2, keepdims=True) + EPS)
    keys = keys * k_norm.astype(jnp.float32)
    kv_cache = jnp.concatenate([keys, heads[:, KVH:]], 1).astype(jnp.bfloat16)
    kv_cache = kv_cache.reshape(1, 1, owner_cap, columns)

    moe_out = plain_experts(rows_out, side, w_gate, w_up, w_down)
    return (moe_out, kv_cache)


def solution(mesh):
    placed = (
        P(("group", "ep"), "tp"),
        P(("group", "ep"), "tp"),
        P(("group", "ep"), None),
        P(("group", "ep"), None),
        P("tp"),
        P("tp"),
        P(),
        P("tp", None),
        P("tp", None),
        P("ep", None, "tp"),
        P("ep", None, "tp"),
        P("ep", "tp", None),
    )
    return jax.shard_map(
        per_device,
        mesh=mesh,
        in_specs=placed,
        out_specs=(P(("group", "ep"), "tp"), P(("group", "ep"), "tp", None, None)),
        check_vma=False,
    )
```

```python
import functools

import jax
import jax.numpy as jnp
from jax import lax
from jax.experimental import pallas as pl
from jax.experimental.pallas import tpu as pltpu
from jax.sharding import PartitionSpec as P

D = 4096
KVH = 4
HD = 128
TOPK = 8


EPS = 1e-06
VMEM_LIMIT = 56 * 1024 * 1024
MXU = 256
SIDE = 8


def weight_work(rows, *weights):
    size = sum(w.size for w in weights)
    return pl.CostEstimate(flops=2 * rows * size, bytes_accessed=2 * size, transcendentals=0)


BRIEF = pl.CostEstimate(flops=1, bytes_accessed=1, transcendentals=0)


def tile_of(size, most):
    for candidate in range(most, 127, -128):
        if size % candidate == 0:
            return candidate
    return size


def silu_up(gate, up, scale, weight):
    gate = gate * scale
    up = up * scale
    return (gate / (1.0 + jnp.exp(-gate)) * up * weight).astype(jnp.bfloat16)


def column_of(side, index):
    lane = lax.broadcasted_iota(jnp.int32, side.shape, 1)
    return jnp.sum(jnp.where(lane == index, side, 0.0), 1, keepdims=True)


def in_vmem(count):
    return [pl.BlockSpec(memory_space=pltpu.VMEM)] * count


def whole_call(body, outs, operands, after=None, kinds=None, scratch=(), limit=2, work=BRIEF, same=None):
    kinds = kinds or [pltpu.VMEM] * len(operands)
    count = len(operands)

    token = jax.ShapeDtypeStruct((8, 128), jnp.float32)
    afters = [] if after is None else [after]

    def with_token(*refs):
        inputs, rest = refs[:count], refs[count + len(afters) :]
        results, spare = rest[: len(outs)], rest[len(outs) + 1 :]
        rest[len(outs)][...] = jnp.zeros((8, 128), jnp.float32)
        body(*inputs, *results, *spare)

    return pl.pallas_call(
        with_token,
        in_specs=[pl.BlockSpec(memory_space=kind) for kind in kinds]
        + [pl.BlockSpec(memory_space=pl.ANY)] * len(afters),
        out_specs=in_vmem(len(outs) + 1),
        out_shape=[*outs, token],
        scratch_shapes=scratch,
        compiler_params=pltpu.CompilerParams(vmem_limit_bytes=limit * 1024 * 1024),
        cost_estimate=work,
        input_output_aliases=same or {},
    )(*operands, *afters)


def copies_of(source_ref, held_refs, sem):
    return [
        pltpu.make_async_copy(source_ref.at[e], held_ref, sem.at[e])
        for e, held_ref in enumerate(held_refs)
    ]


def row_of(gain_ref):
    return gain_ref[...].astype(jnp.float32).reshape(1, -1)


def opening_kernel(x_ref, gain_ref, out_ref):
    out_ref[...] = (x_ref[...].astype(jnp.float32) * row_of(gain_ref)).astype(jnp.bfloat16)


def stats_kernel(first_ref, second_ref, rows_ref, router_ref, small_ref):
    tokens = first_ref.shape[0]
    squares = []
    for ref in (first_ref, second_ref):
        x = ref[...].astype(jnp.float32)
        squares.append(jnp.sum(x * x, 1, keepdims=True))
    squares = jnp.concatenate(squares + [jnp.zeros((tokens, 126), jnp.float32)], 1)
    small_ref[0:SIDE] = jnp.transpose(squares)[0:SIDE]
    small_ref[SIDE:] = lax.dot_general(
        router_ref[...],
        rows_ref[...],
        (((1,), (1,)), ((), ())),
        preferred_element_type=jnp.float32,
    )


def sides_kernel(mine_ref, other_ref, ids_ref, side_ref):
    small = mine_ref[...] + other_ref[...]
    scales = lax.rsqrt(small[0:SIDE] / D + EPS)
    logits = small[SIDE:] * scales[1:2]
    expert = lax.broadcasted_iota(jnp.int32, logits.shape, 0)
    ids = ids_ref[...]
    chosen = expert == ids[0:1]
    for k in range(1, ids.shape[0]):
        chosen = chosen | (expert == ids[k : k + 1])
    top = jnp.max(jnp.where(chosen, logits, -jnp.inf), 0, keepdims=True)
    weights = jnp.where(chosen, jnp.exp(jnp.where(chosen, logits - top, 0.0)), 0.0)
    side_ref[0:SIDE] = scales
    side_ref[SIDE:] = weights / jnp.sum(weights, 0, keepdims=True)


def rows_kernel(
    first_ref, gain_ref, side_ref, owner_ref, w_ref, kept_ref, sent_ref, piece_ref, piece_sem
):
    tokens = first_ref.shape[0]
    slots, depth, _ = piece_ref.shape
    pieces = w_ref.shape[0] // depth

    def fetch(n):
        return pltpu.make_async_copy(
            w_ref.at[pl.ds(n * depth, depth)], piece_ref.at[n % slots], piece_sem.at[n % slots]
        )

    for n in range(slots):
        fetch(n).start()
    attn_in = (first_ref[...].astype(jnp.float32) * row_of(gain_ref)).astype(jnp.bfloat16)
    kv = None
    for n in range(pieces):
        fetch(n).wait()
        term = jnp.dot(
            attn_in[:, n * depth : (n + 1) * depth],
            piece_ref[n % slots],
            preferred_element_type=jnp.float32,
        )
        kv = term if kv is None else kv + term
        if n + slots < pieces:
            fetch(n + slots).start()
    fill = jnp.zeros((tokens - SIDE, tokens), jnp.float32)
    scales = jnp.transpose(jnp.concatenate([side_ref[0:SIDE], fill], 0))
    kv = (kv * scales[:, 0:1]).astype(jnp.bfloat16)
    theirs = jnp.where(owner_ref[...] == lax.axis_index("tp"), 0, 1)
    hot = lax.broadcasted_iota(jnp.int32, (SIDE, tokens), 0) == theirs
    hot = jnp.where(hot, 1.0, 0.0)
    row = lax.broadcasted_iota(jnp.int32, (tokens, tokens), 0)
    column = lax.broadcasted_iota(jnp.int32, (tokens, tokens), 1)
    before = jnp.where(row < column, 1.0, 0.0).astype(jnp.bfloat16)
    earlier = jnp.dot(hot.astype(jnp.bfloat16), before, preferred_element_type=jnp.float32)
    slot = jnp.sum(earlier * hot, 0, keepdims=True).astype(jnp.int32)
    for side, out_ref in enumerate((kept_ref, sent_ref)):
        placing = jnp.where((slot == row) & (theirs == side), 1.0, 0.0).astype(jnp.bfloat16)
        out = jnp.dot(placing, kv, preferred_element_type=jnp.float32)
        out_ref[...] = out.astype(jnp.bfloat16)


def cache_kernel(kept_ref, arrived_ref, gain_ref, out_ref):
    gain = row_of(gain_ref)
    for head in range(2 * KVH):
        columns = slice(head * HD, (head + 1) * HD)
        x = kept_ref[:, columns].astype(jnp.float32) + arrived_ref[:, columns].astype(jnp.float32)
        if head < KVH:
            x = x * lax.rsqrt(jnp.mean(x * x, 1, keepdims=True) + EPS) * gain
        out_ref[:, columns] = x.astype(jnp.bfloat16)


def joined_kernel(first_ref, second_ref, out_ref):
    tokens = first_ref.shape[1]
    out_ref[:, :tokens] = first_ref[...]
    out_ref[:, tokens:] = second_ref[...]


def tied(arrays, after):
    count = len(arrays)
    anywhere = pl.BlockSpec(memory_space=pl.ANY)

    def kernel(*refs):
        refs[-1][...] = jnp.zeros((8, 128), jnp.float32)

    shapes = [jax.ShapeDtypeStruct(x.shape, x.dtype) for x in arrays]
    return pl.pallas_call(
        kernel,
        in_specs=[anywhere] * (count + 1),
        out_specs=[anywhere] * count + in_vmem(1),
        out_shape=[*shapes, jax.ShapeDtypeStruct((8, 128), jnp.float32)],
        input_output_aliases={n: n for n in range(count)},
        compiler_params=pltpu.CompilerParams(vmem_limit_bytes=1024 * 1024),
        cost_estimate=BRIEF,
    )(*arrays, after)


def sum_kernel(*refs):
    refs[-1][...] = total(*[ref[...] for ref in refs[:-1]])


def summed(terms, after, work=BRIEF):
    out = jax.ShapeDtypeStruct(terms[0].shape, jnp.bfloat16)
    return whole_call(sum_kernel, [out], terms, after, work=work)


def paired_products(rows, tiles):
    flat = [(t, k) for t, (steps, _) in enumerate(tiles) for k in range(len(steps))]

    def stage(index):
        t, k = flat[index]
        _, first_tile, second_tile = tiles[t][0][k]
        pltpu.matmul_push_rhs(first_tile(), index % 2, 0)
        pltpu.matmul_push_rhs(second_tile(), index % 2, 1)

    def run(*accs):
        def finish(t):
            first, second = accs[t % 2], accs[2 + t % 2]
            tiles[t][1](pltpu.matmul_pop(first), pltpu.matmul_pop(second))

        stage(0)
        for index, (t, k) in enumerate(flat):
            if index + 1 < len(flat):
                stage(index + 1)
            left = tiles[t][0][k][0]()
            pltpu.matmul_acc_lhs(accs[t % 2], left, index % 2)
            pltpu.matmul_acc_lhs(accs[2 + t % 2], left, index % 2)
            if t and k == 1:
                finish(t - 1)
        finish(len(tiles) - 1)

    kinds = [pltpu.ACC(unit)((rows, MXU), jnp.float32) for unit in (0, 0, 1, 1)]
    pl.run_scoped(run, *kinds)


def load_kernel(source_ref, *refs):
    *held_refs, sem = refs
    copies = copies_of(source_ref, held_refs, sem)
    for copy in copies:
        copy.start()
    for copy in copies:
        copy.wait()


def experts_in_vmem(w):
    return [pltpu.VMEM(w.shape[1:], w.dtype)] * w.shape[0]


def loaded(w, after):
    *held, after = whole_call(
        load_kernel,
        experts_in_vmem(w),
        [pltpu.with_memory_space_constraint(w, pltpu.HBM)],
        after,
        kinds=[pl.ANY],
        scratch=[pltpu.SemaphoreType.DMA((w.shape[0],))],
        limit=1,
        work=weight_work(1, w),
    )
    return held, after


def block_hidden_kernel(experts, *refs):
    own_ref, other_ref, sib_own_ref, sib_other_ref, side_ref, *refs = refs
    w_refs, refs = refs[: 2 * experts], refs[2 * experts :]
    copies = []
    if len(refs) > 2:
        source_ref, out_ref, *held_refs, x_ref, sem = refs
        copies = copies_of(source_ref, held_refs, sem)
    else:
        out_ref, x_ref = refs
    for copy in copies:
        copy.start()
    rows, width = own_ref.shape
    depth, units = w_refs[0].shape
    half = lax.axis_index("tp")
    first_expert = SIDE + lax.axis_index("ep") * experts
    mine = pl.ds(pl.multiple_of(half * width, width), width)
    theirs = pl.ds(pl.multiple_of((1 - half) * width, width), width)
    x_ref[0:rows, mine] = own_ref[...]
    x_ref[0:rows, theirs] = other_ref[...]
    x_ref[rows : 2 * rows, mine] = sib_own_ref[...]
    x_ref[rows : 2 * rows, theirs] = sib_other_ref[...]
    side = jnp.transpose(side_ref[...])
    scale = column_of(side, 1)

    def tile_of_units(e, tile):
        columns = pl.ds(tile * MXU, MXU)

        def step(k):
            part = pl.ds(k * MXU, MXU)
            return (
                lambda: x_ref[:, part],
                lambda: w_refs[e][part, columns],
                lambda: w_refs[experts + e][part, columns],
            )

        def finish(gate, up):
            weight = column_of(side, first_expert + e)
            out_ref[e, :, columns] = silu_up(gate, up, scale, weight)

        return [step(k) for k in range(depth // MXU)], finish

    tiles = [tile_of_units(e, tile) for e in range(experts) for tile in range(units // MXU)]
    paired_products(2 * rows, tiles)
    for copy in copies:
        copy.wait()


def block_hidden(chunks, side, gates, ups, after, w_down=None):
    rows, _ = chunks[0].shape
    experts, (depth, units) = len(gates), gates[0].shape
    outs = [jax.ShapeDtypeStruct((experts, 2 * rows, units), jnp.bfloat16)]
    operands, kinds = [*chunks, side, *gates, *ups], [pltpu.VMEM] * (5 + 2 * experts)
    scratch = [pltpu.VMEM((2 * rows, depth), jnp.bfloat16)]
    if w_down is not None:
        outs += experts_in_vmem(w_down)
        operands, kinds = [*operands, w_down], [*kinds, pl.ANY]
        scratch.append(pltpu.SemaphoreType.DMA((experts,)))
    work = weight_work(2 * rows, *gates, *ups)
    body = functools.partial(block_hidden_kernel, experts)
    return whole_call(body, outs, operands, after, kinds, scratch, 4, work)


def block_down_kernel(half, experts, h_ref, *refs):
    w_refs, (own_ref, sib_ref) = refs[:experts], refs[experts:]
    rows, width = own_ref.shape
    units = h_ref.shape[2]
    here = lax.axis_index("tp")
    first = (here + half - 2 * half * here) * width

    def tile_of_columns(tile):
        start = tile * (2 * MXU)

        def step(e, k):
            part = pl.ds(k * MXU, MXU)
            at = [pl.ds(pl.multiple_of(first + start + MXU * n, MXU), MXU) for n in (0, 1)]
            return (
                lambda: h_ref[e, :, part],
                lambda: w_refs[e][part, at[0]],
                lambda: w_refs[e][part, at[1]],
            )

        def finish(*products):
            for n, y in enumerate(products):
                columns = pl.ds(start + n * MXU, MXU)
                own_ref[:, columns] = y[:rows].astype(jnp.bfloat16)
                sib_ref[:, columns] = y[rows:].astype(jnp.bfloat16)

        return [step(e, k) for e in range(experts) for k in range(units // MXU)], finish

    paired_products(2 * rows, [tile_of_columns(n) for n in range(width // (2 * MXU))])


def block_down(half, hidden, w_down, after):
    _, tokens, _ = hidden.shape
    rows, width = tokens // 2, w_down[0].shape[1] // 2
    out = jax.ShapeDtypeStruct((rows, width), jnp.bfloat16)
    return whole_call(
        functools.partial(block_down_kernel, half, len(w_down)),
        [out, out],
        [hidden, *w_down],
        after,
        work=weight_work(rows, *w_down),
    )


def total(*terms):
    return sum(term.astype(jnp.float32) for term in terms).astype(jnp.bfloat16)


def ring_device(
    layer_input,
    stream,
    expert_ids,
    kv_owner,
    attn_norm,
    moe_norm,
    k_norm,
    w_kv,
    router,
    w_gate,
    w_up,
    w_down,
):
    ep_count = lax.axis_size("ep")
    chips = ep_count // 2
    forward = [(d, (d + 2) % ep_count) for d in range(ep_count)]
    siblings = [(d, d ^ 1) for d in range(ep_count)]
    along = functools.partial(lax.ppermute, axis_name="ep", perm=forward)
    beside = functools.partial(lax.ppermute, axis_name="ep", perm=siblings)
    across = functools.partial(lax.ppermute, axis_name="tp", perm=[(0, 1), (1, 0)])
    rows = stream.shape[0]
    columns = w_kv.shape[1]
    side_rows = SIDE + router.shape[1]
    row_shape = jax.ShapeDtypeStruct(stream.shape, jnp.bfloat16)
    small_shape = jax.ShapeDtypeStruct((side_rows, rows), jnp.float32)
    pair_shape = jax.ShapeDtypeStruct((side_rows, 2 * rows), jnp.float32)
    placed_shape = jax.ShapeDtypeStruct((rows, columns), jnp.bfloat16)
    layer_input, stream, w_kv, w_down = [
        pltpu.with_memory_space_constraint(x, pltpu.HBM)
        for x in (layer_input, stream, w_kv, w_down)
    ]

    rows_out, token = whole_call(
        opening_kernel, [row_shape], [stream, moe_norm], limit=8
    )
    lane, crossed = [rows_out, along(rows_out)], [across(rows_out)]

    small, token = whole_call(
        stats_kernel, [small_shape], [layer_input, stream, rows_out, router.T], token, limit=8
    )
    small_other = across(small)
    gate_held, token = loaded(w_gate, token)
    up_held, token = loaded(w_up, token)
    lane[1], crossed[0], small_other, token = tied([lane[1], crossed[0], small_other], token)
    lane.append(along(lane[1]))
    crossed.append(across(lane[1]))
    side, token = whole_call(
        sides_kernel, [small_shape], [small, small_other, expert_ids.T], token
    )
    side_other = beside(side)
    depth = stream.shape[1] // 4
    kept, sent, token = whole_call(
        rows_kernel,
        [placed_shape, placed_shape],
        [layer_input, attn_norm, side, kv_owner.T, w_kv],
        token,
        kinds=[pltpu.VMEM] * 4 + [pl.ANY],
        scratch=[
            pltpu.VMEM((2, depth, columns), jnp.bfloat16),
            pltpu.SemaphoreType.DMA((2,)),
        ],
        limit=5,
    )
    arrived = across(sent)
    pair, token = whole_call(joined_kernel, [pair_shape], [side, side_other], token)

    def side_at(pair, s):
        ahead = [(d, (d + 2 * s) % ep_count) for d in range(ep_count)]
        return lax.ppermute(pair, "ep", ahead)

    sides = [pair, side_at(pair, 1), None, None]

    down_held = []
    hidden, own, back, swapped = [[None] * chips for _ in range(4)]

    def chunks(s):
        return (lane[s], crossed[s], beside(lane[s]), beside(crossed[s]))

    def up(s, after):
        given = w_down if s else None
        hidden[s], *down_held[:], after = block_hidden(
            chunks(s), sides[s], gate_held, up_held, after, given
        )
        return after

    def down(s, arrays, after, meanwhile=lambda after: after):
        kept, sent, after = block_down(1, hidden[s], down_held, after)
        *arrays, sent, after = tied([*arrays, sent], after)
        own[s], back[s], after = block_down(0, hidden[s], down_held, after)
        after = meanwhile(after)
        passed, after = summed([kept, beside(sent)], after)
        swapped[s] = across(passed)
        return (*arrays, after) if arrays else after

    def exchange(s, after):
        sent, after = tied([back[s]], after)
        back[s] = beside(sent)
        return after

    def gather(s, after):
        terms = [*travelling, swapped[s], back[s], own[s]]
        passed, after = summed(terms, after, weight_work(1, w_gate, w_up))
        travelling[:] = [along(passed)]
        return after

    travelling = []
    token = up(0, token)
    lane[2], crossed[1], sides[1], pair, arrived, token = tied(
        [lane[2], crossed[1], sides[1], pair, arrived], token
    )
    sides[2:] = [side_at(pair, 2), side_at(pair, 3)]
    lane.append(along(lane[2]))
    crossed.append(across(lane[2]))
    token = up(1, token)
    lane[3], crossed[2], *sides[2:], token = down(1, [lane[3], crossed[2], *sides[2:]], token)
    crossed.append(along(crossed[2]))
    token = exchange(1, token)
    token = up(2, token)
    crossed[3], token = down(2, [crossed[3]], token, functools.partial(gather, 1))
    token = exchange(2, token)
    token = up(3, token)
    token = down(3, [], token, functools.partial(gather, 2))
    token = exchange(3, token)
    kv_cache, token = whole_call(cache_kernel, [placed_shape], [kept, arrived, k_norm], token)
    token = down(0, [], token, functools.partial(gather, 3))
    token = exchange(0, token)
    moe_out, _ = summed([*travelling, swapped[0], back[0], own[0]], token)
    return moe_out, kv_cache.reshape(1, 1, rows, columns)


def hidden_kernel(x_ref, wg_ref, wu_ref, scale_ref, weight_ref, out_ref):
    blocks, parts, rows, width = x_ref.shape
    gate = up = None
    for part in range(parts):
        x = x_ref[:, part].reshape(blocks * rows, width)
        depth = pl.ds(part * width, width)
        g = jnp.dot(x, wg_ref[0, depth], preferred_element_type=jnp.float32)
        u = jnp.dot(x, wu_ref[0, depth], preferred_element_type=jnp.float32)
        gate = g if gate is None else gate + g
        up = u if up is None else up + u
    out_ref[0] = silu_up(gate, up, scale_ref[...], weight_ref[0])


def hidden_of(x, w_gate, w_up, scale, weight):
    blocks, parts, rows, width = x.shape
    experts, depth, units = w_gate.shape
    tokens = blocks * rows
    tile = tile_of(units, 256)
    tiles = units // tile
    wspec = pl.BlockSpec((1, depth, tile), lambda e, f: (e, 0, f))
    return pl.pallas_call(
        hidden_kernel,
        grid=(experts, tiles),
        in_specs=[
            pl.BlockSpec(x.shape, lambda e, f: (0, 0, 0, 0)),
            wspec,
            wspec,
            pl.BlockSpec((tokens, 1), lambda e, f: (0, 0)),
            pl.BlockSpec((1, tokens, 1), lambda e, f: (e, 0, 0)),
        ],
        out_specs=pl.BlockSpec((1, tokens, tile), lambda e, f: (e, 0, f)),
        out_shape=jax.ShapeDtypeStruct((experts, tokens, units), jnp.bfloat16),
        compiler_params=pltpu.CompilerParams(vmem_limit_bytes=VMEM_LIMIT),
    )(x, w_gate, w_up, scale, weight)


def down_kernel(h_ref, w_ref, out_ref):
    blocks, _, rows, tile = out_ref.shape
    y = None
    for e in range(h_ref.shape[0]):
        term = jnp.dot(h_ref[e], w_ref[e], preferred_element_type=jnp.float32)
        y = term if y is None else y + term
    out_ref[:, 0] = y.astype(jnp.bfloat16).reshape(blocks, rows, tile)


def down_of(hidden, w_down, blocks, parts):
    experts, tokens, units = hidden.shape
    width = w_down.shape[2] // parts
    rows = tokens // blocks
    tile = tile_of(width, 512)
    tiles = width // tile
    return pl.pallas_call(
        down_kernel,
        grid=(parts * tiles,),
        in_specs=[
            pl.BlockSpec((experts, tokens, units), lambda n: (0, 0, 0)),
            pl.BlockSpec((experts, units, tile), lambda n: (0, 0, n)),
        ],
        out_specs=pl.BlockSpec(
            (blocks, 1, rows, tile), lambda n: (0, n // tiles, 0, n % tiles)
        ),
        out_shape=jax.ShapeDtypeStruct((blocks, parts, rows, width), jnp.bfloat16),
        compiler_params=pltpu.CompilerParams(vmem_limit_bytes=VMEM_LIMIT),
    )(hidden, w_down)


def plain_experts(rows_out, side, w_gate, w_up, w_down):
    tp_count, ep_count = lax.axis_size("tp"), lax.axis_size("ep")
    rows, width = rows_out.shape
    exp_local = w_gate.shape[0]
    gathered = lax.all_gather(rows_out, ("ep", "tp"), axis=0, tiled=False)
    gathered = gathered.reshape(ep_count, tp_count, rows, width)
    side = lax.all_gather(side, "ep", axis=1, tiled=True)
    first_expert = 1 + lax.axis_index("ep") * exp_local
    weight = lax.dynamic_slice_in_dim(side, first_expert, exp_local, 0)[:, :, None]
    hidden = hidden_of(gathered, w_gate, w_up, side[0][:, None], weight)
    partial = down_of(hidden, w_down, ep_count, tp_count)
    partial = partial.reshape(ep_count * tp_count, rows, width)
    return lax.psum_scatter(partial, ("ep", "tp"), scatter_dimension=0, tiled=False)


def per_device(
    layer_input,
    stream,
    expert_ids,
    kv_owner,
    attn_norm,
    moe_norm,
    k_norm,
    w_kv,
    router,
    w_gate,
    w_up,
    w_down,
):
    rows = layer_input.shape[0]
    tp_count = lax.axis_size("tp")
    tiled = w_gate.shape[2] % MXU == 0 and stream.shape[1] % (2 * MXU) == 0
    if tp_count == 2 and tiled and rows == 128 and lax.axis_size("ep") == 8:
        return ring_device(
            layer_input, stream, expert_ids, kv_owner, attn_norm, moe_norm, k_norm, w_kv, router,
            w_gate, w_up, w_down,
        )
    columns = 2 * KVH * HD
    expert_count = router.shape[1]
    first = layer_input.astype(jnp.float32)
    second = stream.astype(jnp.float32)

    rows_out = (second * moe_norm.astype(jnp.float32)).astype(jnp.bfloat16)

    logits = lax.dot_general(
        router, rows_out, (((0,), (1,)), ((), ())), preferred_element_type=jnp.float32
    )
    squares = jnp.stack([jnp.sum(first * first, 1), jnp.sum(second * second, 1)], 0)
    small = jnp.concatenate([squares, logits], 0)
    small = lax.psum(small, "tp")
    first_scale = lax.rsqrt(small[0] / D + EPS)
    second_scale = lax.rsqrt(small[1:2] / D + EPS)
    logits = small[2:] * second_scale
    expert_range = jnp.arange(expert_count, dtype=jnp.int32)
    chosen = jnp.any(expert_ids.T[None, :, :] == expert_range[:, None, None], 1)
    top = jnp.max(jnp.where(chosen, logits, -jnp.inf), 0, keepdims=True)
    weights = jnp.where(chosen, jnp.exp(jnp.where(chosen, logits - top, 0.0)), 0.0)
    weights = weights / jnp.sum(weights, 0, keepdims=True)
    fill = jnp.zeros((-(1 + expert_count) % 8, rows), jnp.float32)
    side = jnp.concatenate([second_scale, weights, fill], 0)

    attn_in = (first * attn_norm.astype(jnp.float32)).astype(jnp.bfloat16)
    kv = jnp.dot(attn_in, w_kv, preferred_element_type=jnp.float32) * first_scale[:, None]
    owner_cap = 2 * rows // tp_count
    owner = kv_owner[:, 0]
    owner_hot = (owner[:, None] == jnp.arange(tp_count, dtype=jnp.int32)[None, :]).astype(jnp.int32)
    owner_slot = jnp.sum(
        (jnp.cumsum(owner_hot, 0, dtype=jnp.int32) - owner_hot) * owner_hot, 1, dtype=jnp.int32
    )
    target = owner * owner_cap + owner_slot
    placing = target[None, :] == jnp.arange(tp_count * owner_cap, dtype=jnp.int32)[:, None]
    placed = jnp.dot(
        placing.astype(jnp.bfloat16), kv.astype(jnp.bfloat16), preferred_element_type=jnp.float32
    )
    placed = placed.astype(jnp.bfloat16).reshape(tp_count, owner_cap, columns)
    arrived = lax.all_to_all(placed, "tp", split_axis=0, concat_axis=0, tiled=True)
    heads = jnp.sum(arrived.astype(jnp.float32), 0)
    heads = heads.reshape(owner_cap, 2 * KVH, HD)
    keys = heads[:, :KVH]
    keys = keys * lax.rsqrt(jnp.mean(keys * keys, 2, keepdims=True) + EPS)
    keys = keys * k_norm.astype(jnp.float32)
    kv_cache = jnp.concatenate([keys, heads[:, KVH:]], 1).astype(jnp.bfloat16)
    kv_cache = kv_cache.reshape(1, 1, owner_cap, columns)

    moe_out = plain_experts(rows_out, side, w_gate, w_up, w_down)
    return (moe_out, kv_cache)


def solution(mesh):
    placed = (
        P(("group", "ep"), "tp"),
        P(("group", "ep"), "tp"),
        P(("group", "ep"), None),
        P(("group", "ep"), None),
        P("tp"),
        P("tp"),
        P(),
        P("tp", None),
        P("tp", None),
        P("ep", None, "tp"),
        P("ep", None, "tp"),
        P("ep", "tp", None),
    )
    return jax.shard_map(
        per_device,
        mesh=mesh,
        in_specs=placed,
        out_specs=(P(("group", "ep"), "tp"), P(("group", "ep"), "tp", None, None)),
        check_vma=False,
    )
```

```python
import functools

import jax
import jax.numpy as jnp
from jax import lax
from jax.experimental import pallas as pl
from jax.experimental.pallas import tpu as pltpu
from jax.sharding import PartitionSpec as P

D = 4096
KVH = 4
HD = 128
TOPK = 8


EPS = 1e-06
VMEM_LIMIT = 56 * 1024 * 1024
MXU = 256
SIDE = 8


def weight_work(rows, *weights):
    size = sum(w.size for w in weights)
    return pl.CostEstimate(flops=2 * rows * size, bytes_accessed=2 * size, transcendentals=0)


BRIEF = pl.CostEstimate(flops=1, bytes_accessed=1, transcendentals=0)


def tile_of(size, most):
    for candidate in range(most, 127, -128):
        if size % candidate == 0:
            return candidate
    return size


def silu_up(gate, up, scale, weight):
    gate = gate * scale
    up = up * scale
    return (gate / (1.0 + jnp.exp(-gate)) * up * weight).astype(jnp.bfloat16)


def column_of(side, index):
    lane = lax.broadcasted_iota(jnp.int32, side.shape, 1)
    return jnp.sum(jnp.where(lane == index, side, 0.0), 1, keepdims=True)


def in_vmem(count):
    return [pl.BlockSpec(memory_space=pltpu.VMEM)] * count


def whole_call(body, outs, operands, after=None, kinds=None, scratch=(), limit=2, work=BRIEF, same=None):
    kinds = kinds or [pltpu.VMEM] * len(operands)
    count = len(operands)

    token = jax.ShapeDtypeStruct((8, 128), jnp.float32)
    afters = [] if after is None else [after]

    def with_token(*refs):
        inputs, rest = refs[:count], refs[count + len(afters) :]
        results, spare = rest[: len(outs)], rest[len(outs) + 1 :]
        rest[len(outs)][...] = jnp.zeros((8, 128), jnp.float32)
        body(*inputs, *results, *spare)

    return pl.pallas_call(
        with_token,
        in_specs=[pl.BlockSpec(memory_space=kind) for kind in kinds]
        + [pl.BlockSpec(memory_space=pl.ANY)] * len(afters),
        out_specs=in_vmem(len(outs) + 1),
        out_shape=[*outs, token],
        scratch_shapes=scratch,
        compiler_params=pltpu.CompilerParams(vmem_limit_bytes=limit * 1024 * 1024),
        cost_estimate=work,
        input_output_aliases=same or {},
    )(*operands, *afters)


def copies_of(source_ref, held_refs, sem):
    return [
        pltpu.make_async_copy(source_ref.at[e], held_ref, sem.at[e])
        for e, held_ref in enumerate(held_refs)
    ]


def row_of(gain_ref):
    return gain_ref[...].astype(jnp.float32).reshape(1, -1)


def opening_kernel(x_ref, gain_ref, out_ref):
    out_ref[...] = (x_ref[...].astype(jnp.float32) * row_of(gain_ref)).astype(jnp.bfloat16)


def stats_kernel(first_ref, second_ref, rows_ref, router_ref, small_ref):
    tokens = first_ref.shape[0]
    squares = []
    for ref in (first_ref, second_ref):
        x = ref[...].astype(jnp.float32)
        squares.append(jnp.sum(x * x, 1, keepdims=True))
    squares = jnp.concatenate(squares + [jnp.zeros((tokens, 126), jnp.float32)], 1)
    small_ref[0:SIDE] = jnp.transpose(squares)[0:SIDE]
    small_ref[SIDE:] = lax.dot_general(
        router_ref[...],
        rows_ref[...],
        (((1,), (1,)), ((), ())),
        preferred_element_type=jnp.float32,
    )


def sides_kernel(mine_ref, other_ref, ids_ref, side_ref):
    small = mine_ref[...] + other_ref[...]
    scales = lax.rsqrt(small[0:SIDE] / D + EPS)
    logits = small[SIDE:] * scales[1:2]
    expert = lax.broadcasted_iota(jnp.int32, logits.shape, 0)
    ids = ids_ref[...]
    chosen = expert == ids[0:1]
    for k in range(1, ids.shape[0]):
        chosen = chosen | (expert == ids[k : k + 1])
    top = jnp.max(jnp.where(chosen, logits, -jnp.inf), 0, keepdims=True)
    weights = jnp.where(chosen, jnp.exp(jnp.where(chosen, logits - top, 0.0)), 0.0)
    side_ref[0:SIDE] = scales
    side_ref[SIDE:] = weights / jnp.sum(weights, 0, keepdims=True)


def rows_kernel(
    first_ref, gain_ref, side_ref, owner_ref, w_ref, kept_ref, sent_ref, piece_ref, piece_sem
):
    tokens = first_ref.shape[0]
    slots, depth, _ = piece_ref.shape
    pieces = w_ref.shape[0] // depth

    def fetch(n):
        return pltpu.make_async_copy(
            w_ref.at[pl.ds(n * depth, depth)], piece_ref.at[n % slots], piece_sem.at[n % slots]
        )

    for n in range(slots):
        fetch(n).start()
    attn_in = (first_ref[...].astype(jnp.float32) * row_of(gain_ref)).astype(jnp.bfloat16)
    kv = None
    for n in range(pieces):
        fetch(n).wait()
        term = jnp.dot(
            attn_in[:, n * depth : (n + 1) * depth],
            piece_ref[n % slots],
            preferred_element_type=jnp.float32,
        )
        kv = term if kv is None else kv + term
        if n + slots < pieces:
            fetch(n + slots).start()
    fill = jnp.zeros((tokens - SIDE, tokens), jnp.float32)
    scales = jnp.transpose(jnp.concatenate([side_ref[0:SIDE], fill], 0))
    kv = (kv * scales[:, 0:1]).astype(jnp.bfloat16)
    theirs = jnp.where(owner_ref[...] == lax.axis_index("tp"), 0, 1)
    hot = lax.broadcasted_iota(jnp.int32, (SIDE, tokens), 0) == theirs
    hot = jnp.where(hot, 1.0, 0.0)
    row = lax.broadcasted_iota(jnp.int32, (tokens, tokens), 0)
    column = lax.broadcasted_iota(jnp.int32, (tokens, tokens), 1)
    before = jnp.where(row < column, 1.0, 0.0).astype(jnp.bfloat16)
    earlier = jnp.dot(hot.astype(jnp.bfloat16), before, preferred_element_type=jnp.float32)
    slot = jnp.sum(earlier * hot, 0, keepdims=True).astype(jnp.int32)
    for side, out_ref in enumerate((kept_ref, sent_ref)):
        placing = jnp.where((slot == row) & (theirs == side), 1.0, 0.0).astype(jnp.bfloat16)
        out = jnp.dot(placing, kv, preferred_element_type=jnp.float32)
        out_ref[...] = out.astype(jnp.bfloat16)


def cache_kernel(kept_ref, arrived_ref, gain_ref, out_ref):
    gain = row_of(gain_ref)
    for head in range(2 * KVH):
        columns = slice(head * HD, (head + 1) * HD)
        x = kept_ref[:, columns].astype(jnp.float32) + arrived_ref[:, columns].astype(jnp.float32)
        if head < KVH:
            x = x * lax.rsqrt(jnp.mean(x * x, 1, keepdims=True) + EPS) * gain
        out_ref[:, columns] = x.astype(jnp.bfloat16)


def joined_kernel(first_ref, second_ref, out_ref):
    tokens = first_ref.shape[1]
    out_ref[:, :tokens] = first_ref[...]
    out_ref[:, tokens:] = second_ref[...]


def tied(arrays, after):
    count = len(arrays)
    anywhere = pl.BlockSpec(memory_space=pl.ANY)

    def kernel(*refs):
        refs[-1][...] = jnp.zeros((8, 128), jnp.float32)

    shapes = [jax.ShapeDtypeStruct(x.shape, x.dtype) for x in arrays]
    return pl.pallas_call(
        kernel,
        in_specs=[anywhere] * (count + 1),
        out_specs=[anywhere] * count + in_vmem(1),
        out_shape=[*shapes, jax.ShapeDtypeStruct((8, 128), jnp.float32)],
        input_output_aliases={n: n for n in range(count)},
        compiler_params=pltpu.CompilerParams(vmem_limit_bytes=1024 * 1024),
        cost_estimate=BRIEF,
    )(*arrays, after)


def sum_kernel(counts, outs, *refs):
    term_refs, out_refs = refs[: sum(counts)], refs[sum(counts) :]
    rows = sum(ref.shape[0] for ref in out_refs)
    step = rows // max(*counts, outs)
    for first in range(0, rows, step):
        taken, at = [], 0
        for count in counts:
            size = rows // count
            taken.append(term_refs[at + first // size][pl.ds(first % size, step)])
            at += count
        size = rows // outs
        out_refs[first // size][pl.ds(first % size, step)] = total(*taken)


def summed(terms, after, outs=1, work=BRIEF):
    rows = sum(part.shape[0] for part in terms[0])
    out = jax.ShapeDtypeStruct((rows // outs, terms[0][0].shape[1]), jnp.bfloat16)
    body = functools.partial(sum_kernel, [len(term) for term in terms], outs)
    *results, after = whole_call(body, [out] * outs, sum(terms, []), after, work=work)
    return results, after


def paired_products(rows, tiles):
    flat = [(t, k) for t, (steps, _) in enumerate(tiles) for k in range(len(steps))]

    def stage(index):
        t, k = flat[index]
        _, first_tile, second_tile = tiles[t][0][k]
        pltpu.matmul_push_rhs(first_tile(), index % 2, 0)
        pltpu.matmul_push_rhs(second_tile(), index % 2, 1)

    def run(*accs):
        def finish(t):
            first, second = accs[t % 2], accs[2 + t % 2]
            tiles[t][1](pltpu.matmul_pop(first), pltpu.matmul_pop(second))

        stage(0)
        for index, (t, k) in enumerate(flat):
            if index + 1 < len(flat):
                stage(index + 1)
            left = tiles[t][0][k][0]()
            pltpu.matmul_acc_lhs(accs[t % 2], left, index % 2)
            pltpu.matmul_acc_lhs(accs[2 + t % 2], left, index % 2)
            if t and k == 1:
                finish(t - 1)
        finish(len(tiles) - 1)

    kinds = [pltpu.ACC(unit)((rows, MXU), jnp.float32) for unit in (0, 0, 1, 1)]
    pl.run_scoped(run, *kinds)


def load_kernel(source_ref, *refs):
    *held_refs, sem = refs
    copies = copies_of(source_ref, held_refs, sem)
    for copy in copies:
        copy.start()
    for copy in copies:
        copy.wait()


def experts_in_vmem(w):
    return [pltpu.VMEM(w.shape[1:], w.dtype)] * w.shape[0]


def loaded(w, after):
    *held, after = whole_call(
        load_kernel,
        experts_in_vmem(w),
        [pltpu.with_memory_space_constraint(w, pltpu.HBM)],
        after,
        kinds=[pl.ANY],
        scratch=[pltpu.SemaphoreType.DMA((w.shape[0],))],
        limit=1,
        work=weight_work(1, w),
    )
    return held, after


def block_hidden_kernel(experts, *refs):
    own_ref, other_ref, sib_own_ref, sib_other_ref, side_ref, *refs = refs
    w_refs, refs = refs[: 2 * experts], refs[2 * experts :]
    copies = []
    if len(refs) > 2:
        source_ref, out_ref, *held_refs, x_ref, sem = refs
        copies = copies_of(source_ref, held_refs, sem)
    else:
        out_ref, x_ref = refs
    for copy in copies:
        copy.start()
    rows, width = own_ref.shape
    depth, units = w_refs[0].shape
    half = lax.axis_index("tp")
    first_expert = SIDE + lax.axis_index("ep") * experts
    mine = pl.ds(pl.multiple_of(half * width, width), width)
    theirs = pl.ds(pl.multiple_of((1 - half) * width, width), width)
    x_ref[0:rows, mine] = own_ref[...]
    x_ref[0:rows, theirs] = other_ref[...]
    x_ref[rows : 2 * rows, mine] = sib_own_ref[...]
    x_ref[rows : 2 * rows, theirs] = sib_other_ref[...]
    side = jnp.transpose(side_ref[...])
    scale = column_of(side, 1)

    def tile_of_units(e, tile):
        columns = pl.ds(tile * MXU, MXU)

        def step(k):
            part = pl.ds(k * MXU, MXU)
            return (
                lambda: x_ref[:, part],
                lambda: w_refs[e][part, columns],
                lambda: w_refs[experts + e][part, columns],
            )

        def finish(gate, up):
            weight = column_of(side, first_expert + e)
            out_ref[e, :, columns] = silu_up(gate, up, scale, weight)

        return [step(k) for k in range(depth // MXU)], finish

    tiles = [tile_of_units(e, tile) for e in range(experts) for tile in range(units // MXU)]
    paired_products(2 * rows, tiles)
    for copy in copies:
        copy.wait()


def block_hidden(chunks, side, gates, ups, after, w_down=None):
    rows, _ = chunks[0].shape
    experts, (depth, units) = len(gates), gates[0].shape
    outs = [jax.ShapeDtypeStruct((experts, 2 * rows, units), jnp.bfloat16)]
    operands, kinds = [*chunks, side, *gates, *ups], [pltpu.VMEM] * (5 + 2 * experts)
    scratch = [pltpu.VMEM((2 * rows, depth), jnp.bfloat16)]
    if w_down is not None:
        outs += experts_in_vmem(w_down)
        operands, kinds = [*operands, w_down], [*kinds, pl.ANY]
        scratch.append(pltpu.SemaphoreType.DMA((experts,)))
    work = weight_work(2 * rows, *gates, *ups)
    body = functools.partial(block_hidden_kernel, experts)
    return whole_call(body, outs, operands, after, kinds, scratch, 4, work)


def block_down_kernel(half, experts, h_ref, *refs):
    w_refs, (own_ref, sib_ref) = refs[:experts], refs[experts:]
    rows, width = own_ref.shape
    units = h_ref.shape[2]
    here = lax.axis_index("tp")
    first = (here + half - 2 * half * here) * width

    def tile_of_columns(tile):
        start = tile * (2 * MXU)

        def step(e, k):
            part = pl.ds(k * MXU, MXU)
            at = [pl.ds(pl.multiple_of(first + start + MXU * n, MXU), MXU) for n in (0, 1)]
            return (
                lambda: h_ref[e, :, part],
                lambda: w_refs[e][part, at[0]],
                lambda: w_refs[e][part, at[1]],
            )

        def finish(*products):
            for n, y in enumerate(products):
                columns = pl.ds(start + n * MXU, MXU)
                own_ref[:, columns] = y[:rows].astype(jnp.bfloat16)
                sib_ref[:, columns] = y[rows:].astype(jnp.bfloat16)

        return [step(e, k) for e in range(experts) for k in range(units // MXU)], finish

    paired_products(2 * rows, [tile_of_columns(n) for n in range(width // (2 * MXU))])


def block_down(half, hidden, w_down, after):
    _, tokens, _ = hidden.shape
    rows, width = tokens // 2, w_down[0].shape[1] // 2
    out = jax.ShapeDtypeStruct((rows, width), jnp.bfloat16)
    return whole_call(
        functools.partial(block_down_kernel, half, len(w_down)),
        [out, out],
        [hidden, *w_down],
        after,
        work=weight_work(rows, *w_down),
    )


def total(*terms):
    return sum(term.astype(jnp.float32) for term in terms).astype(jnp.bfloat16)


def ring_device(
    layer_input,
    stream,
    expert_ids,
    kv_owner,
    attn_norm,
    moe_norm,
    k_norm,
    w_kv,
    router,
    w_gate,
    w_up,
    w_down,
):
    ep_count = lax.axis_size("ep")
    chips = ep_count // 2
    forward = [(d, (d + 2) % ep_count) for d in range(ep_count)]
    siblings = [(d, d ^ 1) for d in range(ep_count)]
    along = functools.partial(lax.ppermute, axis_name="ep", perm=forward)
    beside = functools.partial(lax.ppermute, axis_name="ep", perm=siblings)
    across = functools.partial(lax.ppermute, axis_name="tp", perm=[(0, 1), (1, 0)])
    rows = stream.shape[0]
    columns = w_kv.shape[1]
    side_rows = SIDE + router.shape[1]
    row_shape = jax.ShapeDtypeStruct(stream.shape, jnp.bfloat16)
    small_shape = jax.ShapeDtypeStruct((side_rows, rows), jnp.float32)
    pair_shape = jax.ShapeDtypeStruct((side_rows, 2 * rows), jnp.float32)
    placed_shape = jax.ShapeDtypeStruct((rows, columns), jnp.bfloat16)
    layer_input, stream, w_kv, w_down = [
        pltpu.with_memory_space_constraint(x, pltpu.HBM)
        for x in (layer_input, stream, w_kv, w_down)
    ]

    rows_out, token = whole_call(
        opening_kernel, [row_shape], [stream, moe_norm], limit=8
    )
    lane, crossed = [rows_out, along(rows_out)], [across(rows_out)]

    small, token = whole_call(
        stats_kernel, [small_shape], [layer_input, stream, rows_out, router.T], token, limit=8
    )
    small_other = across(small)
    gate_held, token = loaded(w_gate, token)
    up_held, token = loaded(w_up, token)
    lane[1], crossed[0], small_other, token = tied([lane[1], crossed[0], small_other], token)
    lane.append(along(lane[1]))
    crossed.append(across(lane[1]))
    side, token = whole_call(
        sides_kernel, [small_shape], [small, small_other, expert_ids.T], token
    )
    side_other = beside(side)
    pair, token = whole_call(joined_kernel, [pair_shape], [side, side_other], token)

    def side_at(pair, s):
        ahead = [(d, (d + 2 * s) % ep_count) for d in range(ep_count)]
        return lax.ppermute(pair, "ep", ahead)

    sides = [pair, side_at(pair, 1), None, None]

    down_held = []
    hidden, own, back, swapped = [[None] * chips for _ in range(4)]

    def chunks(s):
        return (lane[s], crossed[s], beside(lane[s]), beside(crossed[s]))

    def up(s, after):
        given = w_down if s else None
        hidden[s], *down_held[:], after = block_hidden(
            chunks(s), sides[s], gate_held, up_held, after, given
        )
        return after

    def down(s, arrays, after, spare=lambda after: after, meanwhile=lambda after: after, outs=1):
        kept[s], sent, after = block_down(1, hidden[s], down_held, after)
        after = spare(after)
        *arrays, sent, after = tied([*arrays, sent], after)
        own[s], back[s], after = block_down(0, hidden[s], down_held, after)
        after = meanwhile(after)
        return *arrays, swap(s, beside(sent), after, outs)

    def swap(s, returned, after, outs=1):
        passed, after = summed([[kept[s]], [returned]], after, outs)
        swapped[s] = passed if s == 0 else [across(part) for part in passed]
        return after

    def exchange(s, after):
        sent, after = tied([back[s]], after)
        back[s] = beside(sent)
        return after

    def gather(s, after, outs=1):
        terms = [*travelling, swapped[s], [back[s]], [own[s]]]
        passed, after = summed(terms, after, outs)
        travelling[:] = [[along(part) for part in passed]]
        return after

    def spare_partner(after):
        kept[0], sent, after = block_down(1, hidden[0], down_held, after)
        first_sent[:] = [sent]
        return after

    def spare_own(after):
        own[0], back[0], after = block_down(0, hidden[0], down_held, after)
        return after

    travelling, kept, first_sent = [], [None] * chips, []
    token = up(0, token)
    depth = stream.shape[1] // 4
    cache_kept, sent, token = whole_call(
        rows_kernel,
        [placed_shape, placed_shape],
        [layer_input, attn_norm, side, kv_owner.T, w_kv],
        token,
        kinds=[pltpu.VMEM] * 4 + [pl.ANY],
        scratch=[
            pltpu.VMEM((2, depth, columns), jnp.bfloat16),
            pltpu.SemaphoreType.DMA((2,)),
        ],
        limit=5,
    )
    lane[2], crossed[1], sides[1], pair, token = tied([lane[2], crossed[1], sides[1], pair], token)
    sides[2:] = [side_at(pair, 2), side_at(pair, 3)]
    lane.append(along(lane[2]))
    crossed.append(across(lane[2]))
    token = up(1, token)
    lane[3], crossed[2], sent, *sides[2:], token = down(
        1, [lane[3], crossed[2], sent, *sides[2:]], token, spare_partner
    )
    arrived = across(sent)
    crossed.append(along(crossed[2]))
    token = exchange(1, token)
    token = up(2, token)
    crossed[3], arrived, first, token = down(
        2,
        [crossed[3], arrived, *first_sent],
        token,
        spare_own,
        functools.partial(gather, 1),
    )
    token = exchange(2, token)
    token = up(3, token)
    (token,) = down(3, [], token, meanwhile=functools.partial(gather, 2))
    token = exchange(3, token)
    token = swap(0, beside(first), token)
    token = exchange(0, token)
    kv_cache, token = whole_call(
        cache_kernel, [placed_shape], [cache_kept, arrived, k_norm], token
    )
    token = gather(3, token)
    last, token = tied(swapped[0], token)
    (moe_out,), _ = summed([*travelling, [across(last)], [back[0]], [own[0]]], token)
    return moe_out, kv_cache.reshape(1, 1, rows, columns)


def hidden_kernel(x_ref, wg_ref, wu_ref, scale_ref, weight_ref, out_ref):
    blocks, parts, rows, width = x_ref.shape
    gate = up = None
    for part in range(parts):
        x = x_ref[:, part].reshape(blocks * rows, width)
        depth = pl.ds(part * width, width)
        g = jnp.dot(x, wg_ref[0, depth], preferred_element_type=jnp.float32)
        u = jnp.dot(x, wu_ref[0, depth], preferred_element_type=jnp.float32)
        gate = g if gate is None else gate + g
        up = u if up is None else up + u
    out_ref[0] = silu_up(gate, up, scale_ref[...], weight_ref[0])


def hidden_of(x, w_gate, w_up, scale, weight):
    blocks, parts, rows, width = x.shape
    experts, depth, units = w_gate.shape
    tokens = blocks * rows
    tile = tile_of(units, 256)
    tiles = units // tile
    wspec = pl.BlockSpec((1, depth, tile), lambda e, f: (e, 0, f))
    return pl.pallas_call(
        hidden_kernel,
        grid=(experts, tiles),
        in_specs=[
            pl.BlockSpec(x.shape, lambda e, f: (0, 0, 0, 0)),
            wspec,
            wspec,
            pl.BlockSpec((tokens, 1), lambda e, f: (0, 0)),
            pl.BlockSpec((1, tokens, 1), lambda e, f: (e, 0, 0)),
        ],
        out_specs=pl.BlockSpec((1, tokens, tile), lambda e, f: (e, 0, f)),
        out_shape=jax.ShapeDtypeStruct((experts, tokens, units), jnp.bfloat16),
        compiler_params=pltpu.CompilerParams(vmem_limit_bytes=VMEM_LIMIT),
    )(x, w_gate, w_up, scale, weight)


def down_kernel(h_ref, w_ref, out_ref):
    blocks, _, rows, tile = out_ref.shape
    y = None
    for e in range(h_ref.shape[0]):
        term = jnp.dot(h_ref[e], w_ref[e], preferred_element_type=jnp.float32)
        y = term if y is None else y + term
    out_ref[:, 0] = y.astype(jnp.bfloat16).reshape(blocks, rows, tile)


def down_of(hidden, w_down, blocks, parts):
    experts, tokens, units = hidden.shape
    width = w_down.shape[2] // parts
    rows = tokens // blocks
    tile = tile_of(width, 512)
    tiles = width // tile
    return pl.pallas_call(
        down_kernel,
        grid=(parts * tiles,),
        in_specs=[
            pl.BlockSpec((experts, tokens, units), lambda n: (0, 0, 0)),
            pl.BlockSpec((experts, units, tile), lambda n: (0, 0, n)),
        ],
        out_specs=pl.BlockSpec(
            (blocks, 1, rows, tile), lambda n: (0, n // tiles, 0, n % tiles)
        ),
        out_shape=jax.ShapeDtypeStruct((blocks, parts, rows, width), jnp.bfloat16),
        compiler_params=pltpu.CompilerParams(vmem_limit_bytes=VMEM_LIMIT),
    )(hidden, w_down)


def plain_experts(rows_out, side, w_gate, w_up, w_down):
    tp_count, ep_count = lax.axis_size("tp"), lax.axis_size("ep")
    rows, width = rows_out.shape
    exp_local = w_gate.shape[0]
    gathered = lax.all_gather(rows_out, ("ep", "tp"), axis=0, tiled=False)
    gathered = gathered.reshape(ep_count, tp_count, rows, width)
    side = lax.all_gather(side, "ep", axis=1, tiled=True)
    first_expert = 1 + lax.axis_index("ep") * exp_local
    weight = lax.dynamic_slice_in_dim(side, first_expert, exp_local, 0)[:, :, None]
    hidden = hidden_of(gathered, w_gate, w_up, side[0][:, None], weight)
    partial = down_of(hidden, w_down, ep_count, tp_count)
    partial = partial.reshape(ep_count * tp_count, rows, width)
    return lax.psum_scatter(partial, ("ep", "tp"), scatter_dimension=0, tiled=False)


def per_device(
    layer_input,
    stream,
    expert_ids,
    kv_owner,
    attn_norm,
    moe_norm,
    k_norm,
    w_kv,
    router,
    w_gate,
    w_up,
    w_down,
):
    rows = layer_input.shape[0]
    tp_count = lax.axis_size("tp")
    tiled = w_gate.shape[2] % MXU == 0 and stream.shape[1] % (2 * MXU) == 0
    if tp_count == 2 and tiled and rows == 128 and lax.axis_size("ep") == 8:
        return ring_device(
            layer_input, stream, expert_ids, kv_owner, attn_norm, moe_norm, k_norm, w_kv, router,
            w_gate, w_up, w_down,
        )
    columns = 2 * KVH * HD
    expert_count = router.shape[1]
    first = layer_input.astype(jnp.float32)
    second = stream.astype(jnp.float32)

    rows_out = (second * moe_norm.astype(jnp.float32)).astype(jnp.bfloat16)

    logits = lax.dot_general(
        router, rows_out, (((0,), (1,)), ((), ())), preferred_element_type=jnp.float32
    )
    squares = jnp.stack([jnp.sum(first * first, 1), jnp.sum(second * second, 1)], 0)
    small = jnp.concatenate([squares, logits], 0)
    small = lax.psum(small, "tp")
    first_scale = lax.rsqrt(small[0] / D + EPS)
    second_scale = lax.rsqrt(small[1:2] / D + EPS)
    logits = small[2:] * second_scale
    expert_range = jnp.arange(expert_count, dtype=jnp.int32)
    chosen = jnp.any(expert_ids.T[None, :, :] == expert_range[:, None, None], 1)
    top = jnp.max(jnp.where(chosen, logits, -jnp.inf), 0, keepdims=True)
    weights = jnp.where(chosen, jnp.exp(jnp.where(chosen, logits - top, 0.0)), 0.0)
    weights = weights / jnp.sum(weights, 0, keepdims=True)
    fill = jnp.zeros((-(1 + expert_count) % 8, rows), jnp.float32)
    side = jnp.concatenate([second_scale, weights, fill], 0)

    attn_in = (first * attn_norm.astype(jnp.float32)).astype(jnp.bfloat16)
    kv = jnp.dot(attn_in, w_kv, preferred_element_type=jnp.float32) * first_scale[:, None]
    owner_cap = 2 * rows // tp_count
    owner = kv_owner[:, 0]
    owner_hot = (owner[:, None] == jnp.arange(tp_count, dtype=jnp.int32)[None, :]).astype(jnp.int32)
    owner_slot = jnp.sum(
        (jnp.cumsum(owner_hot, 0, dtype=jnp.int32) - owner_hot) * owner_hot, 1, dtype=jnp.int32
    )
    target = owner * owner_cap + owner_slot
    placing = target[None, :] == jnp.arange(tp_count * owner_cap, dtype=jnp.int32)[:, None]
    placed = jnp.dot(
        placing.astype(jnp.bfloat16), kv.astype(jnp.bfloat16), preferred_element_type=jnp.float32
    )
    placed = placed.astype(jnp.bfloat16).reshape(tp_count, owner_cap, columns)
    arrived = lax.all_to_all(placed, "tp", split_axis=0, concat_axis=0, tiled=True)
    heads = jnp.sum(arrived.astype(jnp.float32), 0)
    heads = heads.reshape(owner_cap, 2 * KVH, HD)
    keys = heads[:, :KVH]
    keys = keys * lax.rsqrt(jnp.mean(keys * keys, 2, keepdims=True) + EPS)
    keys = keys * k_norm.astype(jnp.float32)
    kv_cache = jnp.concatenate([keys, heads[:, KVH:]], 1).astype(jnp.bfloat16)
    kv_cache = kv_cache.reshape(1, 1, owner_cap, columns)

    moe_out = plain_experts(rows_out, side, w_gate, w_up, w_down)
    return (moe_out, kv_cache)


def solution(mesh):
    placed = (
        P(("group", "ep"), "tp"),
        P(("group", "ep"), "tp"),
        P(("group", "ep"), None),
        P(("group", "ep"), None),
        P("tp"),
        P("tp"),
        P(),
        P("tp", None),
        P("tp", None),
        P("ep", None, "tp"),
        P("ep", None, "tp"),
        P("ep", "tp", None),
    )
    return jax.shard_map(
        per_device,
        mesh=mesh,
        in_specs=placed,
        out_specs=(P(("group", "ep"), "tp"), P(("group", "ep"), "tp", None, None)),
        check_vma=False,
    )
```

```python
import functools

import jax
import jax.numpy as jnp
from jax import lax
from jax.experimental import pallas as pl
from jax.experimental.pallas import tpu as pltpu
from jax.sharding import PartitionSpec as P

D = 4096
KVH = 4
HD = 128
TOPK = 8


EPS = 1e-06
VMEM_LIMIT = 56 * 1024 * 1024
MXU = 256
SIDE = 8


def weight_work(rows, *weights):
    size = sum(w.size for w in weights)
    return pl.CostEstimate(flops=2 * rows * size, bytes_accessed=2 * size, transcendentals=0)


BRIEF = pl.CostEstimate(flops=1, bytes_accessed=1, transcendentals=0)


def tile_of(size, most):
    for candidate in range(most, 127, -128):
        if size % candidate == 0:
            return candidate
    return size


def silu_up(gate, up, scale, weight):
    gate = gate * scale
    up = up * scale
    return (gate / (1.0 + jnp.exp(-gate)) * up * weight).astype(jnp.bfloat16)


def column_of(side, index):
    lane = lax.broadcasted_iota(jnp.int32, side.shape, 1)
    return jnp.sum(jnp.where(lane == index, side, 0.0), 1, keepdims=True)


def in_vmem(count):
    return [pl.BlockSpec(memory_space=pltpu.VMEM)] * count


def whole_call(body, outs, operands, after=None, kinds=None, scratch=(), limit=2, work=BRIEF, same=None):
    kinds = kinds or [pltpu.VMEM] * len(operands)
    count = len(operands)

    token = jax.ShapeDtypeStruct((8, 128), jnp.float32)
    afters = [] if after is None else [after]

    def with_token(*refs):
        inputs, rest = refs[:count], refs[count + len(afters) :]
        results, spare = rest[: len(outs)], rest[len(outs) + 1 :]
        rest[len(outs)][...] = jnp.zeros((8, 128), jnp.float32)
        body(*inputs, *results, *spare)

    return pl.pallas_call(
        with_token,
        in_specs=[pl.BlockSpec(memory_space=kind) for kind in kinds]
        + [pl.BlockSpec(memory_space=pl.ANY)] * len(afters),
        out_specs=in_vmem(len(outs) + 1),
        out_shape=[*outs, token],
        scratch_shapes=scratch,
        compiler_params=pltpu.CompilerParams(vmem_limit_bytes=limit * 1024 * 1024),
        cost_estimate=work,
        input_output_aliases=same or {},
    )(*operands, *afters)


def copies_of(source_ref, held_refs, sem):
    return [
        pltpu.make_async_copy(source_ref.at[e], held_ref, sem.at[e])
        for e, held_ref in enumerate(held_refs)
    ]


def row_of(gain_ref):
    return gain_ref[...].astype(jnp.float32).reshape(1, -1)


def opening_kernel(x_ref, gain_ref, out_ref):
    out_ref[...] = (x_ref[...].astype(jnp.float32) * row_of(gain_ref)).astype(jnp.bfloat16)


def stats_kernel(first_ref, second_ref, rows_ref, router_ref, small_ref):
    tokens = first_ref.shape[0]
    squares = []
    for ref in (first_ref, second_ref):
        x = ref[...].astype(jnp.float32)
        squares.append(jnp.sum(x * x, 1, keepdims=True))
    squares = jnp.concatenate(squares + [jnp.zeros((tokens, 126), jnp.float32)], 1)
    small_ref[0:SIDE] = jnp.transpose(squares)[0:SIDE]
    small_ref[SIDE:] = lax.dot_general(
        router_ref[...],
        rows_ref[...],
        (((1,), (1,)), ((), ())),
        preferred_element_type=jnp.float32,
    )


def sides_kernel(mine_ref, other_ref, ids_ref, side_ref):
    small = mine_ref[...] + other_ref[...]
    scales = lax.rsqrt(small[0:SIDE] / D + EPS)
    logits = small[SIDE:] * scales[1:2]
    expert = lax.broadcasted_iota(jnp.int32, logits.shape, 0)
    ids = ids_ref[...]
    chosen = expert == ids[0:1]
    for k in range(1, ids.shape[0]):
        chosen = chosen | (expert == ids[k : k + 1])
    top = jnp.max(jnp.where(chosen, logits, -jnp.inf), 0, keepdims=True)
    weights = jnp.where(chosen, jnp.exp(jnp.where(chosen, logits - top, 0.0)), 0.0)
    side_ref[0:SIDE] = scales
    side_ref[SIDE:] = weights / jnp.sum(weights, 0, keepdims=True)


def rows_kernel(
    first_ref, gain_ref, side_ref, owner_ref, w_ref, kept_ref, sent_ref, piece_ref, piece_sem
):
    tokens = first_ref.shape[0]
    slots, depth, _ = piece_ref.shape
    pieces = w_ref.shape[0] // depth

    def fetch(n):
        return pltpu.make_async_copy(
            w_ref.at[pl.ds(n * depth, depth)], piece_ref.at[n % slots], piece_sem.at[n % slots]
        )

    for n in range(slots):
        fetch(n).start()
    attn_in = (first_ref[...].astype(jnp.float32) * row_of(gain_ref)).astype(jnp.bfloat16)
    kv = None
    for n in range(pieces):
        fetch(n).wait()
        term = jnp.dot(
            attn_in[:, n * depth : (n + 1) * depth],
            piece_ref[n % slots],
            preferred_element_type=jnp.float32,
        )
        kv = term if kv is None else kv + term
        if n + slots < pieces:
            fetch(n + slots).start()
    fill = jnp.zeros((tokens - SIDE, tokens), jnp.float32)
    scales = jnp.transpose(jnp.concatenate([side_ref[0:SIDE], fill], 0))
    kv = (kv * scales[:, 0:1]).astype(jnp.bfloat16)
    theirs = jnp.where(owner_ref[...] == lax.axis_index("tp"), 0, 1)
    hot = lax.broadcasted_iota(jnp.int32, (SIDE, tokens), 0) == theirs
    hot = jnp.where(hot, 1.0, 0.0)
    row = lax.broadcasted_iota(jnp.int32, (tokens, tokens), 0)
    column = lax.broadcasted_iota(jnp.int32, (tokens, tokens), 1)
    before = jnp.where(row < column, 1.0, 0.0).astype(jnp.bfloat16)
    earlier = jnp.dot(hot.astype(jnp.bfloat16), before, preferred_element_type=jnp.float32)
    slot = jnp.sum(earlier * hot, 0, keepdims=True).astype(jnp.int32)
    for side, out_ref in enumerate((kept_ref, sent_ref)):
        placing = jnp.where((slot == row) & (theirs == side), 1.0, 0.0).astype(jnp.bfloat16)
        out = jnp.dot(placing, kv, preferred_element_type=jnp.float32)
        out_ref[...] = out.astype(jnp.bfloat16)


def cache_kernel(kept_ref, arrived_ref, gain_ref, out_ref):
    gain = row_of(gain_ref)
    for head in range(2 * KVH):
        columns = slice(head * HD, (head + 1) * HD)
        x = kept_ref[:, columns].astype(jnp.float32) + arrived_ref[:, columns].astype(jnp.float32)
        if head < KVH:
            x = x * lax.rsqrt(jnp.mean(x * x, 1, keepdims=True) + EPS) * gain
        out_ref[:, columns] = x.astype(jnp.bfloat16)


def joined_kernel(first_ref, second_ref, out_ref):
    tokens = first_ref.shape[1]
    out_ref[:, :tokens] = first_ref[...]
    out_ref[:, tokens:] = second_ref[...]


def tied(arrays, after):
    count = len(arrays)
    anywhere = pl.BlockSpec(memory_space=pl.ANY)

    def kernel(*refs):
        refs[-1][...] = jnp.zeros((8, 128), jnp.float32)

    shapes = [jax.ShapeDtypeStruct(x.shape, x.dtype) for x in arrays]
    return pl.pallas_call(
        kernel,
        in_specs=[anywhere] * (count + 1),
        out_specs=[anywhere] * count + in_vmem(1),
        out_shape=[*shapes, jax.ShapeDtypeStruct((8, 128), jnp.float32)],
        input_output_aliases={n: n for n in range(count)},
        compiler_params=pltpu.CompilerParams(vmem_limit_bytes=1024 * 1024),
        cost_estimate=BRIEF,
    )(*arrays, after)


def sum_kernel(*refs):
    refs[-1][...] = total(*[ref[...] for ref in refs[:-1]])


def summed(terms, after, work=BRIEF):
    out = jax.ShapeDtypeStruct(terms[0].shape, jnp.bfloat16)
    return whole_call(sum_kernel, [out], terms, after, work=work)


def paired_products(rows, tiles):
    flat = [(t, k) for t, (steps, _) in enumerate(tiles) for k in range(len(steps))]

    def stage(index):
        t, k = flat[index]
        _, first_tile, second_tile = tiles[t][0][k]
        pltpu.matmul_push_rhs(first_tile(), index % 2, 0)
        pltpu.matmul_push_rhs(second_tile(), index % 2, 1)

    def run(*accs):
        def finish(t):
            first, second = accs[t % 2], accs[2 + t % 2]
            tiles[t][1](pltpu.matmul_pop(first), pltpu.matmul_pop(second))

        stage(0)
        for index, (t, k) in enumerate(flat):
            if index + 1 < len(flat):
                stage(index + 1)
            left = tiles[t][0][k][0]()
            pltpu.matmul_acc_lhs(accs[t % 2], left, index % 2)
            pltpu.matmul_acc_lhs(accs[2 + t % 2], left, index % 2)
            if t and k == 1:
                finish(t - 1)
        finish(len(tiles) - 1)

    kinds = [pltpu.ACC(unit)((rows, MXU), jnp.float32) for unit in (0, 0, 1, 1)]
    pl.run_scoped(run, *kinds)


def load_kernel(source_ref, *refs):
    *held_refs, sem = refs
    copies = copies_of(source_ref, held_refs, sem)
    for copy in copies:
        copy.start()
    for copy in copies:
        copy.wait()


def experts_in_vmem(w):
    return [pltpu.VMEM(w.shape[1:], w.dtype)] * w.shape[0]


def loaded(w, after):
    *held, after = whole_call(
        load_kernel,
        experts_in_vmem(w),
        [pltpu.with_memory_space_constraint(w, pltpu.HBM)],
        after,
        kinds=[pl.ANY],
        scratch=[pltpu.SemaphoreType.DMA((w.shape[0],))],
        limit=1,
        work=weight_work(1, w),
    )
    return held, after


def block_hidden_kernel(experts, *refs):
    own_ref, other_ref, sib_own_ref, sib_other_ref, side_ref, *refs = refs
    w_refs, refs = refs[: 2 * experts], refs[2 * experts :]
    copies = []
    if len(refs) > 2:
        source_ref, out_ref, *held_refs, x_ref, sem = refs
        copies = copies_of(source_ref, held_refs, sem)
    else:
        out_ref, x_ref = refs
    for copy in copies:
        copy.start()
    rows, width = own_ref.shape
    depth, units = w_refs[0].shape
    half = lax.axis_index("tp")
    first_expert = SIDE + lax.axis_index("ep") * experts
    mine = pl.ds(pl.multiple_of(half * width, width), width)
    theirs = pl.ds(pl.multiple_of((1 - half) * width, width), width)
    x_ref[0:rows, mine] = own_ref[...]
    x_ref[0:rows, theirs] = other_ref[...]
    x_ref[rows : 2 * rows, mine] = sib_own_ref[...]
    x_ref[rows : 2 * rows, theirs] = sib_other_ref[...]
    side = jnp.transpose(side_ref[...])
    scale = column_of(side, 1)

    def tile_of_units(e, tile):
        columns = pl.ds(tile * MXU, MXU)

        def step(k):
            part = pl.ds(k * MXU, MXU)
            return (
                lambda: x_ref[:, part],
                lambda: w_refs[e][part, columns],
                lambda: w_refs[experts + e][part, columns],
            )

        def finish(gate, up):
            weight = column_of(side, first_expert + e)
            out_ref[e, :, columns] = silu_up(gate, up, scale, weight)

        return [step(k) for k in range(depth // MXU)], finish

    tiles = [tile_of_units(e, tile) for e in range(experts) for tile in range(units // MXU)]
    paired_products(2 * rows, tiles)
    for copy in copies:
        copy.wait()


def block_hidden(chunks, side, gates, ups, after, w_down=None):
    rows, _ = chunks[0].shape
    experts, (depth, units) = len(gates), gates[0].shape
    outs = [jax.ShapeDtypeStruct((experts, 2 * rows, units), jnp.bfloat16)]
    operands, kinds = [*chunks, side, *gates, *ups], [pltpu.VMEM] * (5 + 2 * experts)
    scratch = [pltpu.VMEM((2 * rows, depth), jnp.bfloat16)]
    if w_down is not None:
        outs += experts_in_vmem(w_down)
        operands, kinds = [*operands, w_down], [*kinds, pl.ANY]
        scratch.append(pltpu.SemaphoreType.DMA((experts,)))
    work = weight_work(2 * rows, *gates, *ups)
    body = functools.partial(block_hidden_kernel, experts)
    return whole_call(body, outs, operands, after, kinds, scratch, 4, work)


def block_down_kernel(half, experts, h_ref, *refs):
    w_refs, (own_ref, sib_ref) = refs[:experts], refs[experts:]
    rows, width = own_ref.shape
    units = h_ref.shape[2]
    here = lax.axis_index("tp")
    first = (here + half - 2 * half * here) * width

    def tile_of_columns(tile):
        start = tile * (2 * MXU)

        def step(e, k):
            part = pl.ds(k * MXU, MXU)
            at = [pl.ds(pl.multiple_of(first + start + MXU * n, MXU), MXU) for n in (0, 1)]
            return (
                lambda: h_ref[e, :, part],
                lambda: w_refs[e][part, at[0]],
                lambda: w_refs[e][part, at[1]],
            )

        def finish(*products):
            for n, y in enumerate(products):
                columns = pl.ds(start + n * MXU, MXU)
                own_ref[:, columns] = y[:rows].astype(jnp.bfloat16)
                sib_ref[:, columns] = y[rows:].astype(jnp.bfloat16)

        return [step(e, k) for e in range(experts) for k in range(units // MXU)], finish

    paired_products(2 * rows, [tile_of_columns(n) for n in range(width // (2 * MXU))])


def block_down(half, hidden, w_down, after):
    _, tokens, _ = hidden.shape
    rows, width = tokens // 2, w_down[0].shape[1] // 2
    out = jax.ShapeDtypeStruct((rows, width), jnp.bfloat16)
    return whole_call(
        functools.partial(block_down_kernel, half, len(w_down)),
        [out, out],
        [hidden, *w_down],
        after,
        work=weight_work(rows, *w_down),
    )


def total(*terms):
    return sum(term.astype(jnp.float32) for term in terms).astype(jnp.bfloat16)


def ring_device(
    layer_input,
    stream,
    expert_ids,
    kv_owner,
    attn_norm,
    moe_norm,
    k_norm,
    w_kv,
    router,
    w_gate,
    w_up,
    w_down,
):
    ep_count = lax.axis_size("ep")
    chips = ep_count // 2
    forward = [(d, (d + 2) % ep_count) for d in range(ep_count)]
    siblings = [(d, d ^ 1) for d in range(ep_count)]
    along = functools.partial(lax.ppermute, axis_name="ep", perm=forward)
    beside = functools.partial(lax.ppermute, axis_name="ep", perm=siblings)
    across = functools.partial(lax.ppermute, axis_name="tp", perm=[(0, 1), (1, 0)])
    rows = stream.shape[0]
    columns = w_kv.shape[1]
    side_rows = SIDE + router.shape[1]
    row_shape = jax.ShapeDtypeStruct(stream.shape, jnp.bfloat16)
    small_shape = jax.ShapeDtypeStruct((side_rows, rows), jnp.float32)
    pair_shape = jax.ShapeDtypeStruct((side_rows, 2 * rows), jnp.float32)
    placed_shape = jax.ShapeDtypeStruct((rows, columns), jnp.bfloat16)
    layer_input, stream, moe_norm, w_kv, w_down = [
        pltpu.with_memory_space_constraint(x, pltpu.HBM)
        for x in (layer_input, stream, moe_norm, w_kv, w_down)
    ]

    rows_out, token = whole_call(
        opening_kernel, [row_shape], [stream, moe_norm], limit=8
    )
    lane, crossed = [rows_out, along(rows_out)], [across(rows_out)]

    small, token = whole_call(
        stats_kernel, [small_shape], [layer_input, stream, rows_out, router.T], token, limit=8
    )
    small_other = across(small)
    gate_held, token = loaded(w_gate, token)
    up_held, token = loaded(w_up, token)
    lane[1], crossed[0], small_other, token = tied([lane[1], crossed[0], small_other], token)
    lane.append(along(lane[1]))
    crossed.append(across(lane[1]))
    side, token = whole_call(
        sides_kernel, [small_shape], [small, small_other, expert_ids.T], token
    )
    side_other = beside(side)
    pair, token = whole_call(joined_kernel, [pair_shape], [side, side_other], token)

    def side_at(pair, s):
        ahead = [(d, (d + 2 * s) % ep_count) for d in range(ep_count)]
        return lax.ppermute(pair, "ep", ahead)

    sides = [pair, side_at(pair, 1), None, None]

    down_held = []
    hidden, own, back, swapped = [[None] * chips for _ in range(4)]

    def chunks(s):
        return (lane[s], crossed[s], beside(lane[s]), beside(crossed[s]))

    def up(s, after):
        given = w_down if s else None
        hidden[s], *down_held[:], after = block_hidden(
            chunks(s), sides[s], gate_held, up_held, after, given
        )
        return after

    def down(s, arrays, after, meanwhile=lambda after: after):
        kept, sent, after = block_down(1, hidden[s], down_held, after)
        *arrays, sent, after = tied([*arrays, sent], after)
        own[s], back[s], after = block_down(0, hidden[s], down_held, after)
        after = meanwhile(after)
        passed, after = summed([kept, beside(sent)], after)
        swapped[s] = across(passed)
        return (*arrays, after) if arrays else after

    def exchange(s, after):
        sent, after = tied([back[s]], after)
        back[s] = beside(sent)
        return after

    def gather(s, after):
        terms = [*travelling, swapped[s], back[s], own[s]]
        passed, after = summed(terms, after, weight_work(1, w_gate, w_up))
        travelling[:] = [along(passed)]
        return after

    travelling = []
    token = up(0, token)
    depth = stream.shape[1] // 4
    kept, sent, token = whole_call(
        rows_kernel,
        [placed_shape, placed_shape],
        [layer_input, attn_norm, side, kv_owner.T, w_kv],
        token,
        kinds=[pltpu.VMEM] * 4 + [pl.ANY],
        scratch=[
            pltpu.VMEM((2, depth, columns), jnp.bfloat16),
            pltpu.SemaphoreType.DMA((2,)),
        ],
        limit=5,
    )
    lane[2], crossed[1], sides[1], pair, token = tied([lane[2], crossed[1], sides[1], pair], token)
    sides[2:] = [side_at(pair, 2), side_at(pair, 3)]
    lane.append(along(lane[2]))
    crossed.append(across(lane[2]))
    token = up(1, token)
    lane[3], crossed[2], sent, *sides[2:], token = down(
        1, [lane[3], crossed[2], sent, *sides[2:]], token
    )
    arrived = across(sent)
    crossed.append(along(crossed[2]))
    token = exchange(1, token)
    token = up(2, token)
    crossed[3], arrived, token = down(
        2, [crossed[3], arrived], token, functools.partial(gather, 1)
    )
    token = exchange(2, token)
    token = up(3, token)
    token = down(3, [], token, functools.partial(gather, 2))
    token = exchange(3, token)
    kv_cache, token = whole_call(cache_kernel, [placed_shape], [kept, arrived, k_norm], token)
    token = down(0, [], token, functools.partial(gather, 3))
    token = exchange(0, token)
    moe_out, _ = summed([*travelling, swapped[0], back[0], own[0]], token)
    return moe_out, kv_cache.reshape(1, 1, rows, columns)


def hidden_kernel(x_ref, wg_ref, wu_ref, scale_ref, weight_ref, out_ref):
    blocks, parts, rows, width = x_ref.shape
    gate = up = None
    for part in range(parts):
        x = x_ref[:, part].reshape(blocks * rows, width)
        depth = pl.ds(part * width, width)
        g = jnp.dot(x, wg_ref[0, depth], preferred_element_type=jnp.float32)
        u = jnp.dot(x, wu_ref[0, depth], preferred_element_type=jnp.float32)
        gate = g if gate is None else gate + g
        up = u if up is None else up + u
    out_ref[0] = silu_up(gate, up, scale_ref[...], weight_ref[0])


def hidden_of(x, w_gate, w_up, scale, weight):
    blocks, parts, rows, width = x.shape
    experts, depth, units = w_gate.shape
    tokens = blocks * rows
    tile = tile_of(units, 256)
    tiles = units // tile
    wspec = pl.BlockSpec((1, depth, tile), lambda e, f: (e, 0, f))
    return pl.pallas_call(
        hidden_kernel,
        grid=(experts, tiles),
        in_specs=[
            pl.BlockSpec(x.shape, lambda e, f: (0, 0, 0, 0)),
            wspec,
            wspec,
            pl.BlockSpec((tokens, 1), lambda e, f: (0, 0)),
            pl.BlockSpec((1, tokens, 1), lambda e, f: (e, 0, 0)),
        ],
        out_specs=pl.BlockSpec((1, tokens, tile), lambda e, f: (e, 0, f)),
        out_shape=jax.ShapeDtypeStruct((experts, tokens, units), jnp.bfloat16),
        compiler_params=pltpu.CompilerParams(vmem_limit_bytes=VMEM_LIMIT),
    )(x, w_gate, w_up, scale, weight)


def down_kernel(h_ref, w_ref, out_ref):
    blocks, _, rows, tile = out_ref.shape
    y = None
    for e in range(h_ref.shape[0]):
        term = jnp.dot(h_ref[e], w_ref[e], preferred_element_type=jnp.float32)
        y = term if y is None else y + term
    out_ref[:, 0] = y.astype(jnp.bfloat16).reshape(blocks, rows, tile)


def down_of(hidden, w_down, blocks, parts):
    experts, tokens, units = hidden.shape
    width = w_down.shape[2] // parts
    rows = tokens // blocks
    tile = tile_of(width, 512)
    tiles = width // tile
    return pl.pallas_call(
        down_kernel,
        grid=(parts * tiles,),
        in_specs=[
            pl.BlockSpec((experts, tokens, units), lambda n: (0, 0, 0)),
            pl.BlockSpec((experts, units, tile), lambda n: (0, 0, n)),
        ],
        out_specs=pl.BlockSpec(
            (blocks, 1, rows, tile), lambda n: (0, n // tiles, 0, n % tiles)
        ),
        out_shape=jax.ShapeDtypeStruct((blocks, parts, rows, width), jnp.bfloat16),
        compiler_params=pltpu.CompilerParams(vmem_limit_bytes=VMEM_LIMIT),
    )(hidden, w_down)


def plain_experts(rows_out, side, w_gate, w_up, w_down):
    tp_count, ep_count = lax.axis_size("tp"), lax.axis_size("ep")
    rows, width = rows_out.shape
    exp_local = w_gate.shape[0]
    gathered = lax.all_gather(rows_out, ("ep", "tp"), axis=0, tiled=False)
    gathered = gathered.reshape(ep_count, tp_count, rows, width)
    side = lax.all_gather(side, "ep", axis=1, tiled=True)
    first_expert = 1 + lax.axis_index("ep") * exp_local
    weight = lax.dynamic_slice_in_dim(side, first_expert, exp_local, 0)[:, :, None]
    hidden = hidden_of(gathered, w_gate, w_up, side[0][:, None], weight)
    partial = down_of(hidden, w_down, ep_count, tp_count)
    partial = partial.reshape(ep_count * tp_count, rows, width)
    return lax.psum_scatter(partial, ("ep", "tp"), scatter_dimension=0, tiled=False)


def per_device(
    layer_input,
    stream,
    expert_ids,
    kv_owner,
    attn_norm,
    moe_norm,
    k_norm,
    w_kv,
    router,
    w_gate,
    w_up,
    w_down,
):
    rows = layer_input.shape[0]
    tp_count = lax.axis_size("tp")
    tiled = w_gate.shape[2] % MXU == 0 and stream.shape[1] % (2 * MXU) == 0
    if tp_count == 2 and tiled and rows == 128 and lax.axis_size("ep") == 8:
        return ring_device(
            layer_input, stream, expert_ids, kv_owner, attn_norm, moe_norm, k_norm, w_kv, router,
            w_gate, w_up, w_down,
        )
    columns = 2 * KVH * HD
    expert_count = router.shape[1]
    first = layer_input.astype(jnp.float32)
    second = stream.astype(jnp.float32)

    rows_out = (second * moe_norm.astype(jnp.float32)).astype(jnp.bfloat16)

    logits = lax.dot_general(
        router, rows_out, (((0,), (1,)), ((), ())), preferred_element_type=jnp.float32
    )
    squares = jnp.stack([jnp.sum(first * first, 1), jnp.sum(second * second, 1)], 0)
    small = jnp.concatenate([squares, logits], 0)
    small = lax.psum(small, "tp")
    first_scale = lax.rsqrt(small[0] / D + EPS)
    second_scale = lax.rsqrt(small[1:2] / D + EPS)
    logits = small[2:] * second_scale
    expert_range = jnp.arange(expert_count, dtype=jnp.int32)
    chosen = jnp.any(expert_ids.T[None, :, :] == expert_range[:, None, None], 1)
    top = jnp.max(jnp.where(chosen, logits, -jnp.inf), 0, keepdims=True)
    weights = jnp.where(chosen, jnp.exp(jnp.where(chosen, logits - top, 0.0)), 0.0)
    weights = weights / jnp.sum(weights, 0, keepdims=True)
    fill = jnp.zeros((-(1 + expert_count) % 8, rows), jnp.float32)
    side = jnp.concatenate([second_scale, weights, fill], 0)

    attn_in = (first * attn_norm.astype(jnp.float32)).astype(jnp.bfloat16)
    kv = jnp.dot(attn_in, w_kv, preferred_element_type=jnp.float32) * first_scale[:, None]
    owner_cap = 2 * rows // tp_count
    owner = kv_owner[:, 0]
    owner_hot = (owner[:, None] == jnp.arange(tp_count, dtype=jnp.int32)[None, :]).astype(jnp.int32)
    owner_slot = jnp.sum(
        (jnp.cumsum(owner_hot, 0, dtype=jnp.int32) - owner_hot) * owner_hot, 1, dtype=jnp.int32
    )
    target = owner * owner_cap + owner_slot
    placing = target[None, :] == jnp.arange(tp_count * owner_cap, dtype=jnp.int32)[:, None]
    placed = jnp.dot(
        placing.astype(jnp.bfloat16), kv.astype(jnp.bfloat16), preferred_element_type=jnp.float32
    )
    placed = placed.astype(jnp.bfloat16).reshape(tp_count, owner_cap, columns)
    arrived = lax.all_to_all(placed, "tp", split_axis=0, concat_axis=0, tiled=True)
    heads = jnp.sum(arrived.astype(jnp.float32), 0)
    heads = heads.reshape(owner_cap, 2 * KVH, HD)
    keys = heads[:, :KVH]
    keys = keys * lax.rsqrt(jnp.mean(keys * keys, 2, keepdims=True) + EPS)
    keys = keys * k_norm.astype(jnp.float32)
    kv_cache = jnp.concatenate([keys, heads[:, KVH:]], 1).astype(jnp.bfloat16)
    kv_cache = kv_cache.reshape(1, 1, owner_cap, columns)

    moe_out = plain_experts(rows_out, side, w_gate, w_up, w_down)
    return (moe_out, kv_cache)


def solution(mesh):
    placed = (
        P(("group", "ep"), "tp"),
        P(("group", "ep"), "tp"),
        P(("group", "ep"), None),
        P(("group", "ep"), None),
        P("tp"),
        P("tp"),
        P(),
        P("tp", None),
        P("tp", None),
        P("ep", None, "tp"),
        P("ep", None, "tp"),
        P("ep", "tp", None),
    )
    return jax.shard_map(
        per_device,
        mesh=mesh,
        in_specs=placed,
        out_specs=(P(("group", "ep"), "tp"), P(("group", "ep"), "tp", None, None)),
        check_vma=False,
    )
```
